32 devices in a mesh: gx: 4 (over x, core), gy: 8 (over z, y).
Axes of the slice: x: 2, y: 2, z: 4, core: 2. Of those that a mesh axis runs over, the one named last changes fastest.
Arguments:
- atom_feat: bfloat16 [4, 8, 32, 64], P('gx', 'gy'), may hold values from -6 to 6
- bond_feat: bfloat16 [4, 8, 32, 1024], P('gx', 'gy'), may hold values from -6 to 6
- neighbours: int32 [4, 8, 32, 16], P('gx', 'gy'), may hold values from 0 to 1023, as said below
- bond_dirs: float32 [2, 4, 8, 512], P(None, 'gx', 'gy'), may hold values from -3.140625 to 3.140625
- bond_in_weight: bfloat16 [192, 128], replicated, may hold values from -0.4375 to 0.4375
- bond_mix_weight: bfloat16 [64, 64], replicated, may hold values from -0.75 to 0.75
- pair_weight: bfloat16 [64, 256], replicated, may hold values from -0.75 to 0.75
- angle_weight: bfloat16 [64, 128], replicated, may hold values from -0.75 to 0.75
- pair_hidden_weight: bfloat16 [64, 128], replicated, may hold values from -0.75 to 0.75
- pair_out_weight: bfloat16 [64, 64], replicated, may hold values from -0.1875 to 0.1875
- atom_in_weight: bfloat16 [128, 128], replicated, may hold values from -0.5 to 0.5
- atom_out_weight: bfloat16 [64, 64], replicated, may hold values from -0.75 to 0.75
Outputs:
- atom_out: bfloat16 [4, 8, 32, 64], P('gx', 'gy')
- bond_out: bfloat16 [4, 8, 32, 1024], P('gx', 'gy')
The draws below stay inside these ranges and needn't reach their ends.
Inputs may be any that keep to these rules, and one draw needn't show every extreme that they name: Atom neighbours[i, p] lies in atom i's block or in one of the eight blocks next to it along gx and gy, wrapping round at the ends; atom neighbours[i, p] has atom i at slot 15 - p. Every block has the same numbers of bonds pointing into each of these nine blocks, at most 64, and exactly 64 into itself.
All inputs are finite; a program needn't handle non-finite values.
Results may differ from the reference program's by a relative error of at most 0.008.
Values may be sent and summed in bfloat16 or wider, within the bound.
No kernel may reach another device: no remote copies, remote signals or barrier semaphores. Data moves between devices by JAX's collectives and lax.ppermute only.
A program may use at most 64 MiB of HBM per device.

```python
import math
import jax
import jax.numpy as jnp
from jax import lax

D = 64
ANG = 64
SLOTS = 16
ATOM_DEV = 32
ATOMS = 1024
N_GX = 4
N_GY = 8


def permutations(key, copies, length):
    subkeys = jax.random.split(key, copies)
    return jax.vmap(lambda single: jax.random.permutation(single, length))(subkeys).astype(jnp.int32)


def draw_neighbours(key, part):
    halves = SLOTS // 2
    blocks = N_GX * N_GY
    layout = permutations(jax.random.fold_in(key, 101), halves, ATOM_DEV)
    before = permutations(jax.random.fold_in(key, 202), halves * blocks, ATOM_DEV).reshape(halves, blocks, ATOM_DEV)
    after = permutations(jax.random.fold_in(key, 303), halves * blocks, ATOM_DEV).reshape(halves, blocks, ATOM_DEV)
    heading = layout % 9
    step_first = jnp.broadcast_to((heading // 3 - 1)[:, None, :], (halves, blocks, ATOM_DEV))
    step_second = jnp.broadcast_to((heading % 3 - 1)[:, None, :], (halves, blocks, ATOM_DEV))
    owners = jnp.arange(blocks, dtype=jnp.int32)
    owner_first = (owners // N_GY)[None, :, None]
    owner_second = (owners % N_GY)[None, :, None]
    moved_first = jnp.take_along_axis(step_first, before, axis=2)
    moved_second = jnp.take_along_axis(step_second, before, axis=2)
    target_block = (owner_first + moved_first + N_GX) % N_GX * N_GY + (owner_second + moved_second + N_GY) % N_GY
    landing = jnp.take_along_axis(after.reshape(halves, blocks * ATOM_DEV), (target_block * ATOM_DEV + before).reshape(halves, blocks * ATOM_DEV), axis=1).reshape(halves, blocks, ATOM_DEV)
    forward = target_block * ATOM_DEV + landing
    undo_after = jnp.argsort(after, axis=2, stable=True).astype(jnp.int32)
    undo_before = jnp.argsort(before, axis=2, stable=True).astype(jnp.int32)
    back_first = jnp.take_along_axis(step_first, undo_after, axis=2)
    back_second = jnp.take_along_axis(step_second, undo_after, axis=2)
    source_block = (owner_first - back_first + N_GX) % N_GX * N_GY + (owner_second - back_second + N_GY) % N_GY
    anchor = jnp.take_along_axis(undo_before.reshape(halves, blocks * ATOM_DEV), (source_block * ATOM_DEV + undo_after).reshape(halves, blocks * ATOM_DEV), axis=1).reshape(halves, blocks, ATOM_DEV)
    backward = source_block * ATOM_DEV + anchor
    table = jnp.concatenate([jnp.transpose(forward, (1, 2, 0)), jnp.transpose(backward[::-1], (1, 2, 0))], axis=2)
    return table.reshape(N_GX, N_GY, ATOM_DEV, SLOTS).astype(jnp.int32)


def block_levels(own_key, shape, cuts, least, top_value):
    def one(dim, parts):
        steps = jax.random.uniform(jax.random.fold_in(jax.random.fold_in(own_key, 6), dim), (parts,), jnp.float32, least / len(cuts), top_value / len(cuts))
        return jnp.repeat(jnp.exp(steps), shape[dim] // parts).reshape((-1,) + (1,) * (len(shape) - dim - 1))

    loudness = one(*cuts[0])
    for cut in cuts[1:]:
        loudness = loudness * one(*cut)
    return loudness


def centred(rng, shape, deviation, reach, cuts=(), held_as=jnp.bfloat16):
    array = jax.random.normal(rng, shape, jnp.float32) * deviation
    if len(cuts) > 0:
        array = block_levels(rng, shape, cuts, -0.22, 0.18) * array
    return jnp.clip(array, min=-reach, max=reach).astype(held_as)


def setup_inputs(seed: int = 0) -> dict:
    key_list = jax.random.split(jax.random.key(seed), 13)
    atom_feat = centred(key_list[0], (N_GX, N_GY, ATOM_DEV, D), 1.0, 6.0, ((0, 4), (1, 8)))
    bond_feat = centred(key_list[1], (N_GX, N_GY, ATOM_DEV, SLOTS * D), 1.0, 6.0, ((0, 4), (1, 8)))
    neighbours = draw_neighbours(jax.random.fold_in(key_list[12], 71), 0)
    bond_dirs = jnp.clip(jax.random.uniform(key_list[3], (2, N_GX, N_GY, ATOM_DEV * SLOTS), jnp.float32, -3.140625, 3.140625), -3.140625, 3.140625)
    bond_in_weight = centred(key_list[4], (3 * D, 2 * D), (3 * D) ** -0.5, 0.4375)
    bond_mix_weight = centred(key_list[5], (D, D), D ** -0.5, 0.75)
    pair_weight = centred(key_list[6], (D, 4 * D), D ** -0.5, 0.75)
    angle_weight = centred(key_list[7], (ANG, 2 * D), ANG ** -0.5, 0.75)
    pair_hidden_weight = centred(key_list[8], (D, 2 * D), D ** -0.5, 0.75)
    pair_out_weight = centred(key_list[9], (D, D), (SLOTS * D) ** -0.5, 0.1875)
    atom_in_weight = centred(key_list[10], (2 * D, 2 * D), (2 * D) ** -0.5, 0.5)
    atom_out_weight = centred(key_list[11], (D, D), D ** -0.5, 0.75)
    return {"atom_feat": atom_feat, "bond_feat": bond_feat, "neighbours": neighbours, "bond_dirs": bond_dirs, "bond_in_weight": bond_in_weight, "bond_mix_weight": bond_mix_weight, "pair_weight": pair_weight, "angle_weight": angle_weight, "pair_hidden_weight": pair_hidden_weight, "pair_out_weight": pair_out_weight, "atom_in_weight": atom_in_weight, "atom_out_weight": atom_out_weight}


def gated(values, half_width):
    return jax.nn.silu(values[..., :half_width]) * jax.nn.sigmoid(values[..., half_width:])


def chebyshev(cosine, degrees):
    before = jnp.ones_like(cosine)
    current = cosine
    series = [cosine]
    for degree in range(degrees - 1):
        following = 2.0 * cosine * current - before
        series.append(following)
        before, current = current, following
    return jnp.stack(series, axis=-1)


def pair_sums(projected, unit_vec, angle_weight, pair_hidden_weight):
    feature = projected.shape[-1] // 4
    cosine = jnp.sum(unit_vec[:, :, :, None] * unit_vec[:, :, None, :], axis=0)
    angular = chebyshev(cosine, angle_weight.shape[0]).astype(jnp.bfloat16)
    atom_group, slot_count = cosine.shape[0], cosine.shape[1]
    mixture = jnp.dot(angular.reshape(-1, angular.shape[-1]), angle_weight, preferred_element_type=jnp.float32)
    mixture = mixture.reshape(atom_group, slot_count, slot_count, 2 * feature)
    mixture = mixture + projected[:, :, None, :2 * feature] + projected[:, None, :, 2 * feature:]
    first_pair = gated(mixture, feature).astype(jnp.bfloat16)
    second = jnp.dot(first_pair.reshape(-1, feature), pair_hidden_weight, preferred_element_type=jnp.float32)
    second = second.reshape(atom_group, slot_count, slot_count, 2 * feature)
    return jnp.sum(gated(second, feature), axis=2)


def reference(atom_feat, bond_feat, neighbours, bond_dirs, bond_in_weight, bond_mix_weight, pair_weight, angle_weight, pair_hidden_weight, pair_out_weight, atom_in_weight, atom_out_weight):
    atom_rows = atom_feat.reshape(ATOMS, D)
    bond_rows = bond_feat.reshape(ATOMS * SLOTS, D)
    targets = neighbours.reshape(ATOMS * SLOTS)
    source = jnp.repeat(atom_rows, SLOTS, axis=0)
    far_ends = atom_rows[targets]
    joined = jnp.concatenate([source, far_ends, bond_rows], axis=1)
    hidden_bond = gated(jnp.dot(joined, bond_in_weight, preferred_element_type=jnp.float32), D).astype(jnp.bfloat16)
    bond_new = (bond_rows.astype(jnp.float32) + jnp.dot(hidden_bond, bond_mix_weight, preferred_element_type=jnp.float32)).astype(jnp.bfloat16)
    slot_index = jnp.arange(ATOMS * SLOTS, dtype=jnp.int32) % SLOTS
    reverse = targets * SLOTS + (SLOTS - 1 - slot_index)
    bond_avg = ((bond_new.astype(jnp.float32) + bond_new[reverse].astype(jnp.float32)) * 0.5).astype(jnp.bfloat16)
    projected = jnp.dot(bond_avg, pair_weight, preferred_element_type=jnp.float32).reshape(ATOMS, SLOTS, 4 * D)
    polar = bond_dirs[0].reshape(ATOMS, SLOTS)
    azimuth = bond_dirs[1].reshape(ATOMS, SLOTS)
    unit_vec = jnp.stack([jnp.sin(polar) * jnp.cos(azimuth), jnp.sin(polar) * jnp.sin(azimuth), jnp.cos(polar)])
    group_size = math.gcd(ATOMS, 512)
    blocks = ATOMS // group_size

    def one_block(pieces):
        return pair_sums(pieces[0], pieces[1], angle_weight, pair_hidden_weight)

    pair_total = lax.map(one_block, (projected.reshape(blocks, group_size, SLOTS, 4 * D), unit_vec.reshape(3, blocks, group_size, SLOTS).transpose(1, 0, 2, 3)))
    pair_sum = pair_total.reshape(ATOMS * SLOTS, D).astype(jnp.bfloat16)
    bond_out = (bond_avg.astype(jnp.float32) + jnp.dot(pair_sum, pair_out_weight, preferred_element_type=jnp.float32)).astype(jnp.bfloat16)
    pooled = jnp.mean(bond_out.astype(jnp.float32).reshape(ATOMS, SLOTS, D), axis=1).astype(jnp.bfloat16)
    atom_joined = jnp.concatenate([atom_rows, pooled], axis=1)
    atom_hidden = gated(jnp.dot(atom_joined, atom_in_weight, preferred_element_type=jnp.float32), D).astype(jnp.bfloat16)
    atom_out = (atom_rows.astype(jnp.float32) + jnp.dot(atom_hidden, atom_out_weight, preferred_element_type=jnp.float32)).astype(jnp.bfloat16)
    return atom_out.reshape(N_GX, N_GY, ATOM_DEV, D), bond_out.reshape(N_GX, N_GY, ATOM_DEV, SLOTS * D)
```

```python
import functools

import jax
import jax.numpy as jnp
from jax import lax
from jax.experimental import pallas as pl
from jax.experimental.pallas import tpu as pltpu
from jax.sharding import PartitionSpec as P

F32 = jnp.float32
BF16 = jnp.bfloat16
CAP = 64


def quotient(values, size):
    if size & (size - 1) == 0:
        return values >> (size.bit_length() - 1)
    return lax.div(values, jnp.int32(size))


def remainder(values, size):
    if size & (size - 1) == 0:
        return values & (size - 1)
    return lax.rem(values, jnp.int32(size))


def step_code(owner, home, extent, receives):
    step = remainder(owner - home + 1 + extent, extent)
    if extent % 2 == 0:
        first = remainder(home, 2) == 0
        ahead = jnp.where(first, 2, 0)
    else:
        ahead = 0 if receives else 2
    return jnp.where(step == 1, 0, jnp.where(step == ahead, 1, 2))


def partners(extent):
    if extent % 2 == 0:
        one = [(i, i ^ 1) for i in range(extent)]
        two = [(i, ((i + 1) ^ 1) - 1) for i in range(extent)]
        two = [(i, j % extent) for i, j in two]
        return one, two
    return (
        [(i, (i + 1) % extent) for i in range(extent)],
        [((i + 1) % extent, i) for i in range(extent)],
    )


def own_rows(atom_ref, bond_ref, slots):
    atom = atom_ref[0, 0].astype(F32)
    feature = atom.shape[1]
    rows = []
    for slot in range(slots):
        bond = bond_ref[0, 0, :, slot * feature : (slot + 1) * feature].astype(F32)
        rows.append(jnp.concatenate([atom, bond], axis=1))
    return jnp.concatenate(rows, axis=0).astype(BF16)


def pack_kernel(extents, home_ref, targets_ref, atom_ref, bond_ref, own_ref, one_ref, two_ref):
    atoms = atom_ref.shape[2]
    bonds = targets_ref.shape[1]
    slots = bonds // atoms
    lanes = 128
    groups = bonds // lanes
    owner = quotient(targets_ref[...], atoms)
    code_x = step_code(quotient(owner, extents[1]), home_ref[0], extents[0], False)
    code_y = step_code(remainder(owner, extents[1]), home_ref[1], extents[1], False)
    code = 3 * code_x + code_y
    rows = lax.broadcasted_iota(jnp.int32, (16, lanes), 0)
    marks = [rows == code[:, g * lanes : (g + 1) * lanes] for g in range(groups)]
    stacked = jnp.concatenate([m.astype(F32) for m in marks], axis=0).astype(BF16)
    before = lax.broadcasted_iota(jnp.int32, (lanes, 2 * lanes), 0)
    after = lax.broadcasted_iota(jnp.int32, (lanes, 2 * lanes), 1)
    sums = jnp.where((before < after) | (after >= lanes), 1.0, 0.0).astype(BF16)
    counted = jnp.dot(stacked, sums, preferred_element_type=F32)
    place = []
    earlier = jnp.zeros((16, lanes), F32)
    for g in range(groups):
        part = counted[g * 16 : (g + 1) * 16]
        place.append(
            jnp.sum(jnp.where(marks[g], part[:, :lanes] + earlier, 0.0), axis=0, keepdims=True)
        )
        earlier = earlier + part[:, lanes:]
    place = jnp.concatenate(place, axis=1).astype(jnp.int32) + CAP * code
    values = own_rows(atom_ref, bond_ref, slots)
    for third, ref in enumerate((own_ref, one_ref, two_ref)):
        spot = lax.broadcasted_iota(jnp.int32, (3 * CAP, bonds), 0) + 3 * CAP * third
        chosen = jnp.where(spot == place, 1.0, 0.0).astype(BF16)
        ref[...] = jnp.dot(chosen, values, preferred_element_type=F32).astype(BF16)


def basis_kernel(atoms, dirs_ref, basis_ref):
    slots, degrees, bonds = basis_ref.shape
    angles = dirs_ref[...]
    sines = jnp.sin(angles)
    cosines = jnp.cos(angles)
    parts = (
        sines[0:1] * cosines[1:2],
        sines[0:1] * sines[1:2],
        cosines[0:1],
    )
    unit = [jnp.broadcast_to(part, (8, bonds)) for part in parts]
    row = lax.broadcasted_iota(jnp.int32, (8, bonds), 0)
    for diagonal in range(slots):
        if diagonal == 0:
            cosine = unit[0] * unit[0] + unit[1] * unit[1] + unit[2] * unit[2]
        else:
            shift = bonds - atoms * diagonal
            turned = [pltpu.roll(part, shift, 1) for part in unit]
            cosine = unit[0] * turned[0] + unit[1] * turned[1] + unit[2] * turned[2]
        series = [jnp.ones_like(cosine), cosine]
        double = cosine + cosine
        for _ in range(7):
            series.append(double * series[-1] - series[-2])
        lower = series[7]
        upper = series[1]
        for index in range(1, 8):
            lower = jnp.where(row == index, series[7 - index], lower)
            upper = jnp.where(row == index, series[1 + index], upper)
        double = series[8] + series[8]
        blocks = [lower, upper]
        for _ in range(degrees // 8 - 1):
            blocks.append(double * blocks[-1] - blocks[-2])
        basis_ref[diagonal] = jnp.concatenate(blocks[1:], axis=0).astype(BF16)


def prepare_kernel(
    extents,
    home_ref,
    targets_ref,
    atom_ref,
    bond_ref,
    bond_in_ref,
    bond_mix_ref,
    pair_ref,
    angle_ref,
    pair_hidden_ref,
    pair_out_ref,
    atom_in_ref,
    atom_out_ref,
    chosen_ref,
    values_ref,
    near_ref,
    far_weight_ref,
    mix_weight_ref,
    pair_weight_ref,
    angle_weight_ref,
    hidden_weight_ref,
    out_weight_ref,
    atom_in_weight_ref,
    atom_out_weight_ref,
):
    atoms = atom_ref.shape[2]
    feature = atom_ref.shape[3]
    bonds = targets_ref.shape[1]
    slots = bonds // atoms
    targets = targets_ref[...]
    owner = quotient(targets, atoms)
    code_x = step_code(quotient(owner, extents[1]), home_ref[0], extents[0], True)
    code_y = step_code(remainder(owner, extents[1]), home_ref[1], extents[1], True)
    code = 3 * code_y + code_x
    bond = lax.broadcasted_iota(jnp.int32, (1, bonds), 1)
    far = (slots - 1 - quotient(bond, atoms)) * atoms + remainder(targets, atoms)
    base = (code * bonds).astype(F32)
    key = base + far.astype(F32)
    column = jnp.broadcast_to(key, (128, bonds)).T
    place = []
    for group in range(bonds // 128):
        here = slice(group * 128, (group + 1) * 128)
        inside = (column < key[:, here]) & (column >= base[:, here])
        place.append(jnp.sum(jnp.where(inside, 1.0, 0.0), axis=0, keepdims=True))
    place = jnp.concatenate(place, axis=1).astype(jnp.int32) + CAP * code
    spot = lax.broadcasted_iota(jnp.int32, (9 * CAP, bonds), 0)
    chosen_ref[...] = jnp.where(spot == place, 1.0, 0.0).astype(BF16)

    values = own_rows(atom_ref, bond_ref, slots).astype(F32).T.astype(BF16)
    values_ref[...] = values

    def turned(weight, scale):
        return (weight * scale).T.astype(BF16)

    weight = bond_in_ref[...].astype(F32)
    source, other, own = (weight[k * feature : (k + 1) * feature] for k in range(3))
    empty = jnp.zeros((feature, feature), F32)

    def crossed(left, right):
        return jnp.concatenate(
            [left[:, :feature], right[:, :feature], left[:, feature:], right[:, feature:]], axis=1
        )

    blank = jnp.zeros_like(own)
    near = jnp.concatenate([crossed(source, other), crossed(own, blank)], axis=0)
    away = jnp.concatenate([crossed(other, source), crossed(blank, own)], axis=0)
    near_ref[...] = jnp.dot(turned(near, 0.5), values, preferred_element_type=F32)
    far_weight_ref[...] = turned(away, 0.5)
    mix = bond_mix_ref[...].astype(F32)
    mix = jnp.concatenate(
        [jnp.concatenate([mix, empty], axis=1), jnp.concatenate([empty, mix], axis=1)], axis=0
    )
    mix_weight_ref[...] = turned(mix, 0.5)
    pair_weight_ref[...] = turned(pair_ref[...].astype(F32), 0.5)
    angle_weight_ref[...] = turned(angle_ref[...].astype(F32), 0.5)
    hidden_weight_ref[...] = turned(pair_hidden_ref[...].astype(F32), 0.25)
    out_weight_ref[...] = turned(pair_out_ref[...].astype(F32), 0.5)
    atom_in_weight_ref[...] = turned(atom_in_ref[...].astype(F32), 0.5)
    atom_out_weight_ref[...] = turned(atom_out_ref[...].astype(F32), 0.5)


def doubled_gate(values):
    half = values.shape[0] // 2
    return values[:half] * (1.0 + jnp.tanh(values[:half])) * (1.0 + jnp.tanh(values[half:]))


def main_kernel(
    own_ref,
    one_ref,
    two_ref,
    three_ref,
    four_ref,
    basis_ref,
    chosen_ref,
    values_ref,
    near_ref,
    far_weight_ref,
    mix_weight_ref,
    pair_weight_ref,
    angle_weight_ref,
    hidden_weight_ref,
    out_weight_ref,
    atom_in_weight_ref,
    atom_out_weight_ref,
    atom_result_ref,
    bond_result_ref,
    first_ref,
    second_ref,
):
    slots, degrees, bonds = basis_ref.shape
    atoms = bonds // slots
    feature = values_ref.shape[0] // 2
    received = jnp.concatenate(
        [own_ref[0:CAP], one_ref[0:CAP], two_ref[0:CAP], three_ref[...], four_ref[...]], axis=0
    )
    received = received.astype(F32).T.astype(BF16)
    far = jnp.dot(received, chosen_ref[...], preferred_element_type=F32)
    incoming = near_ref[...] + jnp.dot(
        far_weight_ref[...], far.astype(BF16), preferred_element_type=F32
    )
    hidden = doubled_gate(incoming).astype(BF16)
    mixed = jnp.dot(mix_weight_ref[...], hidden, preferred_element_type=F32)
    ahead = (values_ref[feature:].astype(F32) + mixed[:feature]).astype(BF16).astype(F32)
    back = (far[feature:] + mixed[feature:]).astype(BF16).astype(F32)
    average = ((ahead + back) * 0.5).astype(BF16)
    projected = jnp.dot(pair_weight_ref[...], average, preferred_element_type=F32)
    first_ref[...] = projected[: 2 * feature]
    second = projected[2 * feature :]
    per_group = 128 // atoms
    for turn in range(per_group):
        second_ref[turn] = second if turn == 0 else pltpu.roll(second, bonds - atoms * turn, 1)
    width = 256
    blocks = bonds // 128
    angle_weight = angle_weight_ref[...]
    hidden_weight = hidden_weight_ref[...]
    totals = []
    for start in range(0, bonds, width):
        total = jnp.zeros((feature, width), F32)
        for diagonal in range(slots):
            turn, skip = diagonal % per_group, diagonal // per_group
            pieces = [
                second_ref[turn, :, pl.ds(128 * ((start // 128 + k + skip) % blocks), 128)]
                for k in range(width // 128)
            ]
            mixture = jnp.dot(
                angle_weight,
                basis_ref[diagonal, :, pl.ds(start, width)],
                preferred_element_type=F32,
            )
            mixture = mixture + (first_ref[:, pl.ds(start, width)] + jnp.concatenate(pieces, axis=1))
            pair = doubled_gate(mixture).astype(BF16)
            total = total + doubled_gate(
                jnp.dot(hidden_weight, pair, preferred_element_type=F32)
            )
        totals.append(total)
    pair_sum = jnp.concatenate(totals, axis=1).astype(BF16)
    bond_out = (
        average.astype(F32) + jnp.dot(out_weight_ref[...], pair_sum, preferred_element_type=F32)
    ).astype(BF16).astype(F32)
    rows = bond_out.T.astype(BF16)
    for slot in range(slots):
        bond_result_ref[0, 0, :, slot * feature : (slot + 1) * feature] = rows[
            slot * atoms : (slot + 1) * atoms
        ]
    pooled = bond_out[:, 0:128]
    for block in range(1, blocks):
        pooled = pooled + bond_out[:, block * 128 : (block + 1) * 128]
    shift = 64
    while shift >= atoms:
        pooled = pooled + pltpu.roll(pooled, shift, 1)
        shift //= 2
    pooled = (pooled * (1.0 / slots)).astype(BF16)
    atom = values_ref[0:feature, 0:128]
    joined = jnp.concatenate([atom, pooled], axis=0)
    atom_hidden = doubled_gate(
        jnp.dot(atom_in_weight_ref[...], joined, preferred_element_type=F32)
    ).astype(BF16)
    atom_new = atom.astype(F32) + jnp.dot(
        atom_out_weight_ref[...], atom_hidden, preferred_element_type=F32
    )
    atom_result_ref[0, 0] = atom_new.T[0:atoms].astype(BF16)


def per_device(
    atom_feat,
    bond_feat,
    neighbours,
    bond_dirs,
    bond_in_weight,
    bond_mix_weight,
    pair_weight,
    angle_weight,
    pair_hidden_weight,
    pair_out_weight,
    atom_in_weight,
    atom_out_weight,
):
    atoms, feature = atom_feat.shape[2], atom_feat.shape[3]
    slots = neighbours.shape[3]
    bonds = atoms * slots
    degrees = angle_weight.shape[0]
    extents = (lax.axis_size("gx"), lax.axis_size("gy"))
    home = jnp.stack([lax.axis_index("gx"), lax.axis_index("gy")]).astype(jnp.int32)
    targets = neighbours[0, 0].T.reshape(1, bonds)
    dirs = bond_dirs[:, 0, 0].reshape(2, atoms, slots).transpose(0, 2, 1).reshape(2, bonds)
    smem = pl.BlockSpec(memory_space=pltpu.SMEM)
    vmem = pl.BlockSpec(memory_space=pltpu.VMEM)
    params = pltpu.CompilerParams(vmem_limit_bytes=32 * 2**20)

    def shaped(shape, dtype):
        return jax.ShapeDtypeStruct(shape, dtype)

    payload = shaped((3 * CAP, 2 * feature), BF16)
    own, one, two = pl.pallas_call(
        functools.partial(pack_kernel, extents),
        out_shape=(payload, payload, payload),
        in_specs=[smem, vmem, vmem, vmem],
        out_specs=(vmem, vmem, vmem),
        compiler_params=params,
        name="pack",
    )(home, targets, atom_feat, bond_feat)
    first, second = partners(extents[0])
    one = lax.ppermute(one, "gx", first)
    two = lax.ppermute(two, "gx", second)
    basis = pl.pallas_call(
        functools.partial(basis_kernel, atoms),
        out_shape=shaped((slots, degrees, bonds), BF16),
        in_specs=[vmem],
        out_specs=vmem,
        compiler_params=params,
        cost_estimate=pl.CostEstimate(flops=4 * 2**20, bytes_accessed=2**20, transcendentals=4096),
        name="basis",
    )(dirs)
    first, second = partners(extents[1])
    near = jnp.concatenate([x[CAP : 2 * CAP] for x in (own, one, two)], axis=0)
    away = jnp.concatenate([x[2 * CAP :] for x in (own, one, two)], axis=0)
    three = lax.ppermute(near, "gy", first)
    four = lax.ppermute(away, "gy", second)
    weights = (
        shaped((4 * feature, 2 * feature), BF16),
        shaped((2 * feature, 2 * feature), BF16),
        shaped((4 * feature, feature), BF16),
        shaped((2 * feature, degrees), BF16),
        shaped((2 * feature, feature), BF16),
        shaped((feature, feature), BF16),
        shaped((2 * feature, 2 * feature), BF16),
        shaped((feature, feature), BF16),
    )
    prepared = pl.pallas_call(
        functools.partial(prepare_kernel, extents),
        out_shape=(
            shaped((9 * CAP, bonds), BF16),
            shaped((2 * feature, bonds), BF16),
            shaped((4 * feature, bonds), F32),
        )
        + weights,
        in_specs=[smem] + [vmem] * 11,
        out_specs=(vmem,) * 11,
        compiler_params=params,
        cost_estimate=pl.CostEstimate(flops=64 * 2**20, bytes_accessed=2**21, transcendentals=0),
        name="prepare",
    )(
        home,
        targets,
        atom_feat,
        bond_feat,
        bond_in_weight,
        bond_mix_weight,
        pair_weight,
        angle_weight,
        pair_hidden_weight,
        pair_out_weight,
        atom_in_weight,
        atom_out_weight,
    )
    return pl.pallas_call(
        main_kernel,
        out_shape=(shaped(atom_feat.shape, BF16), shaped(bond_feat.shape, BF16)),
        in_specs=[vmem] * 17,
        out_specs=(vmem, vmem),
        scratch_shapes=[
            pltpu.VMEM((2 * feature, bonds), F32),
            pltpu.VMEM((128 // atoms, 2 * feature, bonds), F32),
        ],
        compiler_params=params,
        cost_estimate=pl.CostEstimate(
            flops=400 * 2**20, bytes_accessed=2**22, transcendentals=2**21
        ),
        name="main",
    )(own, one, two, three, four, basis, *prepared)


def solution(mesh):
    placed = (
        P("gx", "gy", None, None),
        P("gx", "gy", None, None),
        P("gx", "gy", None, None),
        P(None, "gx", "gy", None),
        P(),
        P(),
        P(),
        P(),
        P(),
        P(),
        P(),
        P(),
    )
    return jax.shard_map(
        per_device,
        mesh=mesh,
        in_specs=placed,
        out_specs=(P("gx", "gy", None, None), P("gx", "gy", None, None)),
        check_vma=False,
    )
```

```python
import functools

import jax
import jax.numpy as jnp
from jax import lax
from jax.experimental import pallas as pl
from jax.experimental.pallas import tpu as pltpu
from jax.sharding import PartitionSpec as P

F32 = jnp.float32
BF16 = jnp.bfloat16
CAP = 64


def quotient(values, size):
    if size & (size - 1) == 0:
        return values >> (size.bit_length() - 1)
    return lax.div(values, jnp.int32(size))


def remainder(values, size):
    if size & (size - 1) == 0:
        return values & (size - 1)
    return lax.rem(values, jnp.int32(size))


def step_code(owner, home, extent, receives):
    step = remainder(owner - home + 1 + extent, extent)
    if extent % 2 == 0:
        first = remainder(home, 2) == 0
        ahead = jnp.where(first, 2, 0)
    else:
        ahead = 0 if receives else 2
    return jnp.where(step == 1, 0, jnp.where(step == ahead, 1, 2))


def partners(extent):
    if extent % 2 == 0:
        one = [(i, i ^ 1) for i in range(extent)]
        two = [(i, ((i + 1) ^ 1) - 1) for i in range(extent)]
        two = [(i, j % extent) for i, j in two]
        return one, two
    return (
        [(i, (i + 1) % extent) for i in range(extent)],
        [((i + 1) % extent, i) for i in range(extent)],
    )


def own_rows(atom_ref, bond_ref, slots):
    atom = atom_ref[0, 0].astype(F32)
    feature = atom.shape[1]
    rows = []
    for slot in range(slots):
        bond = bond_ref[0, 0, :, slot * feature : (slot + 1) * feature].astype(F32)
        rows.append(jnp.concatenate([atom, bond], axis=1))
    return jnp.concatenate(rows, axis=0).astype(BF16)


def slot_major(table):
    slots, atoms = table.shape
    per_group = 128 // atoms
    tiled = jnp.concatenate([table.astype(F32)] * per_group, axis=1)
    row = lax.broadcasted_iota(jnp.int32, tiled.shape, 0)
    slot = quotient(lax.broadcasted_iota(jnp.int32, tiled.shape, 1), atoms)
    pieces = [
        jnp.sum(jnp.where(row == slot + group * per_group, tiled, 0.0), axis=0, keepdims=True)
        for group in range(slots // per_group)
    ]
    return jnp.concatenate(pieces, axis=1).astype(jnp.int32)


def bond_codes(targets, atoms, extents, receives):
    owner = quotient(targets, atoms)
    code_x = step_code(quotient(owner, extents[1]), lax.axis_index("gx"), extents[0], receives)
    code_y = step_code(remainder(owner, extents[1]), lax.axis_index("gy"), extents[1], receives)
    return code_x, code_y


def pack_kernel(
    extents,
    targets_hbm,
    atom_hbm,
    bond_hbm,
    own_ref,
    one_ref,
    two_ref,
    targets_ref,
    atom_ref,
    bond_ref,
    sems,
):
    copies = [
        pltpu.make_async_copy(source, target, sems.at[k])
        for k, (source, target) in enumerate(
            ((targets_hbm, targets_ref), (atom_hbm, atom_ref), (bond_hbm, bond_ref))
        )
    ]
    for copy in copies:
        copy.start()
    atoms = atom_ref.shape[2]
    slots = targets_ref.shape[0]
    bonds = slots * atoms
    lanes = 128
    groups = bonds // lanes
    copies[0].wait()
    code_x, code_y = bond_codes(slot_major(targets_ref[...]), atoms, extents, False)
    code = 3 * code_x + code_y
    rows = lax.broadcasted_iota(jnp.int32, (16, lanes), 0)
    marks = [rows == code[:, g * lanes : (g + 1) * lanes] for g in range(groups)]
    stacked = jnp.concatenate([m.astype(F32) for m in marks], axis=0).astype(BF16)
    before = lax.broadcasted_iota(jnp.int32, (lanes, 2 * lanes), 0)
    after = lax.broadcasted_iota(jnp.int32, (lanes, 2 * lanes), 1)
    sums = jnp.where((before < after) | (after >= lanes), 1.0, 0.0).astype(BF16)
    counted = jnp.dot(stacked, sums, preferred_element_type=F32)
    place = []
    earlier = jnp.zeros((16, lanes), F32)
    for g in range(groups):
        part = counted[g * 16 : (g + 1) * 16]
        place.append(
            jnp.sum(jnp.where(marks[g], part[:, :lanes] + earlier, 0.0), axis=0, keepdims=True)
        )
        earlier = earlier + part[:, lanes:]
    place = jnp.concatenate(place, axis=1).astype(jnp.int32) + CAP * code
    copies[1].wait()
    copies[2].wait()
    values = own_rows(atom_ref, bond_ref, slots)
    for third, ref in enumerate((own_ref, one_ref, two_ref)):
        spot = lax.broadcasted_iota(jnp.int32, (3 * CAP, bonds), 0) + 3 * CAP * third
        chosen = jnp.where(spot == place, 1.0, 0.0).astype(BF16)
        ref[...] = jnp.dot(chosen, values, preferred_element_type=F32).astype(BF16)


def basis_kernel(atoms, dirs_ref, basis_ref):
    slots, degrees, bonds = basis_ref.shape
    angles = dirs_ref[...]
    sines = jnp.sin(angles)
    cosines = jnp.cos(angles)
    parts = (
        sines[0:1] * cosines[1:2],
        sines[0:1] * sines[1:2],
        cosines[0:1],
    )
    unit = [jnp.broadcast_to(part, (8, bonds)) for part in parts]
    row = lax.broadcasted_iota(jnp.int32, (8, bonds), 0)
    for diagonal in range(slots):
        if diagonal == 0:
            cosine = unit[0] * unit[0] + unit[1] * unit[1] + unit[2] * unit[2]
        else:
            shift = bonds - atoms * diagonal
            turned = [pltpu.roll(part, shift, 1) for part in unit]
            cosine = unit[0] * turned[0] + unit[1] * turned[1] + unit[2] * turned[2]
        series = [jnp.ones_like(cosine), cosine]
        double = cosine + cosine
        for _ in range(7):
            series.append(double * series[-1] - series[-2])
        lower = series[7]
        upper = series[1]
        for index in range(1, 8):
            lower = jnp.where(row == index, series[7 - index], lower)
            upper = jnp.where(row == index, series[1 + index], upper)
        double = series[8] + series[8]
        blocks = [lower, upper]
        for _ in range(degrees // 8 - 1):
            blocks.append(double * blocks[-1] - blocks[-2])
        basis_ref[diagonal] = jnp.concatenate(blocks[1:], axis=0).astype(BF16)


def prepare_kernel(
    extents,
    targets_ref,
    atom_ref,
    bond_ref,
    bond_in_ref,
    bond_mix_ref,
    pair_ref,
    angle_ref,
    pair_hidden_ref,
    pair_out_ref,
    atom_in_ref,
    atom_out_ref,
    chosen_ref,
    values_ref,
    near_ref,
    far_weight_ref,
    mix_weight_ref,
    pair_weight_ref,
    angle_weight_ref,
    hidden_weight_ref,
    out_weight_ref,
    atom_in_weight_ref,
    atom_out_weight_ref,
):
    atoms = atom_ref.shape[2]
    feature = atom_ref.shape[3]
    slots = targets_ref.shape[0]
    bonds = slots * atoms
    targets = slot_major(targets_ref[...])
    code_x, code_y = bond_codes(targets, atoms, extents, True)
    code = 3 * code_y + code_x
    bond = lax.broadcasted_iota(jnp.int32, (1, bonds), 1)
    far = (slots - 1 - quotient(bond, atoms)) * atoms + remainder(targets, atoms)
    base = (code * bonds).astype(F32)
    key = base + far.astype(F32)
    column = jnp.broadcast_to(key, (128, bonds)).T
    place = []
    for group in range(bonds // 128):
        here = slice(group * 128, (group + 1) * 128)
        inside = (column < key[:, here]) & (column >= base[:, here])
        place.append(jnp.sum(jnp.where(inside, 1.0, 0.0), axis=0, keepdims=True))
    place = jnp.concatenate(place, axis=1).astype(jnp.int32) + CAP * code
    spot = lax.broadcasted_iota(jnp.int32, (9 * CAP, bonds), 0)
    chosen_ref[...] = jnp.where(spot == place, 1.0, 0.0).astype(BF16)

    values = own_rows(atom_ref, bond_ref, slots).astype(F32).T.astype(BF16)
    values_ref[...] = values

    def turned(weight, scale):
        return (weight * scale).T.astype(BF16)

    weight = bond_in_ref[...].astype(F32)
    source, other, own = (weight[k * feature : (k + 1) * feature] for k in range(3))
    empty = jnp.zeros((feature, feature), F32)

    def crossed(left, right):
        return jnp.concatenate(
            [left[:, :feature], right[:, :feature], left[:, feature:], right[:, feature:]], axis=1
        )

    blank = jnp.zeros_like(own)
    near = jnp.concatenate([crossed(source, other), crossed(own, blank)], axis=0)
    away = jnp.concatenate([crossed(other, source), crossed(blank, own)], axis=0)
    near_ref[...] = jnp.dot(turned(near, 0.5), values, preferred_element_type=F32)
    far_weight_ref[...] = turned(away, 0.5)
    mix = bond_mix_ref[...].astype(F32)
    mix = jnp.concatenate(
        [jnp.concatenate([mix, empty], axis=1), jnp.concatenate([empty, mix], axis=1)], axis=0
    )
    mix_weight_ref[...] = turned(mix, 0.5)
    pair_weight_ref[...] = turned(pair_ref[...].astype(F32), 0.5)
    angle_weight_ref[...] = turned(angle_ref[...].astype(F32), 0.5)
    hidden_weight_ref[...] = turned(pair_hidden_ref[...].astype(F32), 0.25)
    out_weight_ref[...] = turned(pair_out_ref[...].astype(F32), 0.5)
    atom_in_weight_ref[...] = turned(atom_in_ref[...].astype(F32), 0.5)
    atom_out_weight_ref[...] = turned(atom_out_ref[...].astype(F32), 0.5)


def doubled_gate(values):
    half = values.shape[0] // 2
    return values[:half] * (1.0 + jnp.tanh(values[:half])) * (1.0 + jnp.tanh(values[half:]))


def main_kernel(
    own_ref,
    one_ref,
    two_ref,
    three_ref,
    four_ref,
    basis_ref,
    chosen_ref,
    values_ref,
    near_ref,
    far_weight_ref,
    mix_weight_ref,
    pair_weight_ref,
    angle_weight_ref,
    hidden_weight_ref,
    out_weight_ref,
    atom_in_weight_ref,
    atom_out_weight_ref,
    atom_result_ref,
    bond_result_ref,
    first_ref,
    second_ref,
):
    slots, degrees, bonds = basis_ref.shape
    atoms = bonds // slots
    feature = values_ref.shape[0] // 2
    received = jnp.concatenate(
        [own_ref[0:CAP], one_ref[0:CAP], two_ref[0:CAP], three_ref[...], four_ref[...]], axis=0
    )
    received = received.astype(F32).T.astype(BF16)
    far = jnp.dot(received, chosen_ref[...], preferred_element_type=F32)
    incoming = near_ref[...] + jnp.dot(
        far_weight_ref[...], far.astype(BF16), preferred_element_type=F32
    )
    hidden = doubled_gate(incoming).astype(BF16)
    mixed = jnp.dot(mix_weight_ref[...], hidden, preferred_element_type=F32)
    ahead = (values_ref[feature:].astype(F32) + mixed[:feature]).astype(BF16).astype(F32)
    back = (far[feature:] + mixed[feature:]).astype(BF16).astype(F32)
    average = ((ahead + back) * 0.5).astype(BF16)
    projected = jnp.dot(pair_weight_ref[...], average, preferred_element_type=F32)
    first_ref[...] = projected[: 2 * feature]
    second = projected[2 * feature :]
    per_group = 128 // atoms
    for turn in range(per_group):
        second_ref[turn] = second if turn == 0 else pltpu.roll(second, bonds - atoms * turn, 1)
    width = 256
    blocks = bonds // 128
    angle_weight = angle_weight_ref[...]
    hidden_weight = hidden_weight_ref[...]
    totals = []
    for start in range(0, bonds, width):
        total = jnp.zeros((feature, width), F32)
        for diagonal in range(slots):
            turn, skip = diagonal % per_group, diagonal // per_group
            pieces = [
                second_ref[turn, :, pl.ds(128 * ((start // 128 + k + skip) % blocks), 128)]
                for k in range(width // 128)
            ]
            mixture = jnp.dot(
                angle_weight,
                basis_ref[diagonal, :, pl.ds(start, width)],
                preferred_element_type=F32,
            )
            mixture = mixture + (first_ref[:, pl.ds(start, width)] + jnp.concatenate(pieces, axis=1))
            pair = doubled_gate(mixture).astype(BF16)
            total = total + doubled_gate(
                jnp.dot(hidden_weight, pair, preferred_element_type=F32)
            )
        totals.append(total)
    pair_sum = jnp.concatenate(totals, axis=1).astype(BF16)
    bond_out = (
        average.astype(F32) + jnp.dot(out_weight_ref[...], pair_sum, preferred_element_type=F32)
    ).astype(BF16).astype(F32)
    rows = bond_out.T.astype(BF16)
    for slot in range(slots):
        bond_result_ref[0, 0, :, slot * feature : (slot + 1) * feature] = rows[
            slot * atoms : (slot + 1) * atoms
        ]
    pooled = bond_out[:, 0:128]
    for block in range(1, blocks):
        pooled = pooled + bond_out[:, block * 128 : (block + 1) * 128]
    shift = 64
    while shift >= atoms:
        pooled = pooled + pltpu.roll(pooled, shift, 1)
        shift //= 2
    pooled = (pooled * (1.0 / slots)).astype(BF16)
    atom = values_ref[0:feature, 0:128]
    joined = jnp.concatenate([atom, pooled], axis=0)
    atom_hidden = doubled_gate(
        jnp.dot(atom_in_weight_ref[...], joined, preferred_element_type=F32)
    ).astype(BF16)
    atom_new = atom.astype(F32) + jnp.dot(
        atom_out_weight_ref[...], atom_hidden, preferred_element_type=F32
    )
    atom_result_ref[0, 0] = atom_new.T[0:atoms].astype(BF16)


def per_device(
    atom_feat,
    bond_feat,
    neighbours,
    bond_dirs,
    bond_in_weight,
    bond_mix_weight,
    pair_weight,
    angle_weight,
    pair_hidden_weight,
    pair_out_weight,
    atom_in_weight,
    atom_out_weight,
):
    atoms, feature = atom_feat.shape[2], atom_feat.shape[3]
    slots = neighbours.shape[3]
    bonds = atoms * slots
    degrees = angle_weight.shape[0]
    extents = (lax.axis_size("gx"), lax.axis_size("gy"))
    targets = neighbours[0, 0].T
    dirs = bond_dirs[:, 0, 0].reshape(2, atoms, slots).transpose(0, 2, 1).reshape(2, bonds)
    hbm = pl.BlockSpec(memory_space=pltpu.HBM)
    vmem = pl.BlockSpec(memory_space=pltpu.VMEM)
    params = pltpu.CompilerParams(vmem_limit_bytes=32 * 2**20)

    def shaped(shape, dtype):
        return jax.ShapeDtypeStruct(shape, dtype)

    payload = shaped((3 * CAP, 2 * feature), BF16)
    own, one, two = pl.pallas_call(
        functools.partial(pack_kernel, extents),
        out_shape=(payload, payload, payload),
        in_specs=[hbm, hbm, hbm],
        out_specs=(vmem, vmem, vmem),
        scratch_shapes=[
            pltpu.VMEM(targets.shape, jnp.int32),
            pltpu.VMEM(atom_feat.shape, BF16),
            pltpu.VMEM(bond_feat.shape, BF16),
            pltpu.SemaphoreType.DMA((3,)),
        ],
        compiler_params=params,
        name="pack",
    )(*(pltpu.with_memory_space_constraint(x, pltpu.HBM) for x in (targets, atom_feat, bond_feat)))
    first, second = partners(extents[0])
    one = lax.ppermute(one, "gx", first)
    two = lax.ppermute(two, "gx", second)
    basis = pl.pallas_call(
        functools.partial(basis_kernel, atoms),
        out_shape=shaped((slots, degrees, bonds), BF16),
        in_specs=[vmem],
        out_specs=vmem,
        compiler_params=params,
        cost_estimate=pl.CostEstimate(flops=4 * 2**20, bytes_accessed=2**20, transcendentals=4096),
        name="basis",
    )(dirs)
    own, one, two, basis = lax.optimization_barrier((own, one, two, basis))
    first, second = partners(extents[1])
    near = jnp.concatenate([x[CAP : 2 * CAP] for x in (own, one, two)], axis=0)
    away = jnp.concatenate([x[2 * CAP :] for x in (own, one, two)], axis=0)
    three = lax.ppermute(near, "gy", first)
    four = lax.ppermute(away, "gy", second)
    weights = (
        shaped((4 * feature, 2 * feature), BF16),
        shaped((2 * feature, 2 * feature), BF16),
        shaped((4 * feature, feature), BF16),
        shaped((2 * feature, degrees), BF16),
        shaped((2 * feature, feature), BF16),
        shaped((feature, feature), BF16),
        shaped((2 * feature, 2 * feature), BF16),
        shaped((feature, feature), BF16),
    )
    prepared = pl.pallas_call(
        functools.partial(prepare_kernel, extents),
        out_shape=(
            shaped((9 * CAP, bonds), BF16),
            shaped((2 * feature, bonds), BF16),
            shaped((4 * feature, bonds), F32),
        )
        + weights,
        in_specs=[vmem] * 11,
        out_specs=(vmem,) * 11,
        compiler_params=params,
        cost_estimate=pl.CostEstimate(flops=64 * 2**20, bytes_accessed=2**21, transcendentals=0),
        name="prepare",
    )(
        targets,
        atom_feat,
        bond_feat,
        bond_in_weight,
        bond_mix_weight,
        pair_weight,
        angle_weight,
        pair_hidden_weight,
        pair_out_weight,
        atom_in_weight,
        atom_out_weight,
    )
    return pl.pallas_call(
        main_kernel,
        out_shape=(shaped(atom_feat.shape, BF16), shaped(bond_feat.shape, BF16)),
        in_specs=[vmem] * 17,
        out_specs=(vmem, vmem),
        scratch_shapes=[
            pltpu.VMEM((2 * feature, bonds), F32),
            pltpu.VMEM((128 // atoms, 2 * feature, bonds), F32),
        ],
        compiler_params=params,
        cost_estimate=pl.CostEstimate(
            flops=400 * 2**20, bytes_accessed=2**22, transcendentals=2**21
        ),
        name="main",
    )(own, one, two, three, four, basis, *prepared)


def solution(mesh):
    placed = (
        P("gx", "gy", None, None),
        P("gx", "gy", None, None),
        P("gx", "gy", None, None),
        P(None, "gx", "gy", None),
        P(),
        P(),
        P(),
        P(),
        P(),
        P(),
        P(),
        P(),
    )
    return jax.shard_map(
        per_device,
        mesh=mesh,
        in_specs=placed,
        out_specs=(P("gx", "gy", None, None), P("gx", "gy", None, None)),
        check_vma=False,
    )
```

```python
import functools

import jax
import jax.numpy as jnp
from jax import lax
from jax.experimental import pallas as pl
from jax.experimental.pallas import tpu as pltpu
from jax.sharding import PartitionSpec as P

F32 = jnp.float32
BF16 = jnp.bfloat16
CAP = 64


def quotient(values, size):
    if size & (size - 1) == 0:
        return values >> (size.bit_length() - 1)
    return lax.div(values, jnp.int32(size))


def remainder(values, size):
    if size & (size - 1) == 0:
        return values & (size - 1)
    return lax.rem(values, jnp.int32(size))


def step_code(owner, home, extent, paired, receives):
    step = remainder(owner - home + 1 + extent, extent)
    if paired:
        ahead = jnp.where(remainder(home, 2) == 0, 0, 2)
    else:
        ahead = 0 if receives else 2
    return jnp.where(step == 1, 0, jnp.where(step == ahead, 1, 2))


def moves(extent, paired):
    if paired:
        near = [(i, i ^ 1) for i in range(extent)]
        return [(i, (((i + 1) ^ 1) - 1) % extent) for i in range(extent)], near
    up = [(i, (i + 1) % extent) for i in range(extent)]
    return up, [(j, i) for i, j in up]


def bond_rows(bond_ref, slots):
    feature = bond_ref.shape[3] // slots
    rows = [bond_ref[0, 0, :, slot * feature : (slot + 1) * feature] for slot in range(slots)]
    return jnp.concatenate(rows, axis=0)


def slot_major(table):
    slots, atoms = table.shape
    per_group = 128 // atoms
    tiled = jnp.concatenate([table.astype(F32)] * per_group, axis=1)
    row = lax.broadcasted_iota(jnp.int32, tiled.shape, 0)
    slot = quotient(lax.broadcasted_iota(jnp.int32, tiled.shape, 1), atoms)
    pieces = [
        jnp.sum(jnp.where(row == slot + group * per_group, tiled, 0.0), axis=0, keepdims=True)
        for group in range(slots // per_group)
    ]
    return jnp.concatenate(pieces, axis=1).astype(jnp.int32)


def bond_codes(targets, atoms, extents, paired, receives):
    owner = quotient(targets, atoms)
    block = (quotient(owner, extents[1]), remainder(owner, extents[1]))
    return tuple(
        step_code(block[k], lax.axis_index(axis), extents[k], paired[k], receives)
        for k, axis in enumerate(("gx", "gy"))
    )


def pack_kernel(
    extents,
    paired,
    targets_hbm,
    atom_hbm,
    bond_hbm,
    own_ref,
    one_ref,
    two_ref,
    targets_ref,
    atom_ref,
    bond_ref,
    sems,
):
    copies = [
        pltpu.make_async_copy(source, target, sems.at[k])
        for k, (source, target) in enumerate(
            ((targets_hbm, targets_ref), (atom_hbm, atom_ref), (bond_hbm, bond_ref))
        )
    ]
    for copy in copies:
        copy.start()
    atoms = atom_ref.shape[2]
    slots = targets_ref.shape[0]
    bonds = slots * atoms
    lanes = 128
    groups = bonds // lanes
    copies[0].wait()
    code_x, code_y = bond_codes(
        slot_major(targets_ref[...]), atoms, extents, paired, False
    )
    code = 3 * code_x + code_y
    rows = lax.broadcasted_iota(jnp.int32, (16, lanes), 0)
    marks = [rows == code[:, g * lanes : (g + 1) * lanes] for g in range(groups)]
    stacked = jnp.concatenate([m.astype(F32) for m in marks], axis=0).astype(BF16)
    before = lax.broadcasted_iota(jnp.int32, (lanes, 2 * lanes), 0)
    after = lax.broadcasted_iota(jnp.int32, (lanes, 2 * lanes), 1)
    sums = jnp.where((before < after) | (after >= lanes), 1.0, 0.0).astype(BF16)
    counted = jnp.dot(stacked, sums, preferred_element_type=F32)
    place = []
    earlier = jnp.zeros((16, lanes), F32)
    for g in range(groups):
        part = counted[g * 16 : (g + 1) * 16]
        place.append(
            jnp.sum(jnp.where(marks[g], part[:, :lanes] + earlier, 0.0), axis=0, keepdims=True)
        )
        earlier = earlier + part[:, lanes:]
    place = jnp.concatenate(place, axis=1).astype(jnp.int32)
    row_count = 3 * CAP // 2
    spot = lax.broadcasted_iota(jnp.int32, (row_count, bonds), 0)
    copies[1].wait()
    copies[2].wait()
    values = bond_rows(bond_ref, slots)
    atom = atom_ref[0, 0]
    atom = jnp.concatenate([atom[: atoms // 2], atom[atoms // 2 :]], axis=1)
    for third, ref in enumerate((own_ref, one_ref, two_ref)):
        halves = []
        for half in range(2):
            inside = quotient(place, CAP // 2) == half
            wanted = place - half * (CAP // 2) + (code - 3 * third) * (CAP // 2)
            wanted = jnp.where(inside, wanted, -1)
            chosen = jnp.where(spot == wanted, 1.0, 0.0).astype(BF16)
            halves.append(jnp.dot(chosen, values, preferred_element_type=F32))
        ref[:row_count] = jnp.concatenate(halves, axis=1).astype(BF16)
        ref[row_count:] = atom


def basis_kernel(atoms, dirs_ref, basis_ref):
    slots, degrees, bonds = basis_ref.shape
    angles = dirs_ref[...]
    sines = jnp.sin(angles)
    cosines = jnp.cos(angles)
    parts = (
        sines[0:1] * cosines[1:2],
        sines[0:1] * sines[1:2],
        cosines[0:1],
    )
    unit = [jnp.broadcast_to(part, (8, bonds)) for part in parts]
    row = lax.broadcasted_iota(jnp.int32, (8, bonds), 0)
    for diagonal in range(slots):
        if diagonal == 0:
            cosine = unit[0] * unit[0] + unit[1] * unit[1] + unit[2] * unit[2]
        else:
            shift = bonds - atoms * diagonal
            turned = [pltpu.roll(part, shift, 1) for part in unit]
            cosine = unit[0] * turned[0] + unit[1] * turned[1] + unit[2] * turned[2]
        series = [jnp.ones_like(cosine), cosine]
        double = cosine + cosine
        for _ in range(7):
            series.append(double * series[-1] - series[-2])
        lower = series[7]
        upper = series[1]
        for index in range(1, 8):
            lower = jnp.where(row == index, series[7 - index], lower)
            upper = jnp.where(row == index, series[1 + index], upper)
        double = series[8] + series[8]
        blocks = [lower, upper]
        for _ in range(degrees // 8 - 1):
            blocks.append(double * blocks[-1] - blocks[-2])
        basis_ref[diagonal] = jnp.concatenate(blocks[1:], axis=0).astype(BF16)


def prepare_kernel(
    extents,
    paired,
    targets_ref,
    atom_ref,
    bond_ref,
    bond_in_ref,
    bond_mix_ref,
    pair_ref,
    angle_ref,
    pair_hidden_ref,
    pair_out_ref,
    atom_in_ref,
    atom_out_ref,
    chosen_bond_ref,
    chosen_atom_ref,
    right_half_ref,
    values_ref,
    near_ref,
    far_weight_ref,
    mix_weight_ref,
    pair_weight_ref,
    angle_weight_ref,
    hidden_weight_ref,
    out_weight_ref,
    atom_in_weight_ref,
    atom_out_weight_ref,
):
    atoms = atom_ref.shape[2]
    feature = atom_ref.shape[3]
    slots = targets_ref.shape[0]
    bonds = slots * atoms
    targets = slot_major(targets_ref[...])
    code_x, code_y = bond_codes(targets, atoms, extents, paired, True)
    code = 3 * code_y + code_x
    bond = lax.broadcasted_iota(jnp.int32, (1, bonds), 1)
    far = (slots - 1 - quotient(bond, atoms)) * atoms + remainder(targets, atoms)
    base = (code * bonds).astype(F32)
    key = base + far.astype(F32)
    column = jnp.broadcast_to(key, (128, bonds)).T
    place = []
    for group in range(bonds // 128):
        here = slice(group * 128, (group + 1) * 128)
        inside = (column < key[:, here]) & (column >= base[:, here])
        place.append(jnp.sum(jnp.where(inside, 1.0, 0.0), axis=0, keepdims=True))
    place = jnp.concatenate(place, axis=1).astype(jnp.int32)
    half = CAP // 2
    spot = lax.broadcasted_iota(jnp.int32, (9 * half, bonds), 0)
    wanted = remainder(place, half) + half * code
    chosen_bond_ref[...] = jnp.where(spot == wanted, 1.0, 0.0).astype(BF16)
    spot = lax.broadcasted_iota(jnp.int32, (9 * atoms // 2, bonds), 0)
    atom = remainder(targets, atoms)
    wanted = remainder(atom, atoms // 2) + atoms // 2 * code
    chosen_atom_ref[...] = jnp.where(spot == wanted, 1.0, 0.0).astype(BF16)
    row = lax.broadcasted_iota(jnp.int32, (8, bonds), 0)
    right_half = jnp.where(row == 0, quotient(place, half), quotient(atom, atoms // 2))
    right_half_ref[...] = right_half.astype(F32)

    atom = atom_ref[0, 0].astype(F32)
    atom = jnp.concatenate([atom] * slots, axis=0)
    values = jnp.concatenate([atom, bond_rows(bond_ref, slots).astype(F32)], axis=1)
    values = values.T.astype(BF16)
    values_ref[...] = values

    def turned(weight, scale):
        return (weight * scale).T.astype(BF16)

    weight = bond_in_ref[...].astype(F32)
    source, other, own = (weight[k * feature : (k + 1) * feature] for k in range(3))
    empty = jnp.zeros((feature, feature), F32)

    def crossed(left, right):
        return jnp.concatenate(
            [left[:, :feature], right[:, :feature], left[:, feature:], right[:, feature:]], axis=1
        )

    blank = jnp.zeros_like(own)
    near = jnp.concatenate([crossed(source, other), crossed(own, blank)], axis=0)
    away = jnp.concatenate([crossed(other, source), crossed(blank, own)], axis=0)
    near_ref[...] = jnp.dot(turned(near, 0.5), values, preferred_element_type=F32)
    far_weight_ref[...] = turned(away, 0.5)
    mix = bond_mix_ref[...].astype(F32)
    mix = jnp.concatenate(
        [jnp.concatenate([mix, empty], axis=1), jnp.concatenate([empty, mix], axis=1)], axis=0
    )
    mix_weight_ref[...] = turned(mix, 0.5)
    pair_weight_ref[...] = turned(pair_ref[...].astype(F32), 0.5)
    angle_weight_ref[...] = turned(angle_ref[...].astype(F32), 0.5)
    hidden_weight_ref[...] = turned(pair_hidden_ref[...].astype(F32), 0.25)
    out_weight_ref[...] = turned(pair_out_ref[...].astype(F32), 0.5)
    atom_in_weight_ref[...] = turned(atom_in_ref[...].astype(F32), 0.5)
    atom_out_weight_ref[...] = turned(atom_out_ref[...].astype(F32), 0.5)


def doubled_gate(values):
    half = values.shape[0] // 2
    return values[:half] * (1.0 + jnp.tanh(values[:half])) * (1.0 + jnp.tanh(values[half:]))


def main_kernel(
    own_ref,
    one_ref,
    two_ref,
    four_ref,
    three_ref,
    basis_ref,
    chosen_bond_ref,
    chosen_atom_ref,
    right_half_ref,
    values_ref,
    near_ref,
    far_weight_ref,
    mix_weight_ref,
    pair_weight_ref,
    angle_weight_ref,
    hidden_weight_ref,
    out_weight_ref,
    atom_in_weight_ref,
    atom_out_weight_ref,
    atom_result_ref,
    bond_result_ref,
    first_ref,
    second_ref,
):
    slots, degrees, bonds = basis_ref.shape
    atoms = bonds // slots
    feature = values_ref.shape[0] // 2
    half = CAP // 2
    near_refs = (own_ref, one_ref, two_ref)
    away_refs = (three_ref, four_ref)

    def unpacked(parts, chosen, right_half):
        rows = jnp.concatenate(parts, axis=0).astype(F32).T.astype(BF16)
        both = jnp.dot(rows, chosen, preferred_element_type=F32)
        return jnp.where(right_half > 0.0, both[feature:], both[:feature])

    far_bond = unpacked(
        [ref[:half] for ref in near_refs] + [ref[: 3 * half] for ref in away_refs],
        chosen_bond_ref[...],
        right_half_ref[0:1],
    )
    far_atom = unpacked(
        [ref[3 * half :] for ref in near_refs + away_refs],
        chosen_atom_ref[...],
        right_half_ref[1:2],
    )
    far = jnp.concatenate([far_atom, far_bond], axis=0)
    incoming = near_ref[...] + jnp.dot(
        far_weight_ref[...], far.astype(BF16), preferred_element_type=F32
    )
    hidden = doubled_gate(incoming).astype(BF16)
    mixed = jnp.dot(mix_weight_ref[...], hidden, preferred_element_type=F32)
    ahead = (values_ref[feature:].astype(F32) + mixed[:feature]).astype(BF16).astype(F32)
    back = (far_bond + mixed[feature:]).astype(BF16).astype(F32)
    average = ((ahead + back) * 0.5).astype(BF16)
    projected = jnp.dot(pair_weight_ref[...], average, preferred_element_type=F32)
    first_ref[...] = projected[: 2 * feature]
    second = projected[2 * feature :]
    per_group = 128 // atoms
    for turn in range(per_group):
        second_ref[turn] = second if turn == 0 else pltpu.roll(second, bonds - atoms * turn, 1)
    width = 256
    blocks = bonds // 128
    angle_weight = angle_weight_ref[...]
    hidden_weight = hidden_weight_ref[...]
    totals = []
    for start in range(0, bonds, width):
        total = jnp.zeros((feature, width), F32)
        for diagonal in range(slots):
            turn, skip = diagonal % per_group, diagonal // per_group
            pieces = [
                second_ref[turn, :, pl.ds(128 * ((start // 128 + k + skip) % blocks), 128)]
                for k in range(width // 128)
            ]
            mixture = jnp.dot(
                angle_weight,
                basis_ref[diagonal, :, pl.ds(start, width)],
                preferred_element_type=F32,
            )
            mixture = mixture + (first_ref[:, pl.ds(start, width)] + jnp.concatenate(pieces, axis=1))
            pair = doubled_gate(mixture).astype(BF16)
            total = total + doubled_gate(
                jnp.dot(hidden_weight, pair, preferred_element_type=F32)
            )
        totals.append(total)
    pair_sum = jnp.concatenate(totals, axis=1).astype(BF16)
    bond_out = (
        average.astype(F32) + jnp.dot(out_weight_ref[...], pair_sum, preferred_element_type=F32)
    ).astype(BF16).astype(F32)
    rows = bond_out.T.astype(BF16)
    for slot in range(slots):
        bond_result_ref[0, 0, :, slot * feature : (slot + 1) * feature] = rows[
            slot * atoms : (slot + 1) * atoms
        ]
    pooled = bond_out[:, 0:128]
    for block in range(1, blocks):
        pooled = pooled + bond_out[:, block * 128 : (block + 1) * 128]
    shift = 64
    while shift >= atoms:
        pooled = pooled + pltpu.roll(pooled, shift, 1)
        shift //= 2
    pooled = (pooled * (1.0 / slots)).astype(BF16)
    atom = values_ref[0:feature, 0:128]
    joined = jnp.concatenate([atom, pooled], axis=0)
    atom_hidden = doubled_gate(
        jnp.dot(atom_in_weight_ref[...], joined, preferred_element_type=F32)
    ).astype(BF16)
    atom_new = atom.astype(F32) + jnp.dot(
        atom_out_weight_ref[...], atom_hidden, preferred_element_type=F32
    )
    atom_result_ref[0, 0] = atom_new.T[0:atoms].astype(BF16)


def per_device(
    atom_feat,
    bond_feat,
    neighbours,
    bond_dirs,
    bond_in_weight,
    bond_mix_weight,
    pair_weight,
    angle_weight,
    pair_hidden_weight,
    pair_out_weight,
    atom_in_weight,
    atom_out_weight,
):
    atoms, feature = atom_feat.shape[2], atom_feat.shape[3]
    slots = neighbours.shape[3]
    bonds = atoms * slots
    degrees = angle_weight.shape[0]
    extents = (lax.axis_size("gx"), lax.axis_size("gy"))
    targets = neighbours[0, 0].T
    dirs = bond_dirs[:, 0, 0].reshape(2, atoms, slots).transpose(0, 2, 1).reshape(2, bonds)
    hbm = pl.BlockSpec(memory_space=pltpu.HBM)
    vmem = pl.BlockSpec(memory_space=pltpu.VMEM)
    params = pltpu.CompilerParams(vmem_limit_bytes=32 * 2**20)

    def shaped(shape, dtype):
        return jax.ShapeDtypeStruct(shape, dtype)

    paired = (extents[0] % 2 == 0, False)
    half = CAP // 2
    payload = shaped((3 * half + atoms // 2, 2 * feature), BF16)
    own, one, two = pl.pallas_call(
        functools.partial(pack_kernel, extents, paired),
        out_shape=(payload, payload, payload),
        in_specs=[hbm, hbm, hbm],
        out_specs=(vmem, vmem, vmem),
        scratch_shapes=[
            pltpu.VMEM(targets.shape, jnp.int32),
            pltpu.VMEM(atom_feat.shape, BF16),
            pltpu.VMEM(bond_feat.shape, BF16),
            pltpu.SemaphoreType.DMA((3,)),
        ],
        compiler_params=params,
        name="pack",
    )(*(pltpu.with_memory_space_constraint(x, pltpu.HBM) for x in (targets, atom_feat, bond_feat)))
    first, second = moves(extents[0], paired[0])
    one = lax.ppermute(one, "gx", first)
    two = lax.ppermute(two, "gx", second)
    basis = pl.pallas_call(
        functools.partial(basis_kernel, atoms),
        out_shape=shaped((slots, degrees, bonds), BF16),
        in_specs=[vmem],
        out_specs=vmem,
        compiler_params=params,
        cost_estimate=pl.CostEstimate(flops=4 * 2**20, bytes_accessed=2**20, transcendentals=4096),
        name="basis",
    )(dirs)
    own, one, two, basis = lax.optimization_barrier((own, one, two, basis))
    first, second = moves(extents[1], paired[1])

    def forwarded(block):
        parts = [x[block * half : (block + 1) * half] for x in (own, one, two)]
        return jnp.concatenate(parts + [x[3 * half :] for x in (own, one, two)], axis=0)

    three = lax.ppermute(forwarded(1), "gy", first)
    four = lax.ppermute(forwarded(2), "gy", second)
    weights = (
        shaped((4 * feature, 2 * feature), BF16),
        shaped((2 * feature, 2 * feature), BF16),
        shaped((4 * feature, feature), BF16),
        shaped((2 * feature, degrees), BF16),
        shaped((2 * feature, feature), BF16),
        shaped((feature, feature), BF16),
        shaped((2 * feature, 2 * feature), BF16),
        shaped((feature, feature), BF16),
    )
    prepared = pl.pallas_call(
        functools.partial(prepare_kernel, extents, paired),
        out_shape=(
            shaped((9 * half, bonds), BF16),
            shaped((9 * atoms // 2, bonds), BF16),
            shaped((8, bonds), F32),
            shaped((2 * feature, bonds), BF16),
            shaped((4 * feature, bonds), F32),
        )
        + weights,
        in_specs=[vmem] * 11,
        out_specs=(vmem,) * 13,
        compiler_params=params,
        cost_estimate=pl.CostEstimate(flops=64 * 2**20, bytes_accessed=2**21, transcendentals=0),
        name="prepare",
    )(
        targets,
        atom_feat,
        bond_feat,
        bond_in_weight,
        bond_mix_weight,
        pair_weight,
        angle_weight,
        pair_hidden_weight,
        pair_out_weight,
        atom_in_weight,
        atom_out_weight,
    )
    return pl.pallas_call(
        main_kernel,
        out_shape=(shaped(atom_feat.shape, BF16), shaped(bond_feat.shape, BF16)),
        in_specs=[vmem] * 19,
        out_specs=(vmem, vmem),
        scratch_shapes=[
            pltpu.VMEM((2 * feature, bonds), F32),
            pltpu.VMEM((128 // atoms, 2 * feature, bonds), F32),
        ],
        compiler_params=params,
        cost_estimate=pl.CostEstimate(
            flops=400 * 2**20, bytes_accessed=2**22, transcendentals=2**21
        ),
        name="main",
    )(own, one, two, four, three, basis, *prepared)


def solution(mesh):
    placed = (
        P("gx", "gy", None, None),
        P("gx", "gy", None, None),
        P("gx", "gy", None, None),
        P(None, "gx", "gy", None),
        P(),
        P(),
        P(),
        P(),
        P(),
        P(),
        P(),
        P(),
    )
    return jax.shard_map(
        per_device,
        mesh=mesh,
        in_specs=placed,
        out_specs=(P("gx", "gy", None, None), P("gx", "gy", None, None)),
        check_vma=False,
    )
```

```python
import functools

import jax
import jax.numpy as jnp
from jax import lax
from jax.experimental import pallas as pl
from jax.experimental.pallas import tpu as pltpu
from jax.sharding import PartitionSpec as P

F32 = jnp.float32
BF16 = jnp.bfloat16
CAP = 64


def quotient(values, size):
    if size & (size - 1) == 0:
        return values >> (size.bit_length() - 1)
    return lax.div(values, jnp.int32(size))


def remainder(values, size):
    if size & (size - 1) == 0:
        return values & (size - 1)
    return lax.rem(values, jnp.int32(size))


def step_code(owner, home, extent, paired, receives):
    step = remainder(owner - home + 1 + extent, extent)
    if paired:
        ahead = jnp.where(remainder(home, 2) == 0, 0, 2)
    else:
        ahead = 0 if receives else 2
    return jnp.where(step == 1, 0, jnp.where(step == ahead, 1, 2))


def moves(extent, paired):
    if paired:
        near = [(i, i ^ 1) for i in range(extent)]
        return [(i, (((i + 1) ^ 1) - 1) % extent) for i in range(extent)], near
    up = [(i, (i + 1) % extent) for i in range(extent)]
    return up, [(j, i) for i, j in up]


def bond_rows(bond_ref, slots):
    feature = bond_ref.shape[3] // slots
    rows = [bond_ref[0, 0, :, slot * feature : (slot + 1) * feature] for slot in range(slots)]
    return jnp.concatenate(rows, axis=0)


def slot_major(table):
    slots, atoms = table.shape
    per_group = 128 // atoms
    tiled = jnp.concatenate([table.astype(F32)] * per_group, axis=1)
    row = lax.broadcasted_iota(jnp.int32, tiled.shape, 0)
    slot = quotient(lax.broadcasted_iota(jnp.int32, tiled.shape, 1), atoms)
    pieces = [
        jnp.sum(jnp.where(row == slot + group * per_group, tiled, 0.0), axis=0, keepdims=True)
        for group in range(slots // per_group)
    ]
    return jnp.concatenate(pieces, axis=1).astype(jnp.int32)


def bond_codes(targets, atoms, extents, paired, receives):
    owner = quotient(targets, atoms)
    block = (quotient(owner, extents[1]), remainder(owner, extents[1]))
    return tuple(
        step_code(block[k], lax.axis_index(axis), extents[k], paired[k], receives)
        for k, axis in enumerate(("gx", "gy"))
    )


def pack_kernel(
    extents,
    paired,
    targets_hbm,
    atom_hbm,
    bond_hbm,
    own_ref,
    one_ref,
    two_ref,
    targets_ref,
    atom_ref,
    bond_ref,
    sems,
):
    copies = [
        pltpu.make_async_copy(source, target, sems.at[k])
        for k, (source, target) in enumerate(
            ((targets_hbm, targets_ref), (atom_hbm, atom_ref), (bond_hbm, bond_ref))
        )
    ]
    for copy in copies:
        copy.start()
    atoms = atom_ref.shape[2]
    slots = targets_ref.shape[0]
    bonds = slots * atoms
    lanes = 128
    groups = bonds // lanes
    copies[0].wait()
    code_x, code_y = bond_codes(
        slot_major(targets_ref[...]), atoms, extents, paired, False
    )
    code = 3 * code_x + code_y
    rows = lax.broadcasted_iota(jnp.int32, (16, lanes), 0)
    marks = [rows == code[:, g * lanes : (g + 1) * lanes] for g in range(groups)]
    stacked = jnp.concatenate([m.astype(F32) for m in marks], axis=0).astype(BF16)
    before = lax.broadcasted_iota(jnp.int32, (lanes, 2 * lanes), 0)
    after = lax.broadcasted_iota(jnp.int32, (lanes, 2 * lanes), 1)
    sums = jnp.where((before < after) | (after >= lanes), 1.0, 0.0).astype(BF16)
    counted = jnp.dot(stacked, sums, preferred_element_type=F32)
    place = []
    earlier = jnp.zeros((16, lanes), F32)
    for g in range(groups):
        part = counted[g * 16 : (g + 1) * 16]
        place.append(
            jnp.sum(jnp.where(marks[g], part[:, :lanes] + earlier, 0.0), axis=0, keepdims=True)
        )
        earlier = earlier + part[:, lanes:]
    place = jnp.concatenate(place, axis=1).astype(jnp.int32)
    row_count = 3 * CAP // 2
    spot = lax.broadcasted_iota(jnp.int32, (row_count, bonds), 0)
    copies[1].wait()
    copies[2].wait()
    values = bond_rows(bond_ref, slots)
    atom = atom_ref[0, 0]
    atom = jnp.concatenate([atom[: atoms // 2], atom[atoms // 2 :]], axis=1)
    for third, ref in enumerate((own_ref, one_ref, two_ref)):
        halves = []
        for half in range(2):
            inside = quotient(place, CAP // 2) == half
            wanted = place - half * (CAP // 2) + (code - 3 * third) * (CAP // 2)
            wanted = jnp.where(inside, wanted, -1)
            chosen = jnp.where(spot == wanted, 1.0, 0.0).astype(BF16)
            halves.append(jnp.dot(chosen, values, preferred_element_type=F32))
        ref[:row_count] = jnp.concatenate(halves, axis=1).astype(BF16)
        ref[row_count:] = atom


def basis_kernel(atoms, dirs_ref, angle_ref, angular_ref):
    slots, _, bonds = angular_ref.shape
    degrees = angle_ref.shape[0]
    weight = (angle_ref[...].astype(F32) * 0.5).T.astype(BF16)
    angles = dirs_ref[...]
    sines = jnp.sin(angles)
    cosines = jnp.cos(angles)
    parts = (
        sines[0:1] * cosines[1:2],
        sines[0:1] * sines[1:2],
        cosines[0:1],
    )
    unit = [jnp.broadcast_to(part, (8, bonds)) for part in parts]
    row = lax.broadcasted_iota(jnp.int32, (8, bonds), 0)
    for diagonal in range(slots):
        if diagonal == 0:
            cosine = unit[0] * unit[0] + unit[1] * unit[1] + unit[2] * unit[2]
        else:
            shift = bonds - atoms * diagonal
            turned = [pltpu.roll(part, shift, 1) for part in unit]
            cosine = unit[0] * turned[0] + unit[1] * turned[1] + unit[2] * turned[2]
        series = [jnp.ones_like(cosine), cosine]
        double = cosine + cosine
        for _ in range(7):
            series.append(double * series[-1] - series[-2])
        lower = series[7]
        upper = series[1]
        for index in range(1, 8):
            lower = jnp.where(row == index, series[7 - index], lower)
            upper = jnp.where(row == index, series[1 + index], upper)
        double = series[8] + series[8]
        blocks = [lower, upper]
        for _ in range(degrees // 8 - 1):
            blocks.append(double * blocks[-1] - blocks[-2])
        basis = jnp.concatenate(blocks[1:], axis=0).astype(BF16)
        angular_ref[diagonal] = jnp.dot(weight, basis, preferred_element_type=F32).astype(BF16)


def prepare_kernel(
    extents,
    paired,
    targets_ref,
    atom_ref,
    bond_ref,
    bond_in_ref,
    bond_mix_ref,
    pair_ref,
    pair_hidden_ref,
    pair_out_ref,
    atom_in_ref,
    atom_out_ref,
    chosen_bond_ref,
    chosen_atom_ref,
    right_half_ref,
    values_ref,
    near_ref,
    far_weight_ref,
    mix_weight_ref,
    pair_weight_ref,
    hidden_weight_ref,
    out_weight_ref,
    atom_in_weight_ref,
    atom_out_weight_ref,
):
    atoms = atom_ref.shape[2]
    feature = atom_ref.shape[3]
    slots = targets_ref.shape[0]
    bonds = slots * atoms
    targets = slot_major(targets_ref[...])
    code_x, code_y = bond_codes(targets, atoms, extents, paired, True)
    code = 3 * code_y + code_x
    bond = lax.broadcasted_iota(jnp.int32, (1, bonds), 1)
    far = (slots - 1 - quotient(bond, atoms)) * atoms + remainder(targets, atoms)
    base = (code * bonds).astype(F32)
    key = base + far.astype(F32)
    column = jnp.broadcast_to(key, (128, bonds)).T
    place = []
    for group in range(bonds // 128):
        here = slice(group * 128, (group + 1) * 128)
        inside = (column < key[:, here]) & (column >= base[:, here])
        place.append(jnp.sum(jnp.where(inside, 1.0, 0.0), axis=0, keepdims=True))
    place = jnp.concatenate(place, axis=1).astype(jnp.int32)
    half = CAP // 2
    spot = lax.broadcasted_iota(jnp.int32, (9 * half, bonds), 0)
    wanted = remainder(place, half) + half * code
    chosen_bond_ref[...] = jnp.where(spot == wanted, 1.0, 0.0).astype(BF16)
    spot = lax.broadcasted_iota(jnp.int32, (9 * atoms // 2, bonds), 0)
    atom = remainder(targets, atoms)
    wanted = remainder(atom, atoms // 2) + atoms // 2 * code
    chosen_atom_ref[...] = jnp.where(spot == wanted, 1.0, 0.0).astype(BF16)
    row = lax.broadcasted_iota(jnp.int32, (8, bonds), 0)
    right_half = jnp.where(row == 0, quotient(place, half), quotient(atom, atoms // 2))
    right_half_ref[...] = right_half.astype(F32)

    atom = atom_ref[0, 0].astype(F32)
    atom = jnp.concatenate([atom] * slots, axis=0)
    values = jnp.concatenate([atom, bond_rows(bond_ref, slots).astype(F32)], axis=1)
    values = values.T.astype(BF16)
    values_ref[...] = values

    def turned(weight, scale):
        return (weight * scale).T.astype(BF16)

    weight = bond_in_ref[...].astype(F32)
    source, other, own = (weight[k * feature : (k + 1) * feature] for k in range(3))
    empty = jnp.zeros((feature, feature), F32)

    def crossed(left, right):
        return jnp.concatenate(
            [left[:, :feature], right[:, :feature], left[:, feature:], right[:, feature:]], axis=1
        )

    blank = jnp.zeros_like(own)
    near = jnp.concatenate([crossed(source, other), crossed(own, blank)], axis=0)
    away = jnp.concatenate([crossed(other, source), crossed(blank, own)], axis=0)
    near_ref[...] = jnp.dot(turned(near, 0.5), values, preferred_element_type=F32)
    far_weight_ref[...] = turned(away, 0.5)
    mix = bond_mix_ref[...].astype(F32)
    mix = jnp.concatenate(
        [jnp.concatenate([mix, empty], axis=1), jnp.concatenate([empty, mix], axis=1)], axis=0
    )
    mix_weight_ref[...] = turned(mix, 0.5)
    pair_weight_ref[...] = turned(pair_ref[...].astype(F32), 0.5)
    hidden_weight_ref[...] = turned(pair_hidden_ref[...].astype(F32), 0.25)
    out_weight = turned(pair_out_ref[...].astype(F32), 0.5)
    out_weight_ref[...] = jnp.concatenate([out_weight] * (slots * atoms // 128), axis=1)
    atom_in_weight_ref[...] = turned(atom_in_ref[...].astype(F32), 0.5)
    atom_out_weight_ref[...] = turned(atom_out_ref[...].astype(F32), 0.5)


def doubled_gate(values):
    half = values.shape[0] // 2
    one = jnp.ones((), values.dtype)
    return values[:half] * (one + jnp.tanh(values[:half])) * (one + jnp.tanh(values[half:]))


def main_kernel(
    own_ref,
    one_ref,
    two_ref,
    four_ref,
    three_ref,
    angular_ref,
    chosen_bond_ref,
    chosen_atom_ref,
    right_half_ref,
    values_ref,
    near_ref,
    far_weight_ref,
    mix_weight_ref,
    pair_weight_ref,
    hidden_weight_ref,
    out_weight_ref,
    atom_in_weight_ref,
    atom_out_weight_ref,
    atom_result_ref,
    bond_result_ref,
    first_ref,
    second_ref,
):
    slots, _, bonds = angular_ref.shape
    atoms = bonds // slots
    feature = values_ref.shape[0] // 2
    half = CAP // 2
    near_refs = (own_ref, one_ref, two_ref)
    away_refs = (three_ref, four_ref)

    def unpacked(parts, chosen, right_half):
        rows = jnp.concatenate(parts, axis=0).astype(F32).T.astype(BF16)
        both = jnp.dot(rows, chosen, preferred_element_type=F32)
        return jnp.where(right_half > 0.0, both[feature:], both[:feature])

    far_bond = unpacked(
        [ref[:half] for ref in near_refs] + [ref[: 3 * half] for ref in away_refs],
        chosen_bond_ref[...],
        right_half_ref[0:1],
    )
    far_atom = unpacked(
        [ref[3 * half :] for ref in near_refs + away_refs],
        chosen_atom_ref[...],
        right_half_ref[1:2],
    )
    far = jnp.concatenate([far_atom, far_bond], axis=0)
    incoming = near_ref[...] + jnp.dot(
        far_weight_ref[...], far.astype(BF16), preferred_element_type=F32
    )
    hidden = doubled_gate(incoming).astype(BF16)
    mixed = jnp.dot(mix_weight_ref[...], hidden, preferred_element_type=F32)
    ahead = (values_ref[feature:].astype(F32) + mixed[:feature]).astype(BF16).astype(F32)
    back = (far_bond + mixed[feature:]).astype(BF16).astype(F32)
    average = ((ahead + back) * 0.5).astype(BF16)
    first_ref[...] = jnp.dot(
        pair_weight_ref[: 2 * feature], average, preferred_element_type=F32
    ).astype(BF16)
    width = 256
    blocks = bonds // 128
    hidden_weight = hidden_weight_ref[...]
    totals = [average.astype(F32)[:, start : start + width] for start in range(0, bonds, width)]
    for turn in range(128 // atoms):
        turned = average.astype(F32)
        if turn > 0:
            turned = pltpu.roll(turned, bonds - atoms * turn, 1)
        second_ref[turn] = jnp.dot(
            pair_weight_ref[2 * feature :], turned.astype(BF16), preferred_element_type=F32
        ).astype(BF16)
        for part, start in enumerate(range(0, bonds, width)):
            gates = []
            for skip in range(blocks):
                pieces = [
                    second_ref[turn, :, pl.ds((start + 128 * (k + skip)) % bonds, 128)]
                    for k in range(width // 128)
                ]
                mixture = angular_ref[skip * (128 // atoms) + turn, :, pl.ds(start, width)] + (
                    first_ref[:, pl.ds(start, width)] + jnp.concatenate(pieces, axis=1)
                )
                second = jnp.dot(
                    hidden_weight, doubled_gate(mixture), preferred_element_type=F32
                )
                gates.append(doubled_gate(second.astype(BF16)))
            totals[part] = totals[part] + jnp.dot(
                out_weight_ref[...], jnp.concatenate(gates, axis=0), preferred_element_type=F32
            )
    bond_out = jnp.concatenate(totals, axis=1).astype(BF16).astype(F32)
    rows = bond_out.T.astype(BF16)
    for slot in range(slots):
        bond_result_ref[0, 0, :, slot * feature : (slot + 1) * feature] = rows[
            slot * atoms : (slot + 1) * atoms
        ]
    pooled = bond_out[:, 0:128]
    for block in range(1, blocks):
        pooled = pooled + bond_out[:, block * 128 : (block + 1) * 128]
    shift = 64
    while shift >= atoms:
        pooled = pooled + pltpu.roll(pooled, shift, 1)
        shift //= 2
    pooled = (pooled * (1.0 / slots)).astype(BF16)
    atom = values_ref[0:feature, 0:128]
    joined = jnp.concatenate([atom, pooled], axis=0)
    atom_hidden = doubled_gate(
        jnp.dot(atom_in_weight_ref[...], joined, preferred_element_type=F32)
    ).astype(BF16)
    atom_new = atom.astype(F32) + jnp.dot(
        atom_out_weight_ref[...], atom_hidden, preferred_element_type=F32
    )
    atom_result_ref[0, 0] = atom_new.T[0:atoms].astype(BF16)


def per_device(
    atom_feat,
    bond_feat,
    neighbours,
    bond_dirs,
    bond_in_weight,
    bond_mix_weight,
    pair_weight,
    angle_weight,
    pair_hidden_weight,
    pair_out_weight,
    atom_in_weight,
    atom_out_weight,
):
    atoms, feature = atom_feat.shape[2], atom_feat.shape[3]
    slots = neighbours.shape[3]
    bonds = atoms * slots
    extents = (lax.axis_size("gx"), lax.axis_size("gy"))
    targets = neighbours[0, 0].T
    dirs = bond_dirs[:, 0, 0].reshape(2, atoms, slots).transpose(0, 2, 1).reshape(2, bonds)
    hbm = pl.BlockSpec(memory_space=pltpu.HBM)
    vmem = pl.BlockSpec(memory_space=pltpu.VMEM)
    params = pltpu.CompilerParams(vmem_limit_bytes=32 * 2**20)

    def shaped(shape, dtype):
        return jax.ShapeDtypeStruct(shape, dtype)

    paired = (extents[0] % 2 == 0, False)
    half = CAP // 2
    payload = shaped((3 * half + atoms // 2, 2 * feature), BF16)
    own, one, two = pl.pallas_call(
        functools.partial(pack_kernel, extents, paired),
        out_shape=(payload, payload, payload),
        in_specs=[hbm, hbm, hbm],
        out_specs=(vmem, vmem, vmem),
        scratch_shapes=[
            pltpu.VMEM(targets.shape, jnp.int32),
            pltpu.VMEM(atom_feat.shape, BF16),
            pltpu.VMEM(bond_feat.shape, BF16),
            pltpu.SemaphoreType.DMA((3,)),
        ],
        compiler_params=params,
        name="pack",
    )(*(pltpu.with_memory_space_constraint(x, pltpu.HBM) for x in (targets, atom_feat, bond_feat)))
    first, second = moves(extents[0], paired[0])
    one = lax.ppermute(one, "gx", first)
    two = lax.ppermute(two, "gx", second)
    angular = pl.pallas_call(
        functools.partial(basis_kernel, atoms),
        out_shape=shaped((slots, 2 * feature, bonds), BF16),
        in_specs=[vmem, vmem],
        out_specs=vmem,
        compiler_params=params,
        cost_estimate=pl.CostEstimate(
            flops=128 * 2**20, bytes_accessed=2**21, transcendentals=4096
        ),
        name="angular",
    )(dirs, angle_weight)
    own, one, two, angular = lax.optimization_barrier((own, one, two, angular))
    first, second = moves(extents[1], paired[1])

    def forwarded(block):
        parts = [x[block * half : (block + 1) * half] for x in (own, one, two)]
        return jnp.concatenate(parts + [x[3 * half :] for x in (own, one, two)], axis=0)

    three = lax.ppermute(forwarded(1), "gy", first)
    four = lax.ppermute(forwarded(2), "gy", second)
    weights = (
        shaped((4 * feature, 2 * feature), BF16),
        shaped((2 * feature, 2 * feature), BF16),
        shaped((4 * feature, feature), BF16),
        shaped((2 * feature, feature), BF16),
        shaped((feature, feature * (bonds // 128)), BF16),
        shaped((2 * feature, 2 * feature), BF16),
        shaped((feature, feature), BF16),
    )
    prepared = pl.pallas_call(
        functools.partial(prepare_kernel, extents, paired),
        out_shape=(
            shaped((9 * half, bonds), BF16),
            shaped((9 * atoms // 2, bonds), BF16),
            shaped((8, bonds), F32),
            shaped((2 * feature, bonds), BF16),
            shaped((4 * feature, bonds), F32),
        )
        + weights,
        in_specs=[vmem] * 10,
        out_specs=(vmem,) * 12,
        compiler_params=params,
        cost_estimate=pl.CostEstimate(flops=64 * 2**20, bytes_accessed=2**21, transcendentals=0),
        name="prepare",
    )(
        targets,
        atom_feat,
        bond_feat,
        bond_in_weight,
        bond_mix_weight,
        pair_weight,
        pair_hidden_weight,
        pair_out_weight,
        atom_in_weight,
        atom_out_weight,
    )
    return pl.pallas_call(
        main_kernel,
        out_shape=(shaped(atom_feat.shape, BF16), shaped(bond_feat.shape, BF16)),
        in_specs=[vmem] * 18,
        out_specs=(vmem, vmem),
        scratch_shapes=[
            pltpu.VMEM((2 * feature, bonds), BF16),
            pltpu.VMEM((128 // atoms, 2 * feature, bonds), BF16),
        ],
        compiler_params=params,
        cost_estimate=pl.CostEstimate(
            flops=400 * 2**20, bytes_accessed=2**22, transcendentals=2**21
        ),
        name="main",
    )(own, one, two, four, three, angular, *prepared)


def solution(mesh):
    placed = (
        P("gx", "gy", None, None),
        P("gx", "gy", None, None),
        P("gx", "gy", None, None),
        P(None, "gx", "gy", None),
        P(),
        P(),
        P(),
        P(),
        P(),
        P(),
        P(),
        P(),
    )
    return jax.shard_map(
        per_device,
        mesh=mesh,
        in_specs=placed,
        out_specs=(P("gx", "gy", None, None), P("gx", "gy", None, None)),
        check_vma=False,
    )
```

```python
import functools

import jax
import jax.numpy as jnp
from jax import lax
from jax.experimental import pallas as pl
from jax.experimental.pallas import tpu as pltpu
from jax.sharding import PartitionSpec as P

F32 = jnp.float32
BF16 = jnp.bfloat16
CAP = 64


def quotient(values, size):
    if size & (size - 1) == 0:
        return values >> (size.bit_length() - 1)
    return lax.div(values, jnp.int32(size))


def remainder(values, size):
    if size & (size - 1) == 0:
        return values & (size - 1)
    return lax.rem(values, jnp.int32(size))


def step_code(owner, home, extent, paired, receives):
    step = remainder(owner - home + 1 + extent, extent)
    if paired:
        ahead = jnp.where(remainder(home, 2) == 0, 0, 2)
    else:
        ahead = 0 if receives else 2
    return jnp.where(step == 1, 0, jnp.where(step == ahead, 1, 2))


def moves(extent, paired):
    if paired:
        near = [(i, i ^ 1) for i in range(extent)]
        return [(i, (((i + 1) ^ 1) - 1) % extent) for i in range(extent)], near
    up = [(i, (i + 1) % extent) for i in range(extent)]
    return up, [(j, i) for i, j in up]


def bond_rows(bond_ref, slots):
    feature = bond_ref.shape[3] // slots
    rows = [bond_ref[0, 0, :, slot * feature : (slot + 1) * feature] for slot in range(slots)]
    return jnp.concatenate(rows, axis=0)


def slot_major(table):
    slots, atoms = table.shape
    per_group = 128 // atoms
    tiled = jnp.concatenate([table.astype(F32)] * per_group, axis=1)
    row = lax.broadcasted_iota(jnp.int32, tiled.shape, 0)
    slot = quotient(lax.broadcasted_iota(jnp.int32, tiled.shape, 1), atoms)
    pieces = [
        jnp.sum(jnp.where(row == slot + group * per_group, tiled, 0.0), axis=0, keepdims=True)
        for group in range(slots // per_group)
    ]
    return jnp.concatenate(pieces, axis=1).astype(jnp.int32)


def bond_codes(targets, atoms, extents, paired, receives):
    owner = quotient(targets, atoms)
    block = (quotient(owner, extents[1]), remainder(owner, extents[1]))
    return tuple(
        step_code(block[k], lax.axis_index(axis), extents[k], paired[k], receives)
        for k, axis in enumerate(("gx", "gy"))
    )


def pack_kernel(
    extents,
    paired,
    targets_hbm,
    atom_hbm,
    bond_hbm,
    dirs_hbm,
    angle_hbm,
    own_ref,
    one_ref,
    two_ref,
    dirs_ref,
    angle_ref,
    targets_ref,
    atom_ref,
    bond_ref,
    sems,
):
    pairs = (
        (targets_hbm, targets_ref),
        (bond_hbm, bond_ref),
        (atom_hbm, atom_ref),
        (dirs_hbm, dirs_ref),
        (angle_hbm, angle_ref),
    )
    copies = [
        pltpu.make_async_copy(source, target, sems.at[k])
        for k, (source, target) in enumerate(pairs)
    ]
    for copy in copies:
        copy.start()
    atoms = atom_ref.shape[2]
    slots = targets_ref.shape[0]
    bonds = slots * atoms
    lanes = 128
    groups = bonds // lanes
    copies[0].wait()
    code_x, code_y = bond_codes(
        slot_major(targets_ref[...]), atoms, extents, paired, False
    )
    code = 3 * code_x + code_y
    rows = lax.broadcasted_iota(jnp.int32, (16, lanes), 0)
    marks = [rows == code[:, g * lanes : (g + 1) * lanes] for g in range(groups)]
    stacked = jnp.concatenate([m.astype(F32) for m in marks], axis=0).astype(BF16)
    before = lax.broadcasted_iota(jnp.int32, (lanes, 2 * lanes), 0)
    after = lax.broadcasted_iota(jnp.int32, (lanes, 2 * lanes), 1)
    sums = jnp.where((before < after) | (after >= lanes), 1.0, 0.0).astype(BF16)
    counted = jnp.dot(stacked, sums, preferred_element_type=F32)
    place = []
    earlier = jnp.zeros((16, lanes), F32)
    for g in range(groups):
        part = counted[g * 16 : (g + 1) * 16]
        place.append(
            jnp.sum(jnp.where(marks[g], part[:, :lanes] + earlier, 0.0), axis=0, keepdims=True)
        )
        earlier = earlier + part[:, lanes:]
    place = jnp.concatenate(place, axis=1).astype(jnp.int32)
    half = CAP // 2
    right = quotient(place, half)
    wanted = 9 * half * right + place - half * right + half * code
    spot = lax.broadcasted_iota(jnp.int32, (9 * CAP, bonds), 0)
    chosen = jnp.where(spot == wanted, 1.0, 0.0).astype(BF16)
    copies[1].wait()
    packed = jnp.dot(chosen, bond_rows(bond_ref, slots), preferred_element_type=F32)
    packed = jnp.concatenate([packed[: 9 * half], packed[9 * half :]], axis=1).astype(BF16)
    copies[2].wait()
    atom = atom_ref[0, 0]
    atom = jnp.concatenate([atom[: atoms // 2], atom[atoms // 2 :]], axis=1)
    for third, ref in enumerate((own_ref, one_ref, two_ref)):
        ref[: 3 * half] = packed[3 * half * third : 3 * half * (third + 1)]
        ref[3 * half :] = atom
    copies[3].wait()
    copies[4].wait()


def basis_kernel(atoms, dirs_ref, angle_ref, angular_ref):
    slots, _, bonds = angular_ref.shape
    degrees = angle_ref.shape[0]
    weight = (angle_ref[...].astype(F32) * 0.5).T.astype(BF16)
    angles = dirs_ref[...]
    sines = jnp.sin(angles)
    cosines = jnp.cos(angles)
    parts = (
        sines[0:1] * cosines[1:2],
        sines[0:1] * sines[1:2],
        cosines[0:1],
    )
    unit = [jnp.broadcast_to(part, (8, bonds)) for part in parts]
    row = lax.broadcasted_iota(jnp.int32, (8, bonds), 0)
    for diagonal in range(slots):
        if diagonal == 0:
            cosine = unit[0] * unit[0] + unit[1] * unit[1] + unit[2] * unit[2]
        else:
            shift = bonds - atoms * diagonal
            turned = [pltpu.roll(part, shift, 1) for part in unit]
            cosine = unit[0] * turned[0] + unit[1] * turned[1] + unit[2] * turned[2]
        series = [jnp.ones_like(cosine), cosine]
        double = cosine + cosine
        for _ in range(7):
            series.append(double * series[-1] - series[-2])
        lower = series[7]
        upper = series[1]
        for index in range(1, 8):
            lower = jnp.where(row == index, series[7 - index], lower)
            upper = jnp.where(row == index, series[1 + index], upper)
        double = series[8] + series[8]
        blocks = [lower, upper]
        for _ in range(degrees // 8 - 1):
            blocks.append(double * blocks[-1] - blocks[-2])
        basis = jnp.concatenate(blocks[1:], axis=0).astype(BF16)
        angular_ref[diagonal] = jnp.dot(weight, basis, preferred_element_type=F32).astype(BF16)


def prepare_kernel(
    extents,
    paired,
    targets_ref,
    atom_ref,
    bond_ref,
    bond_in_ref,
    bond_mix_ref,
    pair_ref,
    pair_hidden_ref,
    pair_out_ref,
    atom_in_ref,
    atom_out_ref,
    chosen_bond_ref,
    chosen_atom_ref,
    right_half_ref,
    values_ref,
    near_ref,
    far_weight_ref,
    mix_weight_ref,
    pair_weight_ref,
    hidden_weight_ref,
    out_weight_ref,
    atom_in_weight_ref,
    atom_out_weight_ref,
):
    atoms = atom_ref.shape[2]
    feature = atom_ref.shape[3]
    slots = targets_ref.shape[0]
    bonds = slots * atoms
    targets = slot_major(targets_ref[...])
    code_x, code_y = bond_codes(targets, atoms, extents, paired, True)
    code = 3 * code_y + code_x
    bond = lax.broadcasted_iota(jnp.int32, (1, bonds), 1)
    far = (slots - 1 - quotient(bond, atoms)) * atoms + remainder(targets, atoms)
    base = (code * bonds).astype(F32)
    key = base + far.astype(F32)
    column = jnp.broadcast_to(key, (128, bonds)).T
    place = []
    for group in range(bonds // 128):
        here = slice(group * 128, (group + 1) * 128)
        inside = (column < key[:, here]) & (column >= base[:, here])
        place.append(jnp.sum(jnp.where(inside, 1.0, 0.0), axis=0, keepdims=True))
    place = jnp.concatenate(place, axis=1).astype(jnp.int32)
    half = CAP // 2
    spot = lax.broadcasted_iota(jnp.int32, (9 * half, bonds), 0)
    wanted = remainder(place, half) + half * code
    chosen_bond_ref[...] = jnp.where(spot == wanted, 1.0, 0.0).astype(BF16)
    spot = lax.broadcasted_iota(jnp.int32, (9 * atoms // 2, bonds), 0)
    atom = remainder(targets, atoms)
    wanted = remainder(atom, atoms // 2) + atoms // 2 * code
    chosen_atom_ref[...] = jnp.where(spot == wanted, 1.0, 0.0).astype(BF16)
    row = lax.broadcasted_iota(jnp.int32, (8, bonds), 0)
    right_half = jnp.where(row == 0, quotient(place, half), quotient(atom, atoms // 2))
    right_half_ref[...] = right_half.astype(F32)

    atom = atom_ref[0, 0].astype(F32)
    atom = jnp.concatenate([atom] * slots, axis=0)
    values = jnp.concatenate([atom, bond_rows(bond_ref, slots).astype(F32)], axis=1)
    values = values.T.astype(BF16)
    values_ref[...] = values

    def turned(weight, scale):
        return (weight * scale).T.astype(BF16)

    weight = bond_in_ref[...].astype(F32)
    source, other, own = (weight[k * feature : (k + 1) * feature] for k in range(3))
    empty = jnp.zeros((feature, feature), F32)

    def crossed(left, right):
        return jnp.concatenate(
            [left[:, :feature], right[:, :feature], left[:, feature:], right[:, feature:]], axis=1
        )

    blank = jnp.zeros_like(own)
    near = jnp.concatenate([crossed(source, other), crossed(own, blank)], axis=0)
    away = jnp.concatenate([crossed(other, source), crossed(blank, own)], axis=0)
    near_ref[...] = jnp.dot(turned(near, 0.5), values, preferred_element_type=F32)
    far_weight_ref[...] = turned(away, 0.5)
    mix = bond_mix_ref[...].astype(F32)
    mix = jnp.concatenate(
        [jnp.concatenate([mix, empty], axis=1), jnp.concatenate([empty, mix], axis=1)], axis=0
    )
    mix_weight_ref[...] = turned(mix, 0.5)
    pair_weight_ref[...] = turned(pair_ref[...].astype(F32), 0.5)
    hidden_weight_ref[...] = turned(pair_hidden_ref[...].astype(F32), 0.25)
    out_weight = turned(pair_out_ref[...].astype(F32), 0.5)
    out_weight_ref[...] = jnp.concatenate([out_weight] * (slots * atoms // 128), axis=1)
    atom_in_weight_ref[...] = turned(atom_in_ref[...].astype(F32), 0.5)
    atom_out_weight_ref[...] = turned(atom_out_ref[...].astype(F32), 0.5)


def doubled_gate(values):
    half = values.shape[0] // 2
    return values[:half] * (1.0 + jnp.tanh(values[:half])) * (1.0 + jnp.tanh(values[half:]))


def main_kernel(
    own_ref,
    one_ref,
    two_ref,
    four_ref,
    three_ref,
    angular_ref,
    chosen_bond_ref,
    chosen_atom_ref,
    right_half_ref,
    values_ref,
    near_ref,
    far_weight_ref,
    mix_weight_ref,
    pair_weight_ref,
    hidden_weight_ref,
    out_weight_ref,
    atom_in_weight_ref,
    atom_out_weight_ref,
    atom_result_hbm,
    bond_result_hbm,
    atom_result_ref,
    bond_result_ref,
    first_ref,
    second_ref,
    sems,
):
    slots, _, bonds = angular_ref.shape
    atoms = bonds // slots
    feature = values_ref.shape[0] // 2
    half = CAP // 2
    near_refs = (own_ref, one_ref, two_ref)
    away_refs = (three_ref, four_ref)

    def unpacked(parts, chosen, right_half):
        rows = jnp.concatenate(parts, axis=0).astype(F32).T.astype(BF16)
        both = jnp.dot(rows, chosen, preferred_element_type=F32)
        return jnp.where(right_half > 0.0, both[feature:], both[:feature])

    far_bond = unpacked(
        [ref[:half] for ref in near_refs] + [ref[: 3 * half] for ref in away_refs],
        chosen_bond_ref[...],
        right_half_ref[0:1],
    )
    far_atom = unpacked(
        [ref[3 * half :] for ref in near_refs + away_refs],
        chosen_atom_ref[...],
        right_half_ref[1:2],
    )
    far = jnp.concatenate([far_atom, far_bond], axis=0)
    incoming = near_ref[...] + jnp.dot(
        far_weight_ref[...], far.astype(BF16), preferred_element_type=F32
    )
    hidden = doubled_gate(incoming).astype(BF16)
    mixed = jnp.dot(mix_weight_ref[...], hidden, preferred_element_type=F32)
    ahead = (values_ref[feature:].astype(F32) + mixed[:feature]).astype(BF16).astype(F32)
    back = (far_bond + mixed[feature:]).astype(BF16).astype(F32)
    average = ((ahead + back) * 0.5).astype(BF16)
    first_ref[...] = jnp.dot(
        pair_weight_ref[: 2 * feature], average, preferred_element_type=F32
    ).astype(BF16)
    width = 256
    blocks = bonds // 128
    hidden_weight = hidden_weight_ref[...]
    totals = [average.astype(F32)[:, start : start + width] for start in range(0, bonds, width)]
    for turn in range(128 // atoms):
        turned = average.astype(F32)
        if turn > 0:
            turned = pltpu.roll(turned, bonds - atoms * turn, 1)
        second_ref[turn] = jnp.dot(
            pair_weight_ref[2 * feature :], turned.astype(BF16), preferred_element_type=F32
        ).astype(BF16)
        for part, start in enumerate(range(0, bonds, width)):
            gates = []
            for skip in range(blocks):
                pieces = [
                    second_ref[turn, :, pl.ds((start + 128 * (k + skip)) % bonds, 128)]
                    for k in range(width // 128)
                ]
                mixture = angular_ref[skip * (128 // atoms) + turn, :, pl.ds(start, width)] + (
                    first_ref[:, pl.ds(start, width)] + jnp.concatenate(pieces, axis=1)
                )
                pair = doubled_gate(mixture.astype(F32)).astype(BF16)
                second = jnp.dot(hidden_weight, pair, preferred_element_type=F32)
                gates.append(doubled_gate(second).astype(BF16))
            totals[part] = totals[part] + jnp.dot(
                out_weight_ref[...], jnp.concatenate(gates, axis=0), preferred_element_type=F32
            )
    bond_out = jnp.concatenate(totals, axis=1).astype(BF16).astype(F32)
    rows = bond_out.T.astype(BF16)
    for slot in range(slots):
        bond_result_ref[0, 0, :, slot * feature : (slot + 1) * feature] = rows[
            slot * atoms : (slot + 1) * atoms
        ]
    bond_copy = pltpu.make_async_copy(bond_result_ref, bond_result_hbm, sems.at[0])
    bond_copy.start()
    pooled = bond_out[:, 0:128]
    for block in range(1, blocks):
        pooled = pooled + bond_out[:, block * 128 : (block + 1) * 128]
    shift = 64
    while shift >= atoms:
        pooled = pooled + pltpu.roll(pooled, shift, 1)
        shift //= 2
    pooled = (pooled * (1.0 / slots)).astype(BF16)
    atom = values_ref[0:feature, 0:128]
    joined = jnp.concatenate([atom, pooled], axis=0)
    atom_hidden = doubled_gate(
        jnp.dot(atom_in_weight_ref[...], joined, preferred_element_type=F32)
    ).astype(BF16)
    atom_new = atom.astype(F32) + jnp.dot(
        atom_out_weight_ref[...], atom_hidden, preferred_element_type=F32
    )
    atom_result_ref[0, 0] = atom_new.T[0:atoms].astype(BF16)
    atom_copy = pltpu.make_async_copy(atom_result_ref, atom_result_hbm, sems.at[1])
    atom_copy.start()
    bond_copy.wait()
    atom_copy.wait()


def per_device(
    atom_feat,
    bond_feat,
    neighbours,
    bond_dirs,
    bond_in_weight,
    bond_mix_weight,
    pair_weight,
    angle_weight,
    pair_hidden_weight,
    pair_out_weight,
    atom_in_weight,
    atom_out_weight,
):
    atoms, feature = atom_feat.shape[2], atom_feat.shape[3]
    slots = neighbours.shape[3]
    bonds = atoms * slots
    extents = (lax.axis_size("gx"), lax.axis_size("gy"))
    targets = neighbours[0, 0].T
    hbm = pl.BlockSpec(memory_space=pltpu.HBM)
    vmem = pl.BlockSpec(memory_space=pltpu.VMEM)
    params = pltpu.CompilerParams(vmem_limit_bytes=32 * 2**20)

    def shaped(shape, dtype):
        return jax.ShapeDtypeStruct(shape, dtype)

    paired = (extents[0] % 2 == 0, False)
    half = CAP // 2
    payload = shaped((3 * half + atoms // 2, 2 * feature), BF16)
    inputs = (targets, atom_feat, bond_feat, bond_dirs, angle_weight)
    own, one, two, bond_dirs, angle_weight = pl.pallas_call(
        functools.partial(pack_kernel, extents, paired),
        out_shape=(payload, payload, payload, shaped(bond_dirs.shape, F32))
        + (shaped(angle_weight.shape, BF16),),
        in_specs=[hbm] * 5,
        out_specs=(vmem,) * 5,
        scratch_shapes=[
            pltpu.VMEM(targets.shape, jnp.int32),
            pltpu.VMEM(atom_feat.shape, BF16),
            pltpu.VMEM(bond_feat.shape, BF16),
            pltpu.SemaphoreType.DMA((5,)),
        ],
        compiler_params=params,
        name="pack",
    )(*(pltpu.with_memory_space_constraint(x, pltpu.HBM) for x in inputs))
    first, second = moves(extents[0], paired[0])
    one = lax.ppermute(one, "gx", first)
    two = lax.ppermute(two, "gx", second)
    dirs = bond_dirs[:, 0, 0].reshape(2, atoms, slots).transpose(0, 2, 1).reshape(2, bonds)
    angular = pl.pallas_call(
        functools.partial(basis_kernel, atoms),
        out_shape=shaped((slots, 2 * feature, bonds), BF16),
        in_specs=[vmem, vmem],
        out_specs=vmem,
        compiler_params=params,
        cost_estimate=pl.CostEstimate(
            flops=128 * 2**20, bytes_accessed=2**21, transcendentals=4096
        ),
        name="angular",
    )(dirs, angle_weight)
    own, one, two, angular = lax.optimization_barrier((own, one, two, angular))
    first, second = moves(extents[1], paired[1])

    def forwarded(block):
        parts = [x[block * half : (block + 1) * half] for x in (own, one, two)]
        return jnp.concatenate(parts + [x[3 * half :] for x in (own, one, two)], axis=0)

    three = lax.ppermute(forwarded(1), "gy", first)
    four = lax.ppermute(forwarded(2), "gy", second)
    weights = (
        shaped((4 * feature, 2 * feature), BF16),
        shaped((2 * feature, 2 * feature), BF16),
        shaped((4 * feature, feature), BF16),
        shaped((2 * feature, feature), BF16),
        shaped((feature, feature * (bonds // 128)), BF16),
        shaped((2 * feature, 2 * feature), BF16),
        shaped((feature, feature), BF16),
    )
    prepared = pl.pallas_call(
        functools.partial(prepare_kernel, extents, paired),
        out_shape=(
            shaped((9 * half, bonds), BF16),
            shaped((9 * atoms // 2, bonds), BF16),
            shaped((8, bonds), F32),
            shaped((2 * feature, bonds), BF16),
            shaped((4 * feature, bonds), F32),
        )
        + weights,
        in_specs=[vmem] * 10,
        out_specs=(vmem,) * 12,
        compiler_params=params,
        cost_estimate=pl.CostEstimate(flops=64 * 2**20, bytes_accessed=2**21, transcendentals=0),
        name="prepare",
    )(
        targets,
        atom_feat,
        bond_feat,
        bond_in_weight,
        bond_mix_weight,
        pair_weight,
        pair_hidden_weight,
        pair_out_weight,
        atom_in_weight,
        atom_out_weight,
    )
    return pl.pallas_call(
        main_kernel,
        out_shape=(shaped(atom_feat.shape, BF16), shaped(bond_feat.shape, BF16)),
        in_specs=[vmem] * 18,
        out_specs=(hbm, hbm),
        scratch_shapes=[
            pltpu.VMEM(atom_feat.shape, BF16),
            pltpu.VMEM(bond_feat.shape, BF16),
            pltpu.VMEM((2 * feature, bonds), BF16),
            pltpu.VMEM((128 // atoms, 2 * feature, bonds), BF16),
            pltpu.SemaphoreType.DMA((2,)),
        ],
        compiler_params=params,
        cost_estimate=pl.CostEstimate(
            flops=400 * 2**20, bytes_accessed=2**22, transcendentals=2**21
        ),
        name="main",
    )(own, one, two, four, three, angular, *prepared)


def solution(mesh):
    placed = (
        P("gx", "gy", None, None),
        P("gx", "gy", None, None),
        P("gx", "gy", None, None),
        P(None, "gx", "gy", None),
        P(),
        P(),
        P(),
        P(),
        P(),
        P(),
        P(),
        P(),
    )
    return jax.shard_map(
        per_device,
        mesh=mesh,
        in_specs=placed,
        out_specs=(P("gx", "gy", None, None), P("gx", "gy", None, None)),
        check_vma=False,
    )
```

```python
import functools

import jax
import jax.numpy as jnp
from jax import lax
from jax.experimental import pallas as pl
from jax.experimental.pallas import tpu as pltpu
from jax.sharding import PartitionSpec as P

F32 = jnp.float32
BF16 = jnp.bfloat16
CAP = 64


def quotient(values, size):
    if size & (size - 1) == 0:
        return values >> (size.bit_length() - 1)
    return lax.div(values, jnp.int32(size))


def remainder(values, size):
    if size & (size - 1) == 0:
        return values & (size - 1)
    return lax.rem(values, jnp.int32(size))


def step_code(owner, home, extent, paired, receives):
    step = remainder(owner - home + 1 + extent, extent)
    if paired:
        ahead = jnp.where(remainder(home, 2) == 0, 0, 2)
    else:
        ahead = 0 if receives else 2
    return jnp.where(step == 1, 0, jnp.where(step == ahead, 1, 2))


def moves(extent, paired):
    if paired:
        near = [(i, i ^ 1) for i in range(extent)]
        return [(i, (((i + 1) ^ 1) - 1) % extent) for i in range(extent)], near
    up = [(i, (i + 1) % extent) for i in range(extent)]
    return up, [(j, i) for i, j in up]


def slot_at(position, slots):
    half = slots // 2
    return jnp.where(position < half, 2 * position, 2 * (position - half) + 1)


def bond_row(table):
    slots, atoms = table.shape
    per_group = 128 // atoms
    tiled = jnp.concatenate([table.astype(F32)] * per_group, axis=1)
    row = lax.broadcasted_iota(jnp.int32, tiled.shape, 0)
    position = quotient(lax.broadcasted_iota(jnp.int32, tiled.shape, 1), atoms)
    pieces = []
    for group in range(slots // per_group):
        chosen = row == slot_at(position + group * per_group, slots)
        pieces.append(jnp.sum(jnp.where(chosen, tiled, 0.0), axis=0, keepdims=True))
    return jnp.concatenate(pieces, axis=1).astype(jnp.int32)


def bond_codes(targets, atoms, extents, paired, receives):
    owner = quotient(targets, atoms)
    block = (quotient(owner, extents[1]), remainder(owner, extents[1]))
    return tuple(
        step_code(block[k], lax.axis_index(axis), extents[k], paired[k], receives)
        for k, axis in enumerate(("gx", "gy"))
    )


def left_lanes(shape):
    return lax.broadcasted_iota(jnp.int32, shape, 1) < shape[1] // 2


def swapped(rows):
    half = rows.shape[1] // 2
    return jnp.concatenate([rows[:, half:], rows[:, :half]], axis=1)


def blocks_of(bond_ref, pairs):
    width = bond_ref.shape[3] // pairs
    return [bond_ref[0, 0, :, k * width : (k + 1) * width] for k in range(pairs)]


def pack_kernel(
    extents,
    paired,
    targets_hbm,
    atom_hbm,
    bond_hbm,
    own_ref,
    one_ref,
    two_ref,
    targets_ref,
    atom_ref,
    bond_ref,
    sems,
):
    sources = ((targets_hbm, targets_ref), (bond_hbm, bond_ref), (atom_hbm, atom_ref))
    copies = [
        pltpu.make_async_copy(source, target, sems.at[k])
        for k, (source, target) in enumerate(sources)
    ]
    for copy in copies:
        copy.start()
    atoms, feature = atom_ref.shape[2], atom_ref.shape[3]
    slots = targets_ref.shape[0]
    bonds = slots * atoms
    lanes = 128
    groups = bonds // lanes
    copies[0].wait()
    code_x, code_y = bond_codes(bond_row(targets_ref[...]), atoms, extents, paired, False)
    code = 3 * code_x + code_y
    rows = lax.broadcasted_iota(jnp.int32, (16, lanes), 0)
    marks = [rows == code[:, g * lanes : (g + 1) * lanes] for g in range(groups)]
    stacked = jnp.concatenate([m.astype(F32) for m in marks], axis=0).astype(BF16)
    before = lax.broadcasted_iota(jnp.int32, (lanes, 2 * lanes), 0)
    after = lax.broadcasted_iota(jnp.int32, (lanes, 2 * lanes), 1)
    sums = jnp.where((before < after) | (after >= lanes), 1.0, 0.0).astype(BF16)
    counted = jnp.dot(stacked, sums, preferred_element_type=F32)
    place = []
    earlier = jnp.zeros((16, lanes), F32)
    for g in range(groups):
        part = counted[g * 16 : (g + 1) * 16]
        place.append(
            jnp.sum(jnp.where(marks[g], part[:, :lanes] + earlier, 0.0), axis=0, keepdims=True)
        )
        earlier = earlier + part[:, lanes:]
    place = jnp.concatenate(place, axis=1).astype(jnp.int32)
    half = CAP // 2
    right = quotient(place, half)
    wanted = 9 * half * right + place - half * right + half * code
    spot = lax.broadcasted_iota(jnp.int32, (9 * CAP, bonds), 0)
    chosen = jnp.where(spot == wanted, 1.0, 0.0).astype(BF16)
    copies[1].wait()
    blocks = blocks_of(bond_ref, slots // 2)
    values = [jnp.concatenate([x[:, :feature]] * 2, axis=1) for x in blocks]
    values += [jnp.concatenate([x[:, feature:]] * 2, axis=1) for x in blocks]
    packed = jnp.dot(chosen, jnp.concatenate(values, axis=0), preferred_element_type=F32)
    packed = jnp.where(
        left_lanes((9 * half, 2 * feature)), packed[: 9 * half], packed[9 * half :]
    ).astype(BF16)
    copies[2].wait()
    atom = atom_ref[0, 0]
    atom = jnp.concatenate([atom[: atoms // 2], atom[atoms // 2 :]], axis=1)
    for third, ref in enumerate((own_ref, one_ref, two_ref)):
        ref[: 3 * half] = packed[3 * half * third : 3 * half * (third + 1)]
        ref[3 * half :] = atom


def crossed(left, right):
    half = left.shape[1] // 2
    parts = [left[:, :half], right[:, :half], left[:, half:], right[:, half:]]
    return jnp.concatenate(parts, axis=1)


def two_blocks(weight):
    blank = jnp.zeros_like(weight)
    return jnp.concatenate([crossed(weight, blank), crossed(blank, weight)], axis=0)


def diagonal_blocks(weight):
    blank = jnp.zeros_like(weight)
    return jnp.concatenate(
        [jnp.concatenate([weight, blank], axis=1), jnp.concatenate([blank, weight], axis=1)],
        axis=0,
    )


def angular_kernel(atoms, dirs_ref, angle_ref, angular_ref):
    slots, pairs, _ = angular_ref.shape
    bonds = 2 * pairs
    degrees = angle_ref.shape[0]
    weight = (two_blocks(angle_ref[...].astype(F32)) * 0.5).astype(BF16)
    polar, azimuth = dirs_ref[0, 0], dirs_ref[1, 0]
    unit = jnp.concatenate(
        [
            jnp.sin(polar) * jnp.cos(azimuth),
            jnp.sin(polar) * jnp.sin(azimuth),
            jnp.cos(polar),
            jnp.zeros((5, bonds), F32),
        ],
        axis=0,
    )
    high = unit.astype(BF16).astype(F32)
    middle = (unit - high).astype(BF16).astype(F32)
    parts = jnp.concatenate([high, middle, unit - high - middle], axis=0).astype(BF16)
    bond = lax.broadcasted_iota(jnp.int32, (1, bonds), 1)
    source = remainder(bond, atoms) * slots + slot_at(quotient(bond, atoms), slots)
    spot = lax.broadcasted_iota(jnp.int32, (bonds, bonds), 0)
    chosen = jnp.where(spot == source, 1.0, 0.0).astype(BF16)
    unit = jnp.dot(parts, chosen, preferred_element_type=F32)
    unit = unit[0:8] + unit[8:16] + unit[16:24]
    even = [jnp.broadcast_to(unit[k : k + 1, :pairs], (8, pairs)) for k in range(3)]
    odd = [jnp.broadcast_to(unit[k : k + 1, pairs:], (8, pairs)) for k in range(3)]
    row = lax.broadcasted_iota(jnp.int32, (8, pairs), 0)

    def turned(vector, places):
        places = places % (pairs // atoms)
        if places == 0:
            return vector
        return [pltpu.roll(part, pairs - atoms * places, 1) for part in vector]

    def basis(first, second):
        cosine = first[0] * second[0] + first[1] * second[1] + first[2] * second[2]
        series = [jnp.ones_like(cosine), cosine]
        double = cosine + cosine
        for _ in range(7):
            series.append(double * series[-1] - series[-2])
        lower = series[7]
        upper = series[1]
        for index in range(1, 8):
            lower = jnp.where(row == index, series[7 - index], lower)
            upper = jnp.where(row == index, series[1 + index], upper)
        double = series[8] + series[8]
        blocks = [lower, upper]
        for _ in range(degrees // 8 - 1):
            blocks.append(double * blocks[-1] - blocks[-2])
        return blocks[1:]

    for diagonal in range(slots):
        places = diagonal // 2
        if diagonal % 2 == 0:
            blocks = basis(even, turned(even, places)) + basis(odd, turned(odd, places))
        else:
            blocks = basis(even, turned(odd, places)) + basis(odd, turned(even, places + 1))
        series = jnp.concatenate(blocks, axis=0).T.astype(BF16)
        angular_ref[diagonal] = jnp.dot(series, weight, preferred_element_type=F32)


def prepare_kernel(
    extents,
    paired,
    targets_ref,
    atom_ref,
    bond_ref,
    bond_in_ref,
    bond_mix_ref,
    pair_ref,
    pair_hidden_ref,
    pair_out_ref,
    atom_in_ref,
    atom_out_ref,
    chosen_ref,
    own_ref,
    near_ref,
    far_weight_ref,
    mix_weight_ref,
    pair_weight_ref,
    hidden_weight_ref,
    out_weight_ref,
    atom_in_weight_ref,
    atom_out_weight_ref,
):
    atoms, feature = atom_ref.shape[2], atom_ref.shape[3]
    slots = targets_ref.shape[0]
    bonds = slots * atoms
    targets = bond_row(targets_ref[...])
    code_x, code_y = bond_codes(targets, atoms, extents, paired, True)
    code = 3 * code_y + code_x
    bond = lax.broadcasted_iota(jnp.int32, (1, bonds), 1)
    far_slot = slots - 1 - slot_at(quotient(bond, atoms), slots)
    far_atom = remainder(targets, atoms)
    far = (remainder(far_slot, 2) * (slots // 2) + quotient(far_slot, 2)) * atoms + far_atom
    base = (code * bonds).astype(F32)
    key = base + far.astype(F32)

    def column(values):
        return jnp.broadcast_to(values.astype(F32), (128, bonds)).T

    keys = column(key)
    place = []
    for group in range(bonds // 128):
        here = slice(group * 128, (group + 1) * 128)
        inside = (keys < key[:, here]) & (keys >= base[:, here])
        place.append(jnp.sum(jnp.where(inside, 1.0, 0.0), axis=0, keepdims=True))
    place = jnp.concatenate(place, axis=1).astype(jnp.int32)
    half, tall = CAP // 2, atoms // 2
    bond_spot = 9 * half * quotient(place, half) + half * code + remainder(place, half)
    atom_spot = 9 * CAP + 9 * tall * quotient(far_atom, tall) + tall * code
    atom_spot = column(atom_spot + remainder(far_atom, tall))
    bond_spot = column(bond_spot)
    total = 9 * CAP + 9 * atoms
    for start in range(0, total, 128):
        width = min(128, total - start)
        spot = lax.broadcasted_iota(jnp.int32, (bonds, 128), 1).astype(F32) + float(start)
        chosen = jnp.where((spot == bond_spot) | (spot == atom_spot), 1.0, 0.0).astype(BF16)
        chosen_ref[:, start : start + width] = chosen[:, :width]

    atom = atom_ref[0, 0]
    blocks = blocks_of(bond_ref, slots // 2)
    own = [jnp.concatenate([atom, x[:, :feature]], axis=1) for x in blocks]
    own += [jnp.concatenate([atom, x[:, feature:]], axis=1) for x in blocks]
    own = jnp.concatenate(own, axis=0)
    own_ref[...] = own

    weight = bond_in_ref[...].astype(F32)
    source, other, bond_part = (weight[k * feature : (k + 1) * feature] for k in range(3))
    blank = jnp.zeros_like(source)
    near = [crossed(other, source), crossed(blank, bond_part)]
    near = (jnp.concatenate(near, axis=0) * 0.5).astype(BF16)
    near_ref[...] = jnp.dot(own, near, preferred_element_type=F32)
    away = [crossed(bond_part, blank), crossed(source, other)]
    far_weight_ref[...] = (jnp.concatenate(away, axis=0) * 0.5).astype(BF16)
    mix_weight_ref[...] = (diagonal_blocks(bond_mix_ref[...].astype(F32)) * 0.5).astype(BF16)
    weight = pair_ref[...].astype(F32) * 0.5
    pair_weight_ref[...] = jnp.concatenate(
        [two_blocks(weight[:, : 2 * feature]), two_blocks(weight[:, 2 * feature :])], axis=1
    ).astype(BF16)
    hidden_weight_ref[...] = (two_blocks(pair_hidden_ref[...].astype(F32)) * 0.25).astype(BF16)
    out_weight_ref[...] = (diagonal_blocks(pair_out_ref[...].astype(F32)) * 0.5).astype(BF16)
    weight = atom_in_ref[...].astype(F32) * 0.5
    atom_in_weight_ref[...] = crossed(weight, jnp.zeros_like(weight)).astype(BF16)
    weight = atom_out_ref[...].astype(F32) * 0.5
    blank = jnp.zeros_like(weight)
    weight = jnp.concatenate([weight, blank], axis=1)
    atom_out_weight_ref[...] = jnp.concatenate([weight, jnp.zeros_like(weight)], axis=0).astype(
        BF16
    )


def doubled_gate(values):
    half = values.shape[1] // 2
    first, second = values[:, :half], values[:, half:]
    return first * (1.0 + jnp.tanh(first)) * (1.0 + jnp.tanh(second))


def main_kernel(
    own_rows_ref,
    one_ref,
    two_ref,
    four_ref,
    three_ref,
    angular_ref,
    chosen_ref,
    own_ref,
    near_ref,
    far_weight_ref,
    mix_weight_ref,
    pair_weight_ref,
    hidden_weight_ref,
    out_weight_ref,
    atom_in_weight_ref,
    atom_out_weight_ref,
    atom_result_hbm,
    bond_result_hbm,
    atom_result_ref,
    bond_result_ref,
    first_ref,
    second_ref,
    sems,
):
    slots, pairs, _ = angular_ref.shape
    bonds = 2 * pairs
    atoms = bonds // slots
    feature = own_ref.shape[1] // 2
    half = CAP // 2
    near_refs = (own_rows_ref, one_ref, two_ref)
    away_refs = (three_ref, four_ref)
    sent = [ref[:half] for ref in near_refs] + [ref[: 3 * half] for ref in away_refs]
    sent = jnp.concatenate(sent, axis=0)
    sent_atom = jnp.concatenate([ref[3 * half :] for ref in near_refs + away_refs], axis=0)
    blank = jnp.zeros((9 * half, feature), BF16)
    blank_atom = jnp.zeros((sent_atom.shape[0], feature), BF16)
    received = jnp.concatenate(
        [
            jnp.concatenate([sent[:, :feature], blank], axis=1),
            jnp.concatenate([sent[:, feature:], blank], axis=1),
            jnp.concatenate([blank_atom, sent_atom[:, :feature]], axis=1),
            jnp.concatenate([blank_atom, sent_atom[:, feature:]], axis=1),
        ],
        axis=0,
    )
    far = jnp.dot(chosen_ref[...], received, preferred_element_type=F32)
    incoming = near_ref[...] + jnp.dot(
        far.astype(BF16), far_weight_ref[...], preferred_element_type=F32
    )
    hidden = doubled_gate(incoming).astype(BF16)
    mixed = jnp.dot(hidden, mix_weight_ref[...], preferred_element_type=F32)
    old = jnp.where(left_lanes((bonds, 2 * feature)), far, own_ref[...].astype(F32))
    new = (old + mixed).astype(BF16).astype(F32)
    average = ((new + pltpu.roll(new, feature, 1)) * 0.5).astype(BF16).astype(F32)
    even, odd = average[:pairs], average[pairs:]
    left = left_lanes((pairs, 2 * feature))
    packed = jnp.where(left, even, odd)
    shifted = jnp.where(left, odd, jnp.concatenate([even[atoms:], even[:atoms]], axis=0))
    width = 4 * feature
    projected = jnp.dot(packed.astype(BF16), pair_weight_ref[...], preferred_element_type=F32)
    first_ref[...] = projected[:, :width]
    second_ref[0] = projected[:, width:]
    second_ref[1] = jnp.dot(
        shifted.astype(BF16), pair_weight_ref[:, width:], preferred_element_type=F32
    )
    hidden_weight = hidden_weight_ref[...]
    height = pairs // 2
    totals = []
    for start in range(0, pairs, height):
        total = jnp.zeros((height, 2 * feature), F32)
        for diagonal in range(slots):
            offset = start + diagonal // 2 * atoms
            pieces = [
                second_ref[diagonal % 2, pl.ds((offset + k) % pairs, atoms)]
                for k in range(0, height, atoms)
            ]
            mixture = angular_ref[diagonal, pl.ds(start, height)] + (
                first_ref[pl.ds(start, height)] + jnp.concatenate(pieces, axis=0)
            )
            pair = doubled_gate(mixture).astype(BF16)
            total = total + doubled_gate(
                jnp.dot(pair, hidden_weight, preferred_element_type=F32)
            )
        totals.append(total)
    pair_sum = jnp.concatenate(totals, axis=0).astype(BF16)
    bond_out = packed + jnp.dot(pair_sum, out_weight_ref[...], preferred_element_type=F32)
    bond_out = bond_out.astype(BF16)
    for k in range(slots // 2):
        bond_result_ref[0, 0, :, 2 * k * feature : 2 * (k + 1) * feature] = bond_out[
            k * atoms : (k + 1) * atoms
        ]
    bond_copy = pltpu.make_async_copy(bond_result_ref, bond_result_hbm, sems.at[0])
    bond_copy.start()
    pooled = jnp.zeros((atoms, 2 * feature), F32)
    for k in range(slots // 2):
        pooled = pooled + bond_out[k * atoms : (k + 1) * atoms].astype(F32)
    pooled = (pooled + pltpu.roll(pooled, feature, 1)) * (1.0 / slots)
    atom = own_ref[0:atoms].astype(F32)
    left = left_lanes((atoms, 2 * feature))
    joined = jnp.where(left, atom, pooled).astype(BF16)
    atom_hidden = doubled_gate(
        jnp.dot(joined, atom_in_weight_ref[...], preferred_element_type=F32)
    ).astype(BF16)
    atom_new = atom + jnp.dot(atom_hidden, atom_out_weight_ref[...], preferred_element_type=F32)
    atom_result_ref[0, 0] = atom_new[:, :feature].astype(BF16)
    atom_copy = pltpu.make_async_copy(atom_result_ref, atom_result_hbm, sems.at[1])
    atom_copy.start()
    bond_copy.wait()
    atom_copy.wait()


def per_device(
    atom_feat,
    bond_feat,
    neighbours,
    bond_dirs,
    bond_in_weight,
    bond_mix_weight,
    pair_weight,
    angle_weight,
    pair_hidden_weight,
    pair_out_weight,
    atom_in_weight,
    atom_out_weight,
):
    atoms, feature = atom_feat.shape[2], atom_feat.shape[3]
    slots = neighbours.shape[3]
    bonds = atoms * slots
    pairs = bonds // 2
    half = CAP // 2
    extents = (lax.axis_size("gx"), lax.axis_size("gy"))
    paired = (extents[0] % 2 == 0, False)
    targets = neighbours[0, 0].T
    hbm = pl.BlockSpec(memory_space=pltpu.HBM)
    vmem = pl.BlockSpec(memory_space=pltpu.VMEM)
    params = pltpu.CompilerParams(vmem_limit_bytes=32 * 2**20)

    def shaped(shape, dtype):
        return jax.ShapeDtypeStruct(shape, dtype)

    payload = shaped((3 * half + atoms // 2, 2 * feature), BF16)
    inputs = (targets, atom_feat, bond_feat)
    own, one, two = pl.pallas_call(
        functools.partial(pack_kernel, extents, paired),
        out_shape=(payload, payload, payload),
        in_specs=[hbm] * 3,
        out_specs=(vmem,) * 3,
        scratch_shapes=[
            pltpu.VMEM(targets.shape, jnp.int32),
            pltpu.VMEM(atom_feat.shape, BF16),
            pltpu.VMEM(bond_feat.shape, BF16),
            pltpu.SemaphoreType.DMA((3,)),
        ],
        compiler_params=params,
        name="pack",
    )(*(pltpu.with_memory_space_constraint(x, pltpu.HBM) for x in inputs))
    first, second = moves(extents[0], paired[0])
    one = lax.ppermute(one, "gx", first)
    two = lax.ppermute(two, "gx", second)
    prepared = pl.pallas_call(
        functools.partial(prepare_kernel, extents, paired),
        out_shape=(
            shaped((bonds, 9 * CAP + 9 * atoms), BF16),
            shaped((bonds, 2 * feature), BF16),
            shaped((bonds, 4 * feature), F32),
            shaped((2 * feature, 4 * feature), BF16),
            shaped((2 * feature, 2 * feature), BF16),
            shaped((2 * feature, 8 * feature), BF16),
            shaped((2 * feature, 4 * feature), BF16),
            shaped((2 * feature, 2 * feature), BF16),
            shaped((2 * feature, 4 * feature), BF16),
            shaped((2 * feature, 2 * feature), BF16),
        ),
        in_specs=[vmem] * 10,
        out_specs=(vmem,) * 10,
        compiler_params=params,
        cost_estimate=pl.CostEstimate(flops=64 * 2**20, bytes_accessed=2**21, transcendentals=0),
        name="prepare",
    )(
        targets,
        atom_feat,
        bond_feat,
        bond_in_weight,
        bond_mix_weight,
        pair_weight,
        pair_hidden_weight,
        pair_out_weight,
        atom_in_weight,
        atom_out_weight,
    )
    own, one, two, prepared = lax.optimization_barrier((own, one, two, prepared))
    first, second = moves(extents[1], paired[1])

    def forwarded(block):
        parts = [x[block * half : (block + 1) * half] for x in (own, one, two)]
        return jnp.concatenate(parts + [x[3 * half :] for x in (own, one, two)], axis=0)

    three = lax.ppermute(forwarded(1), "gy", first)
    four = lax.ppermute(forwarded(2), "gy", second)
    angular = pl.pallas_call(
        functools.partial(angular_kernel, atoms),
        out_shape=shaped((slots, pairs, 4 * feature), F32),
        in_specs=[vmem, vmem],
        out_specs=vmem,
        compiler_params=params,
        cost_estimate=pl.CostEstimate(
            flops=256 * 2**20, bytes_accessed=2**22, transcendentals=4096
        ),
        name="angular",
    )(bond_dirs, angle_weight)
    return pl.pallas_call(
        main_kernel,
        out_shape=(shaped(atom_feat.shape, BF16), shaped(bond_feat.shape, BF16)),
        in_specs=[vmem] * 16,
        out_specs=(hbm, hbm),
        scratch_shapes=[
            pltpu.VMEM(atom_feat.shape, BF16),
            pltpu.VMEM(bond_feat.shape, BF16),
            pltpu.VMEM((pairs, 4 * feature), F32),
            pltpu.VMEM((2, pairs, 4 * feature), F32),
            pltpu.SemaphoreType.DMA((2,)),
        ],
        compiler_params=params,
        cost_estimate=pl.CostEstimate(
            flops=400 * 2**20, bytes_accessed=2**22, transcendentals=2**21
        ),
        name="main",
    )(own, one, two, four, three, angular, *prepared)


def solution(mesh):
    placed = (
        P("gx", "gy", None, None),
        P("gx", "gy", None, None),
        P("gx", "gy", None, None),
        P(None, "gx", "gy", None),
        P(),
        P(),
        P(),
        P(),
        P(),
        P(),
        P(),
        P(),
    )
    return jax.shard_map(
        per_device,
        mesh=mesh,
        in_specs=placed,
        out_specs=(P("gx", "gy", None, None), P("gx", "gy", None, None)),
        check_vma=False,
    )
```

```python
import functools

import jax
import jax.numpy as jnp
from jax import lax
from jax.experimental import pallas as pl
from jax.experimental.pallas import tpu as pltpu
from jax.sharding import PartitionSpec as P

F32 = jnp.float32
BF16 = jnp.bfloat16
CAP = 64


def quotient(values, size):
    if size & (size - 1) == 0:
        return values >> (size.bit_length() - 1)
    return lax.div(values, jnp.int32(size))


def remainder(values, size):
    if size & (size - 1) == 0:
        return values & (size - 1)
    return lax.rem(values, jnp.int32(size))


def step_code(owner, home, extent, paired, receives):
    step = remainder(owner - home + 1 + extent, extent)
    if paired:
        ahead = jnp.where(remainder(home, 2) == 0, 0, 2)
    else:
        ahead = 0 if receives else 2
    return jnp.where(step == 1, 0, jnp.where(step == ahead, 1, 2))


def moves(extent, paired):
    if paired:
        near = [(i, i ^ 1) for i in range(extent)]
        return [(i, (((i + 1) ^ 1) - 1) % extent) for i in range(extent)], near
    up = [(i, (i + 1) % extent) for i in range(extent)]
    return up, [(j, i) for i, j in up]


def slot_at(position, slots):
    half = slots // 2
    return jnp.where(position < half, 2 * position, 2 * (position - half) + 1)


def bond_row(table):
    slots, atoms = table.shape
    per_group = 128 // atoms
    tiled = jnp.concatenate([table.astype(F32)] * per_group, axis=1)
    row = lax.broadcasted_iota(jnp.int32, tiled.shape, 0)
    position = quotient(lax.broadcasted_iota(jnp.int32, tiled.shape, 1), atoms)
    pieces = []
    for group in range(slots // per_group):
        chosen = row == slot_at(position + group * per_group, slots)
        pieces.append(jnp.sum(jnp.where(chosen, tiled, 0.0), axis=0, keepdims=True))
    return jnp.concatenate(pieces, axis=1).astype(jnp.int32)


def bond_codes(targets, atoms, extents, paired, receives):
    owner = quotient(targets, atoms)
    block = (quotient(owner, extents[1]), remainder(owner, extents[1]))
    return tuple(
        step_code(block[k], lax.axis_index(axis), extents[k], paired[k], receives)
        for k, axis in enumerate(("gx", "gy"))
    )


def left_lanes(shape):
    return lax.broadcasted_iota(jnp.int32, shape, 1) < shape[1] // 2


def swapped(rows):
    half = rows.shape[1] // 2
    return jnp.concatenate([rows[:, half:], rows[:, :half]], axis=1)


def blocks_of(bond_ref, pairs):
    width = bond_ref.shape[3] // pairs
    return [bond_ref[0, 0, :, k * width : (k + 1) * width] for k in range(pairs)]


def pack_kernel(
    extents,
    paired,
    targets_hbm,
    atom_hbm,
    bond_hbm,
    own_ref,
    one_ref,
    two_ref,
    targets_ref,
    atom_ref,
    bond_ref,
    sems,
):
    sources = ((targets_hbm, targets_ref), (bond_hbm, bond_ref), (atom_hbm, atom_ref))
    copies = [
        pltpu.make_async_copy(source, target, sems.at[k])
        for k, (source, target) in enumerate(sources)
    ]
    for copy in copies:
        copy.start()
    atoms, feature = atom_ref.shape[2], atom_ref.shape[3]
    slots = targets_ref.shape[0]
    bonds = slots * atoms
    lanes = 128
    groups = bonds // lanes
    copies[0].wait()
    code_x, code_y = bond_codes(bond_row(targets_ref[...]), atoms, extents, paired, False)
    code = 3 * code_x + code_y
    rows = lax.broadcasted_iota(jnp.int32, (16, lanes), 0)
    marks = [rows == code[:, g * lanes : (g + 1) * lanes] for g in range(groups)]
    stacked = jnp.concatenate([m.astype(F32) for m in marks], axis=0).astype(BF16)
    before = lax.broadcasted_iota(jnp.int32, (lanes, 2 * lanes), 0)
    after = lax.broadcasted_iota(jnp.int32, (lanes, 2 * lanes), 1)
    sums = jnp.where((before < after) | (after >= lanes), 1.0, 0.0).astype(BF16)
    counted = jnp.dot(stacked, sums, preferred_element_type=F32)
    place = []
    earlier = jnp.zeros((16, lanes), F32)
    for g in range(groups):
        part = counted[g * 16 : (g + 1) * 16]
        place.append(
            jnp.sum(jnp.where(marks[g], part[:, :lanes] + earlier, 0.0), axis=0, keepdims=True)
        )
        earlier = earlier + part[:, lanes:]
    place = jnp.concatenate(place, axis=1).astype(jnp.int32)
    half = CAP // 2
    right = quotient(place, half)
    wanted = 9 * half * right + place - half * right + half * code
    spot = lax.broadcasted_iota(jnp.int32, (9 * CAP, bonds), 0)
    chosen = jnp.where(spot == wanted, 1.0, 0.0).astype(BF16)
    copies[1].wait()
    blocks = blocks_of(bond_ref, slots // 2)
    values = [jnp.concatenate([x[:, :feature]] * 2, axis=1) for x in blocks]
    values += [jnp.concatenate([x[:, feature:]] * 2, axis=1) for x in blocks]
    packed = jnp.dot(chosen, jnp.concatenate(values, axis=0), preferred_element_type=F32)
    packed = jnp.where(
        left_lanes((9 * half, 2 * feature)), packed[: 9 * half], packed[9 * half :]
    ).astype(BF16)
    copies[2].wait()
    atom = atom_ref[0, 0]
    atom = jnp.concatenate([atom[: atoms // 2], atom[atoms // 2 :]], axis=1)
    for third, ref in enumerate((own_ref, one_ref, two_ref)):
        ref[: 3 * half] = packed[3 * half * third : 3 * half * (third + 1)]
        ref[3 * half :] = atom


def crossed(left, right):
    half = left.shape[1] // 2
    parts = [left[:, :half], right[:, :half], left[:, half:], right[:, half:]]
    return jnp.concatenate(parts, axis=1)


def two_blocks(weight):
    blank = jnp.zeros_like(weight)
    return jnp.concatenate([crossed(weight, blank), crossed(blank, weight)], axis=0)


def diagonal_blocks(weight):
    blank = jnp.zeros_like(weight)
    return jnp.concatenate(
        [jnp.concatenate([weight, blank], axis=1), jnp.concatenate([blank, weight], axis=1)],
        axis=0,
    )


def angular_kernel(atoms, dirs_ref, angle_ref, angular_ref):
    slots, pairs, _ = angular_ref.shape
    bonds = 2 * pairs
    degrees = angle_ref.shape[0]
    weight = (two_blocks(angle_ref[...].astype(F32)) * 0.5).astype(BF16)
    polar, azimuth = dirs_ref[0, 0], dirs_ref[1, 0]
    unit = jnp.concatenate(
        [
            jnp.sin(polar) * jnp.cos(azimuth),
            jnp.sin(polar) * jnp.sin(azimuth),
            jnp.cos(polar),
            jnp.zeros((5, bonds), F32),
        ],
        axis=0,
    )
    high = unit.astype(BF16).astype(F32)
    middle = (unit - high).astype(BF16).astype(F32)
    parts = jnp.concatenate([high, middle, unit - high - middle], axis=0).astype(BF16)
    bond = lax.broadcasted_iota(jnp.int32, (1, bonds), 1)
    source = remainder(bond, atoms) * slots + slot_at(quotient(bond, atoms), slots)
    spot = lax.broadcasted_iota(jnp.int32, (bonds, bonds), 0)
    chosen = jnp.where(spot == source, 1.0, 0.0).astype(BF16)
    unit = jnp.dot(parts, chosen, preferred_element_type=F32)
    unit = unit[0:8] + unit[8:16] + unit[16:24]
    even = [jnp.broadcast_to(unit[k : k + 1, :pairs], (8, pairs)) for k in range(3)]
    odd = [jnp.broadcast_to(unit[k : k + 1, pairs:], (8, pairs)) for k in range(3)]
    row = lax.broadcasted_iota(jnp.int32, (8, pairs), 0)

    def turned(vector, places):
        places = places % (pairs // atoms)
        if places == 0:
            return vector
        return [pltpu.roll(part, pairs - atoms * places, 1) for part in vector]

    def basis(first, second):
        cosine = first[0] * second[0] + first[1] * second[1] + first[2] * second[2]
        series = [jnp.ones_like(cosine), cosine]
        double = cosine + cosine
        for _ in range(7):
            series.append(double * series[-1] - series[-2])
        lower = series[7]
        upper = series[1]
        for index in range(1, 8):
            lower = jnp.where(row == index, series[7 - index], lower)
            upper = jnp.where(row == index, series[1 + index], upper)
        double = series[8] + series[8]
        blocks = [lower, upper]
        for _ in range(degrees // 8 - 1):
            blocks.append(double * blocks[-1] - blocks[-2])
        return blocks[1:]

    for diagonal in range(slots):
        places = diagonal // 2
        if diagonal % 2 == 0:
            blocks = basis(even, turned(even, places)) + basis(odd, turned(odd, places))
        else:
            blocks = basis(even, turned(odd, places)) + basis(odd, turned(even, places + 1))
        series = jnp.concatenate(blocks, axis=0).T.astype(BF16)
        angular_ref[diagonal] = jnp.dot(series, weight, preferred_element_type=F32)


def prepare_kernel(
    extents,
    paired,
    targets_ref,
    atom_ref,
    bond_ref,
    *refs,
):
    sources, results, held, sems = refs[:9], refs[9:21], refs[21:28], refs[28]
    chosen_ref, own_ref, near_ref, far_weight_ref, mix_weight_ref, pair_weight_ref = results[:6]
    hidden_weight_ref, out_weight_ref, atom_in_weight_ref, atom_out_weight_ref = results[6:10]
    bond_in_ref, bond_mix_ref, pair_ref, pair_hidden_ref, pair_out_ref = held[:5]
    atom_in_ref, atom_out_ref = held[5:]
    copies = [
        pltpu.make_async_copy(source, target, sems.at[k])
        for k, (source, target) in enumerate(zip(sources, held + results[10:]))
    ]
    for copy in copies:
        copy.start()
    atoms, feature = atom_ref.shape[2], atom_ref.shape[3]
    slots = targets_ref.shape[0]
    bonds = slots * atoms
    targets = bond_row(targets_ref[...])
    code_x, code_y = bond_codes(targets, atoms, extents, paired, True)
    code = 3 * code_y + code_x
    bond = lax.broadcasted_iota(jnp.int32, (1, bonds), 1)
    far_slot = slots - 1 - slot_at(quotient(bond, atoms), slots)
    far_atom = remainder(targets, atoms)
    far = (remainder(far_slot, 2) * (slots // 2) + quotient(far_slot, 2)) * atoms + far_atom
    base = (code * bonds).astype(F32)
    key = base + far.astype(F32)

    def column(values):
        return jnp.broadcast_to(values.astype(F32), (128, bonds)).T

    keys = column(key)
    place = []
    for group in range(bonds // 128):
        here = slice(group * 128, (group + 1) * 128)
        inside = (keys < key[:, here]) & (keys >= base[:, here])
        place.append(jnp.sum(jnp.where(inside, 1.0, 0.0), axis=0, keepdims=True))
    place = jnp.concatenate(place, axis=1).astype(jnp.int32)
    half, tall = CAP // 2, atoms // 2
    bond_spot = 9 * half * quotient(place, half) + half * code + remainder(place, half)
    atom_spot = 9 * CAP + 9 * tall * quotient(far_atom, tall) + tall * code
    atom_spot = column(atom_spot + remainder(far_atom, tall))
    bond_spot = column(bond_spot)
    total = 9 * CAP + 9 * atoms
    for start in range(0, total, 128):
        width = min(128, total - start)
        spot = lax.broadcasted_iota(jnp.int32, (bonds, 128), 1).astype(F32) + float(start)
        chosen = jnp.where((spot == bond_spot) | (spot == atom_spot), 1.0, 0.0).astype(BF16)
        chosen_ref[:, start : start + width] = chosen[:, :width]

    atom = atom_ref[0, 0]
    blocks = blocks_of(bond_ref, slots // 2)
    own = [jnp.concatenate([atom, x[:, :feature]], axis=1) for x in blocks]
    own += [jnp.concatenate([atom, x[:, feature:]], axis=1) for x in blocks]
    own = jnp.concatenate(own, axis=0)
    own_ref[...] = own

    for copy in copies:
        copy.wait()
    weight = bond_in_ref[...].astype(F32)
    source, other, bond_part = (weight[k * feature : (k + 1) * feature] for k in range(3))
    blank = jnp.zeros_like(source)
    near = [crossed(other, source), crossed(blank, bond_part)]
    near = (jnp.concatenate(near, axis=0) * 0.5).astype(BF16)
    near_ref[...] = jnp.dot(own, near, preferred_element_type=F32)
    away = [crossed(bond_part, blank), crossed(source, other)]
    far_weight_ref[...] = (jnp.concatenate(away, axis=0) * 0.5).astype(BF16)
    mix_weight_ref[...] = (diagonal_blocks(bond_mix_ref[...].astype(F32)) * 0.5).astype(BF16)
    weight = pair_ref[...].astype(F32) * 0.5
    pair_weight_ref[...] = jnp.concatenate(
        [two_blocks(weight[:, : 2 * feature]), two_blocks(weight[:, 2 * feature :])], axis=1
    ).astype(BF16)
    hidden_weight_ref[...] = (two_blocks(pair_hidden_ref[...].astype(F32)) * 0.25).astype(BF16)
    out_weight_ref[...] = (diagonal_blocks(pair_out_ref[...].astype(F32)) * 0.5).astype(BF16)
    weight = atom_in_ref[...].astype(F32) * 0.5
    atom_in_weight_ref[...] = crossed(weight, jnp.zeros_like(weight)).astype(BF16)
    weight = atom_out_ref[...].astype(F32) * 0.5
    blank = jnp.zeros_like(weight)
    weight = jnp.concatenate([weight, blank], axis=1)
    atom_out_weight_ref[...] = jnp.concatenate([weight, jnp.zeros_like(weight)], axis=0).astype(
        BF16
    )


def doubled_gate(values):
    half = values.shape[1] // 2
    first, second = values[:, :half], values[:, half:]
    return first * (1.0 + jnp.tanh(first)) * (1.0 + jnp.tanh(second))


def main_kernel(
    own_rows_ref,
    one_ref,
    two_ref,
    four_ref,
    three_ref,
    angular_ref,
    chosen_ref,
    own_ref,
    near_ref,
    far_weight_ref,
    mix_weight_ref,
    pair_weight_ref,
    hidden_weight_ref,
    out_weight_ref,
    atom_in_weight_ref,
    atom_out_weight_ref,
    atom_result_hbm,
    bond_result_hbm,
    atom_result_ref,
    bond_result_ref,
    first_ref,
    second_ref,
    pair_ref,
    total_ref,
    sems,
):
    slots, pairs, _ = angular_ref.shape
    bonds = 2 * pairs
    atoms = bonds // slots
    feature = own_ref.shape[1] // 2
    half = CAP // 2
    near_refs = (own_rows_ref, one_ref, two_ref)
    away_refs = (three_ref, four_ref)
    sent = [ref[:half] for ref in near_refs] + [ref[: 3 * half] for ref in away_refs]
    sent = jnp.concatenate(sent, axis=0)
    sent_atom = jnp.concatenate([ref[3 * half :] for ref in near_refs + away_refs], axis=0)
    blank = jnp.zeros((9 * half, feature), BF16)
    blank_atom = jnp.zeros((sent_atom.shape[0], feature), BF16)
    received = jnp.concatenate(
        [
            jnp.concatenate([sent[:, :feature], blank], axis=1),
            jnp.concatenate([sent[:, feature:], blank], axis=1),
            jnp.concatenate([blank_atom, sent_atom[:, :feature]], axis=1),
            jnp.concatenate([blank_atom, sent_atom[:, feature:]], axis=1),
        ],
        axis=0,
    )
    far = jnp.dot(chosen_ref[...], received, preferred_element_type=F32)
    incoming = near_ref[...] + jnp.dot(
        far.astype(BF16), far_weight_ref[...], preferred_element_type=F32
    )
    hidden = doubled_gate(incoming).astype(BF16)
    mixed = jnp.dot(hidden, mix_weight_ref[...], preferred_element_type=F32)
    old = jnp.where(left_lanes((bonds, 2 * feature)), far, own_ref[...].astype(F32))
    new = (old + mixed).astype(BF16).astype(F32)
    average = ((new + pltpu.roll(new, feature, 1)) * 0.5).astype(BF16).astype(F32)
    even, odd = average[:pairs], average[pairs:]
    left = left_lanes((pairs, 2 * feature))
    packed = jnp.where(left, even, odd)
    shifted = jnp.where(left, odd, jnp.concatenate([even[atoms:], even[:atoms]], axis=0))
    width = 4 * feature
    projected = jnp.dot(packed.astype(BF16), pair_weight_ref[...], preferred_element_type=F32)
    first_ref[...] = projected[:, :width]
    second = jnp.dot(shifted.astype(BF16), pair_weight_ref[:, width:], preferred_element_type=F32)
    for copy in range(2):
        second_ref[0, copy * pairs : (copy + 1) * pairs] = projected[:, width:]
        second_ref[1, copy * pairs : (copy + 1) * pairs] = second
    hidden_weight = hidden_weight_ref[...]
    height = pairs // 2
    steps = [(parity, start) for start in (0, height) for parity in (0, 1)]

    def first_gates(turn):
        for step, (parity, start) in enumerate(steps):
            offset = pl.multiple_of(start + turn * atoms, atoms)
            mixture = angular_ref[2 * turn + parity, pl.ds(start, height)] + (
                first_ref[pl.ds(start, height)] + second_ref[parity, pl.ds(offset, height)]
            )
            pair_ref[step] = doubled_gate(mixture).astype(BF16)

    def second_gates():
        gates = [
            doubled_gate(jnp.dot(pair_ref[k], hidden_weight, preferred_element_type=F32))
            for k in range(len(steps))
        ]
        for part, start in enumerate((0, height)):
            total_ref[pl.ds(start, height)] += gates[2 * part] + gates[2 * part + 1]

    def body(turn, carry):
        second_gates()
        first_gates(turn)
        return carry

    total_ref[...] = jnp.zeros_like(total_ref)
    first_gates(0)
    lax.fori_loop(1, slots // 2, body, 0)
    second_gates()
    pair_sum = total_ref[...].astype(BF16)
    bond_out = packed + jnp.dot(pair_sum, out_weight_ref[...], preferred_element_type=F32)
    bond_out = bond_out.astype(BF16)
    for k in range(slots // 2):
        bond_result_ref[0, 0, :, 2 * k * feature : 2 * (k + 1) * feature] = bond_out[
            k * atoms : (k + 1) * atoms
        ]
    bond_copy = pltpu.make_async_copy(bond_result_ref, bond_result_hbm, sems.at[0])
    bond_copy.start()
    pooled = jnp.zeros((atoms, 2 * feature), F32)
    for k in range(slots // 2):
        pooled = pooled + bond_out[k * atoms : (k + 1) * atoms].astype(F32)
    pooled = (pooled + pltpu.roll(pooled, feature, 1)) * (1.0 / slots)
    atom = own_ref[0:atoms].astype(F32)
    left = left_lanes((atoms, 2 * feature))
    joined = jnp.where(left, atom, pooled).astype(BF16)
    atom_hidden = doubled_gate(
        jnp.dot(joined, atom_in_weight_ref[...], preferred_element_type=F32)
    ).astype(BF16)
    atom_new = atom + jnp.dot(atom_hidden, atom_out_weight_ref[...], preferred_element_type=F32)
    atom_result_ref[0, 0] = atom_new[:, :feature].astype(BF16)
    atom_copy = pltpu.make_async_copy(atom_result_ref, atom_result_hbm, sems.at[1])
    atom_copy.start()
    bond_copy.wait()
    atom_copy.wait()


def per_device(
    atom_feat,
    bond_feat,
    neighbours,
    bond_dirs,
    bond_in_weight,
    bond_mix_weight,
    pair_weight,
    angle_weight,
    pair_hidden_weight,
    pair_out_weight,
    atom_in_weight,
    atom_out_weight,
):
    atoms, feature = atom_feat.shape[2], atom_feat.shape[3]
    slots = neighbours.shape[3]
    bonds = atoms * slots
    pairs = bonds // 2
    half = CAP // 2
    extents = (lax.axis_size("gx"), lax.axis_size("gy"))
    paired = (extents[0] % 2 == 0, False)
    targets = neighbours[0, 0].T
    hbm = pl.BlockSpec(memory_space=pltpu.HBM)
    vmem = pl.BlockSpec(memory_space=pltpu.VMEM)
    params = pltpu.CompilerParams(vmem_limit_bytes=32 * 2**20)

    def shaped(shape, dtype):
        return jax.ShapeDtypeStruct(shape, dtype)

    def in_hbm(arrays):
        return tuple(pltpu.with_memory_space_constraint(x, pltpu.HBM) for x in arrays)

    payload = shaped((3 * half + atoms // 2, 2 * feature), BF16)
    inputs = (targets, atom_feat, bond_feat)
    own, one, two, *held = pl.pallas_call(
        functools.partial(pack_kernel, extents, paired),
        out_shape=(payload,) * 3 + tuple(shaped(x.shape, x.dtype) for x in inputs),
        in_specs=[hbm] * 3,
        out_specs=(vmem,) * 6,
        scratch_shapes=[pltpu.SemaphoreType.DMA((3,))],
        compiler_params=params,
        name="pack",
    )(*in_hbm(inputs))
    first, second = moves(extents[0], paired[0])
    one = lax.ppermute(one, "gx", first)
    two = lax.ppermute(two, "gx", second)
    weights = (bond_in_weight, bond_mix_weight, pair_weight, pair_hidden_weight)
    weights += (pair_out_weight, atom_in_weight, atom_out_weight)
    *prepared, bond_dirs, angle_weight = pl.pallas_call(
        functools.partial(prepare_kernel, extents, paired),
        out_shape=(
            shaped((bonds, 9 * CAP + 9 * atoms), BF16),
            shaped((bonds, 2 * feature), BF16),
            shaped((bonds, 4 * feature), F32),
            shaped((2 * feature, 4 * feature), BF16),
            shaped((2 * feature, 2 * feature), BF16),
            shaped((2 * feature, 8 * feature), BF16),
            shaped((2 * feature, 4 * feature), BF16),
            shaped((2 * feature, 2 * feature), BF16),
            shaped((2 * feature, 4 * feature), BF16),
            shaped((2 * feature, 2 * feature), BF16),
            shaped(bond_dirs.shape, F32),
            shaped(angle_weight.shape, BF16),
        ),
        in_specs=[vmem] * 3 + [hbm] * 9,
        out_specs=(vmem,) * 12,
        scratch_shapes=[pltpu.VMEM(x.shape, BF16) for x in weights]
        + [pltpu.SemaphoreType.DMA((9,))],
        compiler_params=params,
        cost_estimate=pl.CostEstimate(flops=64 * 2**20, bytes_accessed=2**21, transcendentals=0),
        name="prepare",
    )(*held, *in_hbm(weights + (bond_dirs, angle_weight)))
    own, one, two, prepared = lax.optimization_barrier((own, one, two, prepared))
    first, second = moves(extents[1], paired[1])

    def forwarded(block):
        parts = [x[block * half : (block + 1) * half] for x in (own, one, two)]
        return jnp.concatenate(parts + [x[3 * half :] for x in (own, one, two)], axis=0)

    three = lax.ppermute(forwarded(1), "gy", first)
    four = lax.ppermute(forwarded(2), "gy", second)
    angular = pl.pallas_call(
        functools.partial(angular_kernel, atoms),
        out_shape=shaped((slots, pairs, 4 * feature), F32),
        in_specs=[vmem, vmem],
        out_specs=vmem,
        compiler_params=params,
        cost_estimate=pl.CostEstimate(
            flops=256 * 2**20, bytes_accessed=2**22, transcendentals=4096
        ),
        name="angular",
    )(bond_dirs, angle_weight)
    return pl.pallas_call(
        main_kernel,
        out_shape=(shaped(atom_feat.shape, BF16), shaped(bond_feat.shape, BF16)),
        in_specs=[vmem] * 16,
        out_specs=(hbm, hbm),
        scratch_shapes=[
            pltpu.VMEM(atom_feat.shape, BF16),
            pltpu.VMEM(bond_feat.shape, BF16),
            pltpu.VMEM((pairs, 4 * feature), F32),
            pltpu.VMEM((2, 2 * pairs, 4 * feature), F32),
            pltpu.VMEM((4, pairs // 2, 2 * feature), BF16),
            pltpu.VMEM((pairs, 2 * feature), F32),
            pltpu.SemaphoreType.DMA((2,)),
        ],
        compiler_params=params,
        cost_estimate=pl.CostEstimate(
            flops=400 * 2**20, bytes_accessed=2**22, transcendentals=2**21
        ),
        name="main",
    )(own, one, two, four, three, angular, *prepared)


def solution(mesh):
    placed = (
        P("gx", "gy", None, None),
        P("gx", "gy", None, None),
        P("gx", "gy", None, None),
        P(None, "gx", "gy", None),
        P(),
        P(),
        P(),
        P(),
        P(),
        P(),
        P(),
        P(),
    )
    return jax.shard_map(
        per_device,
        mesh=mesh,
        in_specs=placed,
        out_specs=(P("gx", "gy", None, None), P("gx", "gy", None, None)),
        check_vma=False,
    )
```

```python
import functools

import jax
import jax.numpy as jnp
from jax import lax
from jax.experimental import pallas as pl
from jax.experimental.pallas import tpu as pltpu
from jax.sharding import PartitionSpec as P

F32 = jnp.float32
BF16 = jnp.bfloat16
CAP = 64


def quotient(values, size):
    if size & (size - 1) == 0:
        return values >> (size.bit_length() - 1)
    return lax.div(values, jnp.int32(size))


def remainder(values, size):
    if size & (size - 1) == 0:
        return values & (size - 1)
    return lax.rem(values, jnp.int32(size))


def step_code(owner, home, extent, paired, receives):
    step = remainder(owner - home + 1 + extent, extent)
    if paired:
        ahead = jnp.where(remainder(home, 2) == 0, 0, 2)
    else:
        ahead = 0 if receives else 2
    return jnp.where(step == 1, 0, jnp.where(step == ahead, 1, 2))


def moves(extent, paired):
    if paired:
        near = [(i, i ^ 1) for i in range(extent)]
        return [(i, (((i + 1) ^ 1) - 1) % extent) for i in range(extent)], near
    up = [(i, (i + 1) % extent) for i in range(extent)]
    return up, [(j, i) for i, j in up]


def slot_at(position, slots):
    half = slots // 2
    return jnp.where(position < half, 2 * position, 2 * (position - half) + 1)


def bond_row(table):
    slots, atoms = table.shape
    per_group = 128 // atoms
    tiled = jnp.concatenate([table.astype(F32)] * per_group, axis=1)
    row = lax.broadcasted_iota(jnp.int32, tiled.shape, 0)
    position = quotient(lax.broadcasted_iota(jnp.int32, tiled.shape, 1), atoms)
    pieces = []
    for group in range(slots // per_group):
        chosen = row == slot_at(position + group * per_group, slots)
        pieces.append(jnp.sum(jnp.where(chosen, tiled, 0.0), axis=0, keepdims=True))
    return jnp.concatenate(pieces, axis=1).astype(jnp.int32)


def bond_codes(targets, atoms, extents, paired, receives):
    owner = quotient(targets, atoms)
    block = (quotient(owner, extents[1]), remainder(owner, extents[1]))
    return tuple(
        step_code(block[k], lax.axis_index(axis), extents[k], paired[k], receives)
        for k, axis in enumerate(("gx", "gy"))
    )


def left_lanes(shape):
    return lax.broadcasted_iota(jnp.int32, shape, 1) < shape[1] // 2


def swapped(rows):
    half = rows.shape[1] // 2
    return jnp.concatenate([rows[:, half:], rows[:, :half]], axis=1)


def blocks_of(bond_ref, pairs):
    width = bond_ref.shape[3] // pairs
    return [bond_ref[0, 0, :, k * width : (k + 1) * width] for k in range(pairs)]


def pack_kernel(
    extents,
    paired,
    targets_hbm,
    atom_hbm,
    bond_hbm,
    own_ref,
    one_ref,
    two_ref,
    targets_ref,
    atom_ref,
    bond_ref,
    sems,
):
    sources = ((targets_hbm, targets_ref), (bond_hbm, bond_ref), (atom_hbm, atom_ref))
    copies = [
        pltpu.make_async_copy(source, target, sems.at[k])
        for k, (source, target) in enumerate(sources)
    ]
    for copy in copies:
        copy.start()
    atoms, feature = atom_ref.shape[2], atom_ref.shape[3]
    slots = targets_ref.shape[0]
    bonds = slots * atoms
    lanes = 128
    groups = bonds // lanes
    copies[0].wait()
    code_x, code_y = bond_codes(bond_row(targets_ref[...]), atoms, extents, paired, False)
    code = 3 * code_x + code_y
    rows = lax.broadcasted_iota(jnp.int32, (16, lanes), 0)
    marks = [rows == code[:, g * lanes : (g + 1) * lanes] for g in range(groups)]
    stacked = jnp.concatenate([m.astype(F32) for m in marks], axis=0).astype(BF16)
    before = lax.broadcasted_iota(jnp.int32, (lanes, 2 * lanes), 0)
    after = lax.broadcasted_iota(jnp.int32, (lanes, 2 * lanes), 1)
    sums = jnp.where((before < after) | (after >= lanes), 1.0, 0.0).astype(BF16)
    counted = jnp.dot(stacked, sums, preferred_element_type=F32)
    place = []
    earlier = jnp.zeros((16, lanes), F32)
    for g in range(groups):
        part = counted[g * 16 : (g + 1) * 16]
        place.append(
            jnp.sum(jnp.where(marks[g], part[:, :lanes] + earlier, 0.0), axis=0, keepdims=True)
        )
        earlier = earlier + part[:, lanes:]
    place = jnp.concatenate(place, axis=1).astype(jnp.int32)
    half = CAP // 2
    right = quotient(place, half)
    wanted = 9 * half * right + place - half * right + half * code
    spot = lax.broadcasted_iota(jnp.int32, (9 * CAP, bonds), 0)
    chosen = jnp.where(spot == wanted, 1.0, 0.0).astype(BF16)
    copies[1].wait()
    blocks = blocks_of(bond_ref, slots // 2)
    values = [jnp.concatenate([x[:, :feature]] * 2, axis=1) for x in blocks]
    values += [jnp.concatenate([x[:, feature:]] * 2, axis=1) for x in blocks]
    packed = jnp.dot(chosen, jnp.concatenate(values, axis=0), preferred_element_type=F32)
    packed = jnp.where(
        left_lanes((9 * half, 2 * feature)), packed[: 9 * half], packed[9 * half :]
    ).astype(BF16)
    copies[2].wait()
    atom = atom_ref[0, 0]
    atom = jnp.concatenate([atom[: atoms // 2], atom[atoms // 2 :]], axis=1)
    for third, ref in enumerate((own_ref, one_ref, two_ref)):
        ref[: 3 * half] = packed[3 * half * third : 3 * half * (third + 1)]
        ref[3 * half :] = atom


def crossed(left, right):
    half = left.shape[1] // 2
    parts = [left[:, :half], right[:, :half], left[:, half:], right[:, half:]]
    return jnp.concatenate(parts, axis=1)


def two_blocks(weight):
    blank = jnp.zeros_like(weight)
    return jnp.concatenate([crossed(weight, blank), crossed(blank, weight)], axis=0)


def diagonal_blocks(weight):
    blank = jnp.zeros_like(weight)
    return jnp.concatenate(
        [jnp.concatenate([weight, blank], axis=1), jnp.concatenate([blank, weight], axis=1)],
        axis=0,
    )


def angular_kernel(atoms, dirs_ref, angle_ref, angular_ref):
    slots, pairs, _ = angular_ref.shape
    bonds = 2 * pairs
    degrees = angle_ref.shape[0]
    weight = (two_blocks(angle_ref[...].astype(F32)) * 0.5).astype(BF16)
    polar, azimuth = dirs_ref[0, 0], dirs_ref[1, 0]
    unit = jnp.concatenate(
        [
            jnp.sin(polar) * jnp.cos(azimuth),
            jnp.sin(polar) * jnp.sin(azimuth),
            jnp.cos(polar),
            jnp.zeros((5, bonds), F32),
        ],
        axis=0,
    )
    high = unit.astype(BF16).astype(F32)
    middle = (unit - high).astype(BF16).astype(F32)
    parts = jnp.concatenate([high, middle, unit - high - middle], axis=0).astype(BF16)
    bond = lax.broadcasted_iota(jnp.int32, (1, bonds), 1)
    source = remainder(bond, atoms) * slots + slot_at(quotient(bond, atoms), slots)
    spot = lax.broadcasted_iota(jnp.int32, (bonds, bonds), 0)
    chosen = jnp.where(spot == source, 1.0, 0.0).astype(BF16)
    unit = jnp.dot(parts, chosen, preferred_element_type=F32)
    unit = unit[0:8] + unit[8:16] + unit[16:24]
    even = [jnp.broadcast_to(unit[k : k + 1, :pairs], (8, pairs)) for k in range(3)]
    odd = [jnp.broadcast_to(unit[k : k + 1, pairs:], (8, pairs)) for k in range(3)]
    row = lax.broadcasted_iota(jnp.int32, (8, pairs), 0)

    def turned(vector, places):
        places = places % (pairs // atoms)
        if places == 0:
            return vector
        return [pltpu.roll(part, pairs - atoms * places, 1) for part in vector]

    def basis(first, second):
        cosine = first[0] * second[0] + first[1] * second[1] + first[2] * second[2]
        series = [jnp.ones_like(cosine), cosine]
        double = cosine + cosine
        for _ in range(7):
            series.append(double * series[-1] - series[-2])
        lower = series[7]
        upper = series[1]
        for index in range(1, 8):
            lower = jnp.where(row == index, series[7 - index], lower)
            upper = jnp.where(row == index, series[1 + index], upper)
        double = series[8] + series[8]
        blocks = [lower, upper]
        for _ in range(degrees // 8 - 1):
            blocks.append(double * blocks[-1] - blocks[-2])
        return blocks[1:]

    for diagonal in range(slots):
        places = diagonal // 2
        if diagonal % 2 == 0:
            blocks = basis(even, turned(even, places)) + basis(odd, turned(odd, places))
        else:
            blocks = basis(even, turned(odd, places)) + basis(odd, turned(even, places + 1))
        series = jnp.concatenate(blocks, axis=0).T.astype(BF16)
        angular_ref[diagonal] = jnp.dot(series, weight, preferred_element_type=F32)


def prepare_kernel(
    extents,
    paired,
    targets_ref,
    atom_ref,
    bond_ref,
    *refs,
):
    sources, results, held, sems = refs[:9], refs[9:21], refs[21:28], refs[28]
    chosen_ref, own_ref, near_ref, far_weight_ref, mix_weight_ref, pair_weight_ref = results[:6]
    hidden_weight_ref, out_weight_ref, atom_in_weight_ref, atom_out_weight_ref = results[6:10]
    bond_in_ref, bond_mix_ref, pair_ref, pair_hidden_ref, pair_out_ref = held[:5]
    atom_in_ref, atom_out_ref = held[5:]
    copies = [
        pltpu.make_async_copy(source, target, sems.at[k])
        for k, (source, target) in enumerate(zip(sources, held + results[10:]))
    ]
    for copy in copies:
        copy.start()
    atoms, feature = atom_ref.shape[2], atom_ref.shape[3]
    slots = targets_ref.shape[0]
    bonds = slots * atoms
    targets = bond_row(targets_ref[...])
    code_x, code_y = bond_codes(targets, atoms, extents, paired, True)
    code = 3 * code_y + code_x
    bond = lax.broadcasted_iota(jnp.int32, (1, bonds), 1)
    far_slot = slots - 1 - slot_at(quotient(bond, atoms), slots)
    far_atom = remainder(targets, atoms)
    far = (remainder(far_slot, 2) * (slots // 2) + quotient(far_slot, 2)) * atoms + far_atom
    base = (code * bonds).astype(F32)
    key = base + far.astype(F32)

    def column(values):
        return jnp.broadcast_to(values.astype(F32), (128, bonds)).T

    keys = column(key)
    place = []
    for group in range(bonds // 128):
        here = slice(group * 128, (group + 1) * 128)
        inside = (keys < key[:, here]) & (keys >= base[:, here])
        place.append(jnp.sum(jnp.where(inside, 1.0, 0.0), axis=0, keepdims=True))
    place = jnp.concatenate(place, axis=1).astype(jnp.int32)
    half, tall = CAP // 2, atoms // 2
    bond_spot = 9 * half * quotient(place, half) + half * code + remainder(place, half)
    atom_spot = 9 * CAP + 9 * tall * quotient(far_atom, tall) + tall * code
    atom_spot = column(atom_spot + remainder(far_atom, tall))
    bond_spot = column(bond_spot)
    total = 9 * CAP + 9 * atoms
    for start in range(0, total, 128):
        width = min(128, total - start)
        spot = lax.broadcasted_iota(jnp.int32, (bonds, 128), 1).astype(F32) + float(start)
        chosen = jnp.where((spot == bond_spot) | (spot == atom_spot), 1.0, 0.0).astype(BF16)
        chosen_ref[:, start : start + width] = chosen[:, :width]

    atom = atom_ref[0, 0]
    blocks = blocks_of(bond_ref, slots // 2)
    own = [jnp.concatenate([atom, x[:, :feature]], axis=1) for x in blocks]
    own += [jnp.concatenate([atom, x[:, feature:]], axis=1) for x in blocks]
    own = jnp.concatenate(own, axis=0)
    own_ref[...] = own

    for copy in copies:
        copy.wait()
    weight = bond_in_ref[...].astype(F32)
    source, other, bond_part = (weight[k * feature : (k + 1) * feature] for k in range(3))
    blank = jnp.zeros_like(source)
    near = [crossed(other, source), crossed(blank, bond_part)]
    near = (jnp.concatenate(near, axis=0) * 0.5).astype(BF16)
    near_ref[...] = jnp.dot(own, near, preferred_element_type=F32)
    away = [crossed(bond_part, blank), crossed(source, other)]
    far_weight_ref[...] = (jnp.concatenate(away, axis=0) * 0.5).astype(BF16)
    mix_weight_ref[...] = (diagonal_blocks(bond_mix_ref[...].astype(F32)) * 0.5).astype(BF16)
    weight = pair_ref[...].astype(F32) * 0.5
    pair_weight_ref[...] = jnp.concatenate(
        [two_blocks(weight[:, : 2 * feature]), two_blocks(weight[:, 2 * feature :])], axis=1
    ).astype(BF16)
    hidden_weight_ref[...] = (two_blocks(pair_hidden_ref[...].astype(F32)) * 0.25).astype(BF16)
    out_weight_ref[...] = (diagonal_blocks(pair_out_ref[...].astype(F32)) * 0.5).astype(BF16)
    weight = atom_in_ref[...].astype(F32) * 0.5
    atom_in_weight_ref[...] = crossed(weight, jnp.zeros_like(weight)).astype(BF16)
    weight = atom_out_ref[...].astype(F32) * 0.5
    blank = jnp.zeros_like(weight)
    weight = jnp.concatenate([weight, blank], axis=1)
    atom_out_weight_ref[...] = jnp.concatenate([weight, jnp.zeros_like(weight)], axis=0).astype(
        BF16
    )


def doubled_gate(values):
    half = values.shape[1] // 2
    first, second = values[:, :half], values[:, half:]
    return first * (1.0 + jnp.tanh(first)) * (1.0 + jnp.tanh(second))


def bond_kernel(
    own_rows_ref,
    one_ref,
    two_ref,
    four_ref,
    three_ref,
    chosen_ref,
    own_ref,
    near_ref,
    far_weight_ref,
    mix_weight_ref,
    pair_weight_ref,
    packed_ref,
    first_ref,
    second_ref,
):
    bonds = own_ref.shape[0]
    pairs = bonds // 2
    atoms = 2 * (own_rows_ref.shape[0] - 3 * CAP // 2)
    feature = own_ref.shape[1] // 2
    half = CAP // 2
    near_refs = (own_rows_ref, one_ref, two_ref)
    away_refs = (three_ref, four_ref)
    sent = [ref[:half] for ref in near_refs] + [ref[: 3 * half] for ref in away_refs]
    sent = jnp.concatenate(sent, axis=0)
    sent_atom = jnp.concatenate([ref[3 * half :] for ref in near_refs + away_refs], axis=0)
    blank = jnp.zeros((9 * half, feature), BF16)
    blank_atom = jnp.zeros((sent_atom.shape[0], feature), BF16)
    received = jnp.concatenate(
        [
            jnp.concatenate([sent[:, :feature], blank], axis=1),
            jnp.concatenate([sent[:, feature:], blank], axis=1),
            jnp.concatenate([blank_atom, sent_atom[:, :feature]], axis=1),
            jnp.concatenate([blank_atom, sent_atom[:, feature:]], axis=1),
        ],
        axis=0,
    )
    far = jnp.dot(chosen_ref[...], received, preferred_element_type=F32)
    incoming = near_ref[...] + jnp.dot(
        far.astype(BF16), far_weight_ref[...], preferred_element_type=F32
    )
    hidden = doubled_gate(incoming).astype(BF16)
    mixed = jnp.dot(hidden, mix_weight_ref[...], preferred_element_type=F32)
    old = jnp.where(left_lanes((bonds, 2 * feature)), far, own_ref[...].astype(F32))
    new = (old + mixed).astype(BF16).astype(F32)
    average = ((new + pltpu.roll(new, feature, 1)) * 0.5).astype(BF16).astype(F32)
    even, odd = average[:pairs], average[pairs:]
    left = left_lanes((pairs, 2 * feature))
    packed = jnp.where(left, even, odd)
    shifted = jnp.where(left, odd, jnp.concatenate([even[atoms:], even[:atoms]], axis=0))
    width = 4 * feature
    projected = jnp.dot(packed.astype(BF16), pair_weight_ref[...], preferred_element_type=F32)
    packed_ref[...] = packed
    first_ref[...] = projected[:, :width]
    second_ref[0] = projected[:, width:]
    second_ref[1] = jnp.dot(
        shifted.astype(BF16), pair_weight_ref[:, width:], preferred_element_type=F32
    )


def pair_kernel(
    angular_ref,
    packed_ref,
    first_ref,
    second_ref,
    hidden_weight_ref,
    out_weight_ref,
    bond_result_ref,
):
    slots, pairs, _ = angular_ref.shape
    atoms = 2 * pairs // slots
    width = packed_ref.shape[1]
    hidden_weight = hidden_weight_ref[...]
    height = pairs // 2
    for start in range(0, pairs, height):
        total = jnp.zeros((height, width), F32)
        for diagonal in range(slots):
            offset = start + diagonal // 2 * atoms
            pieces = [
                second_ref[diagonal % 2, pl.ds((offset + k) % pairs, atoms)]
                for k in range(0, height, atoms)
            ]
            mixture = angular_ref[diagonal, pl.ds(start, height)] + (
                first_ref[pl.ds(start, height)] + jnp.concatenate(pieces, axis=0)
            )
            pair = doubled_gate(mixture).astype(BF16)
            total = total + doubled_gate(
                jnp.dot(pair, hidden_weight, preferred_element_type=F32)
            )
        bond_out = packed_ref[pl.ds(start, height)] + jnp.dot(
            total.astype(BF16), out_weight_ref[...], preferred_element_type=F32
        )
        bond_out = bond_out.astype(BF16)
        for k in range(height // atoms):
            place = (start // atoms + k) * width
            bond_result_ref[0, 0, :, place : place + width] = bond_out[k * atoms : (k + 1) * atoms]


def atom_kernel(bond_ref, own_ref, atom_in_weight_ref, atom_out_weight_ref, atom_result_ref):
    atoms, feature = atom_result_ref.shape[2], atom_result_ref.shape[3]
    slots = bond_ref.shape[3] // feature
    pooled = jnp.zeros((atoms, 2 * feature), F32)
    for block in blocks_of(bond_ref, slots // 2):
        pooled = pooled + block.astype(F32)
    pooled = (pooled + pltpu.roll(pooled, feature, 1)) * (1.0 / slots)
    atom = own_ref[0:atoms].astype(F32)
    joined = jnp.where(left_lanes((atoms, 2 * feature)), atom, pooled).astype(BF16)
    atom_hidden = doubled_gate(
        jnp.dot(joined, atom_in_weight_ref[...], preferred_element_type=F32)
    ).astype(BF16)
    atom_new = atom + jnp.dot(atom_hidden, atom_out_weight_ref[...], preferred_element_type=F32)
    atom_result_ref[0, 0] = atom_new[:, :feature].astype(BF16)


def per_device(
    atom_feat,
    bond_feat,
    neighbours,
    bond_dirs,
    bond_in_weight,
    bond_mix_weight,
    pair_weight,
    angle_weight,
    pair_hidden_weight,
    pair_out_weight,
    atom_in_weight,
    atom_out_weight,
):
    atoms, feature = atom_feat.shape[2], atom_feat.shape[3]
    slots = neighbours.shape[3]
    bonds = atoms * slots
    pairs = bonds // 2
    half = CAP // 2
    extents = (lax.axis_size("gx"), lax.axis_size("gy"))
    paired = (extents[0] % 2 == 0, False)
    targets = neighbours[0, 0].T
    hbm = pl.BlockSpec(memory_space=pltpu.HBM)
    vmem = pl.BlockSpec(memory_space=pltpu.VMEM)
    params = pltpu.CompilerParams(vmem_limit_bytes=32 * 2**20)

    def shaped(shape, dtype):
        return jax.ShapeDtypeStruct(shape, dtype)

    def in_hbm(arrays):
        return tuple(pltpu.with_memory_space_constraint(x, pltpu.HBM) for x in arrays)

    payload = shaped((3 * half + atoms // 2, 2 * feature), BF16)
    inputs = (targets, atom_feat, bond_feat)
    own, one, two, *held = pl.pallas_call(
        functools.partial(pack_kernel, extents, paired),
        out_shape=(payload,) * 3 + tuple(shaped(x.shape, x.dtype) for x in inputs),
        in_specs=[hbm] * 3,
        out_specs=(vmem,) * 6,
        scratch_shapes=[pltpu.SemaphoreType.DMA((3,))],
        compiler_params=params,
        name="pack",
    )(*in_hbm(inputs))
    first, second = moves(extents[0], paired[0])
    one = lax.ppermute(one, "gx", first)
    two = lax.ppermute(two, "gx", second)
    weights = (bond_in_weight, bond_mix_weight, pair_weight, pair_hidden_weight)
    weights += (pair_out_weight, atom_in_weight, atom_out_weight)
    *prepared, bond_dirs, angle_weight = pl.pallas_call(
        functools.partial(prepare_kernel, extents, paired),
        out_shape=(
            shaped((bonds, 9 * CAP + 9 * atoms), BF16),
            shaped((bonds, 2 * feature), BF16),
            shaped((bonds, 4 * feature), F32),
            shaped((2 * feature, 4 * feature), BF16),
            shaped((2 * feature, 2 * feature), BF16),
            shaped((2 * feature, 8 * feature), BF16),
            shaped((2 * feature, 4 * feature), BF16),
            shaped((2 * feature, 2 * feature), BF16),
            shaped((2 * feature, 4 * feature), BF16),
            shaped((2 * feature, 2 * feature), BF16),
            shaped(bond_dirs.shape, F32),
            shaped(angle_weight.shape, BF16),
        ),
        in_specs=[vmem] * 3 + [hbm] * 9,
        out_specs=(vmem,) * 12,
        scratch_shapes=[pltpu.VMEM(x.shape, BF16) for x in weights]
        + [pltpu.SemaphoreType.DMA((9,))],
        compiler_params=params,
        cost_estimate=pl.CostEstimate(flops=64 * 2**20, bytes_accessed=2**21, transcendentals=0),
        name="prepare",
    )(*held, *in_hbm(weights + (bond_dirs, angle_weight)))
    own, one, two, prepared = lax.optimization_barrier((own, one, two, prepared))
    first, second = moves(extents[1], paired[1])

    def forwarded(block):
        parts = [x[block * half : (block + 1) * half] for x in (own, one, two)]
        return jnp.concatenate(parts + [x[3 * half :] for x in (own, one, two)], axis=0)

    three = lax.ppermute(forwarded(1), "gy", first)
    four = lax.ppermute(forwarded(2), "gy", second)
    angular = pl.pallas_call(
        functools.partial(angular_kernel, atoms),
        out_shape=shaped((slots, pairs, 4 * feature), F32),
        in_specs=[vmem, vmem],
        out_specs=vmem,
        compiler_params=params,
        cost_estimate=pl.CostEstimate(
            flops=256 * 2**20, bytes_accessed=2**22, transcendentals=4096
        ),
        name="angular",
    )(bond_dirs, angle_weight)
    chosen, own_rows, near, far_weight, mix_weight, pair_weight, *others = prepared
    hidden_weight, out_weight, atom_in_weight, atom_out_weight = others
    packed, projected, turned = pl.pallas_call(
        bond_kernel,
        out_shape=(
            shaped((pairs, 2 * feature), F32),
            shaped((pairs, 4 * feature), F32),
            shaped((2, pairs, 4 * feature), F32),
        ),
        in_specs=[vmem] * 11,
        out_specs=(vmem,) * 3,
        compiler_params=params,
        name="bonds",
    )(own, one, two, four, three, chosen, own_rows, near, far_weight, mix_weight, pair_weight)
    bond_out = pl.pallas_call(
        pair_kernel,
        out_shape=shaped(bond_feat.shape, BF16),
        in_specs=[vmem] * 6,
        out_specs=vmem,
        compiler_params=params,
        name="pairs",
    )(angular, packed, projected, turned, hidden_weight, out_weight)
    atom_out = pl.pallas_call(
        atom_kernel,
        out_shape=shaped(atom_feat.shape, BF16),
        in_specs=[vmem] * 4,
        out_specs=vmem,
        compiler_params=params,
        name="atoms",
    )(bond_out, own_rows, atom_in_weight, atom_out_weight)
    return atom_out, bond_out


def solution(mesh):
    placed = (
        P("gx", "gy", None, None),
        P("gx", "gy", None, None),
        P("gx", "gy", None, None),
        P(None, "gx", "gy", None),
        P(),
        P(),
        P(),
        P(),
        P(),
        P(),
        P(),
        P(),
    )
    return jax.shard_map(
        per_device,
        mesh=mesh,
        in_specs=placed,
        out_specs=(P("gx", "gy", None, None), P("gx", "gy", None, None)),
        check_vma=False,
    )
```

```python
import functools

import jax
import jax.numpy as jnp
from jax import lax
from jax.experimental import pallas as pl
from jax.experimental.pallas import tpu as pltpu
from jax.sharding import PartitionSpec as P

F32 = jnp.float32
BF16 = jnp.bfloat16
CAP = 64


def quotient(values, size):
    if size & (size - 1) == 0:
        return values >> (size.bit_length() - 1)
    return lax.div(values, jnp.int32(size))


def remainder(values, size):
    if size & (size - 1) == 0:
        return values & (size - 1)
    return lax.rem(values, jnp.int32(size))


def step_code(owner, home, extent, paired, receives):
    step = remainder(owner - home + 1 + extent, extent)
    if paired:
        ahead = jnp.where(remainder(home, 2) == 0, 0, 2)
    else:
        ahead = 0 if receives else 2
    return jnp.where(step == 1, 0, jnp.where(step == ahead, 1, 2))


def moves(extent, paired):
    if paired:
        near = [(i, i ^ 1) for i in range(extent)]
        return [(i, (((i + 1) ^ 1) - 1) % extent) for i in range(extent)], near
    up = [(i, (i + 1) % extent) for i in range(extent)]
    return up, [(j, i) for i, j in up]


def slot_at(position, slots):
    half = slots // 2
    return jnp.where(position < half, 2 * position, 2 * (position - half) + 1)


def bond_row(table):
    slots, atoms = table.shape
    per_group = 128 // atoms
    tiled = jnp.concatenate([table.astype(F32)] * per_group, axis=1)
    row = lax.broadcasted_iota(jnp.int32, tiled.shape, 0)
    position = quotient(lax.broadcasted_iota(jnp.int32, tiled.shape, 1), atoms)
    pieces = []
    for group in range(slots // per_group):
        chosen = row == slot_at(position + group * per_group, slots)
        pieces.append(jnp.sum(jnp.where(chosen, tiled, 0.0), axis=0, keepdims=True))
    return jnp.concatenate(pieces, axis=1).astype(jnp.int32)


def bond_codes(targets, atoms, extents, paired, receives):
    owner = quotient(targets, atoms)
    block = (quotient(owner, extents[1]), remainder(owner, extents[1]))
    return tuple(
        step_code(block[k], lax.axis_index(axis), extents[k], paired[k], receives)
        for k, axis in enumerate(("gx", "gy"))
    )


def left_lanes(shape):
    return lax.broadcasted_iota(jnp.int32, shape, 1) < shape[1] // 2


def swapped(rows):
    half = rows.shape[1] // 2
    return jnp.concatenate([rows[:, half:], rows[:, :half]], axis=1)


def blocks_of(bond_ref, pairs):
    width = bond_ref.shape[3] // pairs
    return [bond_ref[0, 0, :, k * width : (k + 1) * width] for k in range(pairs)]


def pack_kernel(
    extents,
    paired,
    targets_hbm,
    atom_hbm,
    bond_hbm,
    own_ref,
    one_ref,
    two_ref,
    targets_ref,
    atom_ref,
    bond_ref,
    sems,
):
    sources = ((targets_hbm, targets_ref), (bond_hbm, bond_ref), (atom_hbm, atom_ref))
    copies = [
        pltpu.make_async_copy(source, target, sems.at[k])
        for k, (source, target) in enumerate(sources)
    ]
    for copy in copies:
        copy.start()
    atoms, feature = atom_ref.shape[2], atom_ref.shape[3]
    slots = targets_ref.shape[0]
    bonds = slots * atoms
    lanes = 128
    groups = bonds // lanes
    copies[0].wait()
    code_x, code_y = bond_codes(bond_row(targets_ref[...]), atoms, extents, paired, False)
    code = 3 * code_x + code_y
    rows = lax.broadcasted_iota(jnp.int32, (16, lanes), 0)
    marks = [rows == code[:, g * lanes : (g + 1) * lanes] for g in range(groups)]
    stacked = jnp.concatenate([m.astype(F32) for m in marks], axis=0).astype(BF16)
    before = lax.broadcasted_iota(jnp.int32, (lanes, 2 * lanes), 0)
    after = lax.broadcasted_iota(jnp.int32, (lanes, 2 * lanes), 1)
    sums = jnp.where((before < after) | (after >= lanes), 1.0, 0.0).astype(BF16)
    counted = jnp.dot(stacked, sums, preferred_element_type=F32)
    place = []
    earlier = jnp.zeros((16, lanes), F32)
    for g in range(groups):
        part = counted[g * 16 : (g + 1) * 16]
        place.append(
            jnp.sum(jnp.where(marks[g], part[:, :lanes] + earlier, 0.0), axis=0, keepdims=True)
        )
        earlier = earlier + part[:, lanes:]
    place = jnp.concatenate(place, axis=1).astype(jnp.int32)
    half = CAP // 2
    right = quotient(place, half)
    wanted = 9 * half * right + place - half * right + half * code
    spot = lax.broadcasted_iota(jnp.int32, (9 * CAP, bonds), 0)
    chosen = jnp.where(spot == wanted, 1.0, 0.0).astype(BF16)
    copies[1].wait()
    blocks = blocks_of(bond_ref, slots // 2)
    values = [x[:, :feature] for x in blocks] + [x[:, feature:] for x in blocks]
    packed = jnp.dot(chosen, jnp.concatenate(values, axis=0), preferred_element_type=F32)
    packed = jnp.concatenate([packed[: 9 * half], packed[9 * half :]], axis=1).astype(BF16)
    copies[2].wait()
    atom = atom_ref[0, 0]
    atom = jnp.concatenate([atom[: atoms // 2], atom[atoms // 2 :]], axis=1)
    for third, ref in enumerate((own_ref, one_ref, two_ref)):
        ref[: 3 * half] = packed[3 * half * third : 3 * half * (third + 1)]
        ref[3 * half :] = atom


def crossed(left, right):
    half = left.shape[1] // 2
    parts = [left[:, :half], right[:, :half], left[:, half:], right[:, half:]]
    return jnp.concatenate(parts, axis=1)


def two_blocks(weight):
    blank = jnp.zeros_like(weight)
    return jnp.concatenate([crossed(weight, blank), crossed(blank, weight)], axis=0)


def diagonal_blocks(weight):
    blank = jnp.zeros_like(weight)
    return jnp.concatenate(
        [jnp.concatenate([weight, blank], axis=1), jnp.concatenate([blank, weight], axis=1)],
        axis=0,
    )


def angular_kernel(atoms, dirs_ref, angle_ref, angular_ref):
    slots, pairs, _ = angular_ref.shape
    bonds = 2 * pairs
    degrees = angle_ref.shape[0]
    weight = (two_blocks(angle_ref[...].astype(F32)) * 0.5).astype(BF16)
    polar, azimuth = dirs_ref[0, 0], dirs_ref[1, 0]
    unit = jnp.concatenate(
        [
            jnp.sin(polar) * jnp.cos(azimuth),
            jnp.sin(polar) * jnp.sin(azimuth),
            jnp.cos(polar),
            jnp.zeros((5, bonds), F32),
        ],
        axis=0,
    )
    high = unit.astype(BF16).astype(F32)
    middle = (unit - high).astype(BF16).astype(F32)
    parts = jnp.concatenate([high, middle, unit - high - middle], axis=0).astype(BF16)
    bond = lax.broadcasted_iota(jnp.int32, (1, bonds), 1)
    source = remainder(bond, atoms) * slots + slot_at(quotient(bond, atoms), slots)
    spot = lax.broadcasted_iota(jnp.int32, (bonds, bonds), 0)
    chosen = jnp.where(spot == source, 1.0, 0.0).astype(BF16)
    unit = jnp.dot(parts, chosen, preferred_element_type=F32)
    unit = unit[0:8] + unit[8:16] + unit[16:24]
    even = [jnp.broadcast_to(unit[k : k + 1, :pairs], (8, pairs)) for k in range(3)]
    odd = [jnp.broadcast_to(unit[k : k + 1, pairs:], (8, pairs)) for k in range(3)]
    row = lax.broadcasted_iota(jnp.int32, (8, pairs), 0)

    def turned(vector, places):
        places = places % (pairs // atoms)
        if places == 0:
            return vector
        return [pltpu.roll(part, pairs - atoms * places, 1) for part in vector]

    def basis(first, second):
        cosine = first[0] * second[0] + first[1] * second[1] + first[2] * second[2]
        series = [jnp.ones_like(cosine), cosine]
        double = cosine + cosine
        for _ in range(7):
            series.append(double * series[-1] - series[-2])
        lower = series[7]
        upper = series[1]
        for index in range(1, 8):
            lower = jnp.where(row == index, series[7 - index], lower)
            upper = jnp.where(row == index, series[1 + index], upper)
        double = series[8] + series[8]
        blocks = [lower, upper]
        for _ in range(degrees // 8 - 1):
            blocks.append(double * blocks[-1] - blocks[-2])
        return blocks[1:]

    for diagonal in range(slots):
        places = diagonal // 2
        if diagonal % 2 == 0:
            blocks = basis(even, turned(even, places)) + basis(odd, turned(odd, places))
        else:
            blocks = basis(even, turned(odd, places)) + basis(odd, turned(even, places + 1))
        series = jnp.concatenate(blocks, axis=0).T.astype(BF16)
        angular_ref[diagonal] = jnp.dot(series, weight, preferred_element_type=F32)


def prepare_kernel(
    extents,
    paired,
    targets_ref,
    atom_ref,
    bond_ref,
    *refs,
):
    sources, results, held, sems = refs[:9], refs[9:22], refs[22:29], refs[29]
    chosen_ref, right_ref, own_ref, near_ref = results[:4]
    far_weight_ref, mix_weight_ref, pair_weight_ref, hidden_weight_ref = results[4:8]
    out_weight_ref, atom_in_weight_ref, atom_out_weight_ref = results[8:11]
    bond_in_ref, bond_mix_ref, pair_ref, pair_hidden_ref, pair_out_ref = held[:5]
    atom_in_ref, atom_out_ref = held[5:]
    copies = [
        pltpu.make_async_copy(source, target, sems.at[k])
        for k, (source, target) in enumerate(zip(sources, held + results[11:]))
    ]
    for copy in copies:
        copy.start()
    atoms, feature = atom_ref.shape[2], atom_ref.shape[3]
    slots = targets_ref.shape[0]
    bonds = slots * atoms
    targets = bond_row(targets_ref[...])
    code_x, code_y = bond_codes(targets, atoms, extents, paired, True)
    code = 3 * code_y + code_x
    bond = lax.broadcasted_iota(jnp.int32, (1, bonds), 1)
    far_slot = slots - 1 - slot_at(quotient(bond, atoms), slots)
    far_atom = remainder(targets, atoms)
    far = (remainder(far_slot, 2) * (slots // 2) + quotient(far_slot, 2)) * atoms + far_atom
    base = (code * bonds).astype(F32)
    key = base + far.astype(F32)

    def column(values):
        return jnp.broadcast_to(values.astype(F32), (128, bonds)).T

    keys = column(key)
    place = []
    for group in range(bonds // 128):
        here = slice(group * 128, (group + 1) * 128)
        inside = (keys < key[:, here]) & (keys >= base[:, here])
        place.append(jnp.sum(jnp.where(inside, 1.0, 0.0), axis=0, keepdims=True))
    place = jnp.concatenate(place, axis=1).astype(jnp.int32)
    half, tall = CAP // 2, atoms // 2
    bond_spot = column(half * code + remainder(place, half))
    atom_spot = column(9 * half + tall * code + remainder(far_atom, tall))
    right = (column(quotient(place, half)), column(quotient(far_atom, tall)))
    right_ref[...] = jnp.where(left_lanes((bonds, 128)), right[0], right[1])
    total = 9 * half + 9 * tall
    for start in range(0, total, 128):
        width = min(128, total - start)
        spot = lax.broadcasted_iota(jnp.int32, (bonds, 128), 1).astype(F32) + float(start)
        chosen = jnp.where((spot == bond_spot) | (spot == atom_spot), 1.0, 0.0).astype(BF16)
        chosen_ref[:, start : start + width] = chosen[:, :width]

    atom = atom_ref[0, 0]
    blocks = blocks_of(bond_ref, slots // 2)
    own = [jnp.concatenate([atom, x[:, :feature]], axis=1) for x in blocks]
    own += [jnp.concatenate([atom, x[:, feature:]], axis=1) for x in blocks]
    own = jnp.concatenate(own, axis=0)
    own_ref[...] = own

    for copy in copies:
        copy.wait()
    weight = bond_in_ref[...].astype(F32)
    source, other, bond_part = (weight[k * feature : (k + 1) * feature] for k in range(3))
    blank = jnp.zeros_like(source)
    near = [crossed(other, source), crossed(blank, bond_part)]
    near = (jnp.concatenate(near, axis=0) * 0.5).astype(BF16)
    near_ref[...] = jnp.dot(own, near, preferred_element_type=F32)
    away = [crossed(bond_part, blank), crossed(source, other)]
    far_weight_ref[...] = (jnp.concatenate(away, axis=0) * 0.5).astype(BF16)
    mix_weight_ref[...] = (diagonal_blocks(bond_mix_ref[...].astype(F32)) * 0.5).astype(BF16)
    weight = pair_ref[...].astype(F32) * 0.5
    pair_weight_ref[...] = jnp.concatenate(
        [two_blocks(weight[:, : 2 * feature]), two_blocks(weight[:, 2 * feature :])], axis=1
    ).astype(BF16)
    hidden_weight_ref[...] = (two_blocks(pair_hidden_ref[...].astype(F32)) * 0.25).astype(BF16)
    out_weight_ref[...] = (diagonal_blocks(pair_out_ref[...].astype(F32)) * 0.5).astype(BF16)
    weight = atom_in_ref[...].astype(F32) * 0.5
    atom_in_weight_ref[...] = crossed(weight, jnp.zeros_like(weight)).astype(BF16)
    weight = atom_out_ref[...].astype(F32) * 0.5
    blank = jnp.zeros_like(weight)
    weight = jnp.concatenate([weight, blank], axis=1)
    atom_out_weight_ref[...] = jnp.concatenate([weight, jnp.zeros_like(weight)], axis=0).astype(
        BF16
    )


def doubled_gate(values):
    half = values.shape[1] // 2
    first, second = values[:, :half], values[:, half:]
    return first * (1.0 + jnp.tanh(first)) * (1.0 + jnp.tanh(second))


def main_kernel(
    own_rows_ref,
    one_ref,
    two_ref,
    four_ref,
    three_ref,
    angular_ref,
    chosen_ref,
    right_ref,
    own_ref,
    near_ref,
    far_weight_ref,
    mix_weight_ref,
    pair_weight_ref,
    hidden_weight_ref,
    out_weight_ref,
    atom_in_weight_ref,
    atom_out_weight_ref,
    atom_result_hbm,
    bond_result_hbm,
    atom_result_ref,
    bond_result_ref,
    first_ref,
    second_ref,
    sems,
):
    slots, pairs, _ = angular_ref.shape
    bonds = 2 * pairs
    atoms = bonds // slots
    feature = own_ref.shape[1] // 2
    width = 2 * feature
    half = CAP // 2
    near_refs = (own_rows_ref, one_ref, two_ref)
    away_refs = (three_ref, four_ref)
    sent = [ref[:half] for ref in near_refs] + [ref[: 3 * half] for ref in away_refs]
    sent = jnp.concatenate(sent, axis=0)
    sent_atom = jnp.concatenate([ref[3 * half :] for ref in near_refs + away_refs], axis=0)
    blank = jnp.zeros((sent.shape[0], feature), BF16)
    blank_atom = jnp.zeros((sent_atom.shape[0], feature), BF16)
    received = jnp.concatenate(
        [
            jnp.concatenate([sent[:, :feature], blank, sent[:, feature:], blank], axis=1),
            jnp.concatenate(
                [blank_atom, sent_atom[:, :feature], blank_atom, sent_atom[:, feature:]], axis=1
            ),
        ],
        axis=0,
    )
    far = jnp.dot(chosen_ref[...], received, preferred_element_type=F32)
    far = jnp.where(right_ref[...] > 0.0, far[:, width:], far[:, :width])
    incoming = near_ref[...] + jnp.dot(
        far.astype(BF16), far_weight_ref[...], preferred_element_type=F32
    )
    hidden = doubled_gate(incoming).astype(BF16)
    mixed = jnp.dot(hidden, mix_weight_ref[...], preferred_element_type=F32)
    old = jnp.where(left_lanes((bonds, width)), far, own_ref[...].astype(F32))
    new = (old + mixed).astype(BF16).astype(F32)
    average = ((new + pltpu.roll(new, feature, 1)) * 0.5).astype(BF16).astype(F32)
    even, odd = average[:pairs], average[pairs:]
    left = left_lanes((pairs, width))
    packed = jnp.where(left, even, odd)
    shifted = jnp.where(left, odd, jnp.concatenate([even[atoms:], even[:atoms]], axis=0))
    projected = jnp.dot(packed.astype(BF16), pair_weight_ref[...], preferred_element_type=F32)
    first_ref[...] = projected[:, : 2 * width]
    second_ref[0] = projected[:, 2 * width :]
    second_ref[1] = jnp.dot(
        shifted.astype(BF16), pair_weight_ref[:, 2 * width :], preferred_element_type=F32
    )
    hidden_weight = hidden_weight_ref[...]
    height = pairs // 2
    pooled = jnp.zeros((atoms, width), F32)
    copies = []
    for part, start in enumerate(range(0, pairs, height)):
        total = jnp.zeros((height, width), F32)
        for diagonal in range(slots):
            offset = start + diagonal // 2 * atoms
            pieces = [
                second_ref[diagonal % 2, pl.ds((offset + k) % pairs, atoms)]
                for k in range(0, height, atoms)
            ]
            mixture = angular_ref[diagonal, pl.ds(start, height)] + (
                first_ref[pl.ds(start, height)] + jnp.concatenate(pieces, axis=0)
            )
            pair = doubled_gate(mixture.astype(BF16))
            second = jnp.dot(pair, hidden_weight, preferred_element_type=F32)
            total = total + doubled_gate(second.astype(BF16)).astype(F32)
        bond_out = packed[start : start + height] + jnp.dot(
            total.astype(BF16), out_weight_ref[...], preferred_element_type=F32
        )
        bond_out = bond_out.astype(BF16)
        for k in range(height // atoms):
            place = (start // atoms + k) * width
            rows = bond_out[k * atoms : (k + 1) * atoms]
            bond_result_ref[0, 0, :, place : place + width] = rows
            pooled = pooled + rows.astype(F32)
        columns = pl.ds(start // atoms * width, height // atoms * width)
        copies.append(
            pltpu.make_async_copy(
                bond_result_ref.at[0, 0, :, columns],
                bond_result_hbm.at[0, 0, :, columns],
                sems.at[part],
            )
        )
        copies[-1].start()
    pooled = (pooled + pltpu.roll(pooled, feature, 1)) * (1.0 / slots)
    atom = own_ref[0:atoms].astype(F32)
    joined = jnp.where(left_lanes((atoms, width)), atom, pooled).astype(BF16)
    atom_hidden = doubled_gate(
        jnp.dot(joined, atom_in_weight_ref[...], preferred_element_type=F32)
    ).astype(BF16)
    atom_new = atom + jnp.dot(atom_hidden, atom_out_weight_ref[...], preferred_element_type=F32)
    atom_result_ref[0, 0] = atom_new[:, :feature].astype(BF16)
    copies.append(pltpu.make_async_copy(atom_result_ref, atom_result_hbm, sems.at[2]))
    copies[-1].start()
    for copy in copies:
        copy.wait()


def per_device(
    atom_feat,
    bond_feat,
    neighbours,
    bond_dirs,
    bond_in_weight,
    bond_mix_weight,
    pair_weight,
    angle_weight,
    pair_hidden_weight,
    pair_out_weight,
    atom_in_weight,
    atom_out_weight,
):
    atoms, feature = atom_feat.shape[2], atom_feat.shape[3]
    slots = neighbours.shape[3]
    bonds = atoms * slots
    pairs = bonds // 2
    half = CAP // 2
    extents = (lax.axis_size("gx"), lax.axis_size("gy"))
    paired = (extents[0] % 2 == 0, False)
    targets = neighbours[0, 0].T
    hbm = pl.BlockSpec(memory_space=pltpu.HBM)
    vmem = pl.BlockSpec(memory_space=pltpu.VMEM)
    params = pltpu.CompilerParams(vmem_limit_bytes=32 * 2**20)

    def shaped(shape, dtype):
        return jax.ShapeDtypeStruct(shape, dtype)

    def in_hbm(arrays):
        return tuple(pltpu.with_memory_space_constraint(x, pltpu.HBM) for x in arrays)

    payload = shaped((3 * half + atoms // 2, 2 * feature), BF16)
    inputs = (targets, atom_feat, bond_feat)
    own, one, two, *held = pl.pallas_call(
        functools.partial(pack_kernel, extents, paired),
        out_shape=(payload,) * 3 + tuple(shaped(x.shape, x.dtype) for x in inputs),
        in_specs=[hbm] * 3,
        out_specs=(vmem,) * 6,
        scratch_shapes=[pltpu.SemaphoreType.DMA((3,))],
        compiler_params=params,
        name="pack",
    )(*in_hbm(inputs))
    first, second = moves(extents[0], paired[0])
    one = lax.ppermute(one, "gx", first)
    two = lax.ppermute(two, "gx", second)
    weights = (bond_in_weight, bond_mix_weight, pair_weight, pair_hidden_weight)
    weights += (pair_out_weight, atom_in_weight, atom_out_weight)
    *prepared, bond_dirs, angle_weight = pl.pallas_call(
        functools.partial(prepare_kernel, extents, paired),
        out_shape=(
            shaped((bonds, 9 * half + 9 * atoms // 2), BF16),
            shaped((bonds, 2 * feature), F32),
            shaped((bonds, 2 * feature), BF16),
            shaped((bonds, 4 * feature), F32),
            shaped((2 * feature, 4 * feature), BF16),
            shaped((2 * feature, 2 * feature), BF16),
            shaped((2 * feature, 8 * feature), BF16),
            shaped((2 * feature, 4 * feature), BF16),
            shaped((2 * feature, 2 * feature), BF16),
            shaped((2 * feature, 4 * feature), BF16),
            shaped((2 * feature, 2 * feature), BF16),
            shaped(bond_dirs.shape, F32),
            shaped(angle_weight.shape, BF16),
        ),
        in_specs=[vmem] * 3 + [hbm] * 9,
        out_specs=(vmem,) * 13,
        scratch_shapes=[pltpu.VMEM(x.shape, BF16) for x in weights]
        + [pltpu.SemaphoreType.DMA((9,))],
        compiler_params=params,
        cost_estimate=pl.CostEstimate(flops=64 * 2**20, bytes_accessed=2**21, transcendentals=0),
        name="prepare",
    )(*held, *in_hbm(weights + (bond_dirs, angle_weight)))
    own, one, two, prepared = lax.optimization_barrier((own, one, two, prepared))
    first, second = moves(extents[1], paired[1])

    def forwarded(block):
        parts = [x[block * half : (block + 1) * half] for x in (own, one, two)]
        return jnp.concatenate(parts + [x[3 * half :] for x in (own, one, two)], axis=0)

    three = lax.ppermute(forwarded(1), "gy", first)
    four = lax.ppermute(forwarded(2), "gy", second)
    angular = pl.pallas_call(
        functools.partial(angular_kernel, atoms),
        out_shape=shaped((slots, pairs, 4 * feature), F32),
        in_specs=[vmem, vmem],
        out_specs=vmem,
        compiler_params=params,
        cost_estimate=pl.CostEstimate(
            flops=256 * 2**20, bytes_accessed=2**22, transcendentals=4096
        ),
        name="angular",
    )(bond_dirs, angle_weight)
    return pl.pallas_call(
        main_kernel,
        out_shape=(shaped(atom_feat.shape, BF16), shaped(bond_feat.shape, BF16)),
        in_specs=[vmem] * 17,
        out_specs=(hbm, hbm),
        scratch_shapes=[
            pltpu.VMEM(atom_feat.shape, BF16),
            pltpu.VMEM(bond_feat.shape, BF16),
            pltpu.VMEM((pairs, 4 * feature), F32),
            pltpu.VMEM((2, pairs, 4 * feature), F32),
            pltpu.SemaphoreType.DMA((3,)),
        ],
        compiler_params=params,
        name="main",
    )(own, one, two, four, three, angular, *prepared)


def solution(mesh):
    placed = (
        P("gx", "gy", None, None),
        P("gx", "gy", None, None),
        P("gx", "gy", None, None),
        P(None, "gx", "gy", None),
        P(),
        P(),
        P(),
        P(),
        P(),
        P(),
        P(),
        P(),
    )
    return jax.shard_map(
        per_device,
        mesh=mesh,
        in_specs=placed,
        out_specs=(P("gx", "gy", None, None), P("gx", "gy", None, None)),
        check_vma=False,
    )
```

```python
import functools

import jax
import jax.numpy as jnp
from jax import lax
from jax.experimental import pallas as pl
from jax.experimental.pallas import tpu as pltpu
from jax.sharding import PartitionSpec as P

F32 = jnp.float32
BF16 = jnp.bfloat16
CAP = 64


def quotient(values, size):
    if size & (size - 1) == 0:
        return values >> (size.bit_length() - 1)
    return lax.div(values, jnp.int32(size))


def remainder(values, size):
    if size & (size - 1) == 0:
        return values & (size - 1)
    return lax.rem(values, jnp.int32(size))


def step_code(owner, home, extent, paired, receives):
    step = remainder(owner - home + 1 + extent, extent)
    if paired:
        ahead = jnp.where(remainder(home, 2) == 0, 0, 2)
    else:
        ahead = 0 if receives else 2
    return jnp.where(step == 1, 0, jnp.where(step == ahead, 1, 2))


def moves(extent, paired):
    if paired:
        near = [(i, i ^ 1) for i in range(extent)]
        return [(i, (((i + 1) ^ 1) - 1) % extent) for i in range(extent)], near
    up = [(i, (i + 1) % extent) for i in range(extent)]
    return up, [(j, i) for i, j in up]


def slot_at(position, slots):
    half = slots // 2
    return jnp.where(position < half, 2 * position, 2 * (position - half) + 1)


def bond_row(table):
    slots, atoms = table.shape
    per_group = 128 // atoms
    tiled = jnp.concatenate([table.astype(F32)] * per_group, axis=1)
    row = lax.broadcasted_iota(jnp.int32, tiled.shape, 0)
    position = quotient(lax.broadcasted_iota(jnp.int32, tiled.shape, 1), atoms)
    pieces = []
    for group in range(slots // per_group):
        chosen = row == slot_at(position + group * per_group, slots)
        pieces.append(jnp.sum(jnp.where(chosen, tiled, 0.0), axis=0, keepdims=True))
    return jnp.concatenate(pieces, axis=1).astype(jnp.int32)


def bond_codes(targets, atoms, extents, paired, receives):
    owner = quotient(targets, atoms)
    block = (quotient(owner, extents[1]), remainder(owner, extents[1]))
    return tuple(
        step_code(block[k], lax.axis_index(axis), extents[k], paired[k], receives)
        for k, axis in enumerate(("gx", "gy"))
    )


def left_lanes(shape):
    return lax.broadcasted_iota(jnp.int32, shape, 1) < shape[1] // 2


def swapped(rows):
    half = rows.shape[1] // 2
    return jnp.concatenate([rows[:, half:], rows[:, :half]], axis=1)


def blocks_of(bond_ref, pairs):
    width = bond_ref.shape[3] // pairs
    return [bond_ref[0, 0, :, k * width : (k + 1) * width] for k in range(pairs)]


def pack_kernel(
    extents,
    paired,
    targets_hbm,
    atom_hbm,
    bond_hbm,
    own_ref,
    one_ref,
    two_ref,
    targets_ref,
    atom_ref,
    bond_ref,
    sems,
):
    sources = ((targets_hbm, targets_ref), (bond_hbm, bond_ref), (atom_hbm, atom_ref))
    copies = [
        pltpu.make_async_copy(source, target, sems.at[k])
        for k, (source, target) in enumerate(sources)
    ]
    for copy in copies:
        copy.start()
    atoms, feature = atom_ref.shape[2], atom_ref.shape[3]
    slots = targets_ref.shape[0]
    bonds = slots * atoms
    lanes = 128
    groups = bonds // lanes
    copies[0].wait()
    code_x, code_y = bond_codes(bond_row(targets_ref[...]), atoms, extents, paired, False)
    code = 3 * code_x + code_y
    rows = lax.broadcasted_iota(jnp.int32, (16, lanes), 0)
    marks = [rows == code[:, g * lanes : (g + 1) * lanes] for g in range(groups)]
    stacked = jnp.concatenate([m.astype(F32) for m in marks], axis=0).astype(BF16)
    before = lax.broadcasted_iota(jnp.int32, (lanes, 2 * lanes), 0)
    after = lax.broadcasted_iota(jnp.int32, (lanes, 2 * lanes), 1)
    sums = jnp.where((before < after) | (after >= lanes), 1.0, 0.0).astype(BF16)
    counted = jnp.dot(stacked, sums, preferred_element_type=F32)
    place = []
    earlier = jnp.zeros((16, lanes), F32)
    for g in range(groups):
        part = counted[g * 16 : (g + 1) * 16]
        place.append(
            jnp.sum(jnp.where(marks[g], part[:, :lanes] + earlier, 0.0), axis=0, keepdims=True)
        )
        earlier = earlier + part[:, lanes:]
    place = jnp.concatenate(place, axis=1).astype(jnp.int32)
    half = CAP // 2
    right = quotient(place, half)
    wanted = 9 * half * right + place - half * right + half * code
    spot = lax.broadcasted_iota(jnp.int32, (9 * CAP, bonds), 0)
    chosen = jnp.where(spot == wanted, 1.0, 0.0).astype(BF16)
    copies[1].wait()
    blocks = blocks_of(bond_ref, slots // 2)
    values = [x[:, :feature] for x in blocks] + [x[:, feature:] for x in blocks]
    packed = jnp.dot(chosen, jnp.concatenate(values, axis=0), preferred_element_type=F32)
    packed = jnp.concatenate([packed[: 9 * half], packed[9 * half :]], axis=1).astype(BF16)
    copies[2].wait()
    atom = atom_ref[0, 0]
    atom = jnp.concatenate([atom[: atoms // 2], atom[atoms // 2 :]], axis=1)
    for third, ref in enumerate((own_ref, one_ref, two_ref)):
        ref[: 3 * half] = packed[3 * half * third : 3 * half * (third + 1)]
        ref[3 * half :] = atom


def crossed(left, right):
    half = left.shape[1] // 2
    parts = [left[:, :half], right[:, :half], left[:, half:], right[:, half:]]
    return jnp.concatenate(parts, axis=1)


def two_blocks(weight):
    blank = jnp.zeros_like(weight)
    return jnp.concatenate([crossed(weight, blank), crossed(blank, weight)], axis=0)


def diagonal_blocks(weight):
    blank = jnp.zeros_like(weight)
    return jnp.concatenate(
        [jnp.concatenate([weight, blank], axis=1), jnp.concatenate([blank, weight], axis=1)],
        axis=0,
    )


def angular_kernel(atoms, dirs_ref, angle_ref, angular_ref):
    slots, pairs, _ = angular_ref.shape
    bonds = 2 * pairs
    degrees = angle_ref.shape[0]
    weight = (two_blocks(angle_ref[...].astype(F32)) * 0.5).astype(BF16)
    polar, azimuth = dirs_ref[0, 0], dirs_ref[1, 0]
    unit = jnp.concatenate(
        [
            jnp.sin(polar) * jnp.cos(azimuth),
            jnp.sin(polar) * jnp.sin(azimuth),
            jnp.cos(polar),
            jnp.zeros((5, bonds), F32),
        ],
        axis=0,
    )
    high = unit.astype(BF16).astype(F32)
    middle = (unit - high).astype(BF16).astype(F32)
    parts = jnp.concatenate([high, middle, unit - high - middle], axis=0).astype(BF16)
    bond = lax.broadcasted_iota(jnp.int32, (1, bonds), 1)
    source = remainder(bond, atoms) * slots + slot_at(quotient(bond, atoms), slots)
    spot = lax.broadcasted_iota(jnp.int32, (bonds, bonds), 0)
    chosen = jnp.where(spot == source, 1.0, 0.0).astype(BF16)
    unit = jnp.dot(parts, chosen, preferred_element_type=F32)
    unit = unit[0:8] + unit[8:16] + unit[16:24]
    even = [jnp.broadcast_to(unit[k : k + 1, :pairs], (8, pairs)) for k in range(3)]
    odd = [jnp.broadcast_to(unit[k : k + 1, pairs:], (8, pairs)) for k in range(3)]
    row = lax.broadcasted_iota(jnp.int32, (8, pairs), 0)

    def turned(vector, places):
        places = places % (pairs // atoms)
        if places == 0:
            return vector
        return [pltpu.roll(part, pairs - atoms * places, 1) for part in vector]

    def basis(first, second):
        cosine = first[0] * second[0] + first[1] * second[1] + first[2] * second[2]
        series = [jnp.ones_like(cosine), cosine]
        double = cosine + cosine
        for _ in range(7):
            series.append(double * series[-1] - series[-2])
        lower = series[7]
        upper = series[1]
        for index in range(1, 8):
            lower = jnp.where(row == index, series[7 - index], lower)
            upper = jnp.where(row == index, series[1 + index], upper)
        double = series[8] + series[8]
        blocks = [lower, upper]
        for _ in range(degrees // 8 - 1):
            blocks.append(double * blocks[-1] - blocks[-2])
        return blocks[1:]

    for diagonal in range(slots):
        places = diagonal // 2
        if diagonal % 2 == 0:
            blocks = basis(even, turned(even, places)) + basis(odd, turned(odd, places))
        else:
            blocks = basis(even, turned(odd, places)) + basis(odd, turned(even, places + 1))
        series = jnp.concatenate(blocks, axis=0).T.astype(BF16)
        angular_ref[diagonal] = jnp.dot(series, weight, preferred_element_type=F32)


def prepare_kernel(
    extents,
    paired,
    targets_ref,
    atom_ref,
    bond_ref,
    *refs,
):
    sources, results, held, sems = refs[:9], refs[9:22], refs[22:29], refs[29]
    chosen_ref, right_ref, own_ref, near_ref = results[:4]
    far_weight_ref, mix_weight_ref, pair_weight_ref, hidden_weight_ref = results[4:8]
    out_weight_ref, atom_in_weight_ref, atom_out_weight_ref = results[8:11]
    bond_in_ref, bond_mix_ref, pair_ref, pair_hidden_ref, pair_out_ref = held[:5]
    atom_in_ref, atom_out_ref = held[5:]
    copies = [
        pltpu.make_async_copy(source, target, sems.at[k])
        for k, (source, target) in enumerate(zip(sources, held + results[11:]))
    ]
    for copy in copies:
        copy.start()
    atoms, feature = atom_ref.shape[2], atom_ref.shape[3]
    slots = targets_ref.shape[0]
    bonds = slots * atoms
    targets = bond_row(targets_ref[...])
    code_x, code_y = bond_codes(targets, atoms, extents, paired, True)
    code = 3 * code_y + code_x
    bond = lax.broadcasted_iota(jnp.int32, (1, bonds), 1)
    far_slot = slots - 1 - slot_at(quotient(bond, atoms), slots)
    far_atom = remainder(targets, atoms)
    far = (remainder(far_slot, 2) * (slots // 2) + quotient(far_slot, 2)) * atoms + far_atom
    base = (code * bonds).astype(F32)
    key = base + far.astype(F32)

    def column(values):
        return jnp.broadcast_to(values.astype(F32), (128, bonds)).T

    keys = column(key)
    place = []
    for group in range(bonds // 128):
        here = slice(group * 128, (group + 1) * 128)
        inside = (keys < key[:, here]) & (keys >= base[:, here])
        place.append(jnp.sum(jnp.where(inside, 1.0, 0.0), axis=0, keepdims=True))
    place = jnp.concatenate(place, axis=1).astype(jnp.int32)
    half, tall = CAP // 2, atoms // 2
    bond_spot = column(half * code + remainder(place, half))
    atom_spot = column(9 * half + tall * code + remainder(far_atom, tall))
    right = (column(quotient(place, half)), column(quotient(far_atom, tall)))
    right_ref[...] = jnp.where(left_lanes((bonds, 128)), right[0], right[1])
    total = 9 * half + 9 * tall
    for start in range(0, total, 128):
        width = min(128, total - start)
        spot = lax.broadcasted_iota(jnp.int32, (bonds, 128), 1).astype(F32) + float(start)
        chosen = jnp.where((spot == bond_spot) | (spot == atom_spot), 1.0, 0.0).astype(BF16)
        chosen_ref[:, start : start + width] = chosen[:, :width]

    atom = atom_ref[0, 0]
    blocks = blocks_of(bond_ref, slots // 2)
    own = [jnp.concatenate([atom, x[:, :feature]], axis=1) for x in blocks]
    own += [jnp.concatenate([atom, x[:, feature:]], axis=1) for x in blocks]
    own = jnp.concatenate(own, axis=0)
    own_ref[...] = own

    for copy in copies:
        copy.wait()
    weight = bond_in_ref[...].astype(F32)
    source, other, bond_part = (weight[k * feature : (k + 1) * feature] for k in range(3))
    blank = jnp.zeros_like(source)
    near = [crossed(other, source), crossed(blank, bond_part)]
    near = (jnp.concatenate(near, axis=0) * 0.5).astype(BF16)
    near_ref[...] = jnp.dot(own, near, preferred_element_type=F32)
    away = [crossed(bond_part, blank), crossed(source, other)]
    far_weight_ref[...] = (jnp.concatenate(away, axis=0) * 0.5).astype(BF16)
    mix_weight_ref[...] = (diagonal_blocks(bond_mix_ref[...].astype(F32)) * 0.5).astype(BF16)
    weight = pair_ref[...].astype(F32) * 0.5
    pair_weight_ref[...] = jnp.concatenate(
        [two_blocks(weight[:, : 2 * feature]), two_blocks(weight[:, 2 * feature :])], axis=1
    ).astype(BF16)
    hidden_weight_ref[...] = (two_blocks(pair_hidden_ref[...].astype(F32)) * 0.25).astype(BF16)
    out_weight_ref[...] = (diagonal_blocks(pair_out_ref[...].astype(F32)) * 0.5).astype(BF16)
    weight = atom_in_ref[...].astype(F32) * 0.5
    atom_in_weight_ref[...] = crossed(weight, jnp.zeros_like(weight)).astype(BF16)
    weight = atom_out_ref[...].astype(F32) * 0.5
    blank = jnp.zeros_like(weight)
    weight = jnp.concatenate([weight, blank], axis=1)
    atom_out_weight_ref[...] = jnp.concatenate([weight, jnp.zeros_like(weight)], axis=0).astype(
        BF16
    )


def doubled_gate(values):
    half = values.shape[1] // 2
    first, second = values[:, :half], values[:, half:]
    return first * (1.0 + jnp.tanh(first)) * (1.0 + jnp.tanh(second))


def main_kernel(
    own_rows_ref,
    one_ref,
    two_ref,
    four_ref,
    three_ref,
    angular_ref,
    chosen_ref,
    right_ref,
    own_ref,
    near_ref,
    far_weight_ref,
    mix_weight_ref,
    pair_weight_ref,
    hidden_weight_ref,
    out_weight_ref,
    atom_in_weight_ref,
    atom_out_weight_ref,
    atom_result_hbm,
    bond_result_hbm,
    atom_result_ref,
    bond_result_ref,
    first_ref,
    second_ref,
    pair_ref,
    sems,
):
    slots, pairs, _ = angular_ref.shape
    bonds = 2 * pairs
    atoms = bonds // slots
    feature = own_ref.shape[1] // 2
    width = 2 * feature
    half = CAP // 2
    near_refs = (own_rows_ref, one_ref, two_ref)
    away_refs = (three_ref, four_ref)
    sent = [ref[:half] for ref in near_refs] + [ref[: 3 * half] for ref in away_refs]
    sent = jnp.concatenate(sent, axis=0)
    sent_atom = jnp.concatenate([ref[3 * half :] for ref in near_refs + away_refs], axis=0)
    blank = jnp.zeros((sent.shape[0], feature), BF16)
    blank_atom = jnp.zeros((sent_atom.shape[0], feature), BF16)
    received = jnp.concatenate(
        [
            jnp.concatenate([sent[:, :feature], blank, sent[:, feature:], blank], axis=1),
            jnp.concatenate(
                [blank_atom, sent_atom[:, :feature], blank_atom, sent_atom[:, feature:]], axis=1
            ),
        ],
        axis=0,
    )
    far = jnp.dot(chosen_ref[...], received, preferred_element_type=F32)
    far = jnp.where(right_ref[...] > 0.0, far[:, width:], far[:, :width])
    incoming = near_ref[...] + jnp.dot(
        far.astype(BF16), far_weight_ref[...], preferred_element_type=F32
    )
    hidden = doubled_gate(incoming).astype(BF16)
    mixed = jnp.dot(hidden, mix_weight_ref[...], preferred_element_type=F32)
    old = jnp.where(left_lanes((bonds, width)), far, own_ref[...].astype(F32))
    new = (old + mixed).astype(BF16).astype(F32)
    average = ((new + pltpu.roll(new, feature, 1)) * 0.5).astype(BF16).astype(F32)
    even, odd = average[:pairs], average[pairs:]
    left = left_lanes((pairs, width))
    packed = jnp.where(left, even, odd)
    shifted = jnp.where(left, odd, jnp.concatenate([even[atoms:], even[:atoms]], axis=0))
    projected = jnp.dot(packed.astype(BF16), pair_weight_ref[...], preferred_element_type=F32)
    first_ref[...] = projected[:, : 2 * width]
    second_ref[0] = projected[:, 2 * width :]
    second_ref[1] = jnp.dot(
        shifted.astype(BF16), pair_weight_ref[:, 2 * width :], preferred_element_type=F32
    )
    group = 4

    def first_gates(base):
        for start in range(0, pairs, atoms):
            here = first_ref[pl.ds(start, atoms)]
            for diagonal in range(base, base + group):
                there = (start + diagonal // 2 * atoms) % pairs
                mixture = angular_ref[diagonal, pl.ds(start, atoms)] + (
                    here + second_ref[diagonal % 2, pl.ds(there, atoms)]
                )
                pair_ref[pl.ds(diagonal * pairs + start, atoms)] = doubled_gate(mixture).astype(
                    BF16
                )

    total = jnp.zeros((pairs, width), F32)
    first_gates(0)
    for base in range(0, slots, group):
        second = jnp.dot(
            pair_ref[pl.ds(base * pairs, group * pairs)],
            hidden_weight_ref[...],
            preferred_element_type=F32,
        )
        if base + group < slots:
            first_gates(base + group)
        gates = doubled_gate(second)
        for k in range(group):
            total = total + gates[k * pairs : (k + 1) * pairs]
    bond_out = packed + jnp.dot(
        total.astype(BF16), out_weight_ref[...], preferred_element_type=F32
    )
    bond_out = bond_out.astype(BF16)
    pooled = jnp.zeros((atoms, width), F32)
    for k in range(slots // 2):
        rows = bond_out[k * atoms : (k + 1) * atoms]
        bond_result_ref[0, 0, :, k * width : (k + 1) * width] = rows
        pooled = pooled + rows.astype(F32)
    copies = [pltpu.make_async_copy(bond_result_ref, bond_result_hbm, sems.at[0])]
    copies[0].start()
    pooled = (pooled + pltpu.roll(pooled, feature, 1)) * (1.0 / slots)
    atom = own_ref[0:atoms].astype(F32)
    joined = jnp.where(left_lanes((atoms, width)), atom, pooled).astype(BF16)
    atom_hidden = doubled_gate(
        jnp.dot(joined, atom_in_weight_ref[...], preferred_element_type=F32)
    ).astype(BF16)
    atom_new = atom + jnp.dot(atom_hidden, atom_out_weight_ref[...], preferred_element_type=F32)
    atom_result_ref[0, 0] = atom_new[:, :feature].astype(BF16)
    copies.append(pltpu.make_async_copy(atom_result_ref, atom_result_hbm, sems.at[1]))
    copies[-1].start()
    for copy in copies:
        copy.wait()


def per_device(
    atom_feat,
    bond_feat,
    neighbours,
    bond_dirs,
    bond_in_weight,
    bond_mix_weight,
    pair_weight,
    angle_weight,
    pair_hidden_weight,
    pair_out_weight,
    atom_in_weight,
    atom_out_weight,
):
    atoms, feature = atom_feat.shape[2], atom_feat.shape[3]
    slots = neighbours.shape[3]
    bonds = atoms * slots
    pairs = bonds // 2
    half = CAP // 2
    extents = (lax.axis_size("gx"), lax.axis_size("gy"))
    paired = (extents[0] % 2 == 0, False)
    targets = neighbours[0, 0].T
    hbm = pl.BlockSpec(memory_space=pltpu.HBM)
    vmem = pl.BlockSpec(memory_space=pltpu.VMEM)
    params = pltpu.CompilerParams(vmem_limit_bytes=32 * 2**20)

    def shaped(shape, dtype):
        return jax.ShapeDtypeStruct(shape, dtype)

    def in_hbm(arrays):
        return tuple(pltpu.with_memory_space_constraint(x, pltpu.HBM) for x in arrays)

    payload = shaped((3 * half + atoms // 2, 2 * feature), BF16)
    inputs = (targets, atom_feat, bond_feat)
    own, one, two, *held = pl.pallas_call(
        functools.partial(pack_kernel, extents, paired),
        out_shape=(payload,) * 3 + tuple(shaped(x.shape, x.dtype) for x in inputs),
        in_specs=[hbm] * 3,
        out_specs=(vmem,) * 6,
        scratch_shapes=[pltpu.SemaphoreType.DMA((3,))],
        compiler_params=params,
        name="pack",
    )(*in_hbm(inputs))
    first, second = moves(extents[0], paired[0])
    one = lax.ppermute(one, "gx", first)
    two = lax.ppermute(two, "gx", second)
    weights = (bond_in_weight, bond_mix_weight, pair_weight, pair_hidden_weight)
    weights += (pair_out_weight, atom_in_weight, atom_out_weight)
    *prepared, bond_dirs, angle_weight = pl.pallas_call(
        functools.partial(prepare_kernel, extents, paired),
        out_shape=(
            shaped((bonds, 9 * half + 9 * atoms // 2), BF16),
            shaped((bonds, 2 * feature), F32),
            shaped((bonds, 2 * feature), BF16),
            shaped((bonds, 4 * feature), F32),
            shaped((2 * feature, 4 * feature), BF16),
            shaped((2 * feature, 2 * feature), BF16),
            shaped((2 * feature, 8 * feature), BF16),
            shaped((2 * feature, 4 * feature), BF16),
            shaped((2 * feature, 2 * feature), BF16),
            shaped((2 * feature, 4 * feature), BF16),
            shaped((2 * feature, 2 * feature), BF16),
            shaped(bond_dirs.shape, F32),
            shaped(angle_weight.shape, BF16),
        ),
        in_specs=[vmem] * 3 + [hbm] * 9,
        out_specs=(vmem,) * 13,
        scratch_shapes=[pltpu.VMEM(x.shape, BF16) for x in weights]
        + [pltpu.SemaphoreType.DMA((9,))],
        compiler_params=params,
        cost_estimate=pl.CostEstimate(flops=64 * 2**20, bytes_accessed=2**21, transcendentals=0),
        name="prepare",
    )(*held, *in_hbm(weights + (bond_dirs, angle_weight)))
    own, one, two, prepared = lax.optimization_barrier((own, one, two, prepared))
    first, second = moves(extents[1], paired[1])

    def forwarded(block):
        parts = [x[block * half : (block + 1) * half] for x in (own, one, two)]
        return jnp.concatenate(parts + [x[3 * half :] for x in (own, one, two)], axis=0)

    three = lax.ppermute(forwarded(1), "gy", first)
    four = lax.ppermute(forwarded(2), "gy", second)
    angular = pl.pallas_call(
        functools.partial(angular_kernel, atoms),
        out_shape=shaped((slots, pairs, 4 * feature), F32),
        in_specs=[vmem, vmem],
        out_specs=vmem,
        compiler_params=params,
        cost_estimate=pl.CostEstimate(
            flops=256 * 2**20, bytes_accessed=2**22, transcendentals=4096
        ),
        name="angular",
    )(bond_dirs, angle_weight)
    return pl.pallas_call(
        main_kernel,
        out_shape=(shaped(atom_feat.shape, BF16), shaped(bond_feat.shape, BF16)),
        in_specs=[vmem] * 17,
        out_specs=(hbm, hbm),
        scratch_shapes=[
            pltpu.VMEM(atom_feat.shape, BF16),
            pltpu.VMEM(bond_feat.shape, BF16),
            pltpu.VMEM((pairs, 4 * feature), F32),
            pltpu.VMEM((2, pairs, 4 * feature), F32),
            pltpu.VMEM((slots * pairs, 2 * feature), BF16),
            pltpu.SemaphoreType.DMA((2,)),
        ],
        compiler_params=params,
        name="main",
    )(own, one, two, four, three, angular, *prepared)


def solution(mesh):
    placed = (
        P("gx", "gy", None, None),
        P("gx", "gy", None, None),
        P("gx", "gy", None, None),
        P(None, "gx", "gy", None),
        P(),
        P(),
        P(),
        P(),
        P(),
        P(),
        P(),
        P(),
    )
    return jax.shard_map(
        per_device,
        mesh=mesh,
        in_specs=placed,
        out_specs=(P("gx", "gy", None, None), P("gx", "gy", None, None)),
        check_vma=False,
    )
```

```python
import functools

import jax
import jax.numpy as jnp
from jax import lax
from jax.experimental import pallas as pl
from jax.experimental.pallas import tpu as pltpu
from jax.sharding import PartitionSpec as P

F32 = jnp.float32
BF16 = jnp.bfloat16
CAP = 64


def quotient(values, size):
    if size & (size - 1) == 0:
        return values >> (size.bit_length() - 1)
    return lax.div(values, jnp.int32(size))


def remainder(values, size):
    if size & (size - 1) == 0:
        return values & (size - 1)
    return lax.rem(values, jnp.int32(size))


def step_code(owner, home, extent, paired, receives):
    step = remainder(owner - home + 1 + extent, extent)
    if paired:
        ahead = jnp.where(remainder(home, 2) == 0, 0, 2)
    else:
        ahead = 0 if receives else 2
    return jnp.where(step == 1, 0, jnp.where(step == ahead, 1, 2))


def moves(extent, paired):
    if paired:
        near = [(i, i ^ 1) for i in range(extent)]
        return [(i, (((i + 1) ^ 1) - 1) % extent) for i in range(extent)], near
    up = [(i, (i + 1) % extent) for i in range(extent)]
    return up, [(j, i) for i, j in up]


def slot_at(position, slots):
    half = slots // 2
    return jnp.where(position < half, 2 * position, 2 * (position - half) + 1)


def bond_row(table):
    slots, atoms = table.shape
    per_group = 128 // atoms
    tiled = jnp.concatenate([table.astype(F32)] * per_group, axis=1)
    row = lax.broadcasted_iota(jnp.int32, tiled.shape, 0)
    position = quotient(lax.broadcasted_iota(jnp.int32, tiled.shape, 1), atoms)
    pieces = []
    for group in range(slots // per_group):
        chosen = row == slot_at(position + group * per_group, slots)
        pieces.append(jnp.sum(jnp.where(chosen, tiled, 0.0), axis=0, keepdims=True))
    return jnp.concatenate(pieces, axis=1).astype(jnp.int32)


def bond_codes(targets, atoms, extents, paired, receives):
    owner = quotient(targets, atoms)
    block = (quotient(owner, extents[1]), remainder(owner, extents[1]))
    return tuple(
        step_code(block[k], lax.axis_index(axis), extents[k], paired[k], receives)
        for k, axis in enumerate(("gx", "gy"))
    )


def left_lanes(shape):
    return lax.broadcasted_iota(jnp.int32, shape, 1) < shape[1] // 2


def swapped(rows):
    half = rows.shape[1] // 2
    return jnp.concatenate([rows[:, half:], rows[:, :half]], axis=1)


def blocks_of(bond_ref, pairs):
    width = bond_ref.shape[3] // pairs
    return [bond_ref[0, 0, :, k * width : (k + 1) * width] for k in range(pairs)]


def pack_kernel(
    extents,
    paired,
    targets_hbm,
    atom_hbm,
    bond_hbm,
    dirs_hbm,
    own_ref,
    one_ref,
    two_ref,
    own_wrap_ref,
    one_wrap_ref,
    two_wrap_ref,
    targets_ref,
    atom_ref,
    bond_ref,
    dirs_ref,
    sems,
):
    sources = ((targets_hbm, targets_ref), (bond_hbm, bond_ref), (atom_hbm, atom_ref))
    sources += ((dirs_hbm, dirs_ref),)
    copies = [
        pltpu.make_async_copy(source, target, sems.at[k])
        for k, (source, target) in enumerate(sources)
    ]
    for copy in copies:
        copy.start()
    atoms, feature = atom_ref.shape[2], atom_ref.shape[3]
    slots = targets_ref.shape[0]
    bonds = slots * atoms
    lanes = 128
    groups = bonds // lanes
    copies[0].wait()
    code_x, code_y = bond_codes(bond_row(targets_ref[...]), atoms, extents, paired, False)
    code = 3 * code_x + code_y
    rows = lax.broadcasted_iota(jnp.int32, (16, lanes), 0)
    marks = [rows == code[:, g * lanes : (g + 1) * lanes] for g in range(groups)]
    stacked = jnp.concatenate([m.astype(F32) for m in marks], axis=0).astype(BF16)
    before = lax.broadcasted_iota(jnp.int32, (lanes, 2 * lanes), 0)
    after = lax.broadcasted_iota(jnp.int32, (lanes, 2 * lanes), 1)
    sums = jnp.where((before < after) | (after >= lanes), 1.0, 0.0).astype(BF16)
    counted = jnp.dot(stacked, sums, preferred_element_type=F32)
    place = []
    earlier = jnp.zeros((16, lanes), F32)
    for g in range(groups):
        part = counted[g * 16 : (g + 1) * 16]
        place.append(
            jnp.sum(jnp.where(marks[g], part[:, :lanes] + earlier, 0.0), axis=0, keepdims=True)
        )
        earlier = earlier + part[:, lanes:]
    place = jnp.concatenate(place, axis=1).astype(jnp.int32)
    half = CAP // 2
    right = quotient(place, half)
    wanted = 9 * half * right + place - half * right + half * code
    spot = lax.broadcasted_iota(jnp.int32, (9 * CAP, bonds), 0)
    chosen = jnp.where(spot == wanted, 1.0, 0.0).astype(BF16)
    copies[1].wait()
    blocks = blocks_of(bond_ref, slots // 2)
    values = [x[:, :feature] for x in blocks] + [x[:, feature:] for x in blocks]
    packed = jnp.dot(chosen, jnp.concatenate(values, axis=0), preferred_element_type=F32)
    packed = jnp.concatenate([packed[: 9 * half], packed[9 * half :]], axis=1).astype(BF16)
    copies[2].wait()
    atom = atom_ref[0, 0]
    atom = jnp.concatenate([atom[: atoms // 2], atom[atoms // 2 :]], axis=1)
    refs = ((own_ref, own_wrap_ref), (one_ref, one_wrap_ref), (two_ref, two_wrap_ref))
    for third, (ref, wrap_ref) in enumerate(refs):
        rows = packed[3 * half * third : 3 * half * (third + 1)]
        ref[: 3 * half] = rows
        ref[3 * half :] = atom
        wrap_ref[:half] = rows[half : 2 * half]
        wrap_ref[half:] = atom
    copies[3].wait()


def crossed(left, right):
    half = left.shape[1] // 2
    parts = [left[:, :half], right[:, :half], left[:, half:], right[:, half:]]
    return jnp.concatenate(parts, axis=1)


def two_blocks(weight):
    blank = jnp.zeros_like(weight)
    return jnp.concatenate([crossed(weight, blank), crossed(blank, weight)], axis=0)


def diagonal_blocks(weight):
    blank = jnp.zeros_like(weight)
    return jnp.concatenate(
        [jnp.concatenate([weight, blank], axis=1), jnp.concatenate([blank, weight], axis=1)],
        axis=0,
    )


def angular_kernel(atoms, dirs_ref, *refs):
    sources, angular_ref, targets, sems = refs[:8], refs[8], refs[9:17], refs[17]
    copies = [
        pltpu.make_async_copy(source, target, sems.at[k])
        for k, (source, target) in enumerate(zip(sources, targets))
    ]
    for copy in copies:
        copy.start()
    angle_ref = targets[0]
    slots, pairs, _ = angular_ref.shape
    bonds = 2 * pairs
    degrees = angle_ref.shape[0]
    polar, azimuth = dirs_ref[0, 0], dirs_ref[1, 0]
    unit = jnp.concatenate(
        [
            jnp.sin(polar) * jnp.cos(azimuth),
            jnp.sin(polar) * jnp.sin(azimuth),
            jnp.cos(polar),
            jnp.zeros((5, bonds), F32),
        ],
        axis=0,
    )
    high = unit.astype(BF16).astype(F32)
    middle = (unit - high).astype(BF16).astype(F32)
    parts = jnp.concatenate([high, middle, unit - high - middle], axis=0).astype(BF16)
    bond = lax.broadcasted_iota(jnp.int32, (1, bonds), 1)
    source = remainder(bond, atoms) * slots + slot_at(quotient(bond, atoms), slots)
    spot = lax.broadcasted_iota(jnp.int32, (bonds, bonds), 0)
    chosen = jnp.where(spot == source, 1.0, 0.0).astype(BF16)
    unit = jnp.dot(parts, chosen, preferred_element_type=F32)
    unit = unit[0:8] + unit[8:16] + unit[16:24]
    even = [jnp.broadcast_to(unit[k : k + 1, :pairs], (8, pairs)) for k in range(3)]
    odd = [jnp.broadcast_to(unit[k : k + 1, pairs:], (8, pairs)) for k in range(3)]
    row = lax.broadcasted_iota(jnp.int32, (8, pairs), 0)

    def turned(vector, places):
        places = places % (pairs // atoms)
        if places == 0:
            return vector
        return [pltpu.roll(part, pairs - atoms * places, 1) for part in vector]

    def basis(first, second):
        cosine = first[0] * second[0] + first[1] * second[1] + first[2] * second[2]
        series = [jnp.ones_like(cosine), cosine]
        double = cosine + cosine
        for _ in range(7):
            series.append(double * series[-1] - series[-2])
        lower = series[7]
        upper = series[1]
        for index in range(1, 8):
            lower = jnp.where(row == index, series[7 - index], lower)
            upper = jnp.where(row == index, series[1 + index], upper)
        double = series[8] + series[8]
        blocks = [lower, upper]
        for _ in range(degrees // 8 - 1):
            blocks.append(double * blocks[-1] - blocks[-2])
        return blocks[1:]

    copies[0].wait()
    weight = (two_blocks(angle_ref[...].astype(F32)) * 0.5).astype(BF16)
    for diagonal in range(slots):
        places = diagonal // 2
        if diagonal % 2 == 0:
            blocks = basis(even, turned(even, places)) + basis(odd, turned(odd, places))
        else:
            blocks = basis(even, turned(odd, places)) + basis(odd, turned(even, places + 1))
        series = jnp.concatenate(blocks, axis=0).T.astype(BF16)
        angular_ref[diagonal] = jnp.dot(series, weight, preferred_element_type=F32)
    for copy in copies[1:]:
        copy.wait()


def prepare_kernel(
    extents,
    paired,
    targets_ref,
    atom_ref,
    bond_ref,
    bond_in_ref,
    bond_mix_ref,
    pair_ref,
    pair_hidden_ref,
    pair_out_ref,
    atom_in_ref,
    atom_out_ref,
    chosen_ref,
    right_ref,
    own_ref,
    near_ref,
    far_weight_ref,
    mix_weight_ref,
    pair_weight_ref,
    hidden_weight_ref,
    out_weight_ref,
    atom_in_weight_ref,
    atom_out_weight_ref,
):
    atoms, feature = atom_ref.shape[2], atom_ref.shape[3]
    slots = targets_ref.shape[0]
    bonds = slots * atoms
    targets = bond_row(targets_ref[...])
    code_x, code_y = bond_codes(targets, atoms, extents, paired, True)
    code = 3 * code_y + code_x
    bond = lax.broadcasted_iota(jnp.int32, (1, bonds), 1)
    far_slot = slots - 1 - slot_at(quotient(bond, atoms), slots)
    far_atom = remainder(targets, atoms)
    far = (remainder(far_slot, 2) * (slots // 2) + quotient(far_slot, 2)) * atoms + far_atom
    base = (code * bonds).astype(F32)
    key = base + far.astype(F32)

    def column(values):
        return jnp.broadcast_to(values.astype(F32), (128, bonds)).T

    keys = column(key)
    place = []
    for group in range(bonds // 128):
        here = slice(group * 128, (group + 1) * 128)
        inside = (keys < key[:, here]) & (keys >= base[:, here])
        place.append(jnp.sum(jnp.where(inside, 1.0, 0.0), axis=0, keepdims=True))
    place = jnp.concatenate(place, axis=1).astype(jnp.int32)
    half, tall = CAP // 2, atoms // 2
    bond_spot = column(half * code + remainder(place, half))
    atom_spot = column(9 * half + tall * code + remainder(far_atom, tall))
    right = (column(quotient(place, half)), column(quotient(far_atom, tall)))
    right_ref[...] = jnp.where(left_lanes((bonds, 128)), right[0], right[1])
    total = 9 * half + 9 * tall
    for start in range(0, total, 128):
        width = min(128, total - start)
        spot = lax.broadcasted_iota(jnp.int32, (bonds, 128), 1).astype(F32) + float(start)
        chosen = jnp.where((spot == bond_spot) | (spot == atom_spot), 1.0, 0.0).astype(BF16)
        chosen_ref[:, start : start + width] = chosen[:, :width]

    atom = atom_ref[0, 0]
    blocks = blocks_of(bond_ref, slots // 2)
    own = [jnp.concatenate([atom, x[:, :feature]], axis=1) for x in blocks]
    own += [jnp.concatenate([atom, x[:, feature:]], axis=1) for x in blocks]
    own = jnp.concatenate(own, axis=0)
    own_ref[...] = own

    weight = bond_in_ref[...].astype(F32)
    source, other, bond_part = (weight[k * feature : (k + 1) * feature] for k in range(3))
    blank = jnp.zeros_like(source)
    near = [crossed(other, source), crossed(blank, bond_part)]
    near = (jnp.concatenate(near, axis=0) * 0.5).astype(BF16)
    near_ref[...] = jnp.dot(own, near, preferred_element_type=F32)
    away = [crossed(bond_part, blank), crossed(source, other)]
    far_weight_ref[...] = (jnp.concatenate(away, axis=0) * 0.5).astype(BF16)
    mix_weight_ref[...] = (diagonal_blocks(bond_mix_ref[...].astype(F32)) * 0.5).astype(BF16)
    weight = pair_ref[...].astype(F32) * 0.5
    pair_weight_ref[...] = jnp.concatenate(
        [two_blocks(weight[:, : 2 * feature]), two_blocks(weight[:, 2 * feature :])], axis=1
    ).astype(BF16)
    hidden_weight_ref[...] = (two_blocks(pair_hidden_ref[...].astype(F32)) * 0.25).astype(BF16)
    out_weight_ref[...] = (diagonal_blocks(pair_out_ref[...].astype(F32)) * 0.5).astype(BF16)
    weight = atom_in_ref[...].astype(F32) * 0.5
    atom_in_weight_ref[...] = crossed(weight, jnp.zeros_like(weight)).astype(BF16)
    weight = atom_out_ref[...].astype(F32) * 0.5
    blank = jnp.zeros_like(weight)
    weight = jnp.concatenate([weight, blank], axis=1)
    atom_out_weight_ref[...] = jnp.concatenate([weight, jnp.zeros_like(weight)], axis=0).astype(
        BF16
    )


def doubled_gate(values):
    half = values.shape[1] // 2
    first, second = values[:, :half], values[:, half:]
    return first * (1.0 + jnp.tanh(first)) * (1.0 + jnp.tanh(second))


def main_kernel(
    own_rows_ref,
    one_ref,
    two_ref,
    three_ref,
    four_ref,
    own_wrap_ref,
    one_wrap_ref,
    two_wrap_ref,
    angular_ref,
    chosen_ref,
    right_ref,
    own_ref,
    near_ref,
    far_weight_ref,
    mix_weight_ref,
    pair_weight_ref,
    hidden_weight_ref,
    out_weight_ref,
    atom_in_weight_ref,
    atom_out_weight_ref,
    atom_result_hbm,
    bond_result_hbm,
    atom_result_ref,
    bond_result_ref,
    first_ref,
    second_ref,
    pair_ref,
    sems,
):
    slots, pairs, _ = angular_ref.shape
    bonds = 2 * pairs
    atoms = bonds // slots
    feature = own_ref.shape[1] // 2
    width = 2 * feature
    half = CAP // 2
    near_refs = (own_rows_ref, one_ref, two_ref)
    wrap_refs = (own_wrap_ref, one_wrap_ref, two_wrap_ref)
    before = three_ref[: 3 * half] + jnp.concatenate([ref[:half] for ref in wrap_refs], axis=0)
    before_atom = three_ref[3 * half :] + jnp.concatenate([ref[half:] for ref in wrap_refs], axis=0)
    sent = [ref[:half] for ref in near_refs] + [before, four_ref[: 3 * half]]
    sent = jnp.concatenate(sent, axis=0)
    sent_atom = [ref[3 * half :] for ref in near_refs] + [before_atom, four_ref[3 * half :]]
    sent_atom = jnp.concatenate(sent_atom, axis=0)
    blank = jnp.zeros((sent.shape[0], feature), BF16)
    blank_atom = jnp.zeros((sent_atom.shape[0], feature), BF16)
    received = jnp.concatenate(
        [
            jnp.concatenate([sent[:, :feature], blank, sent[:, feature:], blank], axis=1),
            jnp.concatenate(
                [blank_atom, sent_atom[:, :feature], blank_atom, sent_atom[:, feature:]], axis=1
            ),
        ],
        axis=0,
    )
    far = jnp.dot(chosen_ref[...], received, preferred_element_type=F32)
    far = jnp.where(right_ref[...] > 0.0, far[:, width:], far[:, :width])
    incoming = near_ref[...] + jnp.dot(
        far.astype(BF16), far_weight_ref[...], preferred_element_type=F32
    )
    hidden = doubled_gate(incoming).astype(BF16)
    mixed = jnp.dot(hidden, mix_weight_ref[...], preferred_element_type=F32)
    old = jnp.where(left_lanes((bonds, width)), far, own_ref[...].astype(F32))
    new = (old + mixed).astype(BF16).astype(F32)
    average = ((new + pltpu.roll(new, feature, 1)) * 0.5).astype(BF16).astype(F32)
    even, odd = average[:pairs], average[pairs:]
    left = left_lanes((pairs, width))
    packed = jnp.where(left, even, odd)
    shifted = jnp.where(left, odd, jnp.concatenate([even[atoms:], even[:atoms]], axis=0))
    projected = jnp.dot(packed.astype(BF16), pair_weight_ref[...], preferred_element_type=F32)
    first_ref[...] = projected[:, : 2 * width]
    second_ref[0] = projected[:, 2 * width :]
    second_ref[1] = jnp.dot(
        shifted.astype(BF16), pair_weight_ref[:, 2 * width :], preferred_element_type=F32
    )
    group = 4

    def first_gates(base):
        for start in range(0, pairs, atoms):
            here = first_ref[pl.ds(start, atoms)]
            for diagonal in range(base, base + group):
                there = (start + diagonal // 2 * atoms) % pairs
                mixture = angular_ref[diagonal, pl.ds(start, atoms)] + (
                    here + second_ref[diagonal % 2, pl.ds(there, atoms)]
                )
                pair_ref[pl.ds(diagonal * pairs + start, atoms)] = doubled_gate(mixture).astype(
                    BF16
                )

    total = jnp.zeros((pairs, width), F32)
    first_gates(0)
    for base in range(0, slots, group):
        second = jnp.dot(
            pair_ref[pl.ds(base * pairs, group * pairs)],
            hidden_weight_ref[...],
            preferred_element_type=F32,
        )
        if base + group < slots:
            first_gates(base + group)
        gates = doubled_gate(second)
        for k in range(group):
            total = total + gates[k * pairs : (k + 1) * pairs]
    bond_out = packed + jnp.dot(
        total.astype(BF16), out_weight_ref[...], preferred_element_type=F32
    )
    bond_out = bond_out.astype(BF16)
    pooled = jnp.zeros((atoms, width), F32)
    for k in range(slots // 2):
        rows = bond_out[k * atoms : (k + 1) * atoms]
        bond_result_ref[0, 0, :, k * width : (k + 1) * width] = rows
        pooled = pooled + rows.astype(F32)
    copies = [pltpu.make_async_copy(bond_result_ref, bond_result_hbm, sems.at[0])]
    copies[0].start()
    pooled = (pooled + pltpu.roll(pooled, feature, 1)) * (1.0 / slots)
    atom = own_ref[0:atoms].astype(F32)
    joined = jnp.where(left_lanes((atoms, width)), atom, pooled).astype(BF16)
    atom_hidden = doubled_gate(
        jnp.dot(joined, atom_in_weight_ref[...], preferred_element_type=F32)
    ).astype(BF16)
    atom_new = atom + jnp.dot(atom_hidden, atom_out_weight_ref[...], preferred_element_type=F32)
    atom_result_ref[0, 0] = atom_new[:, :feature].astype(BF16)
    copies.append(pltpu.make_async_copy(atom_result_ref, atom_result_hbm, sems.at[1]))
    copies[-1].start()
    for copy in copies:
        copy.wait()


def per_device(
    atom_feat,
    bond_feat,
    neighbours,
    bond_dirs,
    bond_in_weight,
    bond_mix_weight,
    pair_weight,
    angle_weight,
    pair_hidden_weight,
    pair_out_weight,
    atom_in_weight,
    atom_out_weight,
):
    atoms, feature = atom_feat.shape[2], atom_feat.shape[3]
    slots = neighbours.shape[3]
    bonds = atoms * slots
    pairs = bonds // 2
    half = CAP // 2
    extents = (lax.axis_size("gx"), lax.axis_size("gy"))
    paired = (extents[0] % 2 == 0, False)
    targets = neighbours[0, 0].T
    hbm = pl.BlockSpec(memory_space=pltpu.HBM)
    vmem = pl.BlockSpec(memory_space=pltpu.VMEM)
    params = pltpu.CompilerParams(vmem_limit_bytes=32 * 2**20)

    def shaped(shape, dtype):
        return jax.ShapeDtypeStruct(shape, dtype)

    def in_hbm(arrays):
        return tuple(pltpu.with_memory_space_constraint(x, pltpu.HBM) for x in arrays)

    payload = shaped((3 * half + atoms // 2, 2 * feature), BF16)
    wrapped = shaped((half + atoms // 2, 2 * feature), BF16)
    inputs = (targets, atom_feat, bond_feat, bond_dirs)
    own, one, two, *wraps, targets, atom_here, bond_here, bond_dirs = pl.pallas_call(
        functools.partial(pack_kernel, extents, paired),
        out_shape=(payload,) * 3
        + (wrapped,) * 3
        + tuple(shaped(x.shape, x.dtype) for x in inputs),
        in_specs=[hbm] * 4,
        out_specs=(vmem,) * 10,
        scratch_shapes=[pltpu.SemaphoreType.DMA((4,))],
        compiler_params=params,
        name="pack",
    )(*in_hbm(inputs))
    first, second = moves(extents[0], paired[0])
    one = lax.ppermute(one, "gx", first)
    two = lax.ppermute(two, "gx", second)
    last = extents[1] - 1
    stay = [(i, i) for i in range(extents[0])]
    wraps = [
        lax.ppermute(x, ("gx", "gy"), [(i * extents[1] + last, j * extents[1]) for i, j in move])
        for x, move in zip(wraps, (stay, first, second))
    ]
    weights = (bond_in_weight, bond_mix_weight, pair_weight, pair_hidden_weight)
    weights = (angle_weight,) + weights + (pair_out_weight, atom_in_weight, atom_out_weight)
    angular, _, *weights = pl.pallas_call(
        functools.partial(angular_kernel, atoms),
        out_shape=(shaped((slots, pairs, 4 * feature), F32),)
        + tuple(shaped(x.shape, BF16) for x in weights),
        in_specs=[vmem] + [hbm] * 8,
        out_specs=(vmem,) * 9,
        scratch_shapes=[pltpu.SemaphoreType.DMA((8,))],
        compiler_params=params,
        cost_estimate=pl.CostEstimate(
            flops=256 * 2**20, bytes_accessed=2**22, transcendentals=4096
        ),
        name="angular",
    )(bond_dirs, *in_hbm(weights))
    own, one, two, angular, weights = lax.optimization_barrier((own, one, two, angular, weights))
    first, second = moves(extents[1], paired[1])

    def forwarded(block):
        parts = [x[block * half : (block + 1) * half] for x in (own, one, two)]
        return jnp.concatenate(parts + [x[3 * half :] for x in (own, one, two)], axis=0)

    three = lax.ppermute(forwarded(1), "gy", first[:-1])
    four = lax.ppermute(forwarded(2), "gy", second)
    prepared = pl.pallas_call(
        functools.partial(prepare_kernel, extents, paired),
        out_shape=(
            shaped((bonds, 9 * half + 9 * atoms // 2), BF16),
            shaped((bonds, 2 * feature), F32),
            shaped((bonds, 2 * feature), BF16),
            shaped((bonds, 4 * feature), F32),
            shaped((2 * feature, 4 * feature), BF16),
            shaped((2 * feature, 2 * feature), BF16),
            shaped((2 * feature, 8 * feature), BF16),
            shaped((2 * feature, 4 * feature), BF16),
            shaped((2 * feature, 2 * feature), BF16),
            shaped((2 * feature, 4 * feature), BF16),
            shaped((2 * feature, 2 * feature), BF16),
        ),
        in_specs=[vmem] * 10,
        out_specs=(vmem,) * 11,
        compiler_params=params,
        cost_estimate=pl.CostEstimate(flops=64000 * 2**20, bytes_accessed=2**25, transcendentals=0),
        name="prepare",
    )(targets, atom_here, bond_here, *weights)
    return pl.pallas_call(
        main_kernel,
        out_shape=(shaped(atom_feat.shape, BF16), shaped(bond_feat.shape, BF16)),
        in_specs=[vmem] * 20,
        out_specs=(hbm, hbm),
        scratch_shapes=[
            pltpu.VMEM(atom_feat.shape, BF16),
            pltpu.VMEM(bond_feat.shape, BF16),
            pltpu.VMEM((pairs, 4 * feature), F32),
            pltpu.VMEM((2, pairs, 4 * feature), F32),
            pltpu.VMEM((slots * pairs, 2 * feature), BF16),
            pltpu.SemaphoreType.DMA((2,)),
        ],
        compiler_params=params,
        name="main",
    )(own, one, two, three, four, *wraps, angular, *prepared)


def solution(mesh):
    placed = (
        P("gx", "gy", None, None),
        P("gx", "gy", None, None),
        P("gx", "gy", None, None),
        P(None, "gx", "gy", None),
        P(),
        P(),
        P(),
        P(),
        P(),
        P(),
        P(),
        P(),
    )
    return jax.shard_map(
        per_device,
        mesh=mesh,
        in_specs=placed,
        out_specs=(P("gx", "gy", None, None), P("gx", "gy", None, None)),
        check_vma=False,
    )
```

```python
import functools

import jax
import jax.numpy as jnp
from jax import lax
from jax.experimental import pallas as pl
from jax.experimental.pallas import tpu as pltpu
from jax.sharding import PartitionSpec as P

F32 = jnp.float32
BF16 = jnp.bfloat16
CAP = 64


def quotient(values, size):
    if size & (size - 1) == 0:
        return values >> (size.bit_length() - 1)
    return lax.div(values, jnp.int32(size))


def remainder(values, size):
    if size & (size - 1) == 0:
        return values & (size - 1)
    return lax.rem(values, jnp.int32(size))


def step_code(owner, home, extent, paired, receives):
    step = remainder(owner - home + 1 + extent, extent)
    if paired:
        ahead = jnp.where(remainder(home, 2) == 0, 0, 2)
    else:
        ahead = 0 if receives else 2
    return jnp.where(step == 1, 0, jnp.where(step == ahead, 1, 2))


def moves(extent, paired):
    if paired:
        near = [(i, i ^ 1) for i in range(extent)]
        return [(i, (((i + 1) ^ 1) - 1) % extent) for i in range(extent)], near
    up = [(i, (i + 1) % extent) for i in range(extent)]
    return up, [(j, i) for i, j in up]


def slot_at(position, slots):
    half = slots // 2
    return jnp.where(position < half, 2 * position, 2 * (position - half) + 1)


def bond_row(table):
    slots, atoms = table.shape
    per_group = 128 // atoms
    tiled = jnp.concatenate([table.astype(F32)] * per_group, axis=1)
    row = lax.broadcasted_iota(jnp.int32, tiled.shape, 0)
    position = quotient(lax.broadcasted_iota(jnp.int32, tiled.shape, 1), atoms)
    pieces = []
    for group in range(slots // per_group):
        chosen = row == slot_at(position + group * per_group, slots)
        pieces.append(jnp.sum(jnp.where(chosen, tiled, 0.0), axis=0, keepdims=True))
    return jnp.concatenate(pieces, axis=1).astype(jnp.int32)


def bond_codes(targets, atoms, extents, paired, receives):
    owner = quotient(targets, atoms)
    block = (quotient(owner, extents[1]), remainder(owner, extents[1]))
    return tuple(
        step_code(block[k], lax.axis_index(axis), extents[k], paired[k], receives)
        for k, axis in enumerate(("gx", "gy"))
    )


def left_lanes(shape):
    return lax.broadcasted_iota(jnp.int32, shape, 1) < shape[1] // 2


def swapped(rows):
    half = rows.shape[1] // 2
    return jnp.concatenate([rows[:, half:], rows[:, :half]], axis=1)


def blocks_of(bond_ref, pairs):
    width = bond_ref.shape[3] // pairs
    return [bond_ref[0, 0, :, k * width : (k + 1) * width] for k in range(pairs)]


def pack_kernel(
    extents,
    paired,
    targets_hbm,
    atom_hbm,
    bond_hbm,
    own_ref,
    one_ref,
    two_ref,
    targets_ref,
    atom_ref,
    bond_ref,
    sems,
):
    sources = ((targets_hbm, targets_ref), (bond_hbm, bond_ref), (atom_hbm, atom_ref))
    copies = [
        pltpu.make_async_copy(source, target, sems.at[k])
        for k, (source, target) in enumerate(sources)
    ]
    for copy in copies:
        copy.start()
    atoms, feature = atom_ref.shape[2], atom_ref.shape[3]
    slots = targets_ref.shape[0]
    bonds = slots * atoms
    lanes = 128
    groups = bonds // lanes
    copies[0].wait()
    code_x, code_y = bond_codes(bond_row(targets_ref[...]), atoms, extents, paired, False)
    code = 3 * code_x + code_y
    rows = lax.broadcasted_iota(jnp.int32, (16, lanes), 0)
    marks = [rows == code[:, g * lanes : (g + 1) * lanes] for g in range(groups)]
    stacked = jnp.concatenate([m.astype(F32) for m in marks], axis=0).astype(BF16)
    before = lax.broadcasted_iota(jnp.int32, (lanes, 2 * lanes), 0)
    after = lax.broadcasted_iota(jnp.int32, (lanes, 2 * lanes), 1)
    sums = jnp.where((before < after) | (after >= lanes), 1.0, 0.0).astype(BF16)
    counted = jnp.dot(stacked, sums, preferred_element_type=F32)
    place = []
    earlier = jnp.zeros((16, lanes), F32)
    for g in range(groups):
        part = counted[g * 16 : (g + 1) * 16]
        place.append(
            jnp.sum(jnp.where(marks[g], part[:, :lanes] + earlier, 0.0), axis=0, keepdims=True)
        )
        earlier = earlier + part[:, lanes:]
    place = jnp.concatenate(place, axis=1).astype(jnp.int32)
    half = CAP // 2
    right = quotient(place, half)
    wanted = 9 * half * right + place - half * right + half * code
    spot = lax.broadcasted_iota(jnp.int32, (9 * CAP, bonds), 0)
    chosen = jnp.where(spot == wanted, 1.0, 0.0).astype(BF16)
    copies[1].wait()
    blocks = blocks_of(bond_ref, slots // 2)
    values = [x[:, :feature] for x in blocks] + [x[:, feature:] for x in blocks]
    packed = jnp.dot(chosen, jnp.concatenate(values, axis=0), preferred_element_type=F32)
    packed = jnp.concatenate([packed[: 9 * half], packed[9 * half :]], axis=1).astype(BF16)
    copies[2].wait()
    atom = atom_ref[0, 0]
    atom = jnp.concatenate([atom[: atoms // 2], atom[atoms // 2 :]], axis=1)
    for third, ref in enumerate((own_ref, one_ref, two_ref)):
        ref[: 3 * half] = packed[3 * half * third : 3 * half * (third + 1)]
        ref[3 * half :] = atom


def crossed(left, right):
    half = left.shape[1] // 2
    parts = [left[:, :half], right[:, :half], left[:, half:], right[:, half:]]
    return jnp.concatenate(parts, axis=1)


def two_blocks(weight):
    blank = jnp.zeros_like(weight)
    return jnp.concatenate([crossed(weight, blank), crossed(blank, weight)], axis=0)


def diagonal_blocks(weight):
    blank = jnp.zeros_like(weight)
    return jnp.concatenate(
        [jnp.concatenate([weight, blank], axis=1), jnp.concatenate([blank, weight], axis=1)],
        axis=0,
    )


def angular_kernel(atoms, dirs_ref, angle_ref, angular_ref):
    slots, pairs, _ = angular_ref.shape
    bonds = 2 * pairs
    degrees = angle_ref.shape[0]
    weight = (two_blocks(angle_ref[...].astype(F32)) * 0.5).astype(BF16)
    polar, azimuth = dirs_ref[0, 0], dirs_ref[1, 0]
    unit = jnp.concatenate(
        [
            jnp.sin(polar) * jnp.cos(azimuth),
            jnp.sin(polar) * jnp.sin(azimuth),
            jnp.cos(polar),
            jnp.zeros((5, bonds), F32),
        ],
        axis=0,
    )
    high = unit.astype(BF16).astype(F32)
    middle = (unit - high).astype(BF16).astype(F32)
    parts = jnp.concatenate([high, middle, unit - high - middle], axis=0).astype(BF16)
    bond = lax.broadcasted_iota(jnp.int32, (1, bonds), 1)
    source = remainder(bond, atoms) * slots + slot_at(quotient(bond, atoms), slots)
    spot = lax.broadcasted_iota(jnp.int32, (bonds, bonds), 0)
    chosen = jnp.where(spot == source, 1.0, 0.0).astype(BF16)
    unit = jnp.dot(parts, chosen, preferred_element_type=F32)
    unit = unit[0:8] + unit[8:16] + unit[16:24]
    even = [jnp.broadcast_to(unit[k : k + 1, :pairs], (8, pairs)) for k in range(3)]
    odd = [jnp.broadcast_to(unit[k : k + 1, pairs:], (8, pairs)) for k in range(3)]
    row = lax.broadcasted_iota(jnp.int32, (8, pairs), 0)

    def turned(vector, places):
        places = places % (pairs // atoms)
        if places == 0:
            return vector
        return [pltpu.roll(part, pairs - atoms * places, 1) for part in vector]

    def basis(first, second):
        cosine = first[0] * second[0] + first[1] * second[1] + first[2] * second[2]
        series = [jnp.ones_like(cosine), cosine]
        double = cosine + cosine
        for _ in range(7):
            series.append(double * series[-1] - series[-2])
        lower = series[7]
        upper = series[1]
        for index in range(1, 8):
            lower = jnp.where(row == index, series[7 - index], lower)
            upper = jnp.where(row == index, series[1 + index], upper)
        double = series[8] + series[8]
        blocks = [lower, upper]
        for _ in range(degrees // 8 - 1):
            blocks.append(double * blocks[-1] - blocks[-2])
        return blocks[1:]

    for diagonal in range(slots):
        places = diagonal // 2
        if diagonal % 2 == 0:
            blocks = basis(even, turned(even, places)) + basis(odd, turned(odd, places))
        else:
            blocks = basis(even, turned(odd, places)) + basis(odd, turned(even, places + 1))
        series = jnp.concatenate(blocks, axis=0).T.astype(BF16)
        angular_ref[diagonal] = jnp.dot(series, weight, preferred_element_type=F32)


def prepare_kernel(
    extents,
    paired,
    targets_ref,
    atom_ref,
    bond_ref,
    *refs,
):
    sources, results, held, sems = refs[:9], refs[9:22], refs[22:29], refs[29]
    chosen_ref, right_ref, own_ref, near_ref = results[:4]
    far_weight_ref, mix_weight_ref, pair_weight_ref, hidden_weight_ref = results[4:8]
    out_weight_ref, atom_in_weight_ref, atom_out_weight_ref = results[8:11]
    bond_in_ref, bond_mix_ref, pair_ref, pair_hidden_ref, pair_out_ref = held[:5]
    atom_in_ref, atom_out_ref = held[5:]
    copies = [
        pltpu.make_async_copy(source, target, sems.at[k])
        for k, (source, target) in enumerate(zip(sources, held + results[11:]))
    ]
    for copy in copies:
        copy.start()
    atoms, feature = atom_ref.shape[2], atom_ref.shape[3]
    slots = targets_ref.shape[0]
    bonds = slots * atoms
    targets = bond_row(targets_ref[...])
    code_x, code_y = bond_codes(targets, atoms, extents, paired, True)
    code = 3 * code_y + code_x
    bond = lax.broadcasted_iota(jnp.int32, (1, bonds), 1)
    far_slot = slots - 1 - slot_at(quotient(bond, atoms), slots)
    far_atom = remainder(targets, atoms)
    far = (remainder(far_slot, 2) * (slots // 2) + quotient(far_slot, 2)) * atoms + far_atom
    base = (code * bonds).astype(F32)
    key = base + far.astype(F32)

    def column(values):
        return jnp.broadcast_to(values.astype(F32), (128, bonds)).T

    keys = column(key)
    place = []
    for group in range(bonds // 128):
        here = slice(group * 128, (group + 1) * 128)
        inside = (keys < key[:, here]) & (keys >= base[:, here])
        place.append(jnp.sum(jnp.where(inside, 1.0, 0.0), axis=0, keepdims=True))
    place = jnp.concatenate(place, axis=1).astype(jnp.int32)
    half, tall = CAP // 2, atoms // 2
    bond_spot = column(half * code + remainder(place, half))
    atom_spot = column(9 * half + tall * code + remainder(far_atom, tall))
    right = (column(quotient(place, half)), column(quotient(far_atom, tall)))
    right_ref[...] = jnp.where(left_lanes((bonds, 128)), right[0], right[1])
    total = 9 * half + 9 * tall
    for start in range(0, total, 128):
        width = min(128, total - start)
        spot = lax.broadcasted_iota(jnp.int32, (bonds, 128), 1).astype(F32) + float(start)
        chosen = jnp.where((spot == bond_spot) | (spot == atom_spot), 1.0, 0.0).astype(BF16)
        chosen_ref[:, start : start + width] = chosen[:, :width]

    atom = atom_ref[0, 0]
    blocks = blocks_of(bond_ref, slots // 2)
    own = [jnp.concatenate([atom, x[:, :feature]], axis=1) for x in blocks]
    own += [jnp.concatenate([atom, x[:, feature:]], axis=1) for x in blocks]
    own = jnp.concatenate(own, axis=0)
    own_ref[...] = own

    for copy in copies:
        copy.wait()
    weight = bond_in_ref[...].astype(F32)
    source, other, bond_part = (weight[k * feature : (k + 1) * feature] for k in range(3))
    blank = jnp.zeros_like(source)
    near = [crossed(other, source), crossed(blank, bond_part)]
    near = (jnp.concatenate(near, axis=0) * 0.5).astype(BF16)
    near_ref[...] = jnp.dot(own, near, preferred_element_type=F32)
    away = [crossed(bond_part, blank), crossed(source, other)]
    far_weight_ref[...] = (jnp.concatenate(away, axis=0) * 0.5).astype(BF16)
    mix_weight_ref[...] = (diagonal_blocks(bond_mix_ref[...].astype(F32)) * 0.5).astype(BF16)
    weight = pair_ref[...].astype(F32) * 0.5
    pair_weight_ref[...] = jnp.concatenate(
        [two_blocks(weight[:, : 2 * feature]), two_blocks(weight[:, 2 * feature :])], axis=1
    ).astype(BF16)
    hidden_weight_ref[...] = (two_blocks(pair_hidden_ref[...].astype(F32)) * 0.25).astype(BF16)
    out_weight_ref[...] = (diagonal_blocks(pair_out_ref[...].astype(F32)) * 0.5).astype(BF16)
    weight = atom_in_ref[...].astype(F32) * 0.5
    atom_in_weight_ref[...] = crossed(weight, jnp.zeros_like(weight)).astype(BF16)
    weight = atom_out_ref[...].astype(F32) * 0.5
    blank = jnp.zeros_like(weight)
    weight = jnp.concatenate([weight, blank], axis=1)
    atom_out_weight_ref[...] = jnp.concatenate([weight, jnp.zeros_like(weight)], axis=0).astype(
        BF16
    )


def doubled_gate(values):
    half = values.shape[1] // 2
    first, second = values[:, :half], values[:, half:]
    return first * (1.0 + jnp.tanh(first)) * (1.0 + jnp.tanh(second))


def main_kernel(
    own_rows_ref,
    one_ref,
    two_ref,
    four_ref,
    three_ref,
    angular_ref,
    chosen_ref,
    right_ref,
    own_ref,
    near_ref,
    far_weight_ref,
    mix_weight_ref,
    pair_weight_ref,
    hidden_weight_ref,
    out_weight_ref,
    atom_in_weight_ref,
    atom_out_weight_ref,
    atom_result_hbm,
    bond_result_hbm,
    atom_result_ref,
    bond_result_ref,
    first_ref,
    second_ref,
    pair_ref,
    sems,
):
    slots, pairs, _ = angular_ref.shape
    bonds = 2 * pairs
    atoms = bonds // slots
    feature = own_ref.shape[1] // 2
    width = 2 * feature
    half = CAP // 2
    near_refs = (own_rows_ref, one_ref, two_ref)
    away_refs = (three_ref, four_ref)
    sent = [ref[:half] for ref in near_refs] + [ref[: 3 * half] for ref in away_refs]
    sent = jnp.concatenate(sent, axis=0)
    sent_atom = jnp.concatenate([ref[3 * half :] for ref in near_refs + away_refs], axis=0)
    blank = jnp.zeros((sent.shape[0], feature), BF16)
    blank_atom = jnp.zeros((sent_atom.shape[0], feature), BF16)
    received = jnp.concatenate(
        [
            jnp.concatenate([sent[:, :feature], blank, sent[:, feature:], blank], axis=1),
            jnp.concatenate(
                [blank_atom, sent_atom[:, :feature], blank_atom, sent_atom[:, feature:]], axis=1
            ),
        ],
        axis=0,
    )
    far = jnp.dot(chosen_ref[...], received, preferred_element_type=F32)
    far = jnp.where(right_ref[...] > 0.0, far[:, width:], far[:, :width])
    incoming = near_ref[...] + jnp.dot(
        far.astype(BF16), far_weight_ref[...], preferred_element_type=F32
    )
    hidden = doubled_gate(incoming).astype(BF16)
    mixed = jnp.dot(hidden, mix_weight_ref[...], preferred_element_type=F32)
    old = jnp.where(left_lanes((bonds, width)), far, own_ref[...].astype(F32))
    new = (old + mixed).astype(BF16).astype(F32)
    average = ((new + pltpu.roll(new, feature, 1)) * 0.5).astype(BF16).astype(F32)
    even, odd = average[:pairs], average[pairs:]
    left = left_lanes((pairs, width))
    packed = jnp.where(left, even, odd)
    shifted = jnp.where(left, odd, jnp.concatenate([even[atoms:], even[:atoms]], axis=0))
    projected = jnp.dot(packed.astype(BF16), pair_weight_ref[...], preferred_element_type=F32)
    first_ref[...] = projected[:, : 2 * width]
    second_ref[0] = projected[:, 2 * width :]
    second_ref[1] = jnp.dot(
        shifted.astype(BF16), pair_weight_ref[:, 2 * width :], preferred_element_type=F32
    )
    group = 4

    def first_gates(base):
        for start in range(0, pairs, atoms):
            here = first_ref[pl.ds(start, atoms)]
            for diagonal in range(base, base + group):
                there = (start + diagonal // 2 * atoms) % pairs
                mixture = angular_ref[diagonal, pl.ds(start, atoms)] + (
                    here + second_ref[diagonal % 2, pl.ds(there, atoms)]
                )
                pair_ref[pl.ds(diagonal * pairs + start, atoms)] = doubled_gate(
                    mixture.astype(BF16)
                )

    total = jnp.zeros((pairs, width), F32)
    first_gates(0)
    for base in range(0, slots, group):
        second = jnp.dot(
            pair_ref[pl.ds(base * pairs, group * pairs)],
            hidden_weight_ref[...],
            preferred_element_type=F32,
        )
        if base + group < slots:
            first_gates(base + group)
        gates = doubled_gate(second.astype(BF16))
        for k in range(group):
            total = total + gates[k * pairs : (k + 1) * pairs].astype(F32)
    bond_out = packed + jnp.dot(
        total.astype(BF16), out_weight_ref[...], preferred_element_type=F32
    )
    bond_out = bond_out.astype(BF16)
    pooled = jnp.zeros((atoms, width), F32)
    for k in range(slots // 2):
        rows = bond_out[k * atoms : (k + 1) * atoms]
        bond_result_ref[0, 0, :, k * width : (k + 1) * width] = rows
        pooled = pooled + rows.astype(F32)
    copies = [pltpu.make_async_copy(bond_result_ref, bond_result_hbm, sems.at[0])]
    copies[0].start()
    pooled = (pooled + pltpu.roll(pooled, feature, 1)) * (1.0 / slots)
    atom = own_ref[0:atoms].astype(F32)
    joined = jnp.where(left_lanes((atoms, width)), atom, pooled).astype(BF16)
    atom_hidden = doubled_gate(
        jnp.dot(joined, atom_in_weight_ref[...], preferred_element_type=F32)
    ).astype(BF16)
    atom_new = atom + jnp.dot(atom_hidden, atom_out_weight_ref[...], preferred_element_type=F32)
    atom_result_ref[0, 0] = atom_new[:, :feature].astype(BF16)
    copies.append(pltpu.make_async_copy(atom_result_ref, atom_result_hbm, sems.at[1]))
    copies[-1].start()
    for copy in copies:
        copy.wait()


def per_device(
    atom_feat,
    bond_feat,
    neighbours,
    bond_dirs,
    bond_in_weight,
    bond_mix_weight,
    pair_weight,
    angle_weight,
    pair_hidden_weight,
    pair_out_weight,
    atom_in_weight,
    atom_out_weight,
):
    atoms, feature = atom_feat.shape[2], atom_feat.shape[3]
    slots = neighbours.shape[3]
    bonds = atoms * slots
    pairs = bonds // 2
    half = CAP // 2
    extents = (lax.axis_size("gx"), lax.axis_size("gy"))
    paired = (extents[0] % 2 == 0, False)
    targets = neighbours[0, 0].T
    hbm = pl.BlockSpec(memory_space=pltpu.HBM)
    vmem = pl.BlockSpec(memory_space=pltpu.VMEM)
    params = pltpu.CompilerParams(vmem_limit_bytes=32 * 2**20)

    def shaped(shape, dtype):
        return jax.ShapeDtypeStruct(shape, dtype)

    def in_hbm(arrays):
        return tuple(pltpu.with_memory_space_constraint(x, pltpu.HBM) for x in arrays)

    payload = shaped((3 * half + atoms // 2, 2 * feature), BF16)
    inputs = (targets, atom_feat, bond_feat)
    own, one, two, *held = pl.pallas_call(
        functools.partial(pack_kernel, extents, paired),
        out_shape=(payload,) * 3 + tuple(shaped(x.shape, x.dtype) for x in inputs),
        in_specs=[hbm] * 3,
        out_specs=(vmem,) * 6,
        scratch_shapes=[pltpu.SemaphoreType.DMA((3,))],
        compiler_params=params,
        name="pack",
    )(*in_hbm(inputs))
    first, second = moves(extents[0], paired[0])
    one = lax.ppermute(one, "gx", first)
    two = lax.ppermute(two, "gx", second)
    weights = (bond_in_weight, bond_mix_weight, pair_weight, pair_hidden_weight)
    weights += (pair_out_weight, atom_in_weight, atom_out_weight)
    *prepared, bond_dirs, angle_weight = pl.pallas_call(
        functools.partial(prepare_kernel, extents, paired),
        out_shape=(
            shaped((bonds, 9 * half + 9 * atoms // 2), BF16),
            shaped((bonds, 2 * feature), F32),
            shaped((bonds, 2 * feature), BF16),
            shaped((bonds, 4 * feature), F32),
            shaped((2 * feature, 4 * feature), BF16),
            shaped((2 * feature, 2 * feature), BF16),
            shaped((2 * feature, 8 * feature), BF16),
            shaped((2 * feature, 4 * feature), BF16),
            shaped((2 * feature, 2 * feature), BF16),
            shaped((2 * feature, 4 * feature), BF16),
            shaped((2 * feature, 2 * feature), BF16),
            shaped(bond_dirs.shape, F32),
            shaped(angle_weight.shape, BF16),
        ),
        in_specs=[vmem] * 3 + [hbm] * 9,
        out_specs=(vmem,) * 13,
        scratch_shapes=[pltpu.VMEM(x.shape, BF16) for x in weights]
        + [pltpu.SemaphoreType.DMA((9,))],
        compiler_params=params,
        cost_estimate=pl.CostEstimate(flops=64 * 2**20, bytes_accessed=2**21, transcendentals=0),
        name="prepare",
    )(*held, *in_hbm(weights + (bond_dirs, angle_weight)))
    own, one, two, prepared = lax.optimization_barrier((own, one, two, prepared))
    first, second = moves(extents[1], paired[1])

    def forwarded(block):
        parts = [x[block * half : (block + 1) * half] for x in (own, one, two)]
        return jnp.concatenate(parts + [x[3 * half :] for x in (own, one, two)], axis=0)

    three = lax.ppermute(forwarded(1), "gy", first)
    four = lax.ppermute(forwarded(2), "gy", second)
    angular = pl.pallas_call(
        functools.partial(angular_kernel, atoms),
        out_shape=shaped((slots, pairs, 4 * feature), F32),
        in_specs=[vmem, vmem],
        out_specs=vmem,
        compiler_params=params,
        cost_estimate=pl.CostEstimate(
            flops=256 * 2**20, bytes_accessed=2**22, transcendentals=4096
        ),
        name="angular",
    )(bond_dirs, angle_weight)
    return pl.pallas_call(
        main_kernel,
        out_shape=(shaped(atom_feat.shape, BF16), shaped(bond_feat.shape, BF16)),
        in_specs=[vmem] * 17,
        out_specs=(hbm, hbm),
        scratch_shapes=[
            pltpu.VMEM(atom_feat.shape, BF16),
            pltpu.VMEM(bond_feat.shape, BF16),
            pltpu.VMEM((pairs, 4 * feature), F32),
            pltpu.VMEM((2, pairs, 4 * feature), F32),
            pltpu.VMEM((slots * pairs, 2 * feature), BF16),
            pltpu.SemaphoreType.DMA((2,)),
        ],
        compiler_params=params,
        name="main",
    )(own, one, two, four, three, angular, *prepared)


def solution(mesh):
    placed = (
        P("gx", "gy", None, None),
        P("gx", "gy", None, None),
        P("gx", "gy", None, None),
        P(None, "gx", "gy", None),
        P(),
        P(),
        P(),
        P(),
        P(),
        P(),
        P(),
        P(),
    )
    return jax.shard_map(
        per_device,
        mesh=mesh,
        in_specs=placed,
        out_specs=(P("gx", "gy", None, None), P("gx", "gy", None, None)),
        check_vma=False,
    )
```

```python
import functools

import jax
import jax.numpy as jnp
from jax import lax
from jax.experimental import pallas as pl
from jax.experimental.pallas import tpu as pltpu
from jax.sharding import PartitionSpec as P

F32 = jnp.float32
BF16 = jnp.bfloat16
CAP = 64


def quotient(values, size):
    if size & (size - 1) == 0:
        return values >> (size.bit_length() - 1)
    return lax.div(values, jnp.int32(size))


def remainder(values, size):
    if size & (size - 1) == 0:
        return values & (size - 1)
    return lax.rem(values, jnp.int32(size))


def step_code(owner, home, extent, paired, receives):
    step = remainder(owner - home + 1 + extent, extent)
    if paired:
        ahead = jnp.where(remainder(home, 2) == 0, 0, 2)
    else:
        ahead = 0 if receives else 2
    return jnp.where(step == 1, 0, jnp.where(step == ahead, 1, 2))


def moves(extent, paired):
    if paired:
        near = [(i, i ^ 1) for i in range(extent)]
        return [(i, (((i + 1) ^ 1) - 1) % extent) for i in range(extent)], near
    up = [(i, (i + 1) % extent) for i in range(extent)]
    return up, [(j, i) for i, j in up]


def slot_at(position, slots):
    half = slots // 2
    return jnp.where(position < half, 2 * position, 2 * (position - half) + 1)


def bond_row(table):
    slots, atoms = table.shape
    per_group = 128 // atoms
    tiled = jnp.concatenate([table.astype(F32)] * per_group, axis=1)
    row = lax.broadcasted_iota(jnp.int32, tiled.shape, 0)
    position = quotient(lax.broadcasted_iota(jnp.int32, tiled.shape, 1), atoms)
    pieces = []
    for group in range(slots // per_group):
        chosen = row == slot_at(position + group * per_group, slots)
        pieces.append(jnp.sum(jnp.where(chosen, tiled, 0.0), axis=0, keepdims=True))
    return jnp.concatenate(pieces, axis=1).astype(jnp.int32)


def bond_codes(targets, atoms, extents, paired, receives):
    owner = quotient(targets, atoms)
    block = (quotient(owner, extents[1]), remainder(owner, extents[1]))
    return tuple(
        step_code(block[k], lax.axis_index(axis), extents[k], paired[k], receives)
        for k, axis in enumerate(("gx", "gy"))
    )


def left_lanes(shape):
    return lax.broadcasted_iota(jnp.int32, shape, 1) < shape[1] // 2


def swapped(rows):
    half = rows.shape[1] // 2
    return jnp.concatenate([rows[:, half:], rows[:, :half]], axis=1)


def blocks_of(bond_ref, pairs):
    width = bond_ref.shape[3] // pairs
    return [bond_ref[0, 0, :, k * width : (k + 1) * width] for k in range(pairs)]


def pack_kernel(
    extents,
    paired,
    targets_hbm,
    atom_hbm,
    bond_hbm,
    own_ref,
    one_ref,
    two_ref,
    targets_ref,
    atom_ref,
    bond_ref,
    sems,
):
    sources = ((targets_hbm, targets_ref), (bond_hbm, bond_ref), (atom_hbm, atom_ref))
    copies = [
        pltpu.make_async_copy(source, target, sems.at[k])
        for k, (source, target) in enumerate(sources)
    ]
    for copy in copies:
        copy.start()
    atoms, feature = atom_ref.shape[2], atom_ref.shape[3]
    slots = targets_ref.shape[0]
    bonds = slots * atoms
    lanes = 128
    groups = bonds // lanes
    copies[0].wait()
    code_x, code_y = bond_codes(bond_row(targets_ref[...]), atoms, extents, paired, False)
    code = 3 * code_x + code_y
    rows = lax.broadcasted_iota(jnp.int32, (16, lanes), 0)
    marks = [rows == code[:, g * lanes : (g + 1) * lanes] for g in range(groups)]
    stacked = jnp.concatenate([m.astype(F32) for m in marks], axis=0).astype(BF16)
    before = lax.broadcasted_iota(jnp.int32, (lanes, 2 * lanes), 0)
    after = lax.broadcasted_iota(jnp.int32, (lanes, 2 * lanes), 1)
    sums = jnp.where((before < after) | (after >= lanes), 1.0, 0.0).astype(BF16)
    counted = jnp.dot(stacked, sums, preferred_element_type=F32)
    place = []
    earlier = jnp.zeros((16, lanes), F32)
    for g in range(groups):
        part = counted[g * 16 : (g + 1) * 16]
        place.append(
            jnp.sum(jnp.where(marks[g], part[:, :lanes] + earlier, 0.0), axis=0, keepdims=True)
        )
        earlier = earlier + part[:, lanes:]
    place = jnp.concatenate(place, axis=1).astype(jnp.int32)
    half = CAP // 2
    right = quotient(place, half)
    wanted = 9 * half * right + place - half * right + half * code
    spot = lax.broadcasted_iota(jnp.int32, (9 * CAP, bonds), 0)
    chosen = jnp.where(spot == wanted, 1.0, 0.0).astype(BF16)
    copies[1].wait()
    blocks = blocks_of(bond_ref, slots // 2)
    values = [x[:, :feature] for x in blocks] + [x[:, feature:] for x in blocks]
    packed = jnp.dot(chosen, jnp.concatenate(values, axis=0), preferred_element_type=F32)
    packed = jnp.concatenate([packed[: 9 * half], packed[9 * half :]], axis=1).astype(BF16)
    copies[2].wait()
    atom = atom_ref[0, 0]
    atom = jnp.concatenate([atom[: atoms // 2], atom[atoms // 2 :]], axis=1)
    for third, ref in enumerate((own_ref, one_ref, two_ref)):
        ref[: 3 * half] = packed[3 * half * third : 3 * half * (third + 1)]
        ref[3 * half :] = atom


def crossed(left, right):
    half = left.shape[1] // 2
    parts = [left[:, :half], right[:, :half], left[:, half:], right[:, half:]]
    return jnp.concatenate(parts, axis=1)


def two_blocks(weight):
    blank = jnp.zeros_like(weight)
    return jnp.concatenate([crossed(weight, blank), crossed(blank, weight)], axis=0)


def diagonal_blocks(weight):
    blank = jnp.zeros_like(weight)
    return jnp.concatenate(
        [jnp.concatenate([weight, blank], axis=1), jnp.concatenate([blank, weight], axis=1)],
        axis=0,
    )


def angular_kernel(atoms, dirs_ref, angle_ref, angular_ref):
    slots, pairs, _ = angular_ref.shape
    bonds = 2 * pairs
    degrees = angle_ref.shape[0]
    weight = (two_blocks(angle_ref[...].astype(F32)) * 0.5).astype(BF16)
    polar, azimuth = dirs_ref[0, 0], dirs_ref[1, 0]
    unit = jnp.concatenate(
        [
            jnp.sin(polar) * jnp.cos(azimuth),
            jnp.sin(polar) * jnp.sin(azimuth),
            jnp.cos(polar),
            jnp.zeros((5, bonds), F32),
        ],
        axis=0,
    )
    high = unit.astype(BF16).astype(F32)
    middle = (unit - high).astype(BF16).astype(F32)
    parts = jnp.concatenate([high, middle, unit - high - middle], axis=0).astype(BF16)
    bond = lax.broadcasted_iota(jnp.int32, (1, bonds), 1)
    source = remainder(bond, atoms) * slots + slot_at(quotient(bond, atoms), slots)
    spot = lax.broadcasted_iota(jnp.int32, (bonds, bonds), 0)
    chosen = jnp.where(spot == source, 1.0, 0.0).astype(BF16)
    unit = jnp.dot(parts, chosen, preferred_element_type=F32)
    unit = unit[0:8] + unit[8:16] + unit[16:24]
    even = [jnp.broadcast_to(unit[k : k + 1, :pairs], (8, pairs)) for k in range(3)]
    odd = [jnp.broadcast_to(unit[k : k + 1, pairs:], (8, pairs)) for k in range(3)]
    row = lax.broadcasted_iota(jnp.int32, (8, pairs), 0)

    def turned(vector, places):
        places = places % (pairs // atoms)
        if places == 0:
            return vector
        return [pltpu.roll(part, pairs - atoms * places, 1) for part in vector]

    def basis(first, second):
        cosine = first[0] * second[0] + first[1] * second[1] + first[2] * second[2]
        series = [jnp.ones_like(cosine), cosine]
        double = cosine + cosine
        for _ in range(7):
            series.append(double * series[-1] - series[-2])
        lower = series[7]
        upper = series[1]
        for index in range(1, 8):
            lower = jnp.where(row == index, series[7 - index], lower)
            upper = jnp.where(row == index, series[1 + index], upper)
        double = series[8] + series[8]
        blocks = [lower, upper]
        for _ in range(degrees // 8 - 1):
            blocks.append(double * blocks[-1] - blocks[-2])
        return blocks[1:]

    for diagonal in range(slots):
        places = diagonal // 2
        if diagonal % 2 == 0:
            blocks = basis(even, turned(even, places)) + basis(odd, turned(odd, places))
        else:
            blocks = basis(even, turned(odd, places)) + basis(odd, turned(even, places + 1))
        series = jnp.concatenate(blocks, axis=0).T.astype(BF16)
        angular_ref[diagonal] = jnp.dot(series, weight, preferred_element_type=F32)


def prepare_kernel(
    extents,
    paired,
    targets_ref,
    atom_ref,
    bond_ref,
    *refs,
):
    sources, results, held, sems = refs[:9], refs[9:22], refs[22:29], refs[29]
    chosen_ref, right_ref, own_ref = results[:3]
    bond_weight_ref, mix_weight_ref, pair_weight_ref, hidden_weight_ref = results[3:7]
    out_weight_ref, atom_in_weight_ref, sum_weight_ref, atom_out_weight_ref = results[7:11]
    bond_in_ref, bond_mix_ref, pair_ref, pair_hidden_ref, pair_out_ref = held[:5]
    atom_in_ref, atom_out_ref = held[5:]
    copies = [
        pltpu.make_async_copy(source, target, sems.at[k])
        for k, (source, target) in enumerate(zip(sources, held + results[11:]))
    ]
    for copy in copies:
        copy.start()
    atoms, feature = atom_ref.shape[2], atom_ref.shape[3]
    slots = targets_ref.shape[0]
    bonds = slots * atoms
    targets = bond_row(targets_ref[...])
    code_x, code_y = bond_codes(targets, atoms, extents, paired, True)
    code = 3 * code_y + code_x
    bond = lax.broadcasted_iota(jnp.int32, (1, bonds), 1)
    far_slot = slots - 1 - slot_at(quotient(bond, atoms), slots)
    far_atom = remainder(targets, atoms)
    far = (remainder(far_slot, 2) * (slots // 2) + quotient(far_slot, 2)) * atoms + far_atom
    base = (code * bonds).astype(F32)
    key = base + far.astype(F32)

    def column(values):
        return jnp.broadcast_to(values.astype(F32), (128, bonds)).T

    keys = column(key)
    place = []
    for group in range(bonds // 128):
        here = slice(group * 128, (group + 1) * 128)
        inside = (keys < key[:, here]) & (keys >= base[:, here])
        place.append(jnp.sum(jnp.where(inside, 1.0, 0.0), axis=0, keepdims=True))
    place = jnp.concatenate(place, axis=1).astype(jnp.int32)
    half, tall = CAP // 2, atoms // 2
    bond_spot = column(half * code + remainder(place, half))
    atom_spot = column(9 * half + tall * code + remainder(far_atom, tall))
    right = (column(quotient(place, half)), column(quotient(far_atom, tall)))
    right_ref[...] = jnp.where(left_lanes((bonds, 128)), right[0], right[1])
    total = 9 * half + 9 * tall
    for start in range(0, total, 128):
        width = min(128, total - start)
        spot = lax.broadcasted_iota(jnp.int32, (bonds, 128), 1).astype(F32) + float(start)
        chosen = jnp.where((spot == bond_spot) | (spot == atom_spot), 1.0, 0.0).astype(BF16)
        chosen_ref[:, start : start + width] = chosen[:, :width]

    atom = atom_ref[0, 0]
    blocks = blocks_of(bond_ref, slots // 2)
    own = [jnp.concatenate([atom, x[:, :feature]], axis=1) for x in blocks]
    own += [jnp.concatenate([atom, x[:, feature:]], axis=1) for x in blocks]
    own = jnp.concatenate(own, axis=0)
    own_ref[...] = own

    for copy in copies:
        copy.wait()
    weight = bond_in_ref[...].astype(F32)
    source, other, bond_part = (weight[k * feature : (k + 1) * feature] for k in range(3))
    blank = jnp.zeros_like(source)
    away = [crossed(bond_part, blank), crossed(source, other)]
    near = [crossed(other, source), crossed(blank, bond_part)]
    bond_weight_ref[...] = (jnp.concatenate(away + near, axis=0) * 0.5).astype(BF16)
    mix_weight_ref[...] = (diagonal_blocks(bond_mix_ref[...].astype(F32)) * 0.5).astype(BF16)
    weight = pair_ref[...].astype(F32) * 0.5
    pair_weight_ref[...] = jnp.concatenate(
        [two_blocks(weight[:, : 2 * feature]), two_blocks(weight[:, 2 * feature :])], axis=1
    ).astype(BF16)
    hidden_weight_ref[...] = (two_blocks(pair_hidden_ref[...].astype(F32)) * 0.25).astype(BF16)
    out_weight_ref[...] = (diagonal_blocks(pair_out_ref[...].astype(F32)) * 0.5).astype(BF16)
    weight = atom_in_ref[...].astype(F32) * 0.5
    weight = crossed(weight, jnp.zeros_like(weight))
    mean = weight[feature:] * (1.0 / slots)
    atom_in_weight_ref[...] = jnp.concatenate([weight[:feature], mean, mean], axis=0).astype(BF16)
    folded = jnp.dot(
        pair_out_ref[...], (mean * 0.5).astype(BF16), preferred_element_type=F32
    )
    high = folded.astype(BF16)
    low = (folded - high.astype(F32)).astype(BF16)
    sum_weight_ref[...] = jnp.concatenate([high, high, low, low], axis=0)
    weight = atom_out_ref[...].astype(F32) * 0.5
    blank = jnp.zeros_like(weight)
    weight = jnp.concatenate([weight, blank], axis=1)
    atom_out_weight_ref[...] = jnp.concatenate([weight, jnp.zeros_like(weight)], axis=0).astype(
        BF16
    )


def doubled_gate(values):
    half = values.shape[1] // 2
    first, second = values[:, :half], values[:, half:]
    return first * (1.0 + jnp.tanh(first)) * (1.0 + jnp.tanh(second))


def main_kernel(
    own_rows_ref,
    one_ref,
    two_ref,
    four_ref,
    three_ref,
    angular_ref,
    chosen_ref,
    right_ref,
    own_ref,
    bond_weight_ref,
    mix_weight_ref,
    pair_weight_ref,
    hidden_weight_ref,
    out_weight_ref,
    atom_in_weight_ref,
    sum_weight_ref,
    atom_out_weight_ref,
    atom_result_hbm,
    bond_result_hbm,
    atom_result_ref,
    bond_result_ref,
    first_ref,
    second_ref,
    pair_ref,
    sems,
):
    slots, pairs, _ = angular_ref.shape
    bonds = 2 * pairs
    atoms = bonds // slots
    feature = own_ref.shape[1] // 2
    width = 2 * feature
    half = CAP // 2
    near_refs = (own_rows_ref, one_ref, two_ref)
    away_refs = (three_ref, four_ref)
    sent = [ref[:half] for ref in near_refs] + [ref[: 3 * half] for ref in away_refs]
    sent = jnp.concatenate(sent, axis=0)
    sent_atom = jnp.concatenate([ref[3 * half :] for ref in near_refs + away_refs], axis=0)
    blank = jnp.zeros((sent.shape[0], feature), BF16)
    blank_atom = jnp.zeros((sent_atom.shape[0], feature), BF16)
    received = jnp.concatenate(
        [
            jnp.concatenate([sent[:, :feature], blank, sent[:, feature:], blank], axis=1),
            jnp.concatenate(
                [blank_atom, sent_atom[:, :feature], blank_atom, sent_atom[:, feature:]], axis=1
            ),
        ],
        axis=0,
    )
    far = jnp.dot(chosen_ref[...], received, preferred_element_type=F32)
    far = jnp.where(right_ref[...] > 0.0, far[:, width:], far[:, :width])
    own = own_ref[...]
    incoming = jnp.dot(
        jnp.concatenate([far.astype(BF16), own], axis=1),
        bond_weight_ref[...],
        preferred_element_type=F32,
    )
    hidden = doubled_gate(incoming).astype(BF16)
    mixed = jnp.dot(hidden, mix_weight_ref[...], preferred_element_type=F32)
    old = jnp.where(left_lanes((bonds, width)), far, own.astype(F32))
    new = (old + mixed).astype(BF16).astype(F32)
    average = ((new + pltpu.roll(new, feature, 1)) * 0.5).astype(BF16).astype(F32)
    even, odd = average[:pairs], average[pairs:]
    left = left_lanes((pairs, width))
    packed = jnp.where(left, even, odd)
    shifted = jnp.where(left, odd, jnp.concatenate([even[atoms:], even[:atoms]], axis=0))
    projected = jnp.dot(packed.astype(BF16), pair_weight_ref[...], preferred_element_type=F32)
    first_ref[...] = projected[:, : 2 * width]
    second_ref[0] = projected[:, 2 * width :]
    second_ref[1] = jnp.dot(
        shifted.astype(BF16), pair_weight_ref[:, 2 * width :], preferred_element_type=F32
    )
    group = 2

    def first_gates(base):
        for start in range(0, pairs, atoms):
            here = first_ref[pl.ds(start, atoms)]
            for diagonal in range(base, base + group):
                there = (start + diagonal // 2 * atoms) % pairs
                mixture = angular_ref[diagonal, pl.ds(start, atoms)] + (
                    here + second_ref[diagonal % 2, pl.ds(there, atoms)]
                )
                pair_ref[pl.ds(diagonal * pairs + start, atoms)] = doubled_gate(mixture).astype(
                    BF16
                )

    def summed(rows):
        parts = [rows[k * atoms : (k + 1) * atoms] for k in range(slots // 2)]
        while len(parts) > 1:
            parts = [x + y for x, y in zip(parts[::2], parts[1::2])]
        return parts[0]

    atom = own[0:atoms]
    atom_incoming = jnp.dot(
        jnp.concatenate([atom[:, :feature], summed(packed).astype(BF16)], axis=1),
        atom_in_weight_ref[...],
        preferred_element_type=F32,
    )
    total = jnp.zeros((pairs, width), F32)
    first_gates(0)
    for base in range(0, slots, group):
        if base + group < slots:
            first_gates(base + group)
        second = jnp.dot(
            pair_ref[pl.ds(base * pairs, group * pairs)],
            hidden_weight_ref[...],
            preferred_element_type=F32,
        )
        gates = doubled_gate(second)
        for k in range(group):
            total = total + gates[k * pairs : (k + 1) * pairs]
    bond_out = packed + jnp.dot(
        total.astype(BF16), out_weight_ref[...], preferred_element_type=F32
    )
    bond_out = bond_out.astype(BF16)
    for k in range(slots // 2):
        bond_result_ref[0, 0, :, k * width : (k + 1) * width] = bond_out[
            k * atoms : (k + 1) * atoms
        ]
    copies = [pltpu.make_async_copy(bond_result_ref, bond_result_hbm, sems.at[0])]
    copies[0].start()
    sums = summed(total).astype(BF16)
    atom_incoming = atom_incoming + jnp.dot(
        jnp.concatenate([sums, sums], axis=1), sum_weight_ref[...], preferred_element_type=F32
    )
    atom_hidden = doubled_gate(atom_incoming).astype(BF16)
    atom_new = atom.astype(F32) + jnp.dot(
        atom_hidden, atom_out_weight_ref[...], preferred_element_type=F32
    )
    atom_result_ref[0, 0] = atom_new[:, :feature].astype(BF16)
    copies.append(pltpu.make_async_copy(atom_result_ref, atom_result_hbm, sems.at[1]))
    copies[-1].start()
    for copy in copies:
        copy.wait()


def per_device(
    atom_feat,
    bond_feat,
    neighbours,
    bond_dirs,
    bond_in_weight,
    bond_mix_weight,
    pair_weight,
    angle_weight,
    pair_hidden_weight,
    pair_out_weight,
    atom_in_weight,
    atom_out_weight,
):
    atoms, feature = atom_feat.shape[2], atom_feat.shape[3]
    slots = neighbours.shape[3]
    bonds = atoms * slots
    pairs = bonds // 2
    half = CAP // 2
    extents = (lax.axis_size("gx"), lax.axis_size("gy"))
    paired = (extents[0] % 2 == 0, False)
    targets = neighbours[0, 0].T
    hbm = pl.BlockSpec(memory_space=pltpu.HBM)
    vmem = pl.BlockSpec(memory_space=pltpu.VMEM)
    params = pltpu.CompilerParams(vmem_limit_bytes=32 * 2**20)

    def shaped(shape, dtype):
        return jax.ShapeDtypeStruct(shape, dtype)

    def in_hbm(arrays):
        return tuple(pltpu.with_memory_space_constraint(x, pltpu.HBM) for x in arrays)

    payload = shaped((3 * half + atoms // 2, 2 * feature), BF16)
    inputs = (targets, atom_feat, bond_feat)
    own, one, two, *held = pl.pallas_call(
        functools.partial(pack_kernel, extents, paired),
        out_shape=(payload,) * 3 + tuple(shaped(x.shape, x.dtype) for x in inputs),
        in_specs=[hbm] * 3,
        out_specs=(vmem,) * 6,
        scratch_shapes=[pltpu.SemaphoreType.DMA((3,))],
        compiler_params=params,
        name="pack",
    )(*in_hbm(inputs))
    first, second = moves(extents[0], paired[0])
    one = lax.ppermute(one, "gx", first)
    two = lax.ppermute(two, "gx", second)
    weights = (bond_in_weight, bond_mix_weight, pair_weight, pair_hidden_weight)
    weights += (pair_out_weight, atom_in_weight, atom_out_weight)
    *prepared, bond_dirs, angle_weight = pl.pallas_call(
        functools.partial(prepare_kernel, extents, paired),
        out_shape=(
            shaped((bonds, 9 * half + 9 * atoms // 2), BF16),
            shaped((bonds, 2 * feature), F32),
            shaped((bonds, 2 * feature), BF16),
            shaped((4 * feature, 4 * feature), BF16),
            shaped((2 * feature, 2 * feature), BF16),
            shaped((2 * feature, 8 * feature), BF16),
            shaped((2 * feature, 4 * feature), BF16),
            shaped((2 * feature, 2 * feature), BF16),
            shaped((3 * feature, 4 * feature), BF16),
            shaped((4 * feature, 4 * feature), BF16),
            shaped((2 * feature, 2 * feature), BF16),
            shaped(bond_dirs.shape, F32),
            shaped(angle_weight.shape, BF16),
        ),
        in_specs=[vmem] * 3 + [hbm] * 9,
        out_specs=(vmem,) * 13,
        scratch_shapes=[pltpu.VMEM(x.shape, BF16) for x in weights]
        + [pltpu.SemaphoreType.DMA((9,))],
        compiler_params=params,
        cost_estimate=pl.CostEstimate(flops=64 * 2**20, bytes_accessed=2**21, transcendentals=0),
        name="prepare",
    )(*held, *in_hbm(weights + (bond_dirs, angle_weight)))
    own, one, two, prepared = lax.optimization_barrier((own, one, two, prepared))
    first, second = moves(extents[1], paired[1])

    def forwarded(block):
        parts = [x[block * half : (block + 1) * half] for x in (own, one, two)]
        return jnp.concatenate(parts + [x[3 * half :] for x in (own, one, two)], axis=0)

    three = lax.ppermute(forwarded(1), "gy", first)
    four = lax.ppermute(forwarded(2), "gy", second)
    angular = pl.pallas_call(
        functools.partial(angular_kernel, atoms),
        out_shape=shaped((slots, pairs, 4 * feature), F32),
        in_specs=[vmem, vmem],
        out_specs=vmem,
        compiler_params=params,
        cost_estimate=pl.CostEstimate(
            flops=256 * 2**20, bytes_accessed=2**22, transcendentals=4096
        ),
        name="angular",
    )(bond_dirs, angle_weight)
    return pl.pallas_call(
        main_kernel,
        out_shape=(shaped(atom_feat.shape, BF16), shaped(bond_feat.shape, BF16)),
        in_specs=[vmem] * 17,
        out_specs=(hbm, hbm),
        scratch_shapes=[
            pltpu.VMEM(atom_feat.shape, BF16),
            pltpu.VMEM(bond_feat.shape, BF16),
            pltpu.VMEM((pairs, 4 * feature), F32),
            pltpu.VMEM((2, pairs, 4 * feature), F32),
            pltpu.VMEM((slots * pairs, 2 * feature), BF16),
            pltpu.SemaphoreType.DMA((2,)),
        ],
        compiler_params=params,
        name="main",
    )(own, one, two, four, three, angular, *prepared)


def solution(mesh):
    placed = (
        P("gx", "gy", None, None),
        P("gx", "gy", None, None),
        P("gx", "gy", None, None),
        P(None, "gx", "gy", None),
        P(),
        P(),
        P(),
        P(),
        P(),
        P(),
        P(),
        P(),
    )
    return jax.shard_map(
        per_device,
        mesh=mesh,
        in_specs=placed,
        out_specs=(P("gx", "gy", None, None), P("gx", "gy", None, None)),
        check_vma=False,
    )
```

```python
import functools

import jax
import jax.numpy as jnp
from jax import lax
from jax.experimental import pallas as pl
from jax.experimental.pallas import tpu as pltpu
from jax.sharding import PartitionSpec as P

F32 = jnp.float32
BF16 = jnp.bfloat16
CAP = 64


def quotient(values, size):
    if size & (size - 1) == 0:
        return values >> (size.bit_length() - 1)
    return lax.div(values, jnp.int32(size))


def remainder(values, size):
    if size & (size - 1) == 0:
        return values & (size - 1)
    return lax.rem(values, jnp.int32(size))


def step_code(owner, home, extent, paired, receives):
    step = remainder(owner - home + 1 + extent, extent)
    if paired:
        ahead = jnp.where(remainder(home, 2) == 0, 0, 2)
    else:
        ahead = 0 if receives else 2
    return jnp.where(step == 1, 0, jnp.where(step == ahead, 1, 2))


def moves(extent, paired):
    if paired:
        near = [(i, i ^ 1) for i in range(extent)]
        return [(i, (((i + 1) ^ 1) - 1) % extent) for i in range(extent)], near
    up = [(i, (i + 1) % extent) for i in range(extent)]
    return up, [(j, i) for i, j in up]


def slot_at(position, slots):
    half = slots // 2
    return jnp.where(position < half, 2 * position, 2 * (position - half) + 1)


def bond_row(table):
    slots, atoms = table.shape
    per_group = 128 // atoms
    tiled = jnp.concatenate([table.astype(F32)] * per_group, axis=1)
    row = lax.broadcasted_iota(jnp.int32, tiled.shape, 0)
    position = quotient(lax.broadcasted_iota(jnp.int32, tiled.shape, 1), atoms)
    pieces = []
    for group in range(slots // per_group):
        chosen = row == slot_at(position + group * per_group, slots)
        pieces.append(jnp.sum(jnp.where(chosen, tiled, 0.0), axis=0, keepdims=True))
    return jnp.concatenate(pieces, axis=1).astype(jnp.int32)


def bond_codes(targets, atoms, extents, paired, receives):
    owner = quotient(targets, atoms)
    block = (quotient(owner, extents[1]), remainder(owner, extents[1]))
    return tuple(
        step_code(block[k], lax.axis_index(axis), extents[k], paired[k], receives)
        for k, axis in enumerate(("gx", "gy"))
    )


def left_lanes(shape):
    return lax.broadcasted_iota(jnp.int32, shape, 1) < shape[1] // 2


def swapped(rows):
    half = rows.shape[1] // 2
    return jnp.concatenate([rows[:, half:], rows[:, :half]], axis=1)


def blocks_of(bond_ref, pairs):
    width = bond_ref.shape[3] // pairs
    return [bond_ref[0, 0, :, k * width : (k + 1) * width] for k in range(pairs)]


def pack_kernel(
    extents,
    paired,
    targets_hbm,
    atom_hbm,
    bond_hbm,
    up_ref,
    down_ref,
    spot_ref,
    targets_ref,
    atom_ref,
    bond_ref,
    sems,
):
    sources = ((targets_hbm, targets_ref), (bond_hbm, bond_ref), (atom_hbm, atom_ref))
    copies = [
        pltpu.make_async_copy(source, target, sems.at[k])
        for k, (source, target) in enumerate(sources)
    ]
    for copy in copies:
        copy.start()
    atoms, feature = atom_ref.shape[2], atom_ref.shape[3]
    slots = targets_ref.shape[0]
    bonds = slots * atoms
    lanes = 128
    groups = bonds // lanes
    copies[0].wait()
    code_x, code_y = bond_codes(bond_row(targets_ref[...]), atoms, extents, paired, False)
    code = 3 * code_y + code_x
    rows = lax.broadcasted_iota(jnp.int32, (16, lanes), 0)
    marks = [rows == code[:, g * lanes : (g + 1) * lanes] for g in range(groups)]
    stacked = jnp.concatenate([m.astype(F32) for m in marks], axis=0).astype(BF16)
    before = lax.broadcasted_iota(jnp.int32, (lanes, 2 * lanes), 0)
    after = lax.broadcasted_iota(jnp.int32, (lanes, 2 * lanes), 1)
    sums = jnp.where((before < after) | (after >= lanes), 1.0, 0.0).astype(BF16)
    counted = jnp.dot(stacked, sums, preferred_element_type=F32)
    place = []
    earlier = jnp.zeros((16, lanes), F32)
    for g in range(groups):
        part = counted[g * 16 : (g + 1) * 16]
        place.append(
            jnp.sum(jnp.where(marks[g], part[:, :lanes] + earlier, 0.0), axis=0, keepdims=True)
        )
        earlier = earlier + part[:, lanes:]
    place = jnp.concatenate(place, axis=1).astype(jnp.int32)
    half = CAP // 2
    right = quotient(place, half)
    spot = place - half * right + half * code
    spot_ref[...] = jnp.where(code < 3, spot + 3 * half * right, -1)
    wanted = jnp.where(code < 3, -1, spot - 3 * half + 6 * half * right)
    copies[1].wait()
    copies[2].wait()
    packed = packed_rows(wanted, bond_ref, slots, 6 * half)
    for k, ref in enumerate((up_ref, down_ref)):
        ref[: 3 * half] = packed[3 * half * k : 3 * half * (k + 1)]
        ref[3 * half :] = atom_rows(atom_ref)


def packed_rows(wanted, bond_ref, slots, count):
    spot = lax.broadcasted_iota(jnp.int32, (2 * count, wanted.shape[1]), 0)
    chosen = jnp.where(spot == wanted, 1.0, 0.0).astype(BF16)
    blocks = blocks_of(bond_ref, slots // 2)
    feature = blocks[0].shape[1] // 2
    values = [x[:, :feature] for x in blocks] + [x[:, feature:] for x in blocks]
    packed = jnp.dot(chosen, jnp.concatenate(values, axis=0), preferred_element_type=F32)
    return jnp.concatenate([packed[:count], packed[count:]], axis=1).astype(BF16)


def atom_rows(atom_ref):
    atom = atom_ref[0, 0]
    half = atom.shape[0] // 2
    return jnp.concatenate([atom[:half], atom[half:]], axis=1)


def crossed(left, right):
    half = left.shape[1] // 2
    parts = [left[:, :half], right[:, :half], left[:, half:], right[:, half:]]
    return jnp.concatenate(parts, axis=1)


def two_blocks(weight):
    blank = jnp.zeros_like(weight)
    return jnp.concatenate([crossed(weight, blank), crossed(blank, weight)], axis=0)


def diagonal_blocks(weight):
    blank = jnp.zeros_like(weight)
    return jnp.concatenate(
        [jnp.concatenate([weight, blank], axis=1), jnp.concatenate([blank, weight], axis=1)],
        axis=0,
    )


def angular_kernel(atoms, dirs_ref, angle_ref, angular_ref):
    slots, pairs, _ = angular_ref.shape
    bonds = 2 * pairs
    degrees = angle_ref.shape[0]
    weight = (two_blocks(angle_ref[...].astype(F32)) * 0.5).astype(BF16)
    polar, azimuth = dirs_ref[0, 0], dirs_ref[1, 0]
    unit = jnp.concatenate(
        [
            jnp.sin(polar) * jnp.cos(azimuth),
            jnp.sin(polar) * jnp.sin(azimuth),
            jnp.cos(polar),
            jnp.zeros((5, bonds), F32),
        ],
        axis=0,
    )
    high = unit.astype(BF16).astype(F32)
    middle = (unit - high).astype(BF16).astype(F32)
    parts = jnp.concatenate([high, middle, unit - high - middle], axis=0).astype(BF16)
    bond = lax.broadcasted_iota(jnp.int32, (1, bonds), 1)
    source = remainder(bond, atoms) * slots + slot_at(quotient(bond, atoms), slots)
    spot = lax.broadcasted_iota(jnp.int32, (bonds, bonds), 0)
    chosen = jnp.where(spot == source, 1.0, 0.0).astype(BF16)
    unit = jnp.dot(parts, chosen, preferred_element_type=F32)
    unit = unit[0:8] + unit[8:16] + unit[16:24]
    even = [jnp.broadcast_to(unit[k : k + 1, :pairs], (8, pairs)) for k in range(3)]
    odd = [jnp.broadcast_to(unit[k : k + 1, pairs:], (8, pairs)) for k in range(3)]
    row = lax.broadcasted_iota(jnp.int32, (8, pairs), 0)

    def turned(vector, places):
        places = places % (pairs // atoms)
        if places == 0:
            return vector
        return [pltpu.roll(part, pairs - atoms * places, 1) for part in vector]

    def basis(first, second):
        cosine = first[0] * second[0] + first[1] * second[1] + first[2] * second[2]
        series = [jnp.ones_like(cosine), cosine]
        double = cosine + cosine
        for _ in range(7):
            series.append(double * series[-1] - series[-2])
        lower = series[7]
        upper = series[1]
        for index in range(1, 8):
            lower = jnp.where(row == index, series[7 - index], lower)
            upper = jnp.where(row == index, series[1 + index], upper)
        double = series[8] + series[8]
        blocks = [lower, upper]
        for _ in range(degrees // 8 - 1):
            blocks.append(double * blocks[-1] - blocks[-2])
        return blocks[1:]

    for diagonal in range(slots):
        places = diagonal // 2
        if diagonal % 2 == 0:
            blocks = basis(even, turned(even, places)) + basis(odd, turned(odd, places))
        else:
            blocks = basis(even, turned(odd, places)) + basis(odd, turned(even, places + 1))
        series = jnp.concatenate(blocks, axis=0).T.astype(BF16)
        angular_ref[diagonal] = jnp.dot(series, weight, preferred_element_type=F32)


def prepare_kernel(
    extents,
    paired,
    spot_ref,
    targets_ref,
    atom_ref,
    bond_ref,
    *refs,
):
    sources, results, held, sems = refs[:9], refs[9:23], refs[23:30], refs[30]
    near_ref, chosen_ref, right_ref, own_ref = results[:4]
    bond_weight_ref, mix_weight_ref, pair_weight_ref, hidden_weight_ref = results[4:8]
    out_weight_ref, atom_in_weight_ref, sum_weight_ref, atom_out_weight_ref = results[8:12]
    bond_in_ref, bond_mix_ref, pair_ref, pair_hidden_ref, pair_out_ref = held[:5]
    atom_in_ref, atom_out_ref = held[5:]
    copies = [
        pltpu.make_async_copy(source, target, sems.at[k])
        for k, (source, target) in enumerate(zip(sources, held + results[12:]))
    ]
    for copy in copies:
        copy.start()
    atoms, feature = atom_ref.shape[2], atom_ref.shape[3]
    slots = targets_ref.shape[0]
    bonds = slots * atoms
    near_ref[: 3 * CAP // 2] = packed_rows(spot_ref[...], bond_ref, slots, 3 * CAP // 2)
    near_ref[3 * CAP // 2 :] = atom_rows(atom_ref)
    targets = bond_row(targets_ref[...])
    code_x, code_y = bond_codes(targets, atoms, extents, paired, True)
    code = 3 * code_x + code_y
    bond = lax.broadcasted_iota(jnp.int32, (1, bonds), 1)
    far_slot = slots - 1 - slot_at(quotient(bond, atoms), slots)
    far_atom = remainder(targets, atoms)
    far = (remainder(far_slot, 2) * (slots // 2) + quotient(far_slot, 2)) * atoms + far_atom
    base = (code * bonds).astype(F32)
    key = base + far.astype(F32)

    def column(values):
        return jnp.broadcast_to(values.astype(F32), (128, bonds)).T

    keys = column(key)
    place = []
    for group in range(bonds // 128):
        here = slice(group * 128, (group + 1) * 128)
        inside = (keys < key[:, here]) & (keys >= base[:, here])
        place.append(jnp.sum(jnp.where(inside, 1.0, 0.0), axis=0, keepdims=True))
    place = jnp.concatenate(place, axis=1).astype(jnp.int32)
    half, tall = CAP // 2, atoms // 2
    bond_spot = column(half * code + remainder(place, half))
    atom_spot = column(9 * half + tall * code + remainder(far_atom, tall))
    right = (column(quotient(place, half)), column(quotient(far_atom, tall)))
    right_ref[...] = jnp.where(left_lanes((bonds, 128)), right[0], right[1])
    total = 9 * half + 9 * tall
    for start in range(0, total, 128):
        width = min(128, total - start)
        spot = lax.broadcasted_iota(jnp.int32, (bonds, 128), 1).astype(F32) + float(start)
        chosen = jnp.where((spot == bond_spot) | (spot == atom_spot), 1.0, 0.0).astype(BF16)
        chosen_ref[:, start : start + width] = chosen[:, :width]

    atom = atom_ref[0, 0]
    blocks = blocks_of(bond_ref, slots // 2)
    own = [jnp.concatenate([atom, x[:, :feature]], axis=1) for x in blocks]
    own += [jnp.concatenate([atom, x[:, feature:]], axis=1) for x in blocks]
    own = jnp.concatenate(own, axis=0)
    own_ref[...] = own

    for copy in copies:
        copy.wait()
    weight = bond_in_ref[...].astype(F32)
    source, other, bond_part = (weight[k * feature : (k + 1) * feature] for k in range(3))
    blank = jnp.zeros_like(source)
    away = [crossed(bond_part, blank), crossed(source, other)]
    near = [crossed(other, source), crossed(blank, bond_part)]
    bond_weight_ref[...] = (jnp.concatenate(away + near, axis=0) * 0.5).astype(BF16)
    mix_weight_ref[...] = (diagonal_blocks(bond_mix_ref[...].astype(F32)) * 0.5).astype(BF16)
    weight = pair_ref[...].astype(F32) * 0.5
    pair_weight_ref[...] = jnp.concatenate(
        [two_blocks(weight[:, : 2 * feature]), two_blocks(weight[:, 2 * feature :])], axis=1
    ).astype(BF16)
    hidden_weight_ref[...] = (two_blocks(pair_hidden_ref[...].astype(F32)) * 0.25).astype(BF16)
    out_weight_ref[...] = (diagonal_blocks(pair_out_ref[...].astype(F32)) * 0.5).astype(BF16)
    weight = atom_in_ref[...].astype(F32) * 0.5
    weight = crossed(weight, jnp.zeros_like(weight))
    mean = weight[feature:] * (1.0 / slots)
    atom_in_weight_ref[...] = jnp.concatenate([weight[:feature], mean, mean], axis=0).astype(BF16)
    folded = jnp.dot(
        pair_out_ref[...], (mean * 0.5).astype(BF16), preferred_element_type=F32
    )
    high = folded.astype(BF16)
    low = (folded - high.astype(F32)).astype(BF16)
    sum_weight_ref[...] = jnp.concatenate([high, high, low, low], axis=0)
    weight = atom_out_ref[...].astype(F32) * 0.5
    blank = jnp.zeros_like(weight)
    weight = jnp.concatenate([weight, blank], axis=1)
    atom_out_weight_ref[...] = jnp.concatenate([weight, jnp.zeros_like(weight)], axis=0).astype(
        BF16
    )


def doubled_gate(values):
    half = values.shape[1] // 2
    first, second = values[:, :half], values[:, half:]
    return first * (1.0 + jnp.tanh(first)) * (1.0 + jnp.tanh(second))


def main_kernel(
    near_ref,
    up_ref,
    down_ref,
    two_ref,
    one_ref,
    angular_ref,
    chosen_ref,
    right_ref,
    own_ref,
    bond_weight_ref,
    mix_weight_ref,
    pair_weight_ref,
    hidden_weight_ref,
    out_weight_ref,
    atom_in_weight_ref,
    sum_weight_ref,
    atom_out_weight_ref,
    atom_result_hbm,
    bond_result_hbm,
    atom_result_ref,
    bond_result_ref,
    first_ref,
    second_ref,
    pair_ref,
    sems,
):
    slots, pairs, _ = angular_ref.shape
    bonds = 2 * pairs
    atoms = bonds // slots
    feature = own_ref.shape[1] // 2
    width = 2 * feature
    half = CAP // 2
    near_refs = (near_ref, up_ref, down_ref)
    away_refs = (one_ref, two_ref)
    sent = [ref[:half] for ref in near_refs] + [ref[: 3 * half] for ref in away_refs]
    sent = jnp.concatenate(sent, axis=0)
    sent_atom = jnp.concatenate([ref[3 * half :] for ref in near_refs + away_refs], axis=0)
    blank = jnp.zeros((sent.shape[0], feature), BF16)
    blank_atom = jnp.zeros((sent_atom.shape[0], feature), BF16)
    received = jnp.concatenate(
        [
            jnp.concatenate([sent[:, :feature], blank, sent[:, feature:], blank], axis=1),
            jnp.concatenate(
                [blank_atom, sent_atom[:, :feature], blank_atom, sent_atom[:, feature:]], axis=1
            ),
        ],
        axis=0,
    )
    far = jnp.dot(chosen_ref[...], received, preferred_element_type=F32)
    far = jnp.where(right_ref[...] > 0.0, far[:, width:], far[:, :width])
    own = own_ref[...]
    incoming = jnp.dot(
        jnp.concatenate([far.astype(BF16), own], axis=1),
        bond_weight_ref[...],
        preferred_element_type=F32,
    )
    hidden = doubled_gate(incoming).astype(BF16)
    mixed = jnp.dot(hidden, mix_weight_ref[...], preferred_element_type=F32)
    old = jnp.where(left_lanes((bonds, width)), far, own.astype(F32))
    new = (old + mixed).astype(BF16).astype(F32)
    average = ((new + pltpu.roll(new, feature, 1)) * 0.5).astype(BF16).astype(F32)
    even, odd = average[:pairs], average[pairs:]
    left = left_lanes((pairs, width))
    packed = jnp.where(left, even, odd)
    shifted = jnp.where(left, odd, jnp.concatenate([even[atoms:], even[:atoms]], axis=0))
    projected = jnp.dot(packed.astype(BF16), pair_weight_ref[...], preferred_element_type=F32)
    first_ref[...] = projected[:, : 2 * width]
    second_ref[0] = projected[:, 2 * width :]
    second_ref[1] = jnp.dot(
        shifted.astype(BF16), pair_weight_ref[:, 2 * width :], preferred_element_type=F32
    )
    group = 2

    def first_gates(base):
        for start in range(0, pairs, atoms):
            here = first_ref[pl.ds(start, atoms)]
            for diagonal in range(base, base + group):
                there = (start + diagonal // 2 * atoms) % pairs
                mixture = angular_ref[diagonal, pl.ds(start, atoms)] + (
                    here + second_ref[diagonal % 2, pl.ds(there, atoms)]
                )
                pair_ref[pl.ds(diagonal * pairs + start, atoms)] = doubled_gate(mixture).astype(
                    BF16
                )

    def summed(rows):
        parts = [rows[k * atoms : (k + 1) * atoms] for k in range(slots // 2)]
        while len(parts) > 1:
            parts = [x + y for x, y in zip(parts[::2], parts[1::2])]
        return parts[0]

    atom = own[0:atoms]
    atom_incoming = jnp.dot(
        jnp.concatenate([atom[:, :feature], summed(packed).astype(BF16)], axis=1),
        atom_in_weight_ref[...],
        preferred_element_type=F32,
    )
    total = jnp.zeros((pairs, width), F32)
    first_gates(0)
    for base in range(0, slots, group):
        if base + group < slots:
            first_gates(base + group)
        second = jnp.dot(
            pair_ref[pl.ds(base * pairs, group * pairs)],
            hidden_weight_ref[...],
            preferred_element_type=F32,
        )
        gates = doubled_gate(second)
        for k in range(group):
            total = total + gates[k * pairs : (k + 1) * pairs]
    bond_out = packed + jnp.dot(
        total.astype(BF16), out_weight_ref[...], preferred_element_type=F32
    )
    bond_out = bond_out.astype(BF16)
    for k in range(slots // 2):
        bond_result_ref[0, 0, :, k * width : (k + 1) * width] = bond_out[
            k * atoms : (k + 1) * atoms
        ]
    copies = [pltpu.make_async_copy(bond_result_ref, bond_result_hbm, sems.at[0])]
    copies[0].start()
    sums = summed(total).astype(BF16)
    atom_incoming = atom_incoming + jnp.dot(
        jnp.concatenate([sums, sums], axis=1), sum_weight_ref[...], preferred_element_type=F32
    )
    atom_hidden = doubled_gate(atom_incoming).astype(BF16)
    atom_new = atom.astype(F32) + jnp.dot(
        atom_hidden, atom_out_weight_ref[...], preferred_element_type=F32
    )
    atom_result_ref[0, 0] = atom_new[:, :feature].astype(BF16)
    copies.append(pltpu.make_async_copy(atom_result_ref, atom_result_hbm, sems.at[1]))
    copies[-1].start()
    for copy in copies:
        copy.wait()


def per_device(
    atom_feat,
    bond_feat,
    neighbours,
    bond_dirs,
    bond_in_weight,
    bond_mix_weight,
    pair_weight,
    angle_weight,
    pair_hidden_weight,
    pair_out_weight,
    atom_in_weight,
    atom_out_weight,
):
    atoms, feature = atom_feat.shape[2], atom_feat.shape[3]
    slots = neighbours.shape[3]
    bonds = atoms * slots
    pairs = bonds // 2
    half = CAP // 2
    extents = (lax.axis_size("gx"), lax.axis_size("gy"))
    paired = (extents[0] % 2 == 0, False)
    targets = neighbours[0, 0].T
    hbm = pl.BlockSpec(memory_space=pltpu.HBM)
    vmem = pl.BlockSpec(memory_space=pltpu.VMEM)
    params = pltpu.CompilerParams(vmem_limit_bytes=32 * 2**20)

    def shaped(shape, dtype):
        return jax.ShapeDtypeStruct(shape, dtype)

    def in_hbm(arrays):
        return tuple(pltpu.with_memory_space_constraint(x, pltpu.HBM) for x in arrays)

    payload = shaped((3 * half + atoms // 2, 2 * feature), BF16)
    inputs = (targets, atom_feat, bond_feat)
    up, down, *held = pl.pallas_call(
        functools.partial(pack_kernel, extents, paired),
        out_shape=(payload, payload, shaped((1, bonds), jnp.int32))
        + tuple(shaped(x.shape, x.dtype) for x in inputs),
        in_specs=[hbm] * 3,
        out_specs=(vmem,) * 6,
        scratch_shapes=[pltpu.SemaphoreType.DMA((3,))],
        compiler_params=params,
        name="pack",
    )(*in_hbm(inputs))
    first, second = moves(extents[1], paired[1])
    up = lax.ppermute(up, "gy", first)
    down = lax.ppermute(down, "gy", second)
    weights = (bond_in_weight, bond_mix_weight, pair_weight, pair_hidden_weight)
    weights += (pair_out_weight, atom_in_weight, atom_out_weight)
    near, *prepared, bond_dirs, angle_weight = pl.pallas_call(
        functools.partial(prepare_kernel, extents, paired),
        out_shape=(
            payload,
            shaped((bonds, 9 * half + 9 * atoms // 2), BF16),
            shaped((bonds, 2 * feature), F32),
            shaped((bonds, 2 * feature), BF16),
            shaped((4 * feature, 4 * feature), BF16),
            shaped((2 * feature, 2 * feature), BF16),
            shaped((2 * feature, 8 * feature), BF16),
            shaped((2 * feature, 4 * feature), BF16),
            shaped((2 * feature, 2 * feature), BF16),
            shaped((3 * feature, 4 * feature), BF16),
            shaped((4 * feature, 4 * feature), BF16),
            shaped((2 * feature, 2 * feature), BF16),
            shaped(bond_dirs.shape, F32),
            shaped(angle_weight.shape, BF16),
        ),
        in_specs=[vmem] * 4 + [hbm] * 9,
        out_specs=(vmem,) * 14,
        scratch_shapes=[pltpu.VMEM(x.shape, BF16) for x in weights]
        + [pltpu.SemaphoreType.DMA((9,))],
        compiler_params=params,
        cost_estimate=pl.CostEstimate(flops=64 * 2**20, bytes_accessed=2**21, transcendentals=0),
        name="prepare",
    )(*held, *in_hbm(weights + (bond_dirs, angle_weight)))
    near, up, down, prepared = lax.optimization_barrier((near, up, down, prepared))
    first, second = moves(extents[0], paired[0])

    def forwarded(block):
        parts = [x[block * half : (block + 1) * half] for x in (near, up, down)]
        return jnp.concatenate(parts + [x[3 * half :] for x in (near, up, down)], axis=0)

    one = lax.ppermute(forwarded(1), "gx", first)
    two = lax.ppermute(forwarded(2), "gx", second)
    angular = pl.pallas_call(
        functools.partial(angular_kernel, atoms),
        out_shape=shaped((slots, pairs, 4 * feature), F32),
        in_specs=[vmem, vmem],
        out_specs=vmem,
        compiler_params=params,
        cost_estimate=pl.CostEstimate(
            flops=256 * 2**20, bytes_accessed=2**22, transcendentals=4096
        ),
        name="angular",
    )(bond_dirs, angle_weight)
    return pl.pallas_call(
        main_kernel,
        out_shape=(shaped(atom_feat.shape, BF16), shaped(bond_feat.shape, BF16)),
        in_specs=[vmem] * 17,
        out_specs=(hbm, hbm),
        scratch_shapes=[
            pltpu.VMEM(atom_feat.shape, BF16),
            pltpu.VMEM(bond_feat.shape, BF16),
            pltpu.VMEM((pairs, 4 * feature), F32),
            pltpu.VMEM((2, pairs, 4 * feature), F32),
            pltpu.VMEM((slots * pairs, 2 * feature), BF16),
            pltpu.SemaphoreType.DMA((2,)),
        ],
        compiler_params=params,
        name="main",
    )(near, up, down, two, one, angular, *prepared)


def solution(mesh):
    placed = (
        P("gx", "gy", None, None),
        P("gx", "gy", None, None),
        P("gx", "gy", None, None),
        P(None, "gx", "gy", None),
        P(),
        P(),
        P(),
        P(),
        P(),
        P(),
        P(),
        P(),
    )
    return jax.shard_map(
        per_device,
        mesh=mesh,
        in_specs=placed,
        out_specs=(P("gx", "gy", None, None), P("gx", "gy", None, None)),
        check_vma=False,
    )
```

```python
import functools

import jax
import jax.numpy as jnp
from jax import lax
from jax.experimental import pallas as pl
from jax.experimental.pallas import tpu as pltpu
from jax.sharding import PartitionSpec as P

F32 = jnp.float32
BF16 = jnp.bfloat16
CAP = 64


def quotient(values, size):
    if size & (size - 1) == 0:
        return values >> (size.bit_length() - 1)
    return lax.div(values, jnp.int32(size))


def remainder(values, size):
    if size & (size - 1) == 0:
        return values & (size - 1)
    return lax.rem(values, jnp.int32(size))


def step_code(owner, home, extent, paired, receives):
    step = remainder(owner - home + 1 + extent, extent)
    if paired:
        ahead = jnp.where(remainder(home, 2) == 0, 0, 2)
    else:
        ahead = 0 if receives else 2
    return jnp.where(step == 1, 0, jnp.where(step == ahead, 1, 2))


def moves(extent, paired):
    if paired:
        near = [(i, i ^ 1) for i in range(extent)]
        return [(i, (((i + 1) ^ 1) - 1) % extent) for i in range(extent)], near
    up = [(i, (i + 1) % extent) for i in range(extent)]
    return up, [(j, i) for i, j in up]


def slot_at(position, slots):
    half = slots // 2
    return jnp.where(position < half, 2 * position, 2 * (position - half) + 1)


def bond_row(table):
    slots, atoms = table.shape
    per_group = 128 // atoms
    tiled = jnp.concatenate([table.astype(F32)] * per_group, axis=1)
    row = lax.broadcasted_iota(jnp.int32, tiled.shape, 0)
    position = quotient(lax.broadcasted_iota(jnp.int32, tiled.shape, 1), atoms)
    pieces = []
    for group in range(slots // per_group):
        chosen = row == slot_at(position + group * per_group, slots)
        pieces.append(jnp.sum(jnp.where(chosen, tiled, 0.0), axis=0, keepdims=True))
    return jnp.concatenate(pieces, axis=1).astype(jnp.int32)


def bond_codes(targets, atoms, extents, paired, receives):
    owner = quotient(targets, atoms)
    block = (quotient(owner, extents[1]), remainder(owner, extents[1]))
    return tuple(
        step_code(block[k], lax.axis_index(axis), extents[k], paired[k], receives)
        for k, axis in enumerate(("gx", "gy"))
    )


def left_lanes(shape):
    return lax.broadcasted_iota(jnp.int32, shape, 1) < shape[1] // 2


def swapped(rows):
    half = rows.shape[1] // 2
    return jnp.concatenate([rows[:, half:], rows[:, :half]], axis=1)


def blocks_of(bond_ref, pairs):
    width = bond_ref.shape[3] // pairs
    return [bond_ref[0, 0, :, k * width : (k + 1) * width] for k in range(pairs)]


def pack_kernel(
    extents,
    paired,
    targets_hbm,
    atom_hbm,
    bond_hbm,
    up_ref,
    down_ref,
    spot_ref,
    targets_ref,
    atom_ref,
    bond_ref,
    sems,
):
    sources = ((targets_hbm, targets_ref), (bond_hbm, bond_ref), (atom_hbm, atom_ref))
    copies = [
        pltpu.make_async_copy(source, target, sems.at[k])
        for k, (source, target) in enumerate(sources)
    ]
    for copy in copies:
        copy.start()
    atoms, feature = atom_ref.shape[2], atom_ref.shape[3]
    slots = targets_ref.shape[0]
    bonds = slots * atoms
    lanes = 128
    groups = bonds // lanes
    copies[0].wait()
    code_x, code_y = bond_codes(bond_row(targets_ref[...]), atoms, extents, paired, False)
    code = 3 * code_y + code_x
    rows = lax.broadcasted_iota(jnp.int32, (16, lanes), 0)
    marks = [rows == code[:, g * lanes : (g + 1) * lanes] for g in range(groups)]
    stacked = jnp.concatenate([m.astype(F32) for m in marks], axis=0).astype(BF16)
    before = lax.broadcasted_iota(jnp.int32, (lanes, 2 * lanes), 0)
    after = lax.broadcasted_iota(jnp.int32, (lanes, 2 * lanes), 1)
    sums = jnp.where((before < after) | (after >= lanes), 1.0, 0.0).astype(BF16)
    counted = jnp.dot(stacked, sums, preferred_element_type=F32)
    place = []
    earlier = jnp.zeros((16, lanes), F32)
    for g in range(groups):
        part = counted[g * 16 : (g + 1) * 16]
        place.append(
            jnp.sum(jnp.where(marks[g], part[:, :lanes] + earlier, 0.0), axis=0, keepdims=True)
        )
        earlier = earlier + part[:, lanes:]
    place = jnp.concatenate(place, axis=1).astype(jnp.int32)
    half = CAP // 2
    right = quotient(place, half)
    spot = place - half * right + half * code
    spot_ref[...] = jnp.where(code < 3, spot + 3 * half * right, -1)
    wanted = jnp.where(code < 3, -1, spot - 3 * half + 6 * half * right)
    copies[1].wait()
    copies[2].wait()
    packed = packed_rows(wanted, bond_ref, slots, 6 * half)
    for k, ref in enumerate((up_ref, down_ref)):
        ref[: 3 * half] = packed[3 * half * k : 3 * half * (k + 1)]
        ref[3 * half :] = atom_rows(atom_ref)


def packed_rows(wanted, bond_ref, slots, count):
    spot = lax.broadcasted_iota(jnp.int32, (2 * count, wanted.shape[1]), 0)
    chosen = jnp.where(spot == wanted, 1.0, 0.0).astype(BF16)
    blocks = blocks_of(bond_ref, slots // 2)
    feature = blocks[0].shape[1] // 2
    values = [x[:, :feature] for x in blocks] + [x[:, feature:] for x in blocks]
    packed = jnp.dot(chosen, jnp.concatenate(values, axis=0), preferred_element_type=F32)
    return jnp.concatenate([packed[:count], packed[count:]], axis=1).astype(BF16)


def atom_rows(atom_ref):
    atom = atom_ref[0, 0]
    half = atom.shape[0] // 2
    return jnp.concatenate([atom[:half], atom[half:]], axis=1)


def crossed(left, right):
    half = left.shape[1] // 2
    parts = [left[:, :half], right[:, :half], left[:, half:], right[:, half:]]
    return jnp.concatenate(parts, axis=1)


def two_blocks(weight):
    blank = jnp.zeros_like(weight)
    return jnp.concatenate([crossed(weight, blank), crossed(blank, weight)], axis=0)


def diagonal_blocks(weight):
    blank = jnp.zeros_like(weight)
    return jnp.concatenate(
        [jnp.concatenate([weight, blank], axis=1), jnp.concatenate([blank, weight], axis=1)],
        axis=0,
    )


def angular_kernel(atoms, dirs_ref, angle_ref, *refs):
    sources, angular_ref, results, held, sems = refs[:7], refs[7], refs[8:16], refs[16:23], refs[23]
    copies = [
        pltpu.make_async_copy(source, target, sems.at[k])
        for k, (source, target) in enumerate(zip(sources, held))
    ]
    for copy in copies:
        copy.start()
    slots, pairs, _ = angular_ref.shape
    bonds = 2 * pairs
    degrees = angle_ref.shape[0]
    weight = (two_blocks(angle_ref[...].astype(F32)) * 0.5).astype(BF16)
    polar, azimuth = dirs_ref[0, 0], dirs_ref[1, 0]
    unit = jnp.concatenate(
        [
            jnp.sin(polar) * jnp.cos(azimuth),
            jnp.sin(polar) * jnp.sin(azimuth),
            jnp.cos(polar),
            jnp.zeros((5, bonds), F32),
        ],
        axis=0,
    )
    high = unit.astype(BF16).astype(F32)
    middle = (unit - high).astype(BF16).astype(F32)
    parts = jnp.concatenate([high, middle, unit - high - middle], axis=0).astype(BF16)
    bond = lax.broadcasted_iota(jnp.int32, (1, bonds), 1)
    source = remainder(bond, atoms) * slots + slot_at(quotient(bond, atoms), slots)
    spot = lax.broadcasted_iota(jnp.int32, (bonds, bonds), 0)
    chosen = jnp.where(spot == source, 1.0, 0.0).astype(BF16)
    unit = jnp.dot(parts, chosen, preferred_element_type=F32)
    unit = unit[0:8] + unit[8:16] + unit[16:24]
    even = [jnp.broadcast_to(unit[k : k + 1, :pairs], (8, pairs)) for k in range(3)]
    odd = [jnp.broadcast_to(unit[k : k + 1, pairs:], (8, pairs)) for k in range(3)]
    row = lax.broadcasted_iota(jnp.int32, (8, pairs), 0)

    def turned(vector, places):
        places = places % (pairs // atoms)
        if places == 0:
            return vector
        return [pltpu.roll(part, pairs - atoms * places, 1) for part in vector]

    def basis(first, second):
        cosine = first[0] * second[0] + first[1] * second[1] + first[2] * second[2]
        series = [jnp.ones_like(cosine), cosine]
        double = cosine + cosine
        for _ in range(7):
            series.append(double * series[-1] - series[-2])
        lower = series[7]
        upper = series[1]
        for index in range(1, 8):
            lower = jnp.where(row == index, series[7 - index], lower)
            upper = jnp.where(row == index, series[1 + index], upper)
        double = series[8] + series[8]
        blocks = [lower, upper]
        for _ in range(degrees // 8 - 1):
            blocks.append(double * blocks[-1] - blocks[-2])
        return blocks[1:]

    for diagonal in range(slots):
        places = diagonal // 2
        if diagonal % 2 == 0:
            blocks = basis(even, turned(even, places)) + basis(odd, turned(odd, places))
        else:
            blocks = basis(even, turned(odd, places)) + basis(odd, turned(even, places + 1))
        series = jnp.concatenate(blocks, axis=0).T.astype(BF16)
        angular_ref[diagonal] = jnp.dot(series, weight, preferred_element_type=F32)
    for copy in copies:
        copy.wait()
    prepare_weights(slots, held, results)


def prepare_weights(slots, held, results):
    bond_in_ref, bond_mix_ref, pair_ref, pair_hidden_ref, pair_out_ref, atom_in_ref = held[:6]
    atom_out_ref = held[6]
    bond_weight_ref, mix_weight_ref, pair_weight_ref, hidden_weight_ref = results[:4]
    out_weight_ref, atom_in_weight_ref, sum_weight_ref, atom_out_weight_ref = results[4:]
    feature = bond_mix_ref.shape[0]
    weight = bond_in_ref[...].astype(F32)
    source, other, bond_part = (weight[k * feature : (k + 1) * feature] for k in range(3))
    blank = jnp.zeros_like(source)
    away = [crossed(bond_part, blank), crossed(source, other)]
    near = [crossed(other, source), crossed(blank, bond_part)]
    bond_weight_ref[...] = (jnp.concatenate(away + near, axis=0) * 0.5).astype(BF16)
    mix_weight_ref[...] = (diagonal_blocks(bond_mix_ref[...].astype(F32)) * 0.5).astype(BF16)
    old = pair_ref[...].astype(F32) * 0.25
    hidden = jnp.dot(bond_mix_ref[...], pair_ref[...], preferred_element_type=F32) * 0.125
    weight = jnp.concatenate([hidden, hidden, old, old], axis=0).astype(BF16)
    pair_weight_ref[...] = jnp.concatenate(
        [two_blocks(weight[:, : 2 * feature]), two_blocks(weight[:, 2 * feature :])], axis=1
    )
    hidden_weight_ref[...] = (two_blocks(pair_hidden_ref[...].astype(F32)) * 0.25).astype(BF16)
    out_weight_ref[...] = (diagonal_blocks(pair_out_ref[...].astype(F32)) * 0.5).astype(BF16)
    weight = atom_in_ref[...].astype(F32) * 0.5
    weight = crossed(weight, jnp.zeros_like(weight))
    mean = weight[feature:] * (1.0 / slots)
    atom_in_weight_ref[...] = jnp.concatenate([weight[:feature], mean, mean], axis=0).astype(BF16)
    folded = jnp.dot(
        pair_out_ref[...], (mean * 0.5).astype(BF16), preferred_element_type=F32
    )
    high = folded.astype(BF16)
    low = (folded - high.astype(F32)).astype(BF16)
    sum_weight_ref[...] = jnp.concatenate([high, high, low, low], axis=0)
    weight = atom_out_ref[...].astype(F32) * 0.5
    blank = jnp.zeros_like(weight)
    weight = jnp.concatenate([weight, blank], axis=1)
    atom_out_weight_ref[...] = jnp.concatenate([weight, jnp.zeros_like(weight)], axis=0).astype(
        BF16
    )


def prepare_kernel(
    extents,
    paired,
    spot_ref,
    targets_ref,
    atom_ref,
    bond_ref,
    dirs_hbm,
    angle_hbm,
    near_ref,
    chosen_ref,
    right_ref,
    own_ref,
    dirs_ref,
    angle_ref,
    sems,
):
    copies = [
        pltpu.make_async_copy(source, target, sems.at[k])
        for k, (source, target) in enumerate(((dirs_hbm, dirs_ref), (angle_hbm, angle_ref)))
    ]
    for copy in copies:
        copy.start()
    atoms, feature = atom_ref.shape[2], atom_ref.shape[3]
    slots = targets_ref.shape[0]
    bonds = slots * atoms
    near_ref[: 3 * CAP // 2] = packed_rows(spot_ref[...], bond_ref, slots, 3 * CAP // 2)
    near_ref[3 * CAP // 2 :] = atom_rows(atom_ref)
    targets = bond_row(targets_ref[...])
    code_x, code_y = bond_codes(targets, atoms, extents, paired, True)
    code = 3 * code_x + code_y
    bond = lax.broadcasted_iota(jnp.int32, (1, bonds), 1)
    far_slot = slots - 1 - slot_at(quotient(bond, atoms), slots)
    far_atom = remainder(targets, atoms)
    far = (remainder(far_slot, 2) * (slots // 2) + quotient(far_slot, 2)) * atoms + far_atom
    base = (code * bonds).astype(F32)
    key = base + far.astype(F32)

    def column(values):
        return jnp.broadcast_to(values.astype(F32), (128, bonds)).T

    keys = column(key)
    place = []
    for group in range(bonds // 128):
        here = slice(group * 128, (group + 1) * 128)
        inside = (keys < key[:, here]) & (keys >= base[:, here])
        place.append(jnp.sum(jnp.where(inside, 1.0, 0.0), axis=0, keepdims=True))
    place = jnp.concatenate(place, axis=1).astype(jnp.int32)
    half, tall = CAP // 2, atoms // 2
    bond_spot = column(half * code + remainder(place, half))
    atom_spot = column(9 * half + tall * code + remainder(far_atom, tall))
    right = (column(quotient(place, half)), column(quotient(far_atom, tall)))
    right_ref[...] = jnp.where(left_lanes((bonds, 128)), right[0], right[1])
    total = 9 * half + 9 * tall
    for start in range(0, total, 128):
        width = min(128, total - start)
        spot = lax.broadcasted_iota(jnp.int32, (bonds, 128), 1).astype(F32) + float(start)
        chosen = jnp.where((spot == bond_spot) | (spot == atom_spot), 1.0, 0.0).astype(BF16)
        chosen_ref[:, start : start + width] = chosen[:, :width]

    atom = atom_ref[0, 0]
    blocks = blocks_of(bond_ref, slots // 2)
    own = [jnp.concatenate([atom, x[:, :feature]], axis=1) for x in blocks]
    own += [jnp.concatenate([atom, x[:, feature:]], axis=1) for x in blocks]
    own = jnp.concatenate(own, axis=0)
    own_ref[...] = own
    for copy in copies:
        copy.wait()


def doubled_gate(values):
    half = values.shape[1] // 2
    first, second = values[:, :half], values[:, half:]
    return first * (1.0 + jnp.tanh(first)) * (1.0 + jnp.tanh(second))


def main_kernel(
    near_ref,
    up_ref,
    down_ref,
    two_ref,
    one_ref,
    angular_ref,
    chosen_ref,
    right_ref,
    own_ref,
    bond_weight_ref,
    mix_weight_ref,
    pair_weight_ref,
    hidden_weight_ref,
    out_weight_ref,
    atom_in_weight_ref,
    sum_weight_ref,
    atom_out_weight_ref,
    atom_result_hbm,
    bond_result_hbm,
    atom_result_ref,
    bond_result_ref,
    first_ref,
    second_ref,
    pair_ref,
    sems,
):
    slots, pairs, _ = angular_ref.shape
    bonds = 2 * pairs
    atoms = bonds // slots
    feature = own_ref.shape[1] // 2
    width = 2 * feature
    half = CAP // 2
    near_refs = (near_ref, up_ref, down_ref)
    away_refs = (one_ref, two_ref)
    sent = [ref[:half] for ref in near_refs] + [ref[: 3 * half] for ref in away_refs]
    sent = jnp.concatenate(sent, axis=0)
    sent_atom = jnp.concatenate([ref[3 * half :] for ref in near_refs + away_refs], axis=0)
    blank = jnp.zeros((sent.shape[0], feature), BF16)
    blank_atom = jnp.zeros((sent_atom.shape[0], feature), BF16)
    received = jnp.concatenate(
        [
            jnp.concatenate([sent[:, :feature], blank, sent[:, feature:], blank], axis=1),
            jnp.concatenate(
                [blank_atom, sent_atom[:, :feature], blank_atom, sent_atom[:, feature:]], axis=1
            ),
        ],
        axis=0,
    )
    far = jnp.dot(chosen_ref[...], received, preferred_element_type=F32)
    far = jnp.where(right_ref[...] > 0.0, far[:, width:], far[:, :width])
    own = own_ref[...]
    incoming = jnp.dot(
        jnp.concatenate([far.astype(BF16), own], axis=1),
        bond_weight_ref[...],
        preferred_element_type=F32,
    )
    hidden = doubled_gate(incoming).astype(BF16)
    old = jnp.where(left_lanes((bonds, width)), far, own.astype(F32))
    both = jnp.concatenate([hidden, old.astype(BF16)], axis=1)
    even, odd = both[:pairs], both[pairs:]
    projected = jnp.dot(
        jnp.concatenate([even, odd], axis=1), pair_weight_ref[...], preferred_element_type=F32
    )
    first_ref[...] = projected[:, : 2 * width]
    second_ref[0] = projected[:, 2 * width :]
    shifted = jnp.concatenate([even[atoms:], even[:atoms]], axis=0)
    second_ref[1] = jnp.dot(
        jnp.concatenate([odd, shifted], axis=1),
        pair_weight_ref[:, 2 * width :],
        preferred_element_type=F32,
    )
    mixed = jnp.dot(hidden, mix_weight_ref[...], preferred_element_type=F32)
    new = (old + mixed).astype(BF16).astype(F32)
    average = ((new + pltpu.roll(new, feature, 1)) * 0.5).astype(BF16).astype(F32)
    packed = jnp.where(left_lanes((pairs, width)), average[:pairs], average[pairs:])
    group = 2

    def first_gates(base):
        for start in range(0, pairs, atoms):
            here = first_ref[pl.ds(start, atoms)]
            for diagonal in range(base, base + group):
                there = (start + diagonal // 2 * atoms) % pairs
                mixture = angular_ref[diagonal, pl.ds(start, atoms)] + (
                    here + second_ref[diagonal % 2, pl.ds(there, atoms)]
                )
                pair_ref[pl.ds(diagonal * pairs + start, atoms)] = doubled_gate(mixture).astype(
                    BF16
                )

    def summed(rows):
        parts = [rows[k * atoms : (k + 1) * atoms] for k in range(slots // 2)]
        while len(parts) > 1:
            parts = [x + y for x, y in zip(parts[::2], parts[1::2])]
        return parts[0]

    atom = own[0:atoms]
    atom_incoming = jnp.dot(
        jnp.concatenate([atom[:, :feature], summed(packed).astype(BF16)], axis=1),
        atom_in_weight_ref[...],
        preferred_element_type=F32,
    )
    total = jnp.zeros((pairs, width), F32)
    first_gates(0)
    for base in range(0, slots, group):
        if base + group < slots:
            first_gates(base + group)
        second = jnp.dot(
            pair_ref[pl.ds(base * pairs, group * pairs)],
            hidden_weight_ref[...],
            preferred_element_type=F32,
        )
        gates = doubled_gate(second)
        for k in range(group):
            total = total + gates[k * pairs : (k + 1) * pairs]
    bond_out = packed + jnp.dot(
        total.astype(BF16), out_weight_ref[...], preferred_element_type=F32
    )
    bond_out = bond_out.astype(BF16)
    for k in range(slots // 2):
        bond_result_ref[0, 0, :, k * width : (k + 1) * width] = bond_out[
            k * atoms : (k + 1) * atoms
        ]
    copies = [pltpu.make_async_copy(bond_result_ref, bond_result_hbm, sems.at[0])]
    copies[0].start()
    sums = summed(total).astype(BF16)
    atom_incoming = atom_incoming + jnp.dot(
        jnp.concatenate([sums, sums], axis=1), sum_weight_ref[...], preferred_element_type=F32
    )
    atom_hidden = doubled_gate(atom_incoming).astype(BF16)
    atom_new = atom.astype(F32) + jnp.dot(
        atom_hidden, atom_out_weight_ref[...], preferred_element_type=F32
    )
    atom_result_ref[0, 0] = atom_new[:, :feature].astype(BF16)
    copies.append(pltpu.make_async_copy(atom_result_ref, atom_result_hbm, sems.at[1]))
    copies[-1].start()
    for copy in copies:
        copy.wait()


def per_device(
    atom_feat,
    bond_feat,
    neighbours,
    bond_dirs,
    bond_in_weight,
    bond_mix_weight,
    pair_weight,
    angle_weight,
    pair_hidden_weight,
    pair_out_weight,
    atom_in_weight,
    atom_out_weight,
):
    atoms, feature = atom_feat.shape[2], atom_feat.shape[3]
    slots = neighbours.shape[3]
    bonds = atoms * slots
    pairs = bonds // 2
    half = CAP // 2
    extents = (lax.axis_size("gx"), lax.axis_size("gy"))
    paired = (extents[0] % 2 == 0, False)
    targets = neighbours[0, 0].T
    hbm = pl.BlockSpec(memory_space=pltpu.HBM)
    vmem = pl.BlockSpec(memory_space=pltpu.VMEM)
    params = pltpu.CompilerParams(vmem_limit_bytes=32 * 2**20)

    def shaped(shape, dtype):
        return jax.ShapeDtypeStruct(shape, dtype)

    def in_hbm(arrays):
        return tuple(pltpu.with_memory_space_constraint(x, pltpu.HBM) for x in arrays)

    payload = shaped((3 * half + atoms // 2, 2 * feature), BF16)
    inputs = (targets, atom_feat, bond_feat)
    up, down, *held = pl.pallas_call(
        functools.partial(pack_kernel, extents, paired),
        out_shape=(payload, payload, shaped((1, bonds), jnp.int32))
        + tuple(shaped(x.shape, x.dtype) for x in inputs),
        in_specs=[hbm] * 3,
        out_specs=(vmem,) * 6,
        scratch_shapes=[pltpu.SemaphoreType.DMA((3,))],
        compiler_params=params,
        name="pack",
    )(*in_hbm(inputs))
    first, second = moves(extents[1], paired[1])
    up = lax.ppermute(up, "gy", first)
    down = lax.ppermute(down, "gy", second)
    weights = (bond_in_weight, bond_mix_weight, pair_weight, pair_hidden_weight)
    weights += (pair_out_weight, atom_in_weight, atom_out_weight)
    near, *prepared, bond_dirs, angle_weight = pl.pallas_call(
        functools.partial(prepare_kernel, extents, paired),
        out_shape=(
            payload,
            shaped((bonds, 9 * half + 9 * atoms // 2), BF16),
            shaped((bonds, 2 * feature), F32),
            shaped((bonds, 2 * feature), BF16),
            shaped(bond_dirs.shape, F32),
            shaped(angle_weight.shape, BF16),
        ),
        in_specs=[vmem] * 4 + [hbm] * 2,
        out_specs=(vmem,) * 6,
        scratch_shapes=[pltpu.SemaphoreType.DMA((2,))],
        compiler_params=params,
        cost_estimate=pl.CostEstimate(flops=64 * 2**20, bytes_accessed=2**21, transcendentals=0),
        name="prepare",
    )(*held, *in_hbm((bond_dirs, angle_weight)))
    near, up, down, prepared = lax.optimization_barrier((near, up, down, prepared))
    first, second = moves(extents[0], paired[0])

    def forwarded(block):
        parts = [x[block * half : (block + 1) * half] for x in (near, up, down)]
        return jnp.concatenate(parts + [x[3 * half :] for x in (near, up, down)], axis=0)

    one = lax.ppermute(forwarded(1), "gx", first)
    two = lax.ppermute(forwarded(2), "gx", second)
    angular, *made = pl.pallas_call(
        functools.partial(angular_kernel, atoms),
        out_shape=(
            shaped((slots, pairs, 4 * feature), F32),
            shaped((4 * feature, 4 * feature), BF16),
            shaped((2 * feature, 2 * feature), BF16),
            shaped((8 * feature, 8 * feature), BF16),
            shaped((2 * feature, 4 * feature), BF16),
            shaped((2 * feature, 2 * feature), BF16),
            shaped((3 * feature, 4 * feature), BF16),
            shaped((4 * feature, 4 * feature), BF16),
            shaped((2 * feature, 2 * feature), BF16),
        ),
        in_specs=[vmem] * 2 + [hbm] * 7,
        out_specs=(vmem,) * 9,
        scratch_shapes=[pltpu.VMEM(x.shape, BF16) for x in weights]
        + [pltpu.SemaphoreType.DMA((7,))],
        compiler_params=params,
        cost_estimate=pl.CostEstimate(
            flops=256 * 2**20, bytes_accessed=2**22, transcendentals=4096
        ),
        name="angular",
    )(bond_dirs, angle_weight, *in_hbm(weights))
    return pl.pallas_call(
        main_kernel,
        out_shape=(shaped(atom_feat.shape, BF16), shaped(bond_feat.shape, BF16)),
        in_specs=[vmem] * 17,
        out_specs=(hbm, hbm),
        scratch_shapes=[
            pltpu.VMEM(atom_feat.shape, BF16),
            pltpu.VMEM(bond_feat.shape, BF16),
            pltpu.VMEM((pairs, 4 * feature), F32),
            pltpu.VMEM((2, pairs, 4 * feature), F32),
            pltpu.VMEM((slots * pairs, 2 * feature), BF16),
            pltpu.SemaphoreType.DMA((2,)),
        ],
        compiler_params=params,
        name="main",
    )(near, up, down, two, one, angular, *prepared, *made)


def solution(mesh):
    placed = (
        P("gx", "gy", None, None),
        P("gx", "gy", None, None),
        P("gx", "gy", None, None),
        P(None, "gx", "gy", None),
        P(),
        P(),
        P(),
        P(),
        P(),
        P(),
        P(),
        P(),
    )
    return jax.shard_map(
        per_device,
        mesh=mesh,
        in_specs=placed,
        out_specs=(P("gx", "gy", None, None), P("gx", "gy", None, None)),
        check_vma=False,
    )
```

```python
import functools

import jax
import jax.numpy as jnp
from jax import lax
from jax.experimental import pallas as pl
from jax.experimental.pallas import tpu as pltpu
from jax.sharding import PartitionSpec as P

F32 = jnp.float32
BF16 = jnp.bfloat16
CAP = 64


def quotient(values, size):
    if size & (size - 1) == 0:
        return values >> (size.bit_length() - 1)
    return lax.div(values, jnp.int32(size))


def remainder(values, size):
    if size & (size - 1) == 0:
        return values & (size - 1)
    return lax.rem(values, jnp.int32(size))


def step_code(owner, home, extent, paired, receives):
    step = remainder(owner - home + 1 + extent, extent)
    if paired:
        ahead = jnp.where(remainder(home, 2) == 0, 0, 2)
    else:
        ahead = 0 if receives else 2
    return jnp.where(step == 1, 0, jnp.where(step == ahead, 1, 2))


def moves(extent, paired):
    if paired:
        near = [(i, i ^ 1) for i in range(extent)]
        return [(i, (((i + 1) ^ 1) - 1) % extent) for i in range(extent)], near
    up = [(i, (i + 1) % extent) for i in range(extent)]
    return up, [(j, i) for i, j in up]


def slot_at(position, slots):
    half = slots // 2
    return jnp.where(position < half, 2 * position, 2 * (position - half) + 1)


def bond_row(table):
    slots, atoms = table.shape
    per_group = 128 // atoms
    tiled = jnp.concatenate([table.astype(F32)] * per_group, axis=1)
    row = lax.broadcasted_iota(jnp.int32, tiled.shape, 0)
    position = quotient(lax.broadcasted_iota(jnp.int32, tiled.shape, 1), atoms)
    pieces = []
    for group in range(slots // per_group):
        chosen = row == slot_at(position + group * per_group, slots)
        pieces.append(jnp.sum(jnp.where(chosen, tiled, 0.0), axis=0, keepdims=True))
    return jnp.concatenate(pieces, axis=1).astype(jnp.int32)


def bond_codes(targets, atoms, extents, paired, receives):
    owner = quotient(targets, atoms)
    block = (quotient(owner, extents[1]), remainder(owner, extents[1]))
    return tuple(
        step_code(block[k], lax.axis_index(axis), extents[k], paired[k], receives)
        for k, axis in enumerate(("gx", "gy"))
    )


def left_lanes(shape):
    return lax.broadcasted_iota(jnp.int32, shape, 1) < shape[1] // 2


def swapped(rows):
    half = rows.shape[1] // 2
    return jnp.concatenate([rows[:, half:], rows[:, :half]], axis=1)


def blocks_of(bond_ref, pairs):
    width = bond_ref.shape[3] // pairs
    return [bond_ref[0, 0, :, k * width : (k + 1) * width] for k in range(pairs)]


def pack_kernel(
    extents,
    paired,
    targets_hbm,
    atom_hbm,
    bond_hbm,
    up_ref,
    down_ref,
    spot_ref,
    targets_ref,
    atom_ref,
    bond_ref,
    sems,
):
    sources = ((targets_hbm, targets_ref), (bond_hbm, bond_ref), (atom_hbm, atom_ref))
    copies = [
        pltpu.make_async_copy(source, target, sems.at[k])
        for k, (source, target) in enumerate(sources)
    ]
    for copy in copies:
        copy.start()
    atoms, feature = atom_ref.shape[2], atom_ref.shape[3]
    slots = targets_ref.shape[0]
    bonds = slots * atoms
    lanes = 128
    groups = bonds // lanes
    copies[0].wait()
    code_x, code_y = bond_codes(bond_row(targets_ref[...]), atoms, extents, paired, False)
    code = 3 * code_y + code_x
    rows = lax.broadcasted_iota(jnp.int32, (16, lanes), 0)
    marks = [rows == code[:, g * lanes : (g + 1) * lanes] for g in range(groups)]
    stacked = jnp.concatenate([m.astype(F32) for m in marks], axis=0).astype(BF16)
    before = lax.broadcasted_iota(jnp.int32, (lanes, 2 * lanes), 0)
    after = lax.broadcasted_iota(jnp.int32, (lanes, 2 * lanes), 1)
    sums = jnp.where((before < after) | (after >= lanes), 1.0, 0.0).astype(BF16)
    counted = jnp.dot(stacked, sums, preferred_element_type=F32)
    place = []
    earlier = jnp.zeros((16, lanes), F32)
    for g in range(groups):
        part = counted[g * 16 : (g + 1) * 16]
        place.append(
            jnp.sum(jnp.where(marks[g], part[:, :lanes] + earlier, 0.0), axis=0, keepdims=True)
        )
        earlier = earlier + part[:, lanes:]
    place = jnp.concatenate(place, axis=1).astype(jnp.int32)
    half = CAP // 2
    right = quotient(place, half)
    spot = place - half * right + half * code
    spot_ref[...] = jnp.where(code < 3, spot + 3 * half * right, -1)
    wanted = jnp.where(code < 3, -1, spot - 3 * half + 6 * half * right)
    copies[1].wait()
    copies[2].wait()
    packed = packed_rows(wanted, bond_ref, slots, 6 * half)
    for k, ref in enumerate((up_ref, down_ref)):
        ref[: 3 * half] = packed[3 * half * k : 3 * half * (k + 1)]
        ref[3 * half :] = atom_rows(atom_ref)


def packed_rows(wanted, bond_ref, slots, count):
    spot = lax.broadcasted_iota(jnp.int32, (2 * count, wanted.shape[1]), 0)
    chosen = jnp.where(spot == wanted, 1.0, 0.0).astype(BF16)
    blocks = blocks_of(bond_ref, slots // 2)
    feature = blocks[0].shape[1] // 2
    values = [x[:, :feature] for x in blocks] + [x[:, feature:] for x in blocks]
    packed = jnp.dot(chosen, jnp.concatenate(values, axis=0), preferred_element_type=F32)
    return jnp.concatenate([packed[:count], packed[count:]], axis=1).astype(BF16)


def atom_rows(atom_ref):
    atom = atom_ref[0, 0]
    half = atom.shape[0] // 2
    return jnp.concatenate([atom[:half], atom[half:]], axis=1)


def crossed(left, right):
    half = left.shape[1] // 2
    parts = [left[:, :half], right[:, :half], left[:, half:], right[:, half:]]
    return jnp.concatenate(parts, axis=1)


def two_blocks(weight):
    blank = jnp.zeros_like(weight)
    return jnp.concatenate([crossed(weight, blank), crossed(blank, weight)], axis=0)


def diagonal_blocks(weight):
    blank = jnp.zeros_like(weight)
    return jnp.concatenate(
        [jnp.concatenate([weight, blank], axis=1), jnp.concatenate([blank, weight], axis=1)],
        axis=0,
    )


def angular_kernel(atoms, dirs_ref, angle_ref, *refs):
    sources, angular_ref, results, held, sems = refs[:7], refs[7], refs[8:16], refs[16:23], refs[23]
    copies = [
        pltpu.make_async_copy(source, target, sems.at[k])
        for k, (source, target) in enumerate(zip(sources, held))
    ]
    for copy in copies:
        copy.start()
    slots, pairs, _ = angular_ref.shape
    bonds = 2 * pairs
    degrees = angle_ref.shape[0]
    weight = (two_blocks(angle_ref[...].astype(F32)) * 0.5).astype(BF16)
    polar, azimuth = dirs_ref[0, 0], dirs_ref[1, 0]
    unit = jnp.concatenate(
        [
            jnp.sin(polar) * jnp.cos(azimuth),
            jnp.sin(polar) * jnp.sin(azimuth),
            jnp.cos(polar),
            jnp.zeros((5, bonds), F32),
        ],
        axis=0,
    )
    high = unit.astype(BF16).astype(F32)
    middle = (unit - high).astype(BF16).astype(F32)
    parts = jnp.concatenate([high, middle, unit - high - middle], axis=0).astype(BF16)
    bond = lax.broadcasted_iota(jnp.int32, (1, bonds), 1)
    source = remainder(bond, atoms) * slots + slot_at(quotient(bond, atoms), slots)
    spot = lax.broadcasted_iota(jnp.int32, (bonds, bonds), 0)
    chosen = jnp.where(spot == source, 1.0, 0.0).astype(BF16)
    unit = jnp.dot(parts, chosen, preferred_element_type=F32)
    unit = unit[0:8] + unit[8:16] + unit[16:24]
    even = [jnp.broadcast_to(unit[k : k + 1, :pairs], (8, pairs)) for k in range(3)]
    odd = [jnp.broadcast_to(unit[k : k + 1, pairs:], (8, pairs)) for k in range(3)]
    row = lax.broadcasted_iota(jnp.int32, (8, pairs), 0)

    def turned(vector, places):
        places = places % (pairs // atoms)
        if places == 0:
            return vector
        return [pltpu.roll(part, pairs - atoms * places, 1) for part in vector]

    def basis(first, second):
        cosine = first[0] * second[0] + first[1] * second[1] + first[2] * second[2]
        series = [jnp.ones_like(cosine), cosine]
        double = cosine + cosine
        for _ in range(7):
            series.append(double * series[-1] - series[-2])
        lower = series[7]
        upper = series[1]
        for index in range(1, 8):
            lower = jnp.where(row == index, series[7 - index], lower)
            upper = jnp.where(row == index, series[1 + index], upper)
        double = series[8] + series[8]
        blocks = [lower, upper]
        for _ in range(degrees // 8 - 1):
            blocks.append(double * blocks[-1] - blocks[-2])
        return blocks[1:]

    for diagonal in range(slots):
        places = diagonal // 2
        if diagonal % 2 == 0:
            blocks = basis(even, turned(even, places)) + basis(odd, turned(odd, places))
        else:
            blocks = basis(even, turned(odd, places)) + basis(odd, turned(even, places + 1))
        series = jnp.concatenate(blocks, axis=0).T.astype(BF16)
        angular_ref[diagonal] = jnp.dot(series, weight, preferred_element_type=F32)
    for copy in copies:
        copy.wait()
    prepare_weights(slots, held, results)


def prepare_weights(slots, held, results):
    bond_in_ref, bond_mix_ref, pair_ref, pair_hidden_ref, pair_out_ref, atom_in_ref = held[:6]
    atom_out_ref = held[6]
    bond_weight_ref, mix_weight_ref, pair_weight_ref, hidden_weight_ref = results[:4]
    out_weight_ref, atom_in_weight_ref, sum_weight_ref, atom_out_weight_ref = results[4:]
    feature = bond_mix_ref.shape[0]
    weight = bond_in_ref[...].astype(F32)
    source, other, bond_part = (weight[k * feature : (k + 1) * feature] for k in range(3))
    blank = jnp.zeros_like(source)
    away = [crossed(bond_part, blank), crossed(source, other)]
    near = [crossed(other, source), crossed(blank, bond_part)]
    bond_weight_ref[...] = (jnp.concatenate(away + near, axis=0) * 0.5).astype(BF16)
    mix_weight_ref[...] = (diagonal_blocks(bond_mix_ref[...].astype(F32)) * 0.5).astype(BF16)
    old = pair_ref[...].astype(F32) * 0.25
    hidden = jnp.dot(bond_mix_ref[...], pair_ref[...], preferred_element_type=F32) * 0.125
    weight = jnp.concatenate([hidden, hidden, old, old], axis=0).astype(BF16)
    pair_weight_ref[...] = jnp.concatenate(
        [two_blocks(weight[:, : 2 * feature]), two_blocks(weight[:, 2 * feature :])], axis=1
    )
    hidden_weight_ref[...] = (two_blocks(pair_hidden_ref[...].astype(F32)) * 0.25).astype(BF16)
    out_weight_ref[...] = (diagonal_blocks(pair_out_ref[...].astype(F32)) * 0.5).astype(BF16)
    weight = atom_in_ref[...].astype(F32) * 0.5
    weight = crossed(weight, jnp.zeros_like(weight))
    mean = weight[feature:] * (1.0 / slots)
    atom_in_weight_ref[...] = jnp.concatenate([weight[:feature], mean, mean], axis=0).astype(BF16)
    folded = jnp.dot(
        pair_out_ref[...], (mean * 0.5).astype(BF16), preferred_element_type=F32
    )
    high = folded.astype(BF16)
    low = (folded - high.astype(F32)).astype(BF16)
    sum_weight_ref[...] = jnp.concatenate([high, high, low, low], axis=0)
    weight = atom_out_ref[...].astype(F32) * 0.5
    blank = jnp.zeros_like(weight)
    weight = jnp.concatenate([weight, blank], axis=1)
    atom_out_weight_ref[...] = jnp.concatenate([weight, jnp.zeros_like(weight)], axis=0).astype(
        BF16
    )


def prepare_kernel(
    extents,
    paired,
    spot_ref,
    targets_ref,
    atom_ref,
    bond_ref,
    dirs_hbm,
    angle_hbm,
    near_ref,
    chosen_ref,
    right_ref,
    own_ref,
    dirs_ref,
    angle_ref,
    sems,
):
    copies = [
        pltpu.make_async_copy(source, target, sems.at[k])
        for k, (source, target) in enumerate(((dirs_hbm, dirs_ref), (angle_hbm, angle_ref)))
    ]
    for copy in copies:
        copy.start()
    atoms, feature = atom_ref.shape[2], atom_ref.shape[3]
    slots = targets_ref.shape[0]
    bonds = slots * atoms
    near_ref[: 3 * CAP // 2] = packed_rows(spot_ref[...], bond_ref, slots, 3 * CAP // 2)
    near_ref[3 * CAP // 2 :] = atom_rows(atom_ref)
    targets = bond_row(targets_ref[...])
    code_x, code_y = bond_codes(targets, atoms, extents, paired, True)
    code = 3 * code_x + code_y
    bond = lax.broadcasted_iota(jnp.int32, (1, bonds), 1)
    far_slot = slots - 1 - slot_at(quotient(bond, atoms), slots)
    far_atom = remainder(targets, atoms)
    far = (remainder(far_slot, 2) * (slots // 2) + quotient(far_slot, 2)) * atoms + far_atom
    base = (code * bonds).astype(F32)
    key = base + far.astype(F32)

    def column(values):
        return jnp.broadcast_to(values.astype(F32), (128, bonds)).T

    keys = column(key)
    place = []
    for group in range(bonds // 128):
        here = slice(group * 128, (group + 1) * 128)
        inside = (keys < key[:, here]) & (keys >= base[:, here])
        place.append(jnp.sum(jnp.where(inside, 1.0, 0.0), axis=0, keepdims=True))
    place = jnp.concatenate(place, axis=1).astype(jnp.int32)
    half, tall = CAP // 2, atoms // 2
    bond_spot = column(half * code + remainder(place, half))
    atom_spot = column(9 * half + tall * code + remainder(far_atom, tall))
    right = (column(quotient(place, half)), column(quotient(far_atom, tall)))
    right_ref[...] = jnp.where(left_lanes((bonds, 128)), right[0], right[1])
    total = 9 * half + 9 * tall
    for start in range(0, total, 128):
        width = min(128, total - start)
        spot = lax.broadcasted_iota(jnp.int32, (bonds, 128), 1).astype(F32) + float(start)
        chosen = jnp.where((spot == bond_spot) | (spot == atom_spot), 1.0, 0.0).astype(BF16)
        chosen_ref[:, start : start + width] = chosen[:, :width]

    atom = atom_ref[0, 0]
    blocks = blocks_of(bond_ref, slots // 2)
    own = [jnp.concatenate([atom, x[:, :feature]], axis=1) for x in blocks]
    own += [jnp.concatenate([atom, x[:, feature:]], axis=1) for x in blocks]
    own = jnp.concatenate(own, axis=0)
    own_ref[...] = own
    for copy in copies:
        copy.wait()


def doubled_gate(values):
    half = values.shape[1] // 2
    first, second = values[:, :half], values[:, half:]
    return first * (1.0 + jnp.tanh(first)) * (1.0 + jnp.tanh(second))


def main_kernel(
    near_ref,
    up_ref,
    down_ref,
    two_ref,
    one_ref,
    angular_ref,
    chosen_ref,
    right_ref,
    own_ref,
    bond_weight_ref,
    mix_weight_ref,
    pair_weight_ref,
    hidden_weight_ref,
    out_weight_ref,
    atom_in_weight_ref,
    sum_weight_ref,
    atom_out_weight_ref,
    atom_result_hbm,
    bond_result_hbm,
    atom_result_ref,
    bond_result_ref,
    first_ref,
    second_ref,
    pair_ref,
    sems,
):
    slots, pairs, _ = angular_ref.shape
    bonds = 2 * pairs
    atoms = bonds // slots
    feature = own_ref.shape[1] // 2
    width = 2 * feature
    half = CAP // 2
    near_refs = (near_ref, up_ref, down_ref)
    away_refs = (one_ref, two_ref)
    sent = [ref[:half] for ref in near_refs] + [ref[: 3 * half] for ref in away_refs]
    sent = jnp.concatenate(sent, axis=0)
    sent_atom = jnp.concatenate([ref[3 * half :] for ref in near_refs + away_refs], axis=0)
    blank = jnp.zeros((sent.shape[0], feature), BF16)
    blank_atom = jnp.zeros((sent_atom.shape[0], feature), BF16)
    received = jnp.concatenate(
        [
            jnp.concatenate([sent[:, :feature], blank, sent[:, feature:], blank], axis=1),
            jnp.concatenate(
                [blank_atom, sent_atom[:, :feature], blank_atom, sent_atom[:, feature:]], axis=1
            ),
        ],
        axis=0,
    )
    far = jnp.dot(chosen_ref[...], received, preferred_element_type=F32)
    far = jnp.where(right_ref[...] > 0.0, far[:, width:], far[:, :width])
    own = own_ref[...]
    incoming = jnp.dot(
        jnp.concatenate([far.astype(BF16), own], axis=1),
        bond_weight_ref[...],
        preferred_element_type=F32,
    )
    hidden = doubled_gate(incoming).astype(BF16)
    old = jnp.where(left_lanes((bonds, width)), far, own.astype(F32))
    both = jnp.concatenate([hidden, old.astype(BF16)], axis=1)
    even, odd = both[:pairs], both[pairs:]
    projected = jnp.dot(
        jnp.concatenate([even, odd], axis=1), pair_weight_ref[...], preferred_element_type=F32
    )
    first_ref[...] = projected[:, : 2 * width]
    second_ref[0] = projected[:, 2 * width :]
    shifted = jnp.concatenate([even[atoms:], even[:atoms]], axis=0)
    second_ref[1] = jnp.dot(
        jnp.concatenate([odd, shifted], axis=1),
        pair_weight_ref[:, 2 * width :],
        preferred_element_type=F32,
    )
    mixed = jnp.dot(hidden, mix_weight_ref[...], preferred_element_type=F32)
    new = (old + mixed).astype(BF16).astype(F32)
    average = ((new + pltpu.roll(new, feature, 1)) * 0.5).astype(BF16).astype(F32)
    packed = jnp.where(left_lanes((pairs, width)), average[:pairs], average[pairs:])
    def first_gates(start):
        here = first_ref[pl.ds(start, atoms)]
        for diagonal in range(slots):
            there = (start + diagonal // 2 * atoms) % pairs
            mixture = angular_ref[diagonal, pl.ds(start, atoms)] + (
                here + second_ref[diagonal % 2, pl.ds(there, atoms)]
            )
            row = start * slots + diagonal * atoms
            pair_ref[pl.ds(row, atoms)] = doubled_gate(mixture).astype(BF16)

    def summed(rows):
        parts = [rows[k * atoms : (k + 1) * atoms] for k in range(slots // 2)]
        while len(parts) > 1:
            parts = [x + y for x, y in zip(parts[::2], parts[1::2])]
        return parts[0]

    atom = own[0:atoms]
    atom_incoming = jnp.dot(
        jnp.concatenate([atom[:, :feature], summed(packed).astype(BF16)], axis=1),
        atom_in_weight_ref[...],
        preferred_element_type=F32,
    )
    copies = []
    sums = jnp.zeros((atoms, width), F32)
    first_gates(0)
    for chunk, start in enumerate(range(0, pairs, atoms)):
        if start + atoms < pairs:
            first_gates(start + atoms)
        second = jnp.dot(
            pair_ref[pl.ds(start * slots, atoms * slots)],
            hidden_weight_ref[...],
            preferred_element_type=F32,
        )
        total = jnp.zeros((atoms, width), F32)
        for diagonal in range(slots):
            total = total + doubled_gate(second[diagonal * atoms : (diagonal + 1) * atoms])
        sums = sums + total
        bond_out = packed[start : start + atoms] + jnp.dot(
            total.astype(BF16), out_weight_ref[...], preferred_element_type=F32
        )
        columns = pl.ds(chunk * width, width)
        bond_result_ref[0, 0, :, columns] = bond_out.astype(BF16)
        copies.append(
            pltpu.make_async_copy(
                bond_result_ref.at[0, 0, :, columns],
                bond_result_hbm.at[0, 0, :, columns],
                sems.at[1 + chunk],
            )
        )
        copies[-1].start()
    sums = sums.astype(BF16)
    atom_incoming = atom_incoming + jnp.dot(
        jnp.concatenate([sums, sums], axis=1), sum_weight_ref[...], preferred_element_type=F32
    )
    atom_hidden = doubled_gate(atom_incoming).astype(BF16)
    atom_new = atom.astype(F32) + jnp.dot(
        atom_hidden, atom_out_weight_ref[...], preferred_element_type=F32
    )
    atom_result_ref[0, 0] = atom_new[:, :feature].astype(BF16)
    copies.append(pltpu.make_async_copy(atom_result_ref, atom_result_hbm, sems.at[0]))
    copies[-1].start()
    for copy in copies:
        copy.wait()


def per_device(
    atom_feat,
    bond_feat,
    neighbours,
    bond_dirs,
    bond_in_weight,
    bond_mix_weight,
    pair_weight,
    angle_weight,
    pair_hidden_weight,
    pair_out_weight,
    atom_in_weight,
    atom_out_weight,
):
    atoms, feature = atom_feat.shape[2], atom_feat.shape[3]
    slots = neighbours.shape[3]
    bonds = atoms * slots
    pairs = bonds // 2
    half = CAP // 2
    extents = (lax.axis_size("gx"), lax.axis_size("gy"))
    paired = (extents[0] % 2 == 0, False)
    targets = neighbours[0, 0].T
    hbm = pl.BlockSpec(memory_space=pltpu.HBM)
    vmem = pl.BlockSpec(memory_space=pltpu.VMEM)
    params = pltpu.CompilerParams(vmem_limit_bytes=32 * 2**20)

    def shaped(shape, dtype):
        return jax.ShapeDtypeStruct(shape, dtype)

    def in_hbm(arrays):
        return tuple(pltpu.with_memory_space_constraint(x, pltpu.HBM) for x in arrays)

    payload = shaped((3 * half + atoms // 2, 2 * feature), BF16)
    inputs = (targets, atom_feat, bond_feat)
    up, down, *held = pl.pallas_call(
        functools.partial(pack_kernel, extents, paired),
        out_shape=(payload, payload, shaped((1, bonds), jnp.int32))
        + tuple(shaped(x.shape, x.dtype) for x in inputs),
        in_specs=[hbm] * 3,
        out_specs=(vmem,) * 6,
        scratch_shapes=[pltpu.SemaphoreType.DMA((3,))],
        compiler_params=params,
        name="pack",
    )(*in_hbm(inputs))
    first, second = moves(extents[1], paired[1])
    up = lax.ppermute(up, "gy", first)
    down = lax.ppermute(down, "gy", second)
    weights = (bond_in_weight, bond_mix_weight, pair_weight, pair_hidden_weight)
    weights += (pair_out_weight, atom_in_weight, atom_out_weight)
    near, *prepared, bond_dirs, angle_weight = pl.pallas_call(
        functools.partial(prepare_kernel, extents, paired),
        out_shape=(
            payload,
            shaped((bonds, 9 * half + 9 * atoms // 2), BF16),
            shaped((bonds, 2 * feature), F32),
            shaped((bonds, 2 * feature), BF16),
            shaped(bond_dirs.shape, F32),
            shaped(angle_weight.shape, BF16),
        ),
        in_specs=[vmem] * 4 + [hbm] * 2,
        out_specs=(vmem,) * 6,
        scratch_shapes=[pltpu.SemaphoreType.DMA((2,))],
        compiler_params=params,
        cost_estimate=pl.CostEstimate(flops=64 * 2**20, bytes_accessed=2**21, transcendentals=0),
        name="prepare",
    )(*held, *in_hbm((bond_dirs, angle_weight)))
    near, up, down, prepared = lax.optimization_barrier((near, up, down, prepared))
    first, second = moves(extents[0], paired[0])

    def forwarded(block):
        parts = [x[block * half : (block + 1) * half] for x in (near, up, down)]
        return jnp.concatenate(parts + [x[3 * half :] for x in (near, up, down)], axis=0)

    one = lax.ppermute(forwarded(1), "gx", first)
    two = lax.ppermute(forwarded(2), "gx", second)
    angular, *made = pl.pallas_call(
        functools.partial(angular_kernel, atoms),
        out_shape=(
            shaped((slots, pairs, 4 * feature), F32),
            shaped((4 * feature, 4 * feature), BF16),
            shaped((2 * feature, 2 * feature), BF16),
            shaped((8 * feature, 8 * feature), BF16),
            shaped((2 * feature, 4 * feature), BF16),
            shaped((2 * feature, 2 * feature), BF16),
            shaped((3 * feature, 4 * feature), BF16),
            shaped((4 * feature, 4 * feature), BF16),
            shaped((2 * feature, 2 * feature), BF16),
        ),
        in_specs=[vmem] * 2 + [hbm] * 7,
        out_specs=(vmem,) * 9,
        scratch_shapes=[pltpu.VMEM(x.shape, BF16) for x in weights]
        + [pltpu.SemaphoreType.DMA((7,))],
        compiler_params=params,
        cost_estimate=pl.CostEstimate(
            flops=256 * 2**20, bytes_accessed=2**22, transcendentals=4096
        ),
        name="angular",
    )(bond_dirs, angle_weight, *in_hbm(weights))
    return pl.pallas_call(
        main_kernel,
        out_shape=(shaped(atom_feat.shape, BF16), shaped(bond_feat.shape, BF16)),
        in_specs=[vmem] * 17,
        out_specs=(hbm, hbm),
        scratch_shapes=[
            pltpu.VMEM(atom_feat.shape, BF16),
            pltpu.VMEM(bond_feat.shape, BF16),
            pltpu.VMEM((pairs, 4 * feature), F32),
            pltpu.VMEM((2, pairs, 4 * feature), F32),
            pltpu.VMEM((slots * pairs, 2 * feature), BF16),
            pltpu.SemaphoreType.DMA((1 + slots // 2,)),
        ],
        compiler_params=params,
        name="main",
    )(near, up, down, two, one, angular, *prepared, *made)


def solution(mesh):
    placed = (
        P("gx", "gy", None, None),
        P("gx", "gy", None, None),
        P("gx", "gy", None, None),
        P(None, "gx", "gy", None),
        P(),
        P(),
        P(),
        P(),
        P(),
        P(),
        P(),
        P(),
    )
    return jax.shard_map(
        per_device,
        mesh=mesh,
        in_specs=placed,
        out_specs=(P("gx", "gy", None, None), P("gx", "gy", None, None)),
        check_vma=False,
    )
```

```python
import functools

import jax
import jax.numpy as jnp
from jax import lax
from jax.experimental import pallas as pl
from jax.experimental.pallas import tpu as pltpu
from jax.sharding import PartitionSpec as P

F32 = jnp.float32
BF16 = jnp.bfloat16
CAP = 64


def quotient(values, size):
    if size & (size - 1) == 0:
        return values >> (size.bit_length() - 1)
    return lax.div(values, jnp.int32(size))


def remainder(values, size):
    if size & (size - 1) == 0:
        return values & (size - 1)
    return lax.rem(values, jnp.int32(size))


def step_code(owner, home, extent, paired, receives):
    step = remainder(owner - home + 1 + extent, extent)
    if paired:
        ahead = jnp.where(remainder(home, 2) == 0, 0, 2)
    else:
        ahead = 0 if receives else 2
    return jnp.where(step == 1, 0, jnp.where(step == ahead, 1, 2))


def moves(extent, paired):
    if paired:
        near = [(i, i ^ 1) for i in range(extent)]
        return [(i, (((i + 1) ^ 1) - 1) % extent) for i in range(extent)], near
    up = [(i, (i + 1) % extent) for i in range(extent)]
    return up, [(j, i) for i, j in up]


def slot_at(position, slots):
    half = slots // 2
    return jnp.where(position < half, 2 * position, 2 * (position - half) + 1)


def bond_row(table):
    slots, atoms = table.shape
    per_group = 128 // atoms
    tiled = jnp.concatenate([table.astype(F32)] * per_group, axis=1)
    row = lax.broadcasted_iota(jnp.int32, tiled.shape, 0)
    position = quotient(lax.broadcasted_iota(jnp.int32, tiled.shape, 1), atoms)
    pieces = []
    for group in range(slots // per_group):
        chosen = row == slot_at(position + group * per_group, slots)
        pieces.append(jnp.sum(jnp.where(chosen, tiled, 0.0), axis=0, keepdims=True))
    return jnp.concatenate(pieces, axis=1).astype(jnp.int32)


def bond_codes(targets, atoms, extents, paired, receives):
    owner = quotient(targets, atoms)
    block = (quotient(owner, extents[1]), remainder(owner, extents[1]))
    return tuple(
        step_code(block[k], lax.axis_index(axis), extents[k], paired[k], receives)
        for k, axis in enumerate(("gx", "gy"))
    )


def left_lanes(shape):
    return lax.broadcasted_iota(jnp.int32, shape, 1) < shape[1] // 2


def swapped(rows):
    half = rows.shape[1] // 2
    return jnp.concatenate([rows[:, half:], rows[:, :half]], axis=1)


def blocks_of(bond_ref, pairs):
    width = bond_ref.shape[3] // pairs
    return [bond_ref[0, 0, :, k * width : (k + 1) * width] for k in range(pairs)]


def pack_kernel(
    extents,
    paired,
    targets_hbm,
    atom_hbm,
    bond_hbm,
    up_ref,
    down_ref,
    spot_ref,
    targets_ref,
    atom_ref,
    bond_ref,
    sems,
):
    sources = ((targets_hbm, targets_ref), (bond_hbm, bond_ref), (atom_hbm, atom_ref))
    copies = [
        pltpu.make_async_copy(source, target, sems.at[k])
        for k, (source, target) in enumerate(sources)
    ]
    for copy in copies:
        copy.start()
    atoms, feature = atom_ref.shape[2], atom_ref.shape[3]
    slots = targets_ref.shape[0]
    bonds = slots * atoms
    lanes = 128
    groups = bonds // lanes
    copies[0].wait()
    code_x, code_y = bond_codes(bond_row(targets_ref[...]), atoms, extents, paired, False)
    code = 3 * code_y + code_x
    rows = lax.broadcasted_iota(jnp.int32, (16, lanes), 0)
    marks = [rows == code[:, g * lanes : (g + 1) * lanes] for g in range(groups)]
    stacked = jnp.concatenate([m.astype(F32) for m in marks], axis=0).astype(BF16)
    before = lax.broadcasted_iota(jnp.int32, (lanes, 2 * lanes), 0)
    after = lax.broadcasted_iota(jnp.int32, (lanes, 2 * lanes), 1)
    sums = jnp.where((before < after) | (after >= lanes), 1.0, 0.0).astype(BF16)
    counted = jnp.dot(stacked, sums, preferred_element_type=F32)
    place = []
    earlier = jnp.zeros((16, lanes), F32)
    for g in range(groups):
        part = counted[g * 16 : (g + 1) * 16]
        place.append(
            jnp.sum(jnp.where(marks[g], part[:, :lanes] + earlier, 0.0), axis=0, keepdims=True)
        )
        earlier = earlier + part[:, lanes:]
    place = jnp.concatenate(place, axis=1).astype(jnp.int32)
    half = CAP // 2
    right = quotient(place, half)
    spot = place - half * right + half * code
    spot_ref[...] = jnp.where(code < 3, spot + 3 * half * right, -1)
    wanted = jnp.where(code < 3, -1, spot - 3 * half + 6 * half * right)
    copies[1].wait()
    copies[2].wait()
    packed = packed_rows(wanted, bond_ref, slots, 6 * half)
    for k, ref in enumerate((up_ref, down_ref)):
        ref[: 3 * half] = packed[3 * half * k : 3 * half * (k + 1)]
        ref[3 * half :] = atom_rows(atom_ref)


def packed_rows(wanted, bond_ref, slots, count):
    spot = lax.broadcasted_iota(jnp.int32, (2 * count, wanted.shape[1]), 0)
    chosen = jnp.where(spot == wanted, 1.0, 0.0).astype(BF16)
    blocks = blocks_of(bond_ref, slots // 2)
    feature = blocks[0].shape[1] // 2
    values = [x[:, :feature] for x in blocks] + [x[:, feature:] for x in blocks]
    packed = jnp.dot(chosen, jnp.concatenate(values, axis=0), preferred_element_type=F32)
    return jnp.concatenate([packed[:count], packed[count:]], axis=1).astype(BF16)


def atom_rows(atom_ref):
    atom = atom_ref[0, 0]
    half = atom.shape[0] // 2
    return jnp.concatenate([atom[:half], atom[half:]], axis=1)


def crossed(left, right):
    half = left.shape[1] // 2
    parts = [left[:, :half], right[:, :half], left[:, half:], right[:, half:]]
    return jnp.concatenate(parts, axis=1)


def two_blocks(weight):
    blank = jnp.zeros_like(weight)
    return jnp.concatenate([crossed(weight, blank), crossed(blank, weight)], axis=0)


def diagonal_blocks(weight):
    blank = jnp.zeros_like(weight)
    return jnp.concatenate(
        [jnp.concatenate([weight, blank], axis=1), jnp.concatenate([blank, weight], axis=1)],
        axis=0,
    )


def angular_kernel(atoms, dirs_ref, angle_ref, *refs):
    sources, angular_ref, results, held, sems = refs[:7], refs[7], refs[8:16], refs[16:23], refs[23]
    copies = [
        pltpu.make_async_copy(source, target, sems.at[k])
        for k, (source, target) in enumerate(zip(sources, held))
    ]
    for copy in copies:
        copy.start()
    slots, pairs, _ = angular_ref.shape
    bonds = 2 * pairs
    degrees = angle_ref.shape[0]
    weight = two_blocks(angle_ref[...].astype(F32)).astype(BF16)
    polar, azimuth = dirs_ref[0, 0], dirs_ref[1, 0]
    unit = jnp.concatenate(
        [
            jnp.sin(polar) * jnp.cos(azimuth),
            jnp.sin(polar) * jnp.sin(azimuth),
            jnp.cos(polar),
            jnp.zeros((5, bonds), F32),
        ],
        axis=0,
    )
    high = unit.astype(BF16).astype(F32)
    middle = (unit - high).astype(BF16).astype(F32)
    parts = jnp.concatenate([high, middle, unit - high - middle], axis=0).astype(BF16)
    bond = lax.broadcasted_iota(jnp.int32, (1, bonds), 1)
    source = remainder(bond, atoms) * slots + slot_at(quotient(bond, atoms), slots)
    spot = lax.broadcasted_iota(jnp.int32, (bonds, bonds), 0)
    chosen = jnp.where(spot == source, 1.0, 0.0).astype(BF16)
    unit = jnp.dot(parts, chosen, preferred_element_type=F32)
    unit = unit[0:8] + unit[8:16] + unit[16:24]
    even = [jnp.broadcast_to(unit[k : k + 1, :pairs], (8, pairs)) for k in range(3)]
    odd = [jnp.broadcast_to(unit[k : k + 1, pairs:], (8, pairs)) for k in range(3)]
    row = lax.broadcasted_iota(jnp.int32, (8, pairs), 0)

    def turned(vector, places):
        places = places % (pairs // atoms)
        if places == 0:
            return vector
        return [pltpu.roll(part, pairs - atoms * places, 1) for part in vector]

    def basis(first, second):
        cosine = first[0] * second[0] + first[1] * second[1] + first[2] * second[2]
        series = [jnp.ones_like(cosine), cosine]
        double = cosine + cosine
        for _ in range(7):
            series.append(double * series[-1] - series[-2])
        lower = series[7]
        upper = series[1]
        for index in range(1, 8):
            lower = jnp.where(row == index, series[7 - index], lower)
            upper = jnp.where(row == index, series[1 + index], upper)
        double = series[8] + series[8]
        blocks = [lower, upper]
        for _ in range(degrees // 8 - 1):
            blocks.append(double * blocks[-1] - blocks[-2])
        return blocks[1:]

    for diagonal in range(slots):
        places = diagonal // 2
        if diagonal % 2 == 0:
            blocks = basis(even, turned(even, places)) + basis(odd, turned(odd, places))
        else:
            blocks = basis(even, turned(odd, places)) + basis(odd, turned(even, places + 1))
        series = jnp.concatenate(blocks, axis=0).T.astype(BF16)
        angular_ref[diagonal] = jnp.dot(series, weight, preferred_element_type=F32)
    for copy in copies:
        copy.wait()
    prepare_weights(slots, held, results)


def prepare_weights(slots, held, results):
    bond_in_ref, bond_mix_ref, pair_ref, pair_hidden_ref, pair_out_ref, atom_in_ref = held[:6]
    atom_out_ref = held[6]
    bond_weight_ref, mix_weight_ref, pair_weight_ref, hidden_weight_ref = results[:4]
    out_weight_ref, atom_in_weight_ref, sum_weight_ref, atom_out_weight_ref = results[4:]
    feature = bond_mix_ref.shape[0]
    weight = bond_in_ref[...].astype(F32)
    source, other, bond_part = (weight[k * feature : (k + 1) * feature] for k in range(3))
    blank = jnp.zeros_like(source)
    away = [crossed(bond_part, blank), crossed(source, other)]
    near = [crossed(other, source), crossed(blank, bond_part)]
    bond_weight_ref[...] = jnp.concatenate(away + near, axis=0).astype(BF16)
    mix_weight_ref[...] = diagonal_blocks(bond_mix_ref[...].astype(F32)).astype(BF16)
    old = pair_ref[...].astype(F32) * 0.5
    hidden = jnp.dot(bond_mix_ref[...], pair_ref[...], preferred_element_type=F32) * 0.5
    weight = jnp.concatenate([hidden, hidden, old, old], axis=0).astype(BF16)
    pair_weight_ref[...] = jnp.concatenate(
        [two_blocks(weight[:, : 2 * feature]), two_blocks(weight[:, 2 * feature :])], axis=1
    )
    hidden_weight_ref[...] = two_blocks(pair_hidden_ref[...].astype(F32)).astype(BF16)
    out_weight_ref[...] = diagonal_blocks(pair_out_ref[...].astype(F32)).astype(BF16)
    weight = atom_in_ref[...].astype(F32)
    weight = crossed(weight, jnp.zeros_like(weight))
    mean = weight[feature:] * (1.0 / slots)
    atom_in_weight_ref[...] = jnp.concatenate([weight[:feature], mean, mean], axis=0).astype(BF16)
    folded = jnp.dot(
        pair_out_ref[...], mean.astype(BF16), preferred_element_type=F32
    )
    high = folded.astype(BF16)
    low = (folded - high.astype(F32)).astype(BF16)
    sum_weight_ref[...] = jnp.concatenate([high, high, low, low], axis=0)
    weight = atom_out_ref[...].astype(F32)
    blank = jnp.zeros_like(weight)
    weight = jnp.concatenate([weight, blank], axis=1)
    atom_out_weight_ref[...] = jnp.concatenate([weight, jnp.zeros_like(weight)], axis=0).astype(
        BF16
    )


def prepare_kernel(
    extents,
    paired,
    spot_ref,
    targets_ref,
    atom_ref,
    bond_ref,
    dirs_hbm,
    angle_hbm,
    near_ref,
    chosen_ref,
    right_ref,
    own_ref,
    dirs_ref,
    angle_ref,
    sems,
):
    copies = [
        pltpu.make_async_copy(source, target, sems.at[k])
        for k, (source, target) in enumerate(((dirs_hbm, dirs_ref), (angle_hbm, angle_ref)))
    ]
    for copy in copies:
        copy.start()
    atoms, feature = atom_ref.shape[2], atom_ref.shape[3]
    slots = targets_ref.shape[0]
    bonds = slots * atoms
    near_ref[: 3 * CAP // 2] = packed_rows(spot_ref[...], bond_ref, slots, 3 * CAP // 2)
    near_ref[3 * CAP // 2 :] = atom_rows(atom_ref)
    targets = bond_row(targets_ref[...])
    code_x, code_y = bond_codes(targets, atoms, extents, paired, True)
    code = 3 * code_x + code_y
    bond = lax.broadcasted_iota(jnp.int32, (1, bonds), 1)
    far_slot = slots - 1 - slot_at(quotient(bond, atoms), slots)
    far_atom = remainder(targets, atoms)
    far = (remainder(far_slot, 2) * (slots // 2) + quotient(far_slot, 2)) * atoms + far_atom
    base = (code * bonds).astype(F32)
    key = base + far.astype(F32)

    def column(values):
        return jnp.broadcast_to(values.astype(F32), (128, bonds)).T

    keys = column(key)
    place = []
    for group in range(bonds // 128):
        here = slice(group * 128, (group + 1) * 128)
        inside = (keys < key[:, here]) & (keys >= base[:, here])
        place.append(jnp.sum(jnp.where(inside, 1.0, 0.0), axis=0, keepdims=True))
    place = jnp.concatenate(place, axis=1).astype(jnp.int32)
    half, tall = CAP // 2, atoms // 2
    bond_spot = column(half * code + remainder(place, half))
    atom_spot = column(9 * half + tall * code + remainder(far_atom, tall))
    right = (column(quotient(place, half)), column(quotient(far_atom, tall)))
    right_ref[...] = jnp.where(left_lanes((bonds, 128)), right[0], right[1])
    total = 9 * half + 9 * tall
    for start in range(0, total, 128):
        width = min(128, total - start)
        spot = lax.broadcasted_iota(jnp.int32, (bonds, 128), 1).astype(F32) + float(start)
        chosen = jnp.where((spot == bond_spot) | (spot == atom_spot), 1.0, 0.0).astype(BF16)
        chosen_ref[:, start : start + width] = chosen[:, :width]

    atom = atom_ref[0, 0]
    blocks = blocks_of(bond_ref, slots // 2)
    own = [jnp.concatenate([atom, x[:, :feature]], axis=1) for x in blocks]
    own += [jnp.concatenate([atom, x[:, feature:]], axis=1) for x in blocks]
    own = jnp.concatenate(own, axis=0)
    own_ref[...] = own
    for copy in copies:
        copy.wait()


def gated(values):
    half = values.shape[1] // 2
    first, second = values[:, :half], values[:, half:]
    return first * jax.nn.sigmoid(first) * jax.nn.sigmoid(second)


def main_kernel(
    near_ref,
    up_ref,
    down_ref,
    two_ref,
    one_ref,
    angular_ref,
    chosen_ref,
    right_ref,
    own_ref,
    bond_weight_ref,
    mix_weight_ref,
    pair_weight_ref,
    hidden_weight_ref,
    out_weight_ref,
    atom_in_weight_ref,
    sum_weight_ref,
    atom_out_weight_ref,
    atom_result_hbm,
    bond_result_hbm,
    atom_result_ref,
    bond_result_ref,
    first_ref,
    second_ref,
    pair_ref,
    sems,
):
    slots, pairs, _ = angular_ref.shape
    bonds = 2 * pairs
    atoms = bonds // slots
    feature = own_ref.shape[1] // 2
    width = 2 * feature
    half = CAP // 2
    near_refs = (near_ref, up_ref, down_ref)
    away_refs = (one_ref, two_ref)
    sent = [ref[:half] for ref in near_refs] + [ref[: 3 * half] for ref in away_refs]
    sent = jnp.concatenate(sent, axis=0)
    sent_atom = jnp.concatenate([ref[3 * half :] for ref in near_refs + away_refs], axis=0)
    blank = jnp.zeros((sent.shape[0], feature), BF16)
    blank_atom = jnp.zeros((sent_atom.shape[0], feature), BF16)
    received = jnp.concatenate(
        [
            jnp.concatenate([sent[:, :feature], blank, sent[:, feature:], blank], axis=1),
            jnp.concatenate(
                [blank_atom, sent_atom[:, :feature], blank_atom, sent_atom[:, feature:]], axis=1
            ),
        ],
        axis=0,
    )
    far = jnp.dot(chosen_ref[...], received, preferred_element_type=F32)
    far = jnp.where(right_ref[...] > 0.0, far[:, width:], far[:, :width])
    own = own_ref[...]
    incoming = jnp.dot(
        jnp.concatenate([far.astype(BF16), own], axis=1),
        bond_weight_ref[...],
        preferred_element_type=F32,
    )
    hidden = gated(incoming).astype(BF16)
    old = jnp.where(left_lanes((bonds, width)), far, own.astype(F32))
    both = jnp.concatenate([hidden, old.astype(BF16)], axis=1)
    even, odd = both[:pairs], both[pairs:]
    projected = jnp.dot(
        jnp.concatenate([even, odd], axis=1), pair_weight_ref[...], preferred_element_type=F32
    )
    first_ref[...] = projected[:, : 2 * width]
    second_ref[0] = projected[:, 2 * width :]
    shifted = jnp.concatenate([even[atoms:], even[:atoms]], axis=0)
    second_ref[1] = jnp.dot(
        jnp.concatenate([odd, shifted], axis=1),
        pair_weight_ref[:, 2 * width :],
        preferred_element_type=F32,
    )
    mixed = jnp.dot(hidden, mix_weight_ref[...], preferred_element_type=F32)
    new = (old + mixed).astype(BF16).astype(F32)
    average = ((new + pltpu.roll(new, feature, 1)) * 0.5).astype(BF16).astype(F32)
    packed = jnp.where(left_lanes((pairs, width)), average[:pairs], average[pairs:])
    group = 2

    def first_gates(base):
        for start in range(0, pairs, atoms):
            here = first_ref[pl.ds(start, atoms)]
            for diagonal in range(base, base + group):
                there = (start + diagonal // 2 * atoms) % pairs
                mixture = angular_ref[diagonal, pl.ds(start, atoms)] + (
                    here + second_ref[diagonal % 2, pl.ds(there, atoms)]
                )
                pair_ref[pl.ds(diagonal * pairs + start, atoms)] = gated(mixture).astype(
                    BF16
                )

    def summed(rows):
        parts = [rows[k * atoms : (k + 1) * atoms] for k in range(slots // 2)]
        while len(parts) > 1:
            parts = [x + y for x, y in zip(parts[::2], parts[1::2])]
        return parts[0]

    atom = own[0:atoms]
    atom_incoming = jnp.dot(
        jnp.concatenate([atom[:, :feature], summed(packed).astype(BF16)], axis=1),
        atom_in_weight_ref[...],
        preferred_element_type=F32,
    )
    total = jnp.zeros((pairs, width), F32)
    first_gates(0)
    for base in range(0, slots, group):
        if base + group < slots:
            first_gates(base + group)
        second = jnp.dot(
            pair_ref[pl.ds(base * pairs, group * pairs)],
            hidden_weight_ref[...],
            preferred_element_type=F32,
        )
        gates = gated(second)
        for k in range(group):
            total = total + gates[k * pairs : (k + 1) * pairs]
    bond_out = packed + jnp.dot(
        total.astype(BF16), out_weight_ref[...], preferred_element_type=F32
    )
    bond_out = bond_out.astype(BF16)
    for k in range(slots // 2):
        bond_result_ref[0, 0, :, k * width : (k + 1) * width] = bond_out[
            k * atoms : (k + 1) * atoms
        ]
    copies = [pltpu.make_async_copy(bond_result_ref, bond_result_hbm, sems.at[0])]
    copies[0].start()
    sums = summed(total).astype(BF16)
    atom_incoming = atom_incoming + jnp.dot(
        jnp.concatenate([sums, sums], axis=1), sum_weight_ref[...], preferred_element_type=F32
    )
    atom_hidden = gated(atom_incoming).astype(BF16)
    atom_new = atom.astype(F32) + jnp.dot(
        atom_hidden, atom_out_weight_ref[...], preferred_element_type=F32
    )
    atom_result_ref[0, 0] = atom_new[:, :feature].astype(BF16)
    copies.append(pltpu.make_async_copy(atom_result_ref, atom_result_hbm, sems.at[1]))
    copies[-1].start()
    for copy in copies:
        copy.wait()


def per_device(
    atom_feat,
    bond_feat,
    neighbours,
    bond_dirs,
    bond_in_weight,
    bond_mix_weight,
    pair_weight,
    angle_weight,
    pair_hidden_weight,
    pair_out_weight,
    atom_in_weight,
    atom_out_weight,
):
    atoms, feature = atom_feat.shape[2], atom_feat.shape[3]
    slots = neighbours.shape[3]
    bonds = atoms * slots
    pairs = bonds // 2
    half = CAP // 2
    extents = (lax.axis_size("gx"), lax.axis_size("gy"))
    paired = (extents[0] % 2 == 0, False)
    targets = neighbours[0, 0].T
    hbm = pl.BlockSpec(memory_space=pltpu.HBM)
    vmem = pl.BlockSpec(memory_space=pltpu.VMEM)
    params = pltpu.CompilerParams(vmem_limit_bytes=32 * 2**20)

    def shaped(shape, dtype):
        return jax.ShapeDtypeStruct(shape, dtype)

    def in_hbm(arrays):
        return tuple(pltpu.with_memory_space_constraint(x, pltpu.HBM) for x in arrays)

    payload = shaped((3 * half + atoms // 2, 2 * feature), BF16)
    inputs = (targets, atom_feat, bond_feat)
    up, down, *held = pl.pallas_call(
        functools.partial(pack_kernel, extents, paired),
        out_shape=(payload, payload, shaped((1, bonds), jnp.int32))
        + tuple(shaped(x.shape, x.dtype) for x in inputs),
        in_specs=[hbm] * 3,
        out_specs=(vmem,) * 6,
        scratch_shapes=[pltpu.SemaphoreType.DMA((3,))],
        compiler_params=params,
        name="pack",
    )(*in_hbm(inputs))
    first, second = moves(extents[1], paired[1])
    up = lax.ppermute(up, "gy", first)
    down = lax.ppermute(down, "gy", second)
    weights = (bond_in_weight, bond_mix_weight, pair_weight, pair_hidden_weight)
    weights += (pair_out_weight, atom_in_weight, atom_out_weight)
    near, *prepared, bond_dirs, angle_weight = pl.pallas_call(
        functools.partial(prepare_kernel, extents, paired),
        out_shape=(
            payload,
            shaped((bonds, 9 * half + 9 * atoms // 2), BF16),
            shaped((bonds, 2 * feature), F32),
            shaped((bonds, 2 * feature), BF16),
            shaped(bond_dirs.shape, F32),
            shaped(angle_weight.shape, BF16),
        ),
        in_specs=[vmem] * 4 + [hbm] * 2,
        out_specs=(vmem,) * 6,
        scratch_shapes=[pltpu.SemaphoreType.DMA((2,))],
        compiler_params=params,
        cost_estimate=pl.CostEstimate(flops=64 * 2**20, bytes_accessed=2**21, transcendentals=0),
        name="prepare",
    )(*held, *in_hbm((bond_dirs, angle_weight)))
    near, up, down, prepared = lax.optimization_barrier((near, up, down, prepared))
    first, second = moves(extents[0], paired[0])

    def forwarded(block):
        parts = [x[block * half : (block + 1) * half] for x in (near, up, down)]
        return jnp.concatenate(parts + [x[3 * half :] for x in (near, up, down)], axis=0)

    one = lax.ppermute(forwarded(1), "gx", first)
    two = lax.ppermute(forwarded(2), "gx", second)
    angular, *made = pl.pallas_call(
        functools.partial(angular_kernel, atoms),
        out_shape=(
            shaped((slots, pairs, 4 * feature), F32),
            shaped((4 * feature, 4 * feature), BF16),
            shaped((2 * feature, 2 * feature), BF16),
            shaped((8 * feature, 8 * feature), BF16),
            shaped((2 * feature, 4 * feature), BF16),
            shaped((2 * feature, 2 * feature), BF16),
            shaped((3 * feature, 4 * feature), BF16),
            shaped((4 * feature, 4 * feature), BF16),
            shaped((2 * feature, 2 * feature), BF16),
        ),
        in_specs=[vmem] * 2 + [hbm] * 7,
        out_specs=(vmem,) * 9,
        scratch_shapes=[pltpu.VMEM(x.shape, BF16) for x in weights]
        + [pltpu.SemaphoreType.DMA((7,))],
        compiler_params=params,
        cost_estimate=pl.CostEstimate(
            flops=256 * 2**20, bytes_accessed=2**22, transcendentals=4096
        ),
        name="angular",
    )(bond_dirs, angle_weight, *in_hbm(weights))
    return pl.pallas_call(
        main_kernel,
        out_shape=(shaped(atom_feat.shape, BF16), shaped(bond_feat.shape, BF16)),
        in_specs=[vmem] * 17,
        out_specs=(hbm, hbm),
        scratch_shapes=[
            pltpu.VMEM(atom_feat.shape, BF16),
            pltpu.VMEM(bond_feat.shape, BF16),
            pltpu.VMEM((pairs, 4 * feature), F32),
            pltpu.VMEM((2, pairs, 4 * feature), F32),
            pltpu.VMEM((slots * pairs, 2 * feature), BF16),
            pltpu.SemaphoreType.DMA((2,)),
        ],
        compiler_params=params,
        name="main",
    )(near, up, down, two, one, angular, *prepared, *made)


def solution(mesh):
    placed = (
        P("gx", "gy", None, None),
        P("gx", "gy", None, None),
        P("gx", "gy", None, None),
        P(None, "gx", "gy", None),
        P(),
        P(),
        P(),
        P(),
        P(),
        P(),
        P(),
        P(),
    )
    return jax.shard_map(
        per_device,
        mesh=mesh,
        in_specs=placed,
        out_specs=(P("gx", "gy", None, None), P("gx", "gy", None, None)),
        check_vma=False,
    )
```

```python
import functools

import jax
import jax.numpy as jnp
from jax import lax
from jax.experimental import pallas as pl
from jax.experimental.pallas import tpu as pltpu
from jax.sharding import PartitionSpec as P

F32 = jnp.float32
BF16 = jnp.bfloat16
CAP = 64


def quotient(values, size):
    if size & (size - 1) == 0:
        return values >> (size.bit_length() - 1)
    return lax.div(values, jnp.int32(size))


def remainder(values, size):
    if size & (size - 1) == 0:
        return values & (size - 1)
    return lax.rem(values, jnp.int32(size))


def step_code(owner, home, extent, paired, receives):
    step = remainder(owner - home + 1 + extent, extent)
    if paired:
        ahead = jnp.where(remainder(home, 2) == 0, 0, 2)
    else:
        ahead = 0 if receives else 2
    return jnp.where(step == 1, 0, jnp.where(step == ahead, 1, 2))


def moves(extent, paired):
    if paired:
        near = [(i, i ^ 1) for i in range(extent)]
        return [(i, (((i + 1) ^ 1) - 1) % extent) for i in range(extent)], near
    up = [(i, (i + 1) % extent) for i in range(extent)]
    return up, [(j, i) for i, j in up]


def slot_at(position, slots):
    half = slots // 2
    return jnp.where(position < half, 2 * position, 2 * (position - half) + 1)


def bond_row(table):
    slots, atoms = table.shape
    per_group = 128 // atoms
    tiled = jnp.concatenate([table.astype(F32)] * per_group, axis=1)
    row = lax.broadcasted_iota(jnp.int32, tiled.shape, 0)
    position = quotient(lax.broadcasted_iota(jnp.int32, tiled.shape, 1), atoms)
    pieces = []
    for group in range(slots // per_group):
        chosen = row == slot_at(position + group * per_group, slots)
        pieces.append(jnp.sum(jnp.where(chosen, tiled, 0.0), axis=0, keepdims=True))
    return jnp.concatenate(pieces, axis=1).astype(jnp.int32)


def bond_codes(targets, atoms, extents, paired, receives):
    owner = quotient(targets, atoms)
    block = (quotient(owner, extents[1]), remainder(owner, extents[1]))
    return tuple(
        step_code(block[k], lax.axis_index(axis), extents[k], paired[k], receives)
        for k, axis in enumerate(("gx", "gy"))
    )


def left_lanes(shape):
    return lax.broadcasted_iota(jnp.int32, shape, 1) < shape[1] // 2


def swapped(rows):
    half = rows.shape[1] // 2
    return jnp.concatenate([rows[:, half:], rows[:, :half]], axis=1)


def blocks_of(bond_ref, pairs):
    width = bond_ref.shape[3] // pairs
    return [bond_ref[0, 0, :, k * width : (k + 1) * width] for k in range(pairs)]


def pack_kernel(
    extents,
    paired,
    targets_hbm,
    atom_hbm,
    bond_hbm,
    up_ref,
    down_ref,
    spot_ref,
    targets_ref,
    atom_ref,
    bond_ref,
    sems,
):
    sources = ((targets_hbm, targets_ref), (bond_hbm, bond_ref), (atom_hbm, atom_ref))
    copies = [
        pltpu.make_async_copy(source, target, sems.at[k])
        for k, (source, target) in enumerate(sources)
    ]
    for copy in copies:
        copy.start()
    atoms, feature = atom_ref.shape[2], atom_ref.shape[3]
    slots = targets_ref.shape[0]
    bonds = slots * atoms
    lanes = 128
    groups = bonds // lanes
    copies[0].wait()
    code_x, code_y = bond_codes(bond_row(targets_ref[...]), atoms, extents, paired, False)
    code = 3 * code_y + code_x
    rows = lax.broadcasted_iota(jnp.int32, (16, lanes), 0)
    marks = [rows == code[:, g * lanes : (g + 1) * lanes] for g in range(groups)]
    stacked = jnp.concatenate([m.astype(F32) for m in marks], axis=0).astype(BF16)
    before = lax.broadcasted_iota(jnp.int32, (lanes, 2 * lanes), 0)
    after = lax.broadcasted_iota(jnp.int32, (lanes, 2 * lanes), 1)
    sums = jnp.where((before < after) | (after >= lanes), 1.0, 0.0).astype(BF16)
    counted = jnp.dot(stacked, sums, preferred_element_type=F32)
    place = []
    earlier = jnp.zeros((16, lanes), F32)
    for g in range(groups):
        part = counted[g * 16 : (g + 1) * 16]
        place.append(
            jnp.sum(jnp.where(marks[g], part[:, :lanes] + earlier, 0.0), axis=0, keepdims=True)
        )
        earlier = earlier + part[:, lanes:]
    place = jnp.concatenate(place, axis=1).astype(jnp.int32)
    half = CAP // 2
    right = quotient(place, half)
    spot = place - half * right + half * code
    spot_ref[...] = jnp.where(code < 3, spot + 3 * half * right, -1)
    wanted = jnp.where(code < 3, -1, spot - 3 * half + 6 * half * right)
    copies[1].wait()
    copies[2].wait()
    packed = packed_rows(wanted, bond_ref, slots, 6 * half)
    for k, ref in enumerate((up_ref, down_ref)):
        ref[: 3 * half] = packed[3 * half * k : 3 * half * (k + 1)]
        ref[3 * half :] = atom_rows(atom_ref)


def packed_rows(wanted, bond_ref, slots, count):
    spot = lax.broadcasted_iota(jnp.int32, (2 * count, wanted.shape[1]), 0)
    chosen = jnp.where(spot == wanted, 1.0, 0.0).astype(BF16)
    blocks = blocks_of(bond_ref, slots // 2)
    feature = blocks[0].shape[1] // 2
    values = [x[:, :feature] for x in blocks] + [x[:, feature:] for x in blocks]
    packed = jnp.dot(chosen, jnp.concatenate(values, axis=0), preferred_element_type=F32)
    return jnp.concatenate([packed[:count], packed[count:]], axis=1).astype(BF16)


def atom_rows(atom_ref):
    atom = atom_ref[0, 0]
    half = atom.shape[0] // 2
    return jnp.concatenate([atom[:half], atom[half:]], axis=1)


def crossed(left, right):
    half = left.shape[1] // 2
    parts = [left[:, :half], right[:, :half], left[:, half:], right[:, half:]]
    return jnp.concatenate(parts, axis=1)


def two_blocks(weight):
    blank = jnp.zeros_like(weight)
    return jnp.concatenate([crossed(weight, blank), crossed(blank, weight)], axis=0)


def diagonal_blocks(weight):
    blank = jnp.zeros_like(weight)
    return jnp.concatenate(
        [jnp.concatenate([weight, blank], axis=1), jnp.concatenate([blank, weight], axis=1)],
        axis=0,
    )


def angular_kernel(atoms, dirs_ref, angle_ref, *refs):
    sources, angular_ref, results, held, sems = refs[:7], refs[7], refs[8:16], refs[16:23], refs[23]
    copies = [
        pltpu.make_async_copy(source, target, sems.at[k])
        for k, (source, target) in enumerate(zip(sources, held))
    ]
    for copy in copies:
        copy.start()
    slots, pairs, _ = angular_ref.shape
    bonds = 2 * pairs
    degrees = angle_ref.shape[0]
    weight = two_blocks(angle_ref[...].astype(F32)).astype(BF16)
    polar, azimuth = dirs_ref[0, 0], dirs_ref[1, 0]
    unit = jnp.concatenate(
        [
            jnp.sin(polar) * jnp.cos(azimuth),
            jnp.sin(polar) * jnp.sin(azimuth),
            jnp.cos(polar),
            jnp.zeros((5, bonds), F32),
        ],
        axis=0,
    )
    high = unit.astype(BF16).astype(F32)
    middle = (unit - high).astype(BF16).astype(F32)
    parts = jnp.concatenate([high, middle, unit - high - middle], axis=0).astype(BF16)
    bond = lax.broadcasted_iota(jnp.int32, (1, bonds), 1)
    source = remainder(bond, atoms) * slots + slot_at(quotient(bond, atoms), slots)
    spot = lax.broadcasted_iota(jnp.int32, (bonds, bonds), 0)
    chosen = jnp.where(spot == source, 1.0, 0.0).astype(BF16)
    unit = jnp.dot(parts, chosen, preferred_element_type=F32)
    unit = unit[0:8] + unit[8:16] + unit[16:24]
    even = [jnp.broadcast_to(unit[k : k + 1, :pairs], (8, pairs)) for k in range(3)]
    odd = [jnp.broadcast_to(unit[k : k + 1, pairs:], (8, pairs)) for k in range(3)]
    row = lax.broadcasted_iota(jnp.int32, (8, pairs), 0)

    def turned(vector, places):
        places = places % (pairs // atoms)
        if places == 0:
            return vector
        return [pltpu.roll(part, pairs - atoms * places, 1) for part in vector]

    def basis(first, second):
        cosine = first[0] * second[0] + first[1] * second[1] + first[2] * second[2]
        series = [jnp.ones_like(cosine), cosine]
        double = cosine + cosine
        for _ in range(7):
            series.append(double * series[-1] - series[-2])
        lower = series[7]
        upper = series[1]
        for index in range(1, 8):
            lower = jnp.where(row == index, series[7 - index], lower)
            upper = jnp.where(row == index, series[1 + index], upper)
        double = series[8] + series[8]
        blocks = [lower, upper]
        for _ in range(degrees // 8 - 1):
            blocks.append(double * blocks[-1] - blocks[-2])
        return blocks[1:]

    for diagonal in range(slots):
        places = diagonal // 2
        if diagonal % 2 == 0:
            blocks = basis(even, turned(even, places)) + basis(odd, turned(odd, places))
        else:
            blocks = basis(even, turned(odd, places)) + basis(odd, turned(even, places + 1))
        series = jnp.concatenate(blocks, axis=0).T.astype(BF16)
        angular_ref[diagonal] = jnp.dot(series, weight, preferred_element_type=F32)
    for copy in copies:
        copy.wait()
    prepare_weights(slots, held, results)


def prepare_weights(slots, held, results):
    bond_in_ref, bond_mix_ref, pair_ref, pair_hidden_ref, pair_out_ref, atom_in_ref = held[:6]
    atom_out_ref = held[6]
    bond_weight_ref, mix_weight_ref, pair_weight_ref, hidden_weight_ref = results[:4]
    out_weight_ref, atom_in_weight_ref, sum_weight_ref, atom_out_weight_ref = results[4:]
    feature = bond_mix_ref.shape[0]
    weight = bond_in_ref[...].astype(F32)
    source, other, bond_part = (weight[k * feature : (k + 1) * feature] for k in range(3))
    blank = jnp.zeros_like(source)
    away = [crossed(bond_part, blank), crossed(source, other)]
    near = [crossed(other, source), crossed(blank, bond_part)]
    bond_weight_ref[...] = jnp.concatenate(away + near, axis=0).astype(BF16)
    mix_weight_ref[...] = diagonal_blocks(bond_mix_ref[...].astype(F32)).astype(BF16)
    old = pair_ref[...].astype(F32) * 0.5
    hidden = jnp.dot(bond_mix_ref[...], pair_ref[...], preferred_element_type=F32) * 0.5
    weight = jnp.concatenate([hidden, hidden, old, old], axis=0).astype(BF16)
    pair_weight_ref[...] = jnp.concatenate(
        [two_blocks(weight[:, : 2 * feature]), two_blocks(weight[:, 2 * feature :])], axis=1
    )
    hidden_weight_ref[...] = two_blocks(two_blocks(pair_hidden_ref[...].astype(F32))).astype(BF16)
    out_weight_ref[...] = diagonal_blocks(pair_out_ref[...].astype(F32)).astype(BF16)
    weight = atom_in_ref[...].astype(F32)
    weight = crossed(weight, jnp.zeros_like(weight))
    mean = weight[feature:] * (1.0 / slots)
    atom_in_weight_ref[...] = jnp.concatenate([weight[:feature], mean, mean], axis=0).astype(BF16)
    folded = jnp.dot(
        pair_out_ref[...], mean.astype(BF16), preferred_element_type=F32
    )
    high = folded.astype(BF16)
    low = (folded - high.astype(F32)).astype(BF16)
    sum_weight_ref[...] = jnp.concatenate([high, high, low, low], axis=0)
    weight = atom_out_ref[...].astype(F32)
    blank = jnp.zeros_like(weight)
    weight = jnp.concatenate([weight, blank], axis=1)
    atom_out_weight_ref[...] = jnp.concatenate([weight, jnp.zeros_like(weight)], axis=0).astype(
        BF16
    )


def prepare_kernel(
    extents,
    paired,
    spot_ref,
    targets_ref,
    atom_ref,
    bond_ref,
    dirs_hbm,
    angle_hbm,
    near_ref,
    chosen_ref,
    right_ref,
    own_ref,
    dirs_ref,
    angle_ref,
    sems,
):
    copies = [
        pltpu.make_async_copy(source, target, sems.at[k])
        for k, (source, target) in enumerate(((dirs_hbm, dirs_ref), (angle_hbm, angle_ref)))
    ]
    for copy in copies:
        copy.start()
    atoms, feature = atom_ref.shape[2], atom_ref.shape[3]
    slots = targets_ref.shape[0]
    bonds = slots * atoms
    near_ref[: 3 * CAP // 2] = packed_rows(spot_ref[...], bond_ref, slots, 3 * CAP // 2)
    near_ref[3 * CAP // 2 :] = atom_rows(atom_ref)
    targets = bond_row(targets_ref[...])
    code_x, code_y = bond_codes(targets, atoms, extents, paired, True)
    code = 3 * code_x + code_y
    bond = lax.broadcasted_iota(jnp.int32, (1, bonds), 1)
    far_slot = slots - 1 - slot_at(quotient(bond, atoms), slots)
    far_atom = remainder(targets, atoms)
    far = (remainder(far_slot, 2) * (slots // 2) + quotient(far_slot, 2)) * atoms + far_atom
    base = (code * bonds).astype(F32)
    key = base + far.astype(F32)

    def column(values):
        return jnp.broadcast_to(values.astype(F32), (128, bonds)).T

    keys = column(key)
    place = []
    for group in range(bonds // 128):
        here = slice(group * 128, (group + 1) * 128)
        inside = (keys < key[:, here]) & (keys >= base[:, here])
        place.append(jnp.sum(jnp.where(inside, 1.0, 0.0), axis=0, keepdims=True))
    place = jnp.concatenate(place, axis=1).astype(jnp.int32)
    half, tall = CAP // 2, atoms // 2
    bond_spot = column(half * code + remainder(place, half))
    atom_spot = column(9 * half + tall * code + remainder(far_atom, tall))
    right = (column(quotient(place, half)), column(quotient(far_atom, tall)))
    right_ref[...] = jnp.where(left_lanes((bonds, 128)), right[0], right[1])
    total = 9 * half + 9 * tall
    for start in range(0, total, 128):
        width = min(128, total - start)
        spot = lax.broadcasted_iota(jnp.int32, (bonds, 128), 1).astype(F32) + float(start)
        chosen = jnp.where((spot == bond_spot) | (spot == atom_spot), 1.0, 0.0).astype(BF16)
        chosen_ref[:, start : start + width] = chosen[:, :width]

    atom = atom_ref[0, 0]
    blocks = blocks_of(bond_ref, slots // 2)
    own = [jnp.concatenate([atom, x[:, :feature]], axis=1) for x in blocks]
    own += [jnp.concatenate([atom, x[:, feature:]], axis=1) for x in blocks]
    own = jnp.concatenate(own, axis=0)
    own_ref[...] = own
    for copy in copies:
        copy.wait()


def gated(values):
    half = values.shape[1] // 2
    first, second = values[:, :half], values[:, half:]
    return first * jax.nn.sigmoid(first) * jax.nn.sigmoid(second)


def main_kernel(
    near_ref,
    up_ref,
    down_ref,
    two_ref,
    one_ref,
    angular_ref,
    chosen_ref,
    right_ref,
    own_ref,
    bond_weight_ref,
    mix_weight_ref,
    pair_weight_ref,
    hidden_weight_ref,
    out_weight_ref,
    atom_in_weight_ref,
    sum_weight_ref,
    atom_out_weight_ref,
    atom_result_hbm,
    bond_result_hbm,
    atom_result_ref,
    bond_result_ref,
    first_ref,
    second_ref,
    pair_ref,
    sems,
):
    slots, pairs, _ = angular_ref.shape
    bonds = 2 * pairs
    atoms = bonds // slots
    feature = own_ref.shape[1] // 2
    width = 2 * feature
    half = CAP // 2
    near_refs = (near_ref, up_ref, down_ref)
    away_refs = (one_ref, two_ref)
    sent = [ref[:half] for ref in near_refs] + [ref[: 3 * half] for ref in away_refs]
    sent = jnp.concatenate(sent, axis=0)
    sent_atom = jnp.concatenate([ref[3 * half :] for ref in near_refs + away_refs], axis=0)
    blank = jnp.zeros((sent.shape[0], feature), BF16)
    blank_atom = jnp.zeros((sent_atom.shape[0], feature), BF16)
    received = jnp.concatenate(
        [
            jnp.concatenate([sent[:, :feature], blank, sent[:, feature:], blank], axis=1),
            jnp.concatenate(
                [blank_atom, sent_atom[:, :feature], blank_atom, sent_atom[:, feature:]], axis=1
            ),
        ],
        axis=0,
    )
    far = jnp.dot(chosen_ref[...], received, preferred_element_type=F32)
    far = jnp.where(right_ref[...] > 0.0, far[:, width:], far[:, :width])
    own = own_ref[...]
    incoming = jnp.dot(
        jnp.concatenate([far.astype(BF16), own], axis=1),
        bond_weight_ref[...],
        preferred_element_type=F32,
    )
    hidden = gated(incoming).astype(BF16)
    old = jnp.where(left_lanes((bonds, width)), far, own.astype(F32))
    both = jnp.concatenate([hidden, old.astype(BF16)], axis=1)
    even, odd = both[:pairs], both[pairs:]
    projected = jnp.dot(
        jnp.concatenate([even, odd], axis=1), pair_weight_ref[...], preferred_element_type=F32
    )
    first_ref[...] = projected[:, : 2 * width]
    second_ref[0] = projected[:, 2 * width :]
    shifted = jnp.concatenate([even[atoms:], even[:atoms]], axis=0)
    second_ref[1] = jnp.dot(
        jnp.concatenate([odd, shifted], axis=1),
        pair_weight_ref[:, 2 * width :],
        preferred_element_type=F32,
    )
    mixed = jnp.dot(hidden, mix_weight_ref[...], preferred_element_type=F32)
    new = (old + mixed).astype(BF16).astype(F32)
    average = ((new + pltpu.roll(new, feature, 1)) * 0.5).astype(BF16).astype(F32)
    packed = jnp.where(left_lanes((pairs, width)), average[:pairs], average[pairs:])
    group = 2

    def first_gates(base):
        for start in range(0, pairs, atoms):
            here = first_ref[pl.ds(start, atoms)]
            for diagonal in range(base, base + group):
                there = (start + diagonal // 2 * atoms) % pairs
                mixture = angular_ref[diagonal, pl.ds(start, atoms)] + (
                    here + second_ref[diagonal % 2, pl.ds(there, atoms)]
                )
                pair_ref[pl.ds(diagonal * pairs + start, atoms)] = gated(mixture).astype(
                    BF16
                )

    def summed(rows):
        parts = [rows[k * atoms : (k + 1) * atoms] for k in range(slots // 2)]
        while len(parts) > 1:
            parts = [x + y for x, y in zip(parts[::2], parts[1::2])]
        return parts[0]

    atom = own[0:atoms]
    atom_incoming = jnp.dot(
        jnp.concatenate([atom[:, :feature], summed(packed).astype(BF16)], axis=1),
        atom_in_weight_ref[...],
        preferred_element_type=F32,
    )
    total = jnp.zeros((pairs, width), F32)
    first_gates(0)
    for base in range(0, slots, group):
        if base + group < slots:
            first_gates(base + group)
        beside = [pair_ref[pl.ds((base + k) * pairs, pairs)] for k in range(group)]
        second = jnp.dot(
            jnp.concatenate(beside, axis=1), hidden_weight_ref[...], preferred_element_type=F32
        )
        gates = gated(second)
        total = total + (gates[:, :width] + gates[:, width:])
    bond_out = packed + jnp.dot(
        total.astype(BF16), out_weight_ref[...], preferred_element_type=F32
    )
    bond_out = bond_out.astype(BF16)
    for k in range(slots // 2):
        bond_result_ref[0, 0, :, k * width : (k + 1) * width] = bond_out[
            k * atoms : (k + 1) * atoms
        ]
    copies = [pltpu.make_async_copy(bond_result_ref, bond_result_hbm, sems.at[0])]
    copies[0].start()
    sums = summed(total).astype(BF16)
    atom_incoming = atom_incoming + jnp.dot(
        jnp.concatenate([sums, sums], axis=1), sum_weight_ref[...], preferred_element_type=F32
    )
    atom_hidden = gated(atom_incoming).astype(BF16)
    atom_new = atom.astype(F32) + jnp.dot(
        atom_hidden, atom_out_weight_ref[...], preferred_element_type=F32
    )
    atom_result_ref[0, 0] = atom_new[:, :feature].astype(BF16)
    copies.append(pltpu.make_async_copy(atom_result_ref, atom_result_hbm, sems.at[1]))
    copies[-1].start()
    for copy in copies:
        copy.wait()


def per_device(
    atom_feat,
    bond_feat,
    neighbours,
    bond_dirs,
    bond_in_weight,
    bond_mix_weight,
    pair_weight,
    angle_weight,
    pair_hidden_weight,
    pair_out_weight,
    atom_in_weight,
    atom_out_weight,
):
    atoms, feature = atom_feat.shape[2], atom_feat.shape[3]
    slots = neighbours.shape[3]
    bonds = atoms * slots
    pairs = bonds // 2
    half = CAP // 2
    extents = (lax.axis_size("gx"), lax.axis_size("gy"))
    paired = (extents[0] % 2 == 0, False)
    targets = neighbours[0, 0].T
    hbm = pl.BlockSpec(memory_space=pltpu.HBM)
    vmem = pl.BlockSpec(memory_space=pltpu.VMEM)
    params = pltpu.CompilerParams(vmem_limit_bytes=32 * 2**20)

    def shaped(shape, dtype):
        return jax.ShapeDtypeStruct(shape, dtype)

    def in_hbm(arrays):
        return tuple(pltpu.with_memory_space_constraint(x, pltpu.HBM) for x in arrays)

    payload = shaped((3 * half + atoms // 2, 2 * feature), BF16)
    inputs = (targets, atom_feat, bond_feat)
    up, down, *held = pl.pallas_call(
        functools.partial(pack_kernel, extents, paired),
        out_shape=(payload, payload, shaped((1, bonds), jnp.int32))
        + tuple(shaped(x.shape, x.dtype) for x in inputs),
        in_specs=[hbm] * 3,
        out_specs=(vmem,) * 6,
        scratch_shapes=[pltpu.SemaphoreType.DMA((3,))],
        compiler_params=params,
        name="pack",
    )(*in_hbm(inputs))
    first, second = moves(extents[1], paired[1])
    up = lax.ppermute(up, "gy", first)
    down = lax.ppermute(down, "gy", second)
    weights = (bond_in_weight, bond_mix_weight, pair_weight, pair_hidden_weight)
    weights += (pair_out_weight, atom_in_weight, atom_out_weight)
    near, *prepared, bond_dirs, angle_weight = pl.pallas_call(
        functools.partial(prepare_kernel, extents, paired),
        out_shape=(
            payload,
            shaped((bonds, 9 * half + 9 * atoms // 2), BF16),
            shaped((bonds, 2 * feature), F32),
            shaped((bonds, 2 * feature), BF16),
            shaped(bond_dirs.shape, F32),
            shaped(angle_weight.shape, BF16),
        ),
        in_specs=[vmem] * 4 + [hbm] * 2,
        out_specs=(vmem,) * 6,
        scratch_shapes=[pltpu.SemaphoreType.DMA((2,))],
        compiler_params=params,
        cost_estimate=pl.CostEstimate(flops=64 * 2**20, bytes_accessed=2**21, transcendentals=0),
        name="prepare",
    )(*held, *in_hbm((bond_dirs, angle_weight)))
    near, up, down, prepared = lax.optimization_barrier((near, up, down, prepared))
    first, second = moves(extents[0], paired[0])

    def forwarded(block):
        parts = [x[block * half : (block + 1) * half] for x in (near, up, down)]
        return jnp.concatenate(parts + [x[3 * half :] for x in (near, up, down)], axis=0)

    one = lax.ppermute(forwarded(1), "gx", first)
    two = lax.ppermute(forwarded(2), "gx", second)
    angular, *made = pl.pallas_call(
        functools.partial(angular_kernel, atoms),
        out_shape=(
            shaped((slots, pairs, 4 * feature), F32),
            shaped((4 * feature, 4 * feature), BF16),
            shaped((2 * feature, 2 * feature), BF16),
            shaped((8 * feature, 8 * feature), BF16),
            shaped((4 * feature, 8 * feature), BF16),
            shaped((2 * feature, 2 * feature), BF16),
            shaped((3 * feature, 4 * feature), BF16),
            shaped((4 * feature, 4 * feature), BF16),
            shaped((2 * feature, 2 * feature), BF16),
        ),
        in_specs=[vmem] * 2 + [hbm] * 7,
        out_specs=(vmem,) * 9,
        scratch_shapes=[pltpu.VMEM(x.shape, BF16) for x in weights]
        + [pltpu.SemaphoreType.DMA((7,))],
        compiler_params=params,
        cost_estimate=pl.CostEstimate(
            flops=256 * 2**20, bytes_accessed=2**22, transcendentals=4096
        ),
        name="angular",
    )(bond_dirs, angle_weight, *in_hbm(weights))
    return pl.pallas_call(
        main_kernel,
        out_shape=(shaped(atom_feat.shape, BF16), shaped(bond_feat.shape, BF16)),
        in_specs=[vmem] * 17,
        out_specs=(hbm, hbm),
        scratch_shapes=[
            pltpu.VMEM(atom_feat.shape, BF16),
            pltpu.VMEM(bond_feat.shape, BF16),
            pltpu.VMEM((pairs, 4 * feature), F32),
            pltpu.VMEM((2, pairs, 4 * feature), F32),
            pltpu.VMEM((slots * pairs, 2 * feature), BF16),
            pltpu.SemaphoreType.DMA((2,)),
        ],
        compiler_params=params,
        name="main",
    )(near, up, down, two, one, angular, *prepared, *made)


def solution(mesh):
    placed = (
        P("gx", "gy", None, None),
        P("gx", "gy", None, None),
        P("gx", "gy", None, None),
        P(None, "gx", "gy", None),
        P(),
        P(),
        P(),
        P(),
        P(),
        P(),
        P(),
        P(),
    )
    return jax.shard_map(
        per_device,
        mesh=mesh,
        in_specs=placed,
        out_specs=(P("gx", "gy", None, None), P("gx", "gy", None, None)),
        check_vma=False,
    )
```

```python
import functools

import jax
import jax.numpy as jnp
from jax import lax
from jax.experimental import pallas as pl
from jax.experimental.pallas import tpu as pltpu
from jax.sharding import PartitionSpec as P

F32 = jnp.float32
BF16 = jnp.bfloat16
CAP = 64


def quotient(values, size):
    if size & (size - 1) == 0:
        return values >> (size.bit_length() - 1)
    return lax.div(values, jnp.int32(size))


def remainder(values, size):
    if size & (size - 1) == 0:
        return values & (size - 1)
    return lax.rem(values, jnp.int32(size))


def step_code(owner, home, extent, paired, receives):
    step = remainder(owner - home + 1 + extent, extent)
    if paired:
        ahead = jnp.where(remainder(home, 2) == 0, 0, 2)
    else:
        ahead = 0 if receives else 2
    return jnp.where(step == 1, 0, jnp.where(step == ahead, 1, 2))


def moves(extent, paired):
    if paired:
        near = [(i, i ^ 1) for i in range(extent)]
        return [(i, (((i + 1) ^ 1) - 1) % extent) for i in range(extent)], near
    up = [(i, (i + 1) % extent) for i in range(extent)]
    return up, [(j, i) for i, j in up]


def slot_at(position, slots):
    half = slots // 2
    return jnp.where(position < half, 2 * position, 2 * (position - half) + 1)


def bond_row(table):
    slots, atoms = table.shape
    per_group = 128 // atoms
    tiled = jnp.concatenate([table.astype(F32)] * per_group, axis=1)
    row = lax.broadcasted_iota(jnp.int32, tiled.shape, 0)
    position = quotient(lax.broadcasted_iota(jnp.int32, tiled.shape, 1), atoms)
    pieces = []
    for group in range(slots // per_group):
        chosen = row == slot_at(position + group * per_group, slots)
        pieces.append(jnp.sum(jnp.where(chosen, tiled, 0.0), axis=0, keepdims=True))
    return jnp.concatenate(pieces, axis=1).astype(jnp.int32)


def bond_codes(targets, atoms, extents, paired, receives):
    owner = quotient(targets, atoms)
    block = (quotient(owner, extents[1]), remainder(owner, extents[1]))
    return tuple(
        step_code(block[k], lax.axis_index(axis), extents[k], paired[k], receives)
        for k, axis in enumerate(("gx", "gy"))
    )


def left_lanes(shape):
    return lax.broadcasted_iota(jnp.int32, shape, 1) < shape[1] // 2


def swapped(rows):
    half = rows.shape[1] // 2
    return jnp.concatenate([rows[:, half:], rows[:, :half]], axis=1)


def blocks_of(bond_ref, pairs):
    width = bond_ref.shape[3] // pairs
    return [bond_ref[0, 0, :, k * width : (k + 1) * width] for k in range(pairs)]


def pack_kernel(
    extents,
    paired,
    targets_hbm,
    atom_hbm,
    bond_hbm,
    up_ref,
    down_ref,
    spot_ref,
    targets_ref,
    atom_ref,
    bond_ref,
    sems,
):
    sources = ((targets_hbm, targets_ref), (bond_hbm, bond_ref), (atom_hbm, atom_ref))
    copies = [
        pltpu.make_async_copy(source, target, sems.at[k])
        for k, (source, target) in enumerate(sources)
    ]
    for copy in copies:
        copy.start()
    atoms, feature = atom_ref.shape[2], atom_ref.shape[3]
    slots = targets_ref.shape[0]
    bonds = slots * atoms
    lanes = 128
    groups = bonds // lanes
    copies[0].wait()
    code_x, code_y = bond_codes(bond_row(targets_ref[...]), atoms, extents, paired, False)
    code = 3 * code_y + code_x
    rows = lax.broadcasted_iota(jnp.int32, (16, lanes), 0)
    marks = [rows == code[:, g * lanes : (g + 1) * lanes] for g in range(groups)]
    stacked = jnp.concatenate([m.astype(F32) for m in marks], axis=0).astype(BF16)
    before = lax.broadcasted_iota(jnp.int32, (lanes, 2 * lanes), 0)
    after = lax.broadcasted_iota(jnp.int32, (lanes, 2 * lanes), 1)
    sums = jnp.where((before < after) | (after >= lanes), 1.0, 0.0).astype(BF16)
    counted = jnp.dot(stacked, sums, preferred_element_type=F32)
    place = []
    earlier = jnp.zeros((16, lanes), F32)
    for g in range(groups):
        part = counted[g * 16 : (g + 1) * 16]
        place.append(
            jnp.sum(jnp.where(marks[g], part[:, :lanes] + earlier, 0.0), axis=0, keepdims=True)
        )
        earlier = earlier + part[:, lanes:]
    place = jnp.concatenate(place, axis=1).astype(jnp.int32)
    half = CAP // 2
    right = quotient(place, half)
    spot = place - half * right + half * code
    spot_ref[...] = jnp.where(code < 3, spot + 3 * half * right, -1)
    wanted = jnp.where(code < 3, -1, spot - 3 * half + 6 * half * right)
    copies[1].wait()
    copies[2].wait()
    packed = packed_rows(wanted, bond_ref, slots, 6 * half)
    for k, ref in enumerate((up_ref, down_ref)):
        ref[: 3 * half] = packed[3 * half * k : 3 * half * (k + 1)]
        ref[3 * half :] = atom_rows(atom_ref)


def packed_rows(wanted, bond_ref, slots, count):
    spot = lax.broadcasted_iota(jnp.int32, (2 * count, wanted.shape[1]), 0)
    chosen = jnp.where(spot == wanted, 1.0, 0.0).astype(BF16)
    blocks = blocks_of(bond_ref, slots // 2)
    feature = blocks[0].shape[1] // 2
    values = [x[:, :feature] for x in blocks] + [x[:, feature:] for x in blocks]
    packed = jnp.dot(chosen, jnp.concatenate(values, axis=0), preferred_element_type=F32)
    return jnp.concatenate([packed[:count], packed[count:]], axis=1).astype(BF16)


def atom_rows(atom_ref):
    atom = atom_ref[0, 0]
    half = atom.shape[0] // 2
    return jnp.concatenate([atom[:half], atom[half:]], axis=1)


def crossed(left, right):
    half = left.shape[1] // 2
    parts = [left[:, :half], right[:, :half], left[:, half:], right[:, half:]]
    return jnp.concatenate(parts, axis=1)


def two_blocks(weight):
    blank = jnp.zeros_like(weight)
    return jnp.concatenate([crossed(weight, blank), crossed(blank, weight)], axis=0)


def diagonal_blocks(weight):
    blank = jnp.zeros_like(weight)
    return jnp.concatenate(
        [jnp.concatenate([weight, blank], axis=1), jnp.concatenate([blank, weight], axis=1)],
        axis=0,
    )


def angular_kernel(atoms, dirs_ref, angle_ref, *refs):
    sources, angular_ref, results, held, sems = refs[:7], refs[7], refs[8:16], refs[16:23], refs[23]
    copies = [
        pltpu.make_async_copy(source, target, sems.at[k])
        for k, (source, target) in enumerate(zip(sources, held))
    ]
    for copy in copies:
        copy.start()
    slots, pairs, _ = angular_ref.shape
    bonds = 2 * pairs
    degrees = angle_ref.shape[0]
    weight = two_blocks(angle_ref[...].astype(F32)).astype(BF16)
    polar, azimuth = dirs_ref[0, 0], dirs_ref[1, 0]
    unit = jnp.concatenate(
        [
            jnp.sin(polar) * jnp.cos(azimuth),
            jnp.sin(polar) * jnp.sin(azimuth),
            jnp.cos(polar),
            jnp.zeros((5, bonds), F32),
        ],
        axis=0,
    )
    high = unit.astype(BF16).astype(F32)
    middle = (unit - high).astype(BF16).astype(F32)
    parts = jnp.concatenate([high, middle, unit - high - middle], axis=0).astype(BF16)
    bond = lax.broadcasted_iota(jnp.int32, (1, bonds), 1)
    source = remainder(bond, atoms) * slots + slot_at(quotient(bond, atoms), slots)
    spot = lax.broadcasted_iota(jnp.int32, (bonds, bonds), 0)
    chosen = jnp.where(spot == source, 1.0, 0.0).astype(BF16)
    unit = jnp.dot(parts, chosen, preferred_element_type=F32)
    unit = unit[0:8] + unit[8:16] + unit[16:24]
    even = [jnp.broadcast_to(unit[k : k + 1, :pairs], (8, pairs)) for k in range(3)]
    odd = [jnp.broadcast_to(unit[k : k + 1, pairs:], (8, pairs)) for k in range(3)]
    row = lax.broadcasted_iota(jnp.int32, (8, pairs), 0)

    def turned(vector, places):
        places = places % (pairs // atoms)
        if places == 0:
            return vector
        return [pltpu.roll(part, pairs - atoms * places, 1) for part in vector]

    def basis(first, second):
        cosine = first[0] * second[0] + first[1] * second[1] + first[2] * second[2]
        series = [jnp.ones_like(cosine), cosine]
        double = cosine + cosine
        for _ in range(7):
            series.append(double * series[-1] - series[-2])
        lower = series[7]
        upper = series[1]
        for index in range(1, 8):
            lower = jnp.where(row == index, series[7 - index], lower)
            upper = jnp.where(row == index, series[1 + index], upper)
        double = series[8] + series[8]
        blocks = [lower, upper]
        for _ in range(degrees // 8 - 1):
            blocks.append(double * blocks[-1] - blocks[-2])
        return blocks[1:]

    for diagonal in range(slots):
        places = diagonal // 2
        if diagonal % 2 == 0:
            blocks = basis(even, turned(even, places)) + basis(odd, turned(odd, places))
        else:
            blocks = basis(even, turned(odd, places)) + basis(odd, turned(even, places + 1))
        series = jnp.concatenate(blocks, axis=0).T.astype(BF16)
        angular_ref[diagonal] = jnp.dot(series, weight, preferred_element_type=F32)
    for copy in copies:
        copy.wait()
    prepare_weights(slots, held, results)


def prepare_weights(slots, held, results):
    bond_in_ref, bond_mix_ref, pair_ref, pair_hidden_ref, pair_out_ref, atom_in_ref = held[:6]
    atom_out_ref = held[6]
    bond_weight_ref, mix_weight_ref, pair_weight_ref, hidden_weight_ref = results[:4]
    out_weight_ref, atom_in_weight_ref, sum_weight_ref, atom_out_weight_ref = results[4:]
    feature = bond_mix_ref.shape[0]
    weight = bond_in_ref[...].astype(F32)
    source, other, bond_part = (weight[k * feature : (k + 1) * feature] for k in range(3))
    blank = jnp.zeros_like(source)
    away = [crossed(bond_part, blank), crossed(source, other)]
    near = [crossed(other, source), crossed(blank, bond_part)]
    bond_weight_ref[...] = jnp.concatenate(away + near, axis=0).astype(BF16)
    mix_weight_ref[...] = diagonal_blocks(bond_mix_ref[...].astype(F32)).astype(BF16)
    old = pair_ref[...].astype(F32) * 0.5
    hidden = jnp.dot(bond_mix_ref[...], pair_ref[...], preferred_element_type=F32) * 0.5
    pair_weight_ref[...] = jnp.concatenate([hidden, hidden, old, old], axis=0).astype(BF16)
    hidden_weight_ref[...] = two_blocks(pair_hidden_ref[...].astype(F32)).astype(BF16)
    out_weight_ref[...] = diagonal_blocks(pair_out_ref[...].astype(F32)).astype(BF16)
    weight = atom_in_ref[...].astype(F32)
    weight = crossed(weight, jnp.zeros_like(weight))
    mean = weight[feature:] * (1.0 / slots)
    atom_in_weight_ref[...] = jnp.concatenate([weight[:feature], mean, mean], axis=0).astype(BF16)
    folded = jnp.dot(
        pair_out_ref[...], mean.astype(BF16), preferred_element_type=F32
    )
    high = folded.astype(BF16)
    low = (folded - high.astype(F32)).astype(BF16)
    sum_weight_ref[...] = jnp.concatenate([high, high, low, low], axis=0)
    weight = atom_out_ref[...].astype(F32)
    blank = jnp.zeros_like(weight)
    weight = jnp.concatenate([weight, blank], axis=1)
    atom_out_weight_ref[...] = jnp.concatenate([weight, jnp.zeros_like(weight)], axis=0).astype(
        BF16
    )


def prepare_kernel(
    extents,
    paired,
    spot_ref,
    targets_ref,
    atom_ref,
    bond_ref,
    dirs_hbm,
    angle_hbm,
    near_ref,
    chosen_ref,
    right_ref,
    own_ref,
    dirs_ref,
    angle_ref,
    sems,
):
    copies = [
        pltpu.make_async_copy(source, target, sems.at[k])
        for k, (source, target) in enumerate(((dirs_hbm, dirs_ref), (angle_hbm, angle_ref)))
    ]
    for copy in copies:
        copy.start()
    atoms, feature = atom_ref.shape[2], atom_ref.shape[3]
    slots = targets_ref.shape[0]
    bonds = slots * atoms
    near_ref[: 3 * CAP // 2] = packed_rows(spot_ref[...], bond_ref, slots, 3 * CAP // 2)
    near_ref[3 * CAP // 2 :] = atom_rows(atom_ref)
    targets = bond_row(targets_ref[...])
    code_x, code_y = bond_codes(targets, atoms, extents, paired, True)
    code = 3 * code_x + code_y
    bond = lax.broadcasted_iota(jnp.int32, (1, bonds), 1)
    far_slot = slots - 1 - slot_at(quotient(bond, atoms), slots)
    far_atom = remainder(targets, atoms)
    far = (remainder(far_slot, 2) * (slots // 2) + quotient(far_slot, 2)) * atoms + far_atom
    base = (code * bonds).astype(F32)
    key = base + far.astype(F32)

    def column(values):
        return jnp.broadcast_to(values.astype(F32), (128, bonds)).T

    keys = column(key)
    place = []
    for group in range(bonds // 128):
        here = slice(group * 128, (group + 1) * 128)
        inside = (keys < key[:, here]) & (keys >= base[:, here])
        place.append(jnp.sum(jnp.where(inside, 1.0, 0.0), axis=0, keepdims=True))
    place = jnp.concatenate(place, axis=1).astype(jnp.int32)
    half, tall = CAP // 2, atoms // 2
    bond_spot = column(half * code + remainder(place, half))
    atom_spot = column(9 * half + tall * code + remainder(far_atom, tall))
    right = (column(quotient(place, half)), column(quotient(far_atom, tall)))
    right_ref[...] = jnp.where(left_lanes((bonds, 128)), right[0], right[1])
    total = 9 * half + 9 * tall
    for start in range(0, total, 128):
        width = min(128, total - start)
        spot = lax.broadcasted_iota(jnp.int32, (bonds, 128), 1).astype(F32) + float(start)
        chosen = jnp.where((spot == bond_spot) | (spot == atom_spot), 1.0, 0.0).astype(BF16)
        chosen_ref[:, start : start + width] = chosen[:, :width]

    atom = atom_ref[0, 0]
    blocks = blocks_of(bond_ref, slots // 2)
    own = [jnp.concatenate([atom, x[:, :feature]], axis=1) for x in blocks]
    own += [jnp.concatenate([atom, x[:, feature:]], axis=1) for x in blocks]
    own = jnp.concatenate(own, axis=0)
    own_ref[...] = own
    for copy in copies:
        copy.wait()


def gated(values):
    half = values.shape[1] // 2
    first, second = values[:, :half], values[:, half:]
    return first * jax.nn.sigmoid(first) * jax.nn.sigmoid(second)


def main_kernel(
    near_ref,
    up_ref,
    down_ref,
    two_ref,
    one_ref,
    angular_ref,
    chosen_ref,
    right_ref,
    own_ref,
    bond_weight_ref,
    mix_weight_ref,
    pair_weight_ref,
    hidden_weight_ref,
    out_weight_ref,
    atom_in_weight_ref,
    sum_weight_ref,
    atom_out_weight_ref,
    atom_result_hbm,
    bond_result_hbm,
    atom_result_ref,
    bond_result_ref,
    first_ref,
    second_ref,
    pair_ref,
    sems,
):
    slots, pairs, _ = angular_ref.shape
    bonds = 2 * pairs
    atoms = bonds // slots
    feature = own_ref.shape[1] // 2
    width = 2 * feature
    half = CAP // 2
    near_refs = (near_ref, up_ref, down_ref)
    away_refs = (one_ref, two_ref)
    sent = [ref[:half] for ref in near_refs] + [ref[: 3 * half] for ref in away_refs]
    sent = jnp.concatenate(sent, axis=0)
    sent_atom = jnp.concatenate([ref[3 * half :] for ref in near_refs + away_refs], axis=0)
    blank = jnp.zeros((sent.shape[0], feature), BF16)
    blank_atom = jnp.zeros((sent_atom.shape[0], feature), BF16)
    received = jnp.concatenate(
        [
            jnp.concatenate([sent[:, :feature], blank, sent[:, feature:], blank], axis=1),
            jnp.concatenate(
                [blank_atom, sent_atom[:, :feature], blank_atom, sent_atom[:, feature:]], axis=1
            ),
        ],
        axis=0,
    )
    far = jnp.dot(chosen_ref[...], received, preferred_element_type=F32)
    far = jnp.where(right_ref[...] > 0.0, far[:, width:], far[:, :width])
    own = own_ref[...]
    incoming = jnp.dot(
        jnp.concatenate([far.astype(BF16), own], axis=1),
        bond_weight_ref[...],
        preferred_element_type=F32,
    )
    hidden = gated(incoming).astype(BF16)
    old = jnp.where(left_lanes((bonds, width)), far, own.astype(F32))
    both = jnp.concatenate([hidden, old.astype(BF16)], axis=1)
    projected = jnp.dot(both, pair_weight_ref[...], preferred_element_type=F32)
    left = left_lanes((pairs, width))

    def beside(one, other, one_turned, other_turned):
        silu = jnp.where(left, one, other_turned)
        return jnp.concatenate([silu, jnp.where(left, one_turned, other)], axis=1)

    def parities(columns):
        turned = pltpu.roll(columns, feature, 1)
        return columns[:pairs], columns[pairs:], turned[:pairs], turned[pairs:]

    first_ref[...] = beside(*parities(projected[:, :width]))
    even, odd, even_turned, odd_turned = parities(projected[:, width:])
    second_ref[0] = beside(even, odd, even_turned, odd_turned)
    even, even_turned = (
        jnp.concatenate([x[atoms:], x[:atoms]], axis=0) for x in (even, even_turned)
    )
    second_ref[1] = beside(odd, even, odd_turned, even_turned)
    mixed = jnp.dot(hidden, mix_weight_ref[...], preferred_element_type=F32)
    new = (old + mixed).astype(BF16).astype(F32)
    average = ((new + pltpu.roll(new, feature, 1)) * 0.5).astype(BF16).astype(F32)
    packed = jnp.where(left, average[:pairs], average[pairs:])
    group = 4

    def first_gates(base):
        for start in range(0, pairs, atoms):
            here = first_ref[pl.ds(start, atoms)]
            for diagonal in range(base, base + group):
                there = (start + diagonal // 2 * atoms) % pairs
                mixture = angular_ref[diagonal, pl.ds(start, atoms)] + (
                    here + second_ref[diagonal % 2, pl.ds(there, atoms)]
                )
                pair_ref[pl.ds(diagonal * pairs + start, atoms)] = gated(mixture).astype(
                    BF16
                )

    def summed(rows):
        parts = [rows[k * atoms : (k + 1) * atoms] for k in range(slots // 2)]
        while len(parts) > 1:
            parts = [x + y for x, y in zip(parts[::2], parts[1::2])]
        return parts[0]

    atom = own[0:atoms]
    atom_incoming = jnp.dot(
        jnp.concatenate([atom[:, :feature], summed(packed).astype(BF16)], axis=1),
        atom_in_weight_ref[...],
        preferred_element_type=F32,
    )
    total = jnp.zeros((pairs, width), F32)
    first_gates(0)
    for base in range(0, slots, group):
        if base + group < slots:
            first_gates(base + group)
        second = jnp.dot(
            pair_ref[pl.ds(base * pairs, group * pairs)],
            hidden_weight_ref[...],
            preferred_element_type=F32,
        )
        gates = gated(second)
        for k in range(group):
            total = total + gates[k * pairs : (k + 1) * pairs]
    bond_out = packed + jnp.dot(
        total.astype(BF16), out_weight_ref[...], preferred_element_type=F32
    )
    bond_out = bond_out.astype(BF16)
    for k in range(slots // 2):
        bond_result_ref[0, 0, :, k * width : (k + 1) * width] = bond_out[
            k * atoms : (k + 1) * atoms
        ]
    copies = [pltpu.make_async_copy(bond_result_ref, bond_result_hbm, sems.at[0])]
    copies[0].start()
    sums = summed(total).astype(BF16)
    atom_incoming = atom_incoming + jnp.dot(
        jnp.concatenate([sums, sums], axis=1), sum_weight_ref[...], preferred_element_type=F32
    )
    atom_hidden = gated(atom_incoming).astype(BF16)
    atom_new = atom.astype(F32) + jnp.dot(
        atom_hidden, atom_out_weight_ref[...], preferred_element_type=F32
    )
    atom_result_ref[0, 0] = atom_new[:, :feature].astype(BF16)
    copies.append(pltpu.make_async_copy(atom_result_ref, atom_result_hbm, sems.at[1]))
    copies[-1].start()
    for copy in copies:
        copy.wait()


def per_device(
    atom_feat,
    bond_feat,
    neighbours,
    bond_dirs,
    bond_in_weight,
    bond_mix_weight,
    pair_weight,
    angle_weight,
    pair_hidden_weight,
    pair_out_weight,
    atom_in_weight,
    atom_out_weight,
):
    atoms, feature = atom_feat.shape[2], atom_feat.shape[3]
    slots = neighbours.shape[3]
    bonds = atoms * slots
    pairs = bonds // 2
    half = CAP // 2
    extents = (lax.axis_size("gx"), lax.axis_size("gy"))
    paired = (extents[0] % 2 == 0, False)
    targets = neighbours[0, 0].T
    hbm = pl.BlockSpec(memory_space=pltpu.HBM)
    vmem = pl.BlockSpec(memory_space=pltpu.VMEM)
    params = pltpu.CompilerParams(vmem_limit_bytes=32 * 2**20)

    def shaped(shape, dtype):
        return jax.ShapeDtypeStruct(shape, dtype)

    def in_hbm(arrays):
        return tuple(pltpu.with_memory_space_constraint(x, pltpu.HBM) for x in arrays)

    payload = shaped((3 * half + atoms // 2, 2 * feature), BF16)
    inputs = (targets, atom_feat, bond_feat)
    up, down, *held = pl.pallas_call(
        functools.partial(pack_kernel, extents, paired),
        out_shape=(payload, payload, shaped((1, bonds), jnp.int32))
        + tuple(shaped(x.shape, x.dtype) for x in inputs),
        in_specs=[hbm] * 3,
        out_specs=(vmem,) * 6,
        scratch_shapes=[pltpu.SemaphoreType.DMA((3,))],
        compiler_params=params,
        name="pack",
    )(*in_hbm(inputs))
    first, second = moves(extents[1], paired[1])
    up = lax.ppermute(up, "gy", first)
    down = lax.ppermute(down, "gy", second)
    weights = (bond_in_weight, bond_mix_weight, pair_weight, pair_hidden_weight)
    weights += (pair_out_weight, atom_in_weight, atom_out_weight)
    near, *prepared, bond_dirs, angle_weight = pl.pallas_call(
        functools.partial(prepare_kernel, extents, paired),
        out_shape=(
            payload,
            shaped((bonds, 9 * half + 9 * atoms // 2), BF16),
            shaped((bonds, 2 * feature), F32),
            shaped((bonds, 2 * feature), BF16),
            shaped(bond_dirs.shape, F32),
            shaped(angle_weight.shape, BF16),
        ),
        in_specs=[vmem] * 4 + [hbm] * 2,
        out_specs=(vmem,) * 6,
        scratch_shapes=[pltpu.SemaphoreType.DMA((2,))],
        compiler_params=params,
        cost_estimate=pl.CostEstimate(flops=64 * 2**20, bytes_accessed=2**21, transcendentals=0),
        name="prepare",
    )(*held, *in_hbm((bond_dirs, angle_weight)))
    near, up, down, prepared = lax.optimization_barrier((near, up, down, prepared))
    first, second = moves(extents[0], paired[0])

    def forwarded(block):
        parts = [x[block * half : (block + 1) * half] for x in (near, up, down)]
        return jnp.concatenate(parts + [x[3 * half :] for x in (near, up, down)], axis=0)

    one = lax.ppermute(forwarded(1), "gx", first)
    two = lax.ppermute(forwarded(2), "gx", second)
    angular, *made = pl.pallas_call(
        functools.partial(angular_kernel, atoms),
        out_shape=(
            shaped((slots, pairs, 4 * feature), F32),
            shaped((4 * feature, 4 * feature), BF16),
            shaped((2 * feature, 2 * feature), BF16),
            shaped((4 * feature, 4 * feature), BF16),
            shaped((2 * feature, 4 * feature), BF16),
            shaped((2 * feature, 2 * feature), BF16),
            shaped((3 * feature, 4 * feature), BF16),
            shaped((4 * feature, 4 * feature), BF16),
            shaped((2 * feature, 2 * feature), BF16),
        ),
        in_specs=[vmem] * 2 + [hbm] * 7,
        out_specs=(vmem,) * 9,
        scratch_shapes=[pltpu.VMEM(x.shape, BF16) for x in weights]
        + [pltpu.SemaphoreType.DMA((7,))],
        compiler_params=params,
        cost_estimate=pl.CostEstimate(
            flops=256 * 2**20, bytes_accessed=2**22, transcendentals=4096
        ),
        name="angular",
    )(bond_dirs, angle_weight, *in_hbm(weights))
    return pl.pallas_call(
        main_kernel,
        out_shape=(shaped(atom_feat.shape, BF16), shaped(bond_feat.shape, BF16)),
        in_specs=[vmem] * 17,
        out_specs=(hbm, hbm),
        scratch_shapes=[
            pltpu.VMEM(atom_feat.shape, BF16),
            pltpu.VMEM(bond_feat.shape, BF16),
            pltpu.VMEM((pairs, 4 * feature), F32),
            pltpu.VMEM((2, pairs, 4 * feature), F32),
            pltpu.VMEM((slots * pairs, 2 * feature), BF16),
            pltpu.SemaphoreType.DMA((2,)),
        ],
        compiler_params=params,
        name="main",
    )(near, up, down, two, one, angular, *prepared, *made)


def solution(mesh):
    placed = (
        P("gx", "gy", None, None),
        P("gx", "gy", None, None),
        P("gx", "gy", None, None),
        P(None, "gx", "gy", None),
        P(),
        P(),
        P(),
        P(),
        P(),
        P(),
        P(),
        P(),
    )
    return jax.shard_map(
        per_device,
        mesh=mesh,
        in_specs=placed,
        out_specs=(P("gx", "gy", None, None), P("gx", "gy", None, None)),
        check_vma=False,
    )
```

```python
import functools

import jax
import jax.numpy as jnp
from jax import lax
from jax.experimental import pallas as pl
from jax.experimental.pallas import tpu as pltpu
from jax.sharding import PartitionSpec as P

F32 = jnp.float32
BF16 = jnp.bfloat16
CAP = 64


def quotient(values, size):
    if size & (size - 1) == 0:
        return values >> (size.bit_length() - 1)
    return lax.div(values, jnp.int32(size))


def remainder(values, size):
    if size & (size - 1) == 0:
        return values & (size - 1)
    return lax.rem(values, jnp.int32(size))


def step_code(owner, home, extent, paired, receives):
    step = remainder(owner - home + 1 + extent, extent)
    if paired:
        ahead = jnp.where(remainder(home, 2) == 0, 0, 2)
    else:
        ahead = 0 if receives else 2
    return jnp.where(step == 1, 0, jnp.where(step == ahead, 1, 2))


def moves(extent, paired):
    if paired:
        near = [(i, i ^ 1) for i in range(extent)]
        return [(i, (((i + 1) ^ 1) - 1) % extent) for i in range(extent)], near
    up = [(i, (i + 1) % extent) for i in range(extent)]
    return up, [(j, i) for i, j in up]


def slot_at(position, slots):
    half = slots // 2
    return jnp.where(position < half, 2 * position, 2 * (position - half) + 1)


def bond_row(table):
    slots, atoms = table.shape
    per_group = 128 // atoms
    tiled = jnp.concatenate([table.astype(F32)] * per_group, axis=1)
    row = lax.broadcasted_iota(jnp.int32, tiled.shape, 0)
    position = quotient(lax.broadcasted_iota(jnp.int32, tiled.shape, 1), atoms)
    pieces = []
    for group in range(slots // per_group):
        chosen = row == slot_at(position + group * per_group, slots)
        pieces.append(jnp.sum(jnp.where(chosen, tiled, 0.0), axis=0, keepdims=True))
    return jnp.concatenate(pieces, axis=1).astype(jnp.int32)


def bond_codes(targets, atoms, extents, paired, receives):
    owner = quotient(targets, atoms)
    block = (quotient(owner, extents[1]), remainder(owner, extents[1]))
    return tuple(
        step_code(block[k], lax.axis_index(axis), extents[k], paired[k], receives)
        for k, axis in enumerate(("gx", "gy"))
    )


def left_lanes(shape):
    return lax.broadcasted_iota(jnp.int32, shape, 1) < shape[1] // 2


def swapped(rows):
    half = rows.shape[1] // 2
    return jnp.concatenate([rows[:, half:], rows[:, :half]], axis=1)


def blocks_of(bond_ref, pairs):
    width = bond_ref.shape[3] // pairs
    return [bond_ref[0, 0, :, k * width : (k + 1) * width] for k in range(pairs)]


def pack_kernel(
    extents,
    paired,
    targets_hbm,
    atom_hbm,
    bond_hbm,
    up_ref,
    down_ref,
    spot_ref,
    targets_ref,
    atom_ref,
    bond_ref,
    sems,
):
    sources = ((targets_hbm, targets_ref), (bond_hbm, bond_ref), (atom_hbm, atom_ref))
    copies = [
        pltpu.make_async_copy(source, target, sems.at[k])
        for k, (source, target) in enumerate(sources)
    ]
    for copy in copies:
        copy.start()
    atoms, feature = atom_ref.shape[2], atom_ref.shape[3]
    slots = targets_ref.shape[0]
    bonds = slots * atoms
    lanes = 128
    groups = bonds // lanes
    copies[0].wait()
    code_x, code_y = bond_codes(bond_row(targets_ref[...]), atoms, extents, paired, False)
    code = 3 * code_y + code_x
    rows = lax.broadcasted_iota(jnp.int32, (16, lanes), 0)
    marks = [rows == code[:, g * lanes : (g + 1) * lanes] for g in range(groups)]
    stacked = jnp.concatenate([m.astype(F32) for m in marks], axis=0).astype(BF16)
    before = lax.broadcasted_iota(jnp.int32, (lanes, 2 * lanes), 0)
    after = lax.broadcasted_iota(jnp.int32, (lanes, 2 * lanes), 1)
    sums = jnp.where((before < after) | (after >= lanes), 1.0, 0.0).astype(BF16)
    counted = jnp.dot(stacked, sums, preferred_element_type=F32)
    place = []
    earlier = jnp.zeros((16, lanes), F32)
    for g in range(groups):
        part = counted[g * 16 : (g + 1) * 16]
        place.append(
            jnp.sum(jnp.where(marks[g], part[:, :lanes] + earlier, 0.0), axis=0, keepdims=True)
        )
        earlier = earlier + part[:, lanes:]
    place = jnp.concatenate(place, axis=1).astype(jnp.int32)
    half = CAP // 2
    right = quotient(place, half)
    spot = place - half * right + half * code
    spot_ref[...] = jnp.where(code < 3, spot + 3 * half * right, -1)
    wanted = jnp.where(code < 3, -1, spot - 3 * half + 6 * half * right)
    copies[1].wait()
    copies[2].wait()
    packed = packed_rows(wanted, bond_ref, slots, 6 * half)
    for k, ref in enumerate((up_ref, down_ref)):
        ref[: 3 * half] = packed[3 * half * k : 3 * half * (k + 1)]
        ref[3 * half :] = atom_rows(atom_ref)


def packed_rows(wanted, bond_ref, slots, count):
    spot = lax.broadcasted_iota(jnp.int32, (2 * count, wanted.shape[1]), 0)
    chosen = jnp.where(spot == wanted, 1.0, 0.0).astype(BF16)
    blocks = blocks_of(bond_ref, slots // 2)
    feature = blocks[0].shape[1] // 2
    values = [x[:, :feature] for x in blocks] + [x[:, feature:] for x in blocks]
    packed = jnp.dot(chosen, jnp.concatenate(values, axis=0), preferred_element_type=F32)
    return jnp.concatenate([packed[:count], packed[count:]], axis=1).astype(BF16)


def atom_rows(atom_ref):
    atom = atom_ref[0, 0]
    half = atom.shape[0] // 2
    return jnp.concatenate([atom[:half], atom[half:]], axis=1)


def crossed(left, right):
    half = left.shape[1] // 2
    parts = [left[:, :half], right[:, :half], left[:, half:], right[:, half:]]
    return jnp.concatenate(parts, axis=1)


def two_blocks(weight):
    blank = jnp.zeros_like(weight)
    return jnp.concatenate([crossed(weight, blank), crossed(blank, weight)], axis=0)


def diagonal_blocks(weight):
    blank = jnp.zeros_like(weight)
    return jnp.concatenate(
        [jnp.concatenate([weight, blank], axis=1), jnp.concatenate([blank, weight], axis=1)],
        axis=0,
    )


def angular_kernel(atoms, dirs_ref, angle_ref, *refs):
    sources, angular_ref, results, held, sems = refs[:7], refs[7], refs[8:16], refs[16:23], refs[23]
    copies = [
        pltpu.make_async_copy(source, target, sems.at[k])
        for k, (source, target) in enumerate(zip(sources, held))
    ]
    for copy in copies:
        copy.start()
    slots, pairs, _ = angular_ref.shape
    bonds = 2 * pairs
    degrees = angle_ref.shape[0]
    weight = two_blocks(angle_ref[...].astype(F32)).astype(BF16)
    polar, azimuth = dirs_ref[0, 0], dirs_ref[1, 0]
    unit = jnp.concatenate(
        [
            jnp.sin(polar) * jnp.cos(azimuth),
            jnp.sin(polar) * jnp.sin(azimuth),
            jnp.cos(polar),
            jnp.zeros((5, bonds), F32),
        ],
        axis=0,
    )
    high = unit.astype(BF16).astype(F32)
    middle = (unit - high).astype(BF16).astype(F32)
    parts = jnp.concatenate([high, middle, unit - high - middle], axis=0).astype(BF16)
    bond = lax.broadcasted_iota(jnp.int32, (1, bonds), 1)
    source = remainder(bond, atoms) * slots + slot_at(quotient(bond, atoms), slots)
    spot = lax.broadcasted_iota(jnp.int32, (bonds, bonds), 0)
    chosen = jnp.where(spot == source, 1.0, 0.0).astype(BF16)
    unit = jnp.dot(parts, chosen, preferred_element_type=F32)
    unit = unit[0:8] + unit[8:16] + unit[16:24]
    even = [jnp.broadcast_to(unit[k : k + 1, :pairs], (8, pairs)) for k in range(3)]
    odd = [jnp.broadcast_to(unit[k : k + 1, pairs:], (8, pairs)) for k in range(3)]
    row = lax.broadcasted_iota(jnp.int32, (8, pairs), 0)

    def turned(vector, places):
        places = places % (pairs // atoms)
        if places == 0:
            return vector
        return [pltpu.roll(part, pairs - atoms * places, 1) for part in vector]

    def basis(first, second):
        cosine = first[0] * second[0] + first[1] * second[1] + first[2] * second[2]
        series = [jnp.ones_like(cosine), cosine]
        double = cosine + cosine
        for _ in range(7):
            series.append(double * series[-1] - series[-2])
        lower = series[7]
        upper = series[1]
        for index in range(1, 8):
            lower = jnp.where(row == index, series[7 - index], lower)
            upper = jnp.where(row == index, series[1 + index], upper)
        double = series[8] + series[8]
        blocks = [lower, upper]
        for _ in range(degrees // 8 - 1):
            blocks.append(double * blocks[-1] - blocks[-2])
        return blocks[1:]

    for diagonal in range(slots):
        places = diagonal // 2
        if diagonal % 2 == 0:
            blocks = basis(even, turned(even, places)) + basis(odd, turned(odd, places))
        else:
            blocks = basis(even, turned(odd, places)) + basis(odd, turned(even, places + 1))
        series = jnp.concatenate(blocks, axis=0).T.astype(BF16)
        angular_ref[diagonal] = jnp.dot(series, weight, preferred_element_type=F32)
    for copy in copies:
        copy.wait()
    prepare_weights(slots, held, results)


def prepare_weights(slots, held, results):
    bond_in_ref, bond_mix_ref, pair_ref, pair_hidden_ref, pair_out_ref, atom_in_ref = held[:6]
    atom_out_ref = held[6]
    bond_weight_ref, mix_weight_ref, pair_weight_ref, hidden_weight_ref = results[:4]
    out_weight_ref, atom_in_weight_ref, sum_weight_ref, atom_out_weight_ref = results[4:]
    feature = bond_mix_ref.shape[0]
    weight = bond_in_ref[...].astype(F32)
    source, other, bond_part = (weight[k * feature : (k + 1) * feature] for k in range(3))
    blank = jnp.zeros_like(source)
    away = [crossed(bond_part, blank), crossed(source, other)]
    near = [crossed(other, source), crossed(blank, bond_part)]
    bond_weight_ref[...] = jnp.concatenate(away + near, axis=0).astype(BF16)
    mix_weight_ref[...] = diagonal_blocks(bond_mix_ref[...].astype(F32)).astype(BF16)
    old = pair_ref[...].astype(F32) * 0.5
    hidden = jnp.dot(bond_mix_ref[...], pair_ref[...], preferred_element_type=F32) * 0.5
    pair_weight_ref[...] = jnp.concatenate([hidden, hidden, old, old], axis=0).astype(BF16)
    hidden_weight_ref[...] = two_blocks(pair_hidden_ref[...].astype(F32)).astype(BF16)
    out_weight_ref[...] = diagonal_blocks(pair_out_ref[...].astype(F32)).astype(BF16)
    weight = atom_in_ref[...].astype(F32)
    weight = crossed(weight, jnp.zeros_like(weight))
    mean = weight[feature:] * (1.0 / slots)
    atom_in_weight_ref[...] = jnp.concatenate([weight[:feature], mean, mean], axis=0).astype(BF16)
    folded = jnp.dot(
        pair_out_ref[...], mean.astype(BF16), preferred_element_type=F32
    )
    high = folded.astype(BF16)
    low = (folded - high.astype(F32)).astype(BF16)
    sum_weight_ref[...] = jnp.concatenate([high, high, low, low], axis=0)
    weight = atom_out_ref[...].astype(F32)
    blank = jnp.zeros_like(weight)
    weight = jnp.concatenate([weight, blank], axis=1)
    atom_out_weight_ref[...] = jnp.concatenate([weight, jnp.zeros_like(weight)], axis=0).astype(
        BF16
    )


def prepare_kernel(
    extents,
    paired,
    spot_ref,
    targets_ref,
    atom_ref,
    bond_ref,
    dirs_hbm,
    angle_hbm,
    near_ref,
    chosen_ref,
    right_ref,
    own_ref,
    dirs_ref,
    angle_ref,
    sems,
):
    copies = [
        pltpu.make_async_copy(source, target, sems.at[k])
        for k, (source, target) in enumerate(((dirs_hbm, dirs_ref), (angle_hbm, angle_ref)))
    ]
    for copy in copies:
        copy.start()
    atoms, feature = atom_ref.shape[2], atom_ref.shape[3]
    slots = targets_ref.shape[0]
    bonds = slots * atoms
    near_ref[: 3 * CAP // 2] = packed_rows(spot_ref[...], bond_ref, slots, 3 * CAP // 2)
    near_ref[3 * CAP // 2 :] = atom_rows(atom_ref)
    targets = bond_row(targets_ref[...])
    code_x, code_y = bond_codes(targets, atoms, extents, paired, True)
    code = 3 * code_x + code_y
    bond = lax.broadcasted_iota(jnp.int32, (1, bonds), 1)
    far_slot = slots - 1 - slot_at(quotient(bond, atoms), slots)
    far_atom = remainder(targets, atoms)
    far = (remainder(far_slot, 2) * (slots // 2) + quotient(far_slot, 2)) * atoms + far_atom
    base = (code * bonds).astype(F32)
    key = base + far.astype(F32)

    def column(values):
        return jnp.broadcast_to(values.astype(F32), (128, bonds)).T

    keys = column(key)
    place = []
    for group in range(bonds // 128):
        here = slice(group * 128, (group + 1) * 128)
        inside = (keys < key[:, here]) & (keys >= base[:, here])
        place.append(jnp.sum(jnp.where(inside, 1.0, 0.0), axis=0, keepdims=True))
    place = jnp.concatenate(place, axis=1).astype(jnp.int32)
    half, tall = CAP // 2, atoms // 2
    bond_spot = column(half * code + remainder(place, half))
    atom_spot = column(9 * half + tall * code + remainder(far_atom, tall))
    right = (column(quotient(place, half)), column(quotient(far_atom, tall)))
    right_ref[...] = jnp.where(left_lanes((bonds, 128)), right[0], right[1])
    total = 9 * half + 9 * tall
    for start in range(0, total, 128):
        width = min(128, total - start)
        spot = lax.broadcasted_iota(jnp.int32, (bonds, 128), 1).astype(F32) + float(start)
        chosen = jnp.where((spot == bond_spot) | (spot == atom_spot), 1.0, 0.0).astype(BF16)
        chosen_ref[:, start : start + width] = chosen[:, :width]

    atom = atom_ref[0, 0]
    blocks = blocks_of(bond_ref, slots // 2)
    own = [jnp.concatenate([atom, x[:, :feature]], axis=1) for x in blocks]
    own += [jnp.concatenate([atom, x[:, feature:]], axis=1) for x in blocks]
    own = jnp.concatenate(own, axis=0)
    own_ref[...] = own
    for copy in copies:
        copy.wait()


def gated(values):
    half = values.shape[1] // 2
    first, second = values[:, :half], values[:, half:]
    return first * jax.nn.sigmoid(first) * jax.nn.sigmoid(second)


def main_kernel(
    near_ref,
    up_ref,
    down_ref,
    two_ref,
    one_ref,
    angular_ref,
    chosen_ref,
    right_ref,
    own_ref,
    bond_weight_ref,
    mix_weight_ref,
    pair_weight_ref,
    hidden_weight_ref,
    out_weight_ref,
    atom_in_weight_ref,
    sum_weight_ref,
    atom_out_weight_ref,
    atom_result_hbm,
    bond_result_hbm,
    atom_result_ref,
    bond_result_ref,
    first_ref,
    second_ref,
    pair_ref,
    sems,
):
    slots, pairs, _ = angular_ref.shape
    bonds = 2 * pairs
    atoms = bonds // slots
    feature = own_ref.shape[1] // 2
    width = 2 * feature
    half = CAP // 2
    near_refs = (near_ref, up_ref, down_ref)
    away_refs = (one_ref, two_ref)
    sent = [ref[:half] for ref in near_refs] + [ref[: 3 * half] for ref in away_refs]
    sent = jnp.concatenate(sent, axis=0)
    sent_atom = jnp.concatenate([ref[3 * half :] for ref in near_refs + away_refs], axis=0)
    blank = jnp.zeros((sent.shape[0], feature), BF16)
    blank_atom = jnp.zeros((sent_atom.shape[0], feature), BF16)
    received = jnp.concatenate(
        [
            jnp.concatenate([sent[:, :feature], blank, sent[:, feature:], blank], axis=1),
            jnp.concatenate(
                [blank_atom, sent_atom[:, :feature], blank_atom, sent_atom[:, feature:]], axis=1
            ),
        ],
        axis=0,
    )
    far = jnp.dot(chosen_ref[...], received, preferred_element_type=F32)
    far = jnp.where(right_ref[...] > 0.0, far[:, width:], far[:, :width])
    own = own_ref[...]
    incoming = jnp.dot(
        jnp.concatenate([far.astype(BF16), own], axis=1),
        bond_weight_ref[...],
        preferred_element_type=F32,
    )
    hidden = gated(incoming).astype(BF16)
    old = jnp.where(left_lanes((bonds, width)), far, own.astype(F32))
    both = jnp.concatenate([hidden, old.astype(BF16)], axis=1)
    projected = jnp.dot(both, pair_weight_ref[...], preferred_element_type=F32)
    left = left_lanes((pairs, width))

    def beside(one, other, one_turned, other_turned):
        silu = jnp.where(left, one, other_turned)
        return jnp.concatenate([silu, jnp.where(left, one_turned, other)], axis=1)

    def parities(columns):
        turned = pltpu.roll(columns, feature, 1)
        return columns[:pairs], columns[pairs:], turned[:pairs], turned[pairs:]

    first_ref[...] = beside(*parities(projected[:, :width]))
    even, odd, even_turned, odd_turned = parities(projected[:, width:])
    second_ref[0] = beside(even, odd, even_turned, odd_turned)
    even, even_turned = (
        jnp.concatenate([x[atoms:], x[:atoms]], axis=0) for x in (even, even_turned)
    )
    second_ref[1] = beside(odd, even, odd_turned, even_turned)
    mixed = jnp.dot(hidden, mix_weight_ref[...], preferred_element_type=F32)
    new = (old + mixed).astype(BF16).astype(F32)
    average = ((new + pltpu.roll(new, feature, 1)) * 0.5).astype(BF16).astype(F32)
    packed = jnp.where(left, average[:pairs], average[pairs:])
    group = 2

    def first_gates(base):
        for start in range(0, pairs, atoms):
            here = first_ref[pl.ds(start, atoms)]
            for diagonal in range(base, base + group):
                there = (start + diagonal // 2 * atoms) % pairs
                mixture = angular_ref[diagonal, pl.ds(start, atoms)] + (
                    here + second_ref[diagonal % 2, pl.ds(there, atoms)]
                )
                pair_ref[pl.ds(diagonal * pairs + start, atoms)] = gated(mixture).astype(
                    BF16
                )

    def summed(rows):
        parts = [rows[k * atoms : (k + 1) * atoms] for k in range(slots // 2)]
        while len(parts) > 1:
            parts = [x + y for x, y in zip(parts[::2], parts[1::2])]
        return parts[0]

    atom = own[0:atoms]
    atom_incoming = jnp.dot(
        jnp.concatenate([atom[:, :feature], summed(packed).astype(BF16)], axis=1),
        atom_in_weight_ref[...],
        preferred_element_type=F32,
    )
    total = jnp.zeros((pairs, width), F32)
    first_gates(0)
    for base in range(0, slots, group):
        if base + group < slots:
            first_gates(base + group)
        second = jnp.dot(
            pair_ref[pl.ds(base * pairs, group * pairs)],
            hidden_weight_ref[...],
            preferred_element_type=F32,
        )
        gates = gated(second)
        for k in range(group):
            total = total + gates[k * pairs : (k + 1) * pairs]
    bond_out = packed + jnp.dot(
        total.astype(BF16), out_weight_ref[...], preferred_element_type=F32
    )
    bond_out = bond_out.astype(BF16)
    for k in range(slots // 2):
        bond_result_ref[0, 0, :, k * width : (k + 1) * width] = bond_out[
            k * atoms : (k + 1) * atoms
        ]
    copies = [pltpu.make_async_copy(bond_result_ref, bond_result_hbm, sems.at[0])]
    copies[0].start()
    sums = summed(total).astype(BF16)
    atom_incoming = atom_incoming + jnp.dot(
        jnp.concatenate([sums, sums], axis=1), sum_weight_ref[...], preferred_element_type=F32
    )
    atom_hidden = gated(atom_incoming).astype(BF16)
    atom_new = atom.astype(F32) + jnp.dot(
        atom_hidden, atom_out_weight_ref[...], preferred_element_type=F32
    )
    atom_result_ref[0, 0] = atom_new[:, :feature].astype(BF16)
    copies.append(pltpu.make_async_copy(atom_result_ref, atom_result_hbm, sems.at[1]))
    copies[-1].start()
    for copy in copies:
        copy.wait()


def per_device(
    atom_feat,
    bond_feat,
    neighbours,
    bond_dirs,
    bond_in_weight,
    bond_mix_weight,
    pair_weight,
    angle_weight,
    pair_hidden_weight,
    pair_out_weight,
    atom_in_weight,
    atom_out_weight,
):
    atoms, feature = atom_feat.shape[2], atom_feat.shape[3]
    slots = neighbours.shape[3]
    bonds = atoms * slots
    pairs = bonds // 2
    half = CAP // 2
    extents = (lax.axis_size("gx"), lax.axis_size("gy"))
    paired = (extents[0] % 2 == 0, False)
    targets = neighbours[0, 0].T
    hbm = pl.BlockSpec(memory_space=pltpu.HBM)
    vmem = pl.BlockSpec(memory_space=pltpu.VMEM)
    params = pltpu.CompilerParams(vmem_limit_bytes=32 * 2**20)

    def shaped(shape, dtype):
        return jax.ShapeDtypeStruct(shape, dtype)

    def in_hbm(arrays):
        return tuple(pltpu.with_memory_space_constraint(x, pltpu.HBM) for x in arrays)

    payload = shaped((3 * half + atoms // 2, 2 * feature), BF16)
    inputs = (targets, atom_feat, bond_feat)
    up, down, *held = pl.pallas_call(
        functools.partial(pack_kernel, extents, paired),
        out_shape=(payload, payload, shaped((1, bonds), jnp.int32))
        + tuple(shaped(x.shape, x.dtype) for x in inputs),
        in_specs=[hbm] * 3,
        out_specs=(vmem,) * 6,
        scratch_shapes=[pltpu.SemaphoreType.DMA((3,))],
        compiler_params=params,
        name="pack",
    )(*in_hbm(inputs))
    first, second = moves(extents[1], paired[1])
    up = lax.ppermute(up, "gy", first)
    down = lax.ppermute(down, "gy", second)
    weights = (bond_in_weight, bond_mix_weight, pair_weight, pair_hidden_weight)
    weights += (pair_out_weight, atom_in_weight, atom_out_weight)
    near, *prepared, bond_dirs, angle_weight = pl.pallas_call(
        functools.partial(prepare_kernel, extents, paired),
        out_shape=(
            payload,
            shaped((bonds, 9 * half + 9 * atoms // 2), BF16),
            shaped((bonds, 2 * feature), F32),
            shaped((bonds, 2 * feature), BF16),
            shaped(bond_dirs.shape, F32),
            shaped(angle_weight.shape, BF16),
        ),
        in_specs=[vmem] * 4 + [hbm] * 2,
        out_specs=(vmem,) * 6,
        scratch_shapes=[pltpu.SemaphoreType.DMA((2,))],
        compiler_params=params,
        cost_estimate=pl.CostEstimate(flops=64 * 2**20, bytes_accessed=2**21, transcendentals=0),
        name="prepare",
    )(*held, *in_hbm((bond_dirs, angle_weight)))
    near, up, down, prepared = lax.optimization_barrier((near, up, down, prepared))
    first, second = moves(extents[0], paired[0])

    def forwarded(block):
        parts = [x[block * half : (block + 1) * half] for x in (near, up, down)]
        return jnp.concatenate(parts + [x[3 * half :] for x in (near, up, down)], axis=0)

    one = lax.ppermute(forwarded(1), "gx", first)
    two = lax.ppermute(forwarded(2), "gx", second)
    angular, *made = pl.pallas_call(
        functools.partial(angular_kernel, atoms),
        out_shape=(
            shaped((slots, pairs, 4 * feature), F32),
            shaped((4 * feature, 4 * feature), BF16),
            shaped((2 * feature, 2 * feature), BF16),
            shaped((4 * feature, 4 * feature), BF16),
            shaped((2 * feature, 4 * feature), BF16),
            shaped((2 * feature, 2 * feature), BF16),
            shaped((3 * feature, 4 * feature), BF16),
            shaped((4 * feature, 4 * feature), BF16),
            shaped((2 * feature, 2 * feature), BF16),
        ),
        in_specs=[vmem] * 2 + [hbm] * 7,
        out_specs=(vmem,) * 9,
        scratch_shapes=[pltpu.VMEM(x.shape, BF16) for x in weights]
        + [pltpu.SemaphoreType.DMA((7,))],
        compiler_params=params,
        cost_estimate=pl.CostEstimate(
            flops=256 * 2**20, bytes_accessed=2**22, transcendentals=4096
        ),
        name="angular",
    )(bond_dirs, angle_weight, *in_hbm(weights))
    return pl.pallas_call(
        main_kernel,
        out_shape=(shaped(atom_feat.shape, BF16), shaped(bond_feat.shape, BF16)),
        in_specs=[vmem] * 17,
        out_specs=(hbm, hbm),
        scratch_shapes=[
            pltpu.VMEM(atom_feat.shape, BF16),
            pltpu.VMEM(bond_feat.shape, BF16),
            pltpu.VMEM((pairs, 4 * feature), F32),
            pltpu.VMEM((2, pairs, 4 * feature), F32),
            pltpu.VMEM((slots * pairs, 2 * feature), BF16),
            pltpu.SemaphoreType.DMA((2,)),
        ],
        compiler_params=params,
        name="main",
    )(near, up, down, two, one, angular, *prepared, *made)


def solution(mesh):
    placed = (
        P("gx", "gy", None, None),
        P("gx", "gy", None, None),
        P("gx", "gy", None, None),
        P(None, "gx", "gy", None),
        P(),
        P(),
        P(),
        P(),
        P(),
        P(),
        P(),
        P(),
    )
    return jax.shard_map(
        per_device,
        mesh=mesh,
        in_specs=placed,
        out_specs=(P("gx", "gy", None, None), P("gx", "gy", None, None)),
        check_vma=False,
    )
```

```python
import functools

import jax
import jax.numpy as jnp
from jax import lax
from jax.experimental import pallas as pl
from jax.experimental.pallas import tpu as pltpu
from jax.sharding import PartitionSpec as P

F32 = jnp.float32
BF16 = jnp.bfloat16
CAP = 64


def quotient(values, size):
    if size & (size - 1) == 0:
        return values >> (size.bit_length() - 1)
    return lax.div(values, jnp.int32(size))


def remainder(values, size):
    if size & (size - 1) == 0:
        return values & (size - 1)
    return lax.rem(values, jnp.int32(size))


def step_code(owner, home, extent, paired, receives):
    step = remainder(owner - home + 1 + extent, extent)
    if paired:
        ahead = jnp.where(remainder(home, 2) == 0, 0, 2)
    else:
        ahead = 0 if receives else 2
    return jnp.where(step == 1, 0, jnp.where(step == ahead, 1, 2))


def moves(extent, paired):
    if paired:
        near = [(i, i ^ 1) for i in range(extent)]
        return [(i, (((i + 1) ^ 1) - 1) % extent) for i in range(extent)], near
    up = [(i, (i + 1) % extent) for i in range(extent)]
    return up, [(j, i) for i, j in up]


def slot_at(position, slots):
    half = slots // 2
    return jnp.where(position < half, 2 * position, 2 * (position - half) + 1)


def bond_row(table):
    slots, atoms = table.shape
    per_group = 128 // atoms
    tiled = jnp.concatenate([table.astype(F32)] * per_group, axis=1)
    row = lax.broadcasted_iota(jnp.int32, tiled.shape, 0)
    position = quotient(lax.broadcasted_iota(jnp.int32, tiled.shape, 1), atoms)
    pieces = []
    for group in range(slots // per_group):
        chosen = row == slot_at(position + group * per_group, slots)
        pieces.append(jnp.sum(jnp.where(chosen, tiled, 0.0), axis=0, keepdims=True))
    return jnp.concatenate(pieces, axis=1).astype(jnp.int32)


def bond_codes(targets, atoms, extents, paired, receives):
    owner = quotient(targets, atoms)
    block = (quotient(owner, extents[1]), remainder(owner, extents[1]))
    return tuple(
        step_code(block[k], lax.axis_index(axis), extents[k], paired[k], receives)
        for k, axis in enumerate(("gx", "gy"))
    )


def left_lanes(shape):
    return lax.broadcasted_iota(jnp.int32, shape, 1) < shape[1] // 2


def swapped(rows):
    half = rows.shape[1] // 2
    return jnp.concatenate([rows[:, half:], rows[:, :half]], axis=1)


def blocks_of(bond_ref, pairs):
    width = bond_ref.shape[3] // pairs
    return [bond_ref[0, 0, :, k * width : (k + 1) * width] for k in range(pairs)]


def pack_kernel(
    extents,
    paired,
    targets_hbm,
    atom_hbm,
    bond_hbm,
    up_ref,
    down_ref,
    spot_ref,
    targets_ref,
    atom_ref,
    bond_ref,
    sems,
):
    sources = ((targets_hbm, targets_ref), (bond_hbm, bond_ref), (atom_hbm, atom_ref))
    copies = [
        pltpu.make_async_copy(source, target, sems.at[k])
        for k, (source, target) in enumerate(sources)
    ]
    for copy in copies:
        copy.start()
    atoms, feature = atom_ref.shape[2], atom_ref.shape[3]
    slots = targets_ref.shape[0]
    bonds = slots * atoms
    lanes = 128
    groups = bonds // lanes
    copies[0].wait()
    code_x, code_y = bond_codes(bond_row(targets_ref[...]), atoms, extents, paired, False)
    code = 3 * code_y + code_x
    rows = lax.broadcasted_iota(jnp.int32, (16, lanes), 0)
    marks = [rows == code[:, g * lanes : (g + 1) * lanes] for g in range(groups)]
    stacked = jnp.concatenate([m.astype(F32) for m in marks], axis=0).astype(BF16)
    before = lax.broadcasted_iota(jnp.int32, (lanes, 2 * lanes), 0)
    after = lax.broadcasted_iota(jnp.int32, (lanes, 2 * lanes), 1)
    sums = jnp.where((before < after) | (after >= lanes), 1.0, 0.0).astype(BF16)
    counted = jnp.dot(stacked, sums, preferred_element_type=F32)
    place = []
    earlier = jnp.zeros((16, lanes), F32)
    for g in range(groups):
        part = counted[g * 16 : (g + 1) * 16]
        place.append(
            jnp.sum(jnp.where(marks[g], part[:, :lanes] + earlier, 0.0), axis=0, keepdims=True)
        )
        earlier = earlier + part[:, lanes:]
    place = jnp.concatenate(place, axis=1).astype(jnp.int32)
    half = CAP // 2
    right = quotient(place, half)
    spot = place - half * right + half * code
    spot_ref[...] = jnp.where(code < 3, spot + 3 * half * right, -1)
    wanted = jnp.where(code < 3, -1, spot - 3 * half + 6 * half * right)
    copies[1].wait()
    copies[2].wait()
    packed = packed_rows(wanted, bond_ref, slots, 6 * half)
    for k, ref in enumerate((up_ref, down_ref)):
        ref[: 3 * half] = packed[3 * half * k : 3 * half * (k + 1)]
        ref[3 * half :] = atom_rows(atom_ref)


def packed_rows(wanted, bond_ref, slots, count):
    spot = lax.broadcasted_iota(jnp.int32, (2 * count, wanted.shape[1]), 0)
    chosen = jnp.where(spot == wanted, 1.0, 0.0).astype(BF16)
    blocks = blocks_of(bond_ref, slots // 2)
    feature = blocks[0].shape[1] // 2
    values = [jnp.concatenate([x[:, :feature]] * 2, axis=1) for x in blocks]
    values += [jnp.concatenate([x[:, feature:]] * 2, axis=1) for x in blocks]
    packed = jnp.dot(chosen, jnp.concatenate(values, axis=0), preferred_element_type=F32)
    left = left_lanes((count, 2 * feature))
    return jnp.where(left, packed[:count], packed[count:]).astype(BF16)


def atom_rows(atom_ref):
    atom = atom_ref[0, 0]
    half = atom.shape[0] // 2
    return jnp.concatenate([atom[:half], atom[half:]], axis=1)


def crossed(left, right):
    half = left.shape[1] // 2
    parts = [left[:, :half], right[:, :half], left[:, half:], right[:, half:]]
    return jnp.concatenate(parts, axis=1)


def two_blocks(weight):
    blank = jnp.zeros_like(weight)
    return jnp.concatenate([crossed(weight, blank), crossed(blank, weight)], axis=0)


def diagonal_blocks(weight):
    blank = jnp.zeros_like(weight)
    return jnp.concatenate(
        [jnp.concatenate([weight, blank], axis=1), jnp.concatenate([blank, weight], axis=1)],
        axis=0,
    )


def angular_kernel(atoms, dirs_ref, angle_ref, *refs):
    sources, angular_ref, results, held, sems = refs[:7], refs[7], refs[8:16], refs[16:23], refs[23]
    copies = [
        pltpu.make_async_copy(source, target, sems.at[k])
        for k, (source, target) in enumerate(zip(sources, held))
    ]
    for copy in copies:
        copy.start()
    slots, pairs, _ = angular_ref.shape
    bonds = 2 * pairs
    degrees = angle_ref.shape[0]
    weight = two_blocks(angle_ref[...].astype(F32)).astype(BF16)
    polar, azimuth = dirs_ref[0, 0], dirs_ref[1, 0]
    unit = jnp.concatenate(
        [
            jnp.sin(polar) * jnp.cos(azimuth),
            jnp.sin(polar) * jnp.sin(azimuth),
            jnp.cos(polar),
            jnp.zeros((5, bonds), F32),
        ],
        axis=0,
    )
    high = unit.astype(BF16).astype(F32)
    middle = (unit - high).astype(BF16).astype(F32)
    parts = jnp.concatenate([high, middle, unit - high - middle], axis=0).astype(BF16)
    bond = lax.broadcasted_iota(jnp.int32, (1, bonds), 1)
    source = remainder(bond, atoms) * slots + slot_at(quotient(bond, atoms), slots)
    spot = lax.broadcasted_iota(jnp.int32, (bonds, bonds), 0)
    chosen = jnp.where(spot == source, 1.0, 0.0).astype(BF16)
    unit = jnp.dot(parts, chosen, preferred_element_type=F32)
    unit = unit[0:8] + unit[8:16] + unit[16:24]
    even = [jnp.broadcast_to(unit[k : k + 1, :pairs], (8, pairs)) for k in range(3)]
    odd = [jnp.broadcast_to(unit[k : k + 1, pairs:], (8, pairs)) for k in range(3)]
    row = lax.broadcasted_iota(jnp.int32, (8, pairs), 0)

    def turned(vector, places):
        places = places % (pairs // atoms)
        if places == 0:
            return vector
        return [pltpu.roll(part, pairs - atoms * places, 1) for part in vector]

    def basis(first, second):
        cosine = first[0] * second[0] + first[1] * second[1] + first[2] * second[2]
        series = [jnp.ones_like(cosine), cosine]
        double = cosine + cosine
        for _ in range(7):
            series.append(double * series[-1] - series[-2])
        lower = series[7]
        upper = series[1]
        for index in range(1, 8):
            lower = jnp.where(row == index, series[7 - index], lower)
            upper = jnp.where(row == index, series[1 + index], upper)
        double = series[8] + series[8]
        blocks = [lower, upper]
        for _ in range(degrees // 8 - 1):
            blocks.append(double * blocks[-1] - blocks[-2])
        return blocks[1:]

    for diagonal in range(slots):
        places = diagonal // 2
        if diagonal % 2 == 0:
            blocks = basis(even, turned(even, places)) + basis(odd, turned(odd, places))
        else:
            blocks = basis(even, turned(odd, places)) + basis(odd, turned(even, places + 1))
        series = jnp.concatenate(blocks, axis=0).T.astype(BF16)
        angular_ref[diagonal] = jnp.dot(series, weight, preferred_element_type=F32)
    for copy in copies:
        copy.wait()
    prepare_weights(slots, held, results)


def prepare_weights(slots, held, results):
    bond_in_ref, bond_mix_ref, pair_ref, pair_hidden_ref, pair_out_ref, atom_in_ref = held[:6]
    atom_out_ref = held[6]
    bond_weight_ref, mix_weight_ref, pair_weight_ref, hidden_weight_ref = results[:4]
    out_weight_ref, atom_in_weight_ref, sum_weight_ref, atom_out_weight_ref = results[4:]
    feature = bond_mix_ref.shape[0]
    weight = bond_in_ref[...].astype(F32)
    source, other, bond_part = (weight[k * feature : (k + 1) * feature] for k in range(3))
    blank = jnp.zeros_like(source)
    away = [crossed(bond_part, blank), crossed(source, other)]
    near = [crossed(other, source), crossed(blank, bond_part)]
    bond_weight_ref[...] = jnp.concatenate(away + near, axis=0).astype(BF16)
    mix_weight_ref[...] = diagonal_blocks(bond_mix_ref[...].astype(F32)).astype(BF16)
    old = pair_ref[...].astype(F32) * 0.5
    hidden = jnp.dot(bond_mix_ref[...], pair_ref[...], preferred_element_type=F32) * 0.5
    weight = jnp.concatenate([hidden, hidden, old, old], axis=0).astype(BF16)
    pair_weight_ref[...] = jnp.concatenate(
        [two_blocks(weight[:, : 2 * feature]), two_blocks(weight[:, 2 * feature :])], axis=1
    )
    hidden_weight_ref[...] = two_blocks(pair_hidden_ref[...].astype(F32)).astype(BF16)
    out_weight_ref[...] = diagonal_blocks(pair_out_ref[...].astype(F32)).astype(BF16)
    weight = atom_in_ref[...].astype(F32)
    weight = crossed(weight, jnp.zeros_like(weight))
    mean = weight[feature:] * (1.0 / slots)
    atom_in_weight_ref[...] = jnp.concatenate([weight[:feature], mean, mean], axis=0).astype(BF16)
    folded = jnp.dot(
        pair_out_ref[...], mean.astype(BF16), preferred_element_type=F32
    )
    high = folded.astype(BF16)
    low = (folded - high.astype(F32)).astype(BF16)
    sum_weight_ref[...] = jnp.concatenate([high, high, low, low], axis=0)
    weight = atom_out_ref[...].astype(F32)
    blank = jnp.zeros_like(weight)
    weight = jnp.concatenate([weight, blank], axis=1)
    atom_out_weight_ref[...] = jnp.concatenate([weight, jnp.zeros_like(weight)], axis=0).astype(
        BF16
    )


def prepare_kernel(
    extents,
    paired,
    spot_ref,
    targets_ref,
    atom_ref,
    bond_ref,
    dirs_hbm,
    angle_hbm,
    near_ref,
    chosen_ref,
    right_ref,
    own_ref,
    dirs_ref,
    angle_ref,
    sems,
):
    copies = [
        pltpu.make_async_copy(source, target, sems.at[k])
        for k, (source, target) in enumerate(((dirs_hbm, dirs_ref), (angle_hbm, angle_ref)))
    ]
    for copy in copies:
        copy.start()
    atoms, feature = atom_ref.shape[2], atom_ref.shape[3]
    slots = targets_ref.shape[0]
    bonds = slots * atoms
    near_ref[: 3 * CAP // 2] = packed_rows(spot_ref[...], bond_ref, slots, 3 * CAP // 2)
    near_ref[3 * CAP // 2 :] = atom_rows(atom_ref)
    targets = bond_row(targets_ref[...])
    code_x, code_y = bond_codes(targets, atoms, extents, paired, True)
    code = 3 * code_x + code_y
    bond = lax.broadcasted_iota(jnp.int32, (1, bonds), 1)
    far_slot = slots - 1 - slot_at(quotient(bond, atoms), slots)
    far_atom = remainder(targets, atoms)
    far = (remainder(far_slot, 2) * (slots // 2) + quotient(far_slot, 2)) * atoms + far_atom
    base = (code * bonds).astype(F32)
    key = base + far.astype(F32)

    def column(values):
        return jnp.broadcast_to(values.astype(F32), (128, bonds)).T

    keys = column(key)
    place = []
    for group in range(bonds // 128):
        here = slice(group * 128, (group + 1) * 128)
        inside = (keys < key[:, here]) & (keys >= base[:, here])
        place.append(jnp.sum(jnp.where(inside, 1.0, 0.0), axis=0, keepdims=True))
    place = jnp.concatenate(place, axis=1).astype(jnp.int32)
    half, tall = CAP // 2, atoms // 2
    bond_spot = column(half * code + remainder(place, half))
    atom_spot = column(9 * half + tall * code + remainder(far_atom, tall))
    right = (column(quotient(place, half)), column(quotient(far_atom, tall)))
    right_ref[...] = jnp.where(left_lanes((bonds, 128)), right[0], right[1])
    total = 9 * half + 9 * tall
    for start in range(0, total, 128):
        width = min(128, total - start)
        spot = lax.broadcasted_iota(jnp.int32, (bonds, 128), 1).astype(F32) + float(start)
        chosen = jnp.where((spot == bond_spot) | (spot == atom_spot), 1.0, 0.0).astype(BF16)
        chosen_ref[:, start : start + width] = chosen[:, :width]

    atom = atom_ref[0, 0]
    blocks = blocks_of(bond_ref, slots // 2)
    own = [jnp.concatenate([atom, x[:, :feature]], axis=1) for x in blocks]
    own += [jnp.concatenate([atom, x[:, feature:]], axis=1) for x in blocks]
    own = jnp.concatenate(own, axis=0)
    own_ref[...] = own
    for copy in copies:
        copy.wait()


def gated(values):
    half = values.shape[1] // 2
    first, second = values[:, :half], values[:, half:]
    return first * jax.nn.sigmoid(first) * jax.nn.sigmoid(second)


def main_kernel(
    near_ref,
    up_ref,
    down_ref,
    two_ref,
    one_ref,
    angular_ref,
    chosen_ref,
    right_ref,
    own_ref,
    bond_weight_ref,
    mix_weight_ref,
    pair_weight_ref,
    hidden_weight_ref,
    out_weight_ref,
    atom_in_weight_ref,
    sum_weight_ref,
    atom_out_weight_ref,
    atom_result_hbm,
    bond_result_hbm,
    atom_result_ref,
    bond_result_ref,
    first_ref,
    second_ref,
    pair_ref,
    sems,
):
    slots, pairs, _ = angular_ref.shape
    bonds = 2 * pairs
    atoms = bonds // slots
    feature = own_ref.shape[1] // 2
    width = 2 * feature
    half = CAP // 2
    near_refs = (near_ref, up_ref, down_ref)
    away_refs = (one_ref, two_ref)
    sent = [ref[:half] for ref in near_refs] + [ref[: 3 * half] for ref in away_refs]
    sent = jnp.concatenate(sent, axis=0)
    sent_atom = jnp.concatenate([ref[3 * half :] for ref in near_refs + away_refs], axis=0)
    blank = jnp.zeros((sent.shape[0], feature), BF16)
    blank_atom = jnp.zeros((sent_atom.shape[0], feature), BF16)
    received = jnp.concatenate(
        [
            jnp.concatenate([sent[:, :feature], blank, sent[:, feature:], blank], axis=1),
            jnp.concatenate(
                [blank_atom, sent_atom[:, :feature], blank_atom, sent_atom[:, feature:]], axis=1
            ),
        ],
        axis=0,
    )
    far = jnp.dot(chosen_ref[...], received, preferred_element_type=F32)
    far = jnp.where(right_ref[...] > 0.0, far[:, width:], far[:, :width])
    own = own_ref[...]
    incoming = jnp.dot(
        jnp.concatenate([far.astype(BF16), own], axis=1),
        bond_weight_ref[...],
        preferred_element_type=F32,
    )
    hidden = gated(incoming).astype(BF16)
    old = jnp.where(left_lanes((bonds, width)), far, own.astype(F32))
    both = jnp.concatenate([hidden, old.astype(BF16)], axis=1)
    even, odd = both[:pairs], both[pairs:]
    projected = jnp.dot(
        jnp.concatenate([even, odd], axis=1), pair_weight_ref[...], preferred_element_type=F32
    )
    first_ref[...] = projected[:, : 2 * width]
    second_ref[0] = projected[:, 2 * width :]
    shifted = jnp.concatenate([even[atoms:], even[:atoms]], axis=0)
    second_ref[1] = jnp.dot(
        jnp.concatenate([odd, shifted], axis=1),
        pair_weight_ref[:, 2 * width :],
        preferred_element_type=F32,
    )
    group = 2

    def first_gates(base):
        for start in range(0, pairs, atoms):
            here = first_ref[pl.ds(start, atoms)]
            for diagonal in range(base, base + group):
                there = (start + diagonal // 2 * atoms) % pairs
                mixture = angular_ref[diagonal, pl.ds(start, atoms)] + (
                    here + second_ref[diagonal % 2, pl.ds(there, atoms)]
                )
                pair_ref[pl.ds(diagonal * pairs + start, atoms)] = gated(mixture).astype(
                    BF16
                )

    def summed(rows):
        parts = [rows[k * atoms : (k + 1) * atoms] for k in range(slots // 2)]
        while len(parts) > 1:
            parts = [x + y for x, y in zip(parts[::2], parts[1::2])]
        return parts[0]

    total = jnp.zeros((pairs, width), F32)
    first_gates(0)
    for base in range(0, slots, group):
        if base + group < slots:
            first_gates(base + group)
        second = jnp.dot(
            pair_ref[pl.ds(base * pairs, group * pairs)],
            hidden_weight_ref[...],
            preferred_element_type=F32,
        )
        gates = gated(second)
        for k in range(group):
            total = total + gates[k * pairs : (k + 1) * pairs]
        if base == slots // 2:
            mixed = jnp.dot(hidden, mix_weight_ref[...], preferred_element_type=F32)
            new = (old + mixed).astype(BF16).astype(F32)
            average = ((new + pltpu.roll(new, feature, 1)) * 0.5).astype(BF16).astype(F32)
            packed = jnp.where(left_lanes((pairs, width)), average[:pairs], average[pairs:])
            atom = own[0:atoms]
            atom_incoming = jnp.dot(
                jnp.concatenate([atom[:, :feature], summed(packed).astype(BF16)], axis=1),
                atom_in_weight_ref[...],
                preferred_element_type=F32,
            )
    bond_out = packed + jnp.dot(
        total.astype(BF16), out_weight_ref[...], preferred_element_type=F32
    )
    bond_out = bond_out.astype(BF16)
    for k in range(slots // 2):
        bond_result_ref[0, 0, :, k * width : (k + 1) * width] = bond_out[
            k * atoms : (k + 1) * atoms
        ]
    copies = [pltpu.make_async_copy(bond_result_ref, bond_result_hbm, sems.at[0])]
    copies[0].start()
    sums = summed(total).astype(BF16)
    atom_incoming = atom_incoming + jnp.dot(
        jnp.concatenate([sums, sums], axis=1), sum_weight_ref[...], preferred_element_type=F32
    )
    atom_hidden = gated(atom_incoming).astype(BF16)
    atom_new = atom.astype(F32) + jnp.dot(
        atom_hidden, atom_out_weight_ref[...], preferred_element_type=F32
    )
    atom_result_ref[0, 0] = atom_new[:, :feature].astype(BF16)
    copies.append(pltpu.make_async_copy(atom_result_ref, atom_result_hbm, sems.at[1]))
    copies[-1].start()
    for copy in copies:
        copy.wait()


def per_device(
    atom_feat,
    bond_feat,
    neighbours,
    bond_dirs,
    bond_in_weight,
    bond_mix_weight,
    pair_weight,
    angle_weight,
    pair_hidden_weight,
    pair_out_weight,
    atom_in_weight,
    atom_out_weight,
):
    atoms, feature = atom_feat.shape[2], atom_feat.shape[3]
    slots = neighbours.shape[3]
    bonds = atoms * slots
    pairs = bonds // 2
    half = CAP // 2
    extents = (lax.axis_size("gx"), lax.axis_size("gy"))
    paired = (extents[0] % 2 == 0, False)
    targets = neighbours[0, 0].T
    hbm = pl.BlockSpec(memory_space=pltpu.HBM)
    vmem = pl.BlockSpec(memory_space=pltpu.VMEM)
    params = pltpu.CompilerParams(vmem_limit_bytes=32 * 2**20)

    def shaped(shape, dtype):
        return jax.ShapeDtypeStruct(shape, dtype)

    def in_hbm(arrays):
        return tuple(pltpu.with_memory_space_constraint(x, pltpu.HBM) for x in arrays)

    payload = shaped((3 * half + atoms // 2, 2 * feature), BF16)
    inputs = (targets, atom_feat, bond_feat)
    up, down, *held = pl.pallas_call(
        functools.partial(pack_kernel, extents, paired),
        out_shape=(payload, payload, shaped((1, bonds), jnp.int32))
        + tuple(shaped(x.shape, x.dtype) for x in inputs),
        in_specs=[hbm] * 3,
        out_specs=(vmem,) * 6,
        scratch_shapes=[pltpu.SemaphoreType.DMA((3,))],
        compiler_params=params,
        name="pack",
    )(*in_hbm(inputs))
    first, second = moves(extents[1], paired[1])
    up = lax.ppermute(up, "gy", first)
    down = lax.ppermute(down, "gy", second)
    weights = (bond_in_weight, bond_mix_weight, pair_weight, pair_hidden_weight)
    weights += (pair_out_weight, atom_in_weight, atom_out_weight)
    near, *prepared, bond_dirs, angle_weight = pl.pallas_call(
        functools.partial(prepare_kernel, extents, paired),
        out_shape=(
            payload,
            shaped((bonds, 9 * half + 9 * atoms // 2), BF16),
            shaped((bonds, 2 * feature), F32),
            shaped((bonds, 2 * feature), BF16),
            shaped(bond_dirs.shape, F32),
            shaped(angle_weight.shape, BF16),
        ),
        in_specs=[vmem] * 4 + [hbm] * 2,
        out_specs=(vmem,) * 6,
        scratch_shapes=[pltpu.SemaphoreType.DMA((2,))],
        compiler_params=params,
        cost_estimate=pl.CostEstimate(flops=64 * 2**20, bytes_accessed=2**21, transcendentals=0),
        name="prepare",
    )(*held, *in_hbm((bond_dirs, angle_weight)))
    near, up, down, prepared = lax.optimization_barrier((near, up, down, prepared))
    first, second = moves(extents[0], paired[0])

    def forwarded(block):
        parts = [x[block * half : (block + 1) * half] for x in (near, up, down)]
        return jnp.concatenate(parts + [x[3 * half :] for x in (near, up, down)], axis=0)

    one = lax.ppermute(forwarded(1), "gx", first)
    two = lax.ppermute(forwarded(2), "gx", second)
    angular, *made = pl.pallas_call(
        functools.partial(angular_kernel, atoms),
        out_shape=(
            shaped((slots, pairs, 4 * feature), F32),
            shaped((4 * feature, 4 * feature), BF16),
            shaped((2 * feature, 2 * feature), BF16),
            shaped((8 * feature, 8 * feature), BF16),
            shaped((2 * feature, 4 * feature), BF16),
            shaped((2 * feature, 2 * feature), BF16),
            shaped((3 * feature, 4 * feature), BF16),
            shaped((4 * feature, 4 * feature), BF16),
            shaped((2 * feature, 2 * feature), BF16),
        ),
        in_specs=[vmem] * 2 + [hbm] * 7,
        out_specs=(vmem,) * 9,
        scratch_shapes=[pltpu.VMEM(x.shape, BF16) for x in weights]
        + [pltpu.SemaphoreType.DMA((7,))],
        compiler_params=params,
        cost_estimate=pl.CostEstimate(
            flops=256 * 2**20, bytes_accessed=2**22, transcendentals=4096
        ),
        name="angular",
    )(bond_dirs, angle_weight, *in_hbm(weights))
    return pl.pallas_call(
        main_kernel,
        out_shape=(shaped(atom_feat.shape, BF16), shaped(bond_feat.shape, BF16)),
        in_specs=[vmem] * 17,
        out_specs=(hbm, hbm),
        scratch_shapes=[
            pltpu.VMEM(atom_feat.shape, BF16),
            pltpu.VMEM(bond_feat.shape, BF16),
            pltpu.VMEM((pairs, 4 * feature), F32),
            pltpu.VMEM((2, pairs, 4 * feature), F32),
            pltpu.VMEM((slots * pairs, 2 * feature), BF16),
            pltpu.SemaphoreType.DMA((2,)),
        ],
        compiler_params=params,
        name="main",
    )(near, up, down, two, one, angular, *prepared, *made)


def solution(mesh):
    placed = (
        P("gx", "gy", None, None),
        P("gx", "gy", None, None),
        P("gx", "gy", None, None),
        P(None, "gx", "gy", None),
        P(),
        P(),
        P(),
        P(),
        P(),
        P(),
        P(),
        P(),
    )
    return jax.shard_map(
        per_device,
        mesh=mesh,
        in_specs=placed,
        out_specs=(P("gx", "gy", None, None), P("gx", "gy", None, None)),
        check_vma=False,
    )
```

```python
import functools

import jax
import jax.numpy as jnp
from jax import lax
from jax.experimental import pallas as pl
from jax.experimental.pallas import tpu as pltpu
from jax.sharding import PartitionSpec as P

F32 = jnp.float32
BF16 = jnp.bfloat16
CAP = 64


def quotient(values, size):
    if size & (size - 1) == 0:
        return values >> (size.bit_length() - 1)
    return lax.div(values, jnp.int32(size))


def remainder(values, size):
    if size & (size - 1) == 0:
        return values & (size - 1)
    return lax.rem(values, jnp.int32(size))


def step_code(owner, home, extent, paired, receives):
    step = remainder(owner - home + 1 + extent, extent)
    if paired:
        ahead = jnp.where(remainder(home, 2) == 0, 0, 2)
    else:
        ahead = 0 if receives else 2
    return jnp.where(step == 1, 0, jnp.where(step == ahead, 1, 2))


def moves(extent, paired):
    if paired:
        near = [(i, i ^ 1) for i in range(extent)]
        return [(i, (((i + 1) ^ 1) - 1) % extent) for i in range(extent)], near
    up = [(i, (i + 1) % extent) for i in range(extent)]
    return up, [(j, i) for i, j in up]


def slot_at(position, slots):
    half = slots // 2
    return jnp.where(position < half, 2 * position, 2 * (position - half) + 1)


def bond_row(table):
    slots, atoms = table.shape
    per_group = 128 // atoms
    tiled = jnp.concatenate([table.astype(F32)] * per_group, axis=1)
    row = lax.broadcasted_iota(jnp.int32, tiled.shape, 0)
    position = quotient(lax.broadcasted_iota(jnp.int32, tiled.shape, 1), atoms)
    pieces = []
    for group in range(slots // per_group):
        chosen = row == slot_at(position + group * per_group, slots)
        pieces.append(jnp.sum(jnp.where(chosen, tiled, 0.0), axis=0, keepdims=True))
    return jnp.concatenate(pieces, axis=1).astype(jnp.int32)


def bond_codes(targets, atoms, extents, paired, receives):
    owner = quotient(targets, atoms)
    block = (quotient(owner, extents[1]), remainder(owner, extents[1]))
    return tuple(
        step_code(block[k], lax.axis_index(axis), extents[k], paired[k], receives)
        for k, axis in enumerate(("gx", "gy"))
    )


def left_lanes(shape):
    return lax.broadcasted_iota(jnp.int32, shape, 1) < shape[1] // 2


def swapped(rows):
    half = rows.shape[1] // 2
    return jnp.concatenate([rows[:, half:], rows[:, :half]], axis=1)


def blocks_of(bond_ref, pairs):
    width = bond_ref.shape[3] // pairs
    return [bond_ref[0, 0, :, k * width : (k + 1) * width] for k in range(pairs)]


def pack_kernel(
    extents,
    paired,
    targets_hbm,
    atom_hbm,
    bond_hbm,
    up_ref,
    down_ref,
    spot_ref,
    targets_ref,
    atom_ref,
    bond_ref,
    sems,
):
    sources = ((targets_hbm, targets_ref), (bond_hbm, bond_ref), (atom_hbm, atom_ref))
    copies = [
        pltpu.make_async_copy(source, target, sems.at[k])
        for k, (source, target) in enumerate(sources)
    ]
    for copy in copies:
        copy.start()
    atoms, feature = atom_ref.shape[2], atom_ref.shape[3]
    slots = targets_ref.shape[0]
    bonds = slots * atoms
    lanes = 128
    groups = bonds // lanes
    copies[0].wait()
    code_x, code_y = bond_codes(bond_row(targets_ref[...]), atoms, extents, paired, False)
    code = 3 * code_y + code_x
    rows = lax.broadcasted_iota(jnp.int32, (16, lanes), 0)
    marks = [rows == code[:, g * lanes : (g + 1) * lanes] for g in range(groups)]
    stacked = jnp.concatenate([m.astype(F32) for m in marks], axis=0).astype(BF16)
    before = lax.broadcasted_iota(jnp.int32, (lanes, 2 * lanes), 0)
    after = lax.broadcasted_iota(jnp.int32, (lanes, 2 * lanes), 1)
    sums = jnp.where((before < after) | (after >= lanes), 1.0, 0.0).astype(BF16)
    counted = jnp.dot(stacked, sums, preferred_element_type=F32)
    place = []
    earlier = jnp.zeros((16, lanes), F32)
    for g in range(groups):
        part = counted[g * 16 : (g + 1) * 16]
        place.append(
            jnp.sum(jnp.where(marks[g], part[:, :lanes] + earlier, 0.0), axis=0, keepdims=True)
        )
        earlier = earlier + part[:, lanes:]
    place = jnp.concatenate(place, axis=1).astype(jnp.int32)
    half = CAP // 2
    right = quotient(place, half)
    spot = place - half * right + half * code
    spot_ref[...] = jnp.where(code < 3, spot + 3 * half * right, -1)
    wanted = jnp.where(code < 3, -1, spot - 3 * half + 6 * half * right)
    copies[1].wait()
    copies[2].wait()
    packed = packed_rows(wanted, bond_ref, slots, 6 * half)
    for k, ref in enumerate((up_ref, down_ref)):
        ref[: 3 * half] = packed[3 * half * k : 3 * half * (k + 1)]
        ref[3 * half :] = atom_rows(atom_ref)


def packed_rows(wanted, bond_ref, slots, count):
    spot = lax.broadcasted_iota(jnp.int32, (2 * count, wanted.shape[1]), 0)
    chosen = jnp.where(spot == wanted, 1.0, 0.0).astype(BF16)
    blocks = blocks_of(bond_ref, slots // 2)
    feature = blocks[0].shape[1] // 2
    values = [jnp.concatenate([x[:, :feature]] * 2, axis=1) for x in blocks]
    values += [jnp.concatenate([x[:, feature:]] * 2, axis=1) for x in blocks]
    packed = jnp.dot(chosen, jnp.concatenate(values, axis=0), preferred_element_type=F32)
    left = left_lanes((count, 2 * feature))
    return jnp.where(left, packed[:count], packed[count:]).astype(BF16)


def atom_rows(atom_ref):
    atom = atom_ref[0, 0]
    half = atom.shape[0] // 2
    return jnp.concatenate([atom[:half], atom[half:]], axis=1)


def crossed(left, right):
    half = left.shape[1] // 2
    parts = [left[:, :half], right[:, :half], left[:, half:], right[:, half:]]
    return jnp.concatenate(parts, axis=1)


def two_blocks(weight):
    blank = jnp.zeros_like(weight)
    return jnp.concatenate([crossed(weight, blank), crossed(blank, weight)], axis=0)


def diagonal_blocks(weight):
    blank = jnp.zeros_like(weight)
    return jnp.concatenate(
        [jnp.concatenate([weight, blank], axis=1), jnp.concatenate([blank, weight], axis=1)],
        axis=0,
    )


def angular_kernel(atoms, dirs_ref, angle_ref, *refs):
    sources, angular_ref, results, held, sems = refs[:7], refs[7], refs[8:16], refs[16:23], refs[23]
    copies = [
        pltpu.make_async_copy(source, target, sems.at[k])
        for k, (source, target) in enumerate(zip(sources, held))
    ]
    for copy in copies:
        copy.start()
    slots, pairs, _ = angular_ref.shape
    bonds = 2 * pairs
    degrees = angle_ref.shape[0]
    weight = two_blocks(angle_ref[...].astype(F32)).astype(BF16)
    polar, azimuth = dirs_ref[0, 0], dirs_ref[1, 0]
    unit = jnp.concatenate(
        [
            jnp.sin(polar) * jnp.cos(azimuth),
            jnp.sin(polar) * jnp.sin(azimuth),
            jnp.cos(polar),
            jnp.zeros((5, bonds), F32),
        ],
        axis=0,
    )
    high = unit.astype(BF16).astype(F32)
    middle = (unit - high).astype(BF16).astype(F32)
    parts = jnp.concatenate([high, middle, unit - high - middle], axis=0).astype(BF16)
    bond = lax.broadcasted_iota(jnp.int32, (1, bonds), 1)
    source = remainder(bond, atoms) * slots + slot_at(quotient(bond, atoms), slots)
    spot = lax.broadcasted_iota(jnp.int32, (bonds, bonds), 0)
    chosen = jnp.where(spot == source, 1.0, 0.0).astype(BF16)
    unit = jnp.dot(parts, chosen, preferred_element_type=F32)
    unit = unit[0:8] + unit[8:16] + unit[16:24]
    even = [jnp.broadcast_to(unit[k : k + 1, :pairs], (8, pairs)) for k in range(3)]
    odd = [jnp.broadcast_to(unit[k : k + 1, pairs:], (8, pairs)) for k in range(3)]
    row = lax.broadcasted_iota(jnp.int32, (8, pairs), 0)

    def turned(vector, places):
        places = places % (pairs // atoms)
        if places == 0:
            return vector
        return [pltpu.roll(part, pairs - atoms * places, 1) for part in vector]

    def basis(first, second):
        cosine = first[0] * second[0] + first[1] * second[1] + first[2] * second[2]
        series = [jnp.ones_like(cosine), cosine]
        double = cosine + cosine
        for _ in range(7):
            series.append(double * series[-1] - series[-2])
        lower = series[7]
        upper = series[1]
        for index in range(1, 8):
            lower = jnp.where(row == index, series[7 - index], lower)
            upper = jnp.where(row == index, series[1 + index], upper)
        double = series[8] + series[8]
        blocks = [lower, upper]
        for _ in range(degrees // 8 - 1):
            blocks.append(double * blocks[-1] - blocks[-2])
        return blocks[1:]

    for diagonal in range(slots):
        places = diagonal // 2
        if diagonal % 2 == 0:
            blocks = basis(even, turned(even, places)) + basis(odd, turned(odd, places))
        else:
            blocks = basis(even, turned(odd, places)) + basis(odd, turned(even, places + 1))
        series = jnp.concatenate(blocks, axis=0).T.astype(BF16)
        angular_ref[diagonal] = jnp.dot(series, weight, preferred_element_type=F32)
    for copy in copies:
        copy.wait()
    prepare_weights(slots, held, results)


def prepare_weights(slots, held, results):
    bond_in_ref, bond_mix_ref, pair_ref, pair_hidden_ref, pair_out_ref, atom_in_ref = held[:6]
    atom_out_ref = held[6]
    bond_weight_ref, mix_weight_ref, pair_weight_ref, hidden_weight_ref = results[:4]
    out_weight_ref, atom_in_weight_ref, sum_weight_ref, atom_out_weight_ref = results[4:]
    feature = bond_mix_ref.shape[0]
    weight = bond_in_ref[...].astype(F32)
    source, other, bond_part = (weight[k * feature : (k + 1) * feature] for k in range(3))
    blank = jnp.zeros_like(source)
    away = [crossed(bond_part, blank), crossed(source, other)]
    near = [crossed(other, source), crossed(blank, bond_part)]
    bond_weight_ref[...] = jnp.concatenate(away + near, axis=0).astype(BF16)
    mix_weight_ref[...] = diagonal_blocks(bond_mix_ref[...].astype(F32)).astype(BF16)
    old = pair_ref[...].astype(F32) * 0.5
    hidden = jnp.dot(bond_mix_ref[...], pair_ref[...], preferred_element_type=F32) * 0.5
    weight = jnp.concatenate([hidden, hidden, old, old], axis=0).astype(BF16)
    pair_weight_ref[...] = jnp.concatenate(
        [two_blocks(weight[:, : 2 * feature]), two_blocks(weight[:, 2 * feature :])], axis=1
    )
    hidden_weight_ref[...] = two_blocks(pair_hidden_ref[...].astype(F32)).astype(BF16)
    out_weight_ref[...] = diagonal_blocks(pair_out_ref[...].astype(F32)).astype(BF16)
    weight = atom_in_ref[...].astype(F32)
    weight = crossed(weight, jnp.zeros_like(weight))
    mean = weight[feature:] * (1.0 / slots)
    atom_in_weight_ref[...] = jnp.concatenate([weight[:feature], mean, mean], axis=0).astype(BF16)
    folded = jnp.dot(
        pair_out_ref[...], mean.astype(BF16), preferred_element_type=F32
    )
    high = folded.astype(BF16)
    low = (folded - high.astype(F32)).astype(BF16)
    sum_weight_ref[...] = jnp.concatenate([high, high, low, low], axis=0)
    weight = atom_out_ref[...].astype(F32)
    blank = jnp.zeros_like(weight)
    weight = jnp.concatenate([weight, blank], axis=1)
    atom_out_weight_ref[...] = jnp.concatenate([weight, jnp.zeros_like(weight)], axis=0).astype(
        BF16
    )


def prepare_kernel(
    extents,
    paired,
    spot_ref,
    targets_ref,
    atom_ref,
    bond_ref,
    dirs_hbm,
    angle_hbm,
    near_ref,
    chosen_ref,
    right_ref,
    own_ref,
    dirs_ref,
    angle_ref,
    sems,
):
    copies = [
        pltpu.make_async_copy(source, target, sems.at[k])
        for k, (source, target) in enumerate(((dirs_hbm, dirs_ref), (angle_hbm, angle_ref)))
    ]
    for copy in copies:
        copy.start()
    atoms, feature = atom_ref.shape[2], atom_ref.shape[3]
    slots = targets_ref.shape[0]
    bonds = slots * atoms
    near_ref[: 3 * CAP // 2] = packed_rows(spot_ref[...], bond_ref, slots, 3 * CAP // 2)
    near_ref[3 * CAP // 2 :] = atom_rows(atom_ref)
    targets = bond_row(targets_ref[...])
    code_x, code_y = bond_codes(targets, atoms, extents, paired, True)
    code = 3 * code_x + code_y
    bond = lax.broadcasted_iota(jnp.int32, (1, bonds), 1)
    far_slot = slots - 1 - slot_at(quotient(bond, atoms), slots)
    far_atom = remainder(targets, atoms)
    far = (remainder(far_slot, 2) * (slots // 2) + quotient(far_slot, 2)) * atoms + far_atom
    base = (code * bonds).astype(F32)
    key = base + far.astype(F32)

    def column(values):
        return jnp.broadcast_to(values.astype(F32), (128, bonds)).T

    keys = column(key)
    place = []
    for group in range(bonds // 128):
        here = slice(group * 128, (group + 1) * 128)
        inside = (keys < key[:, here]) & (keys >= base[:, here])
        place.append(jnp.sum(jnp.where(inside, 1.0, 0.0), axis=0, keepdims=True))
    place = jnp.concatenate(place, axis=1).astype(jnp.int32)
    half, tall = CAP // 2, atoms // 2
    bond_spot = column(half * code + remainder(place, half))
    atom_spot = column(9 * half + tall * code + remainder(far_atom, tall))
    right = (column(quotient(place, half)), column(quotient(far_atom, tall)))
    right_ref[...] = jnp.where(left_lanes((bonds, 128)), right[0], right[1])
    total = 9 * half + 9 * tall
    for start in range(0, total, 128):
        width = min(128, total - start)
        spot = lax.broadcasted_iota(jnp.int32, (bonds, 128), 1).astype(F32) + float(start)
        chosen = jnp.where((spot == bond_spot) | (spot == atom_spot), 1.0, 0.0).astype(BF16)
        chosen_ref[:, start : start + width] = chosen[:, :width]

    atom = atom_ref[0, 0]
    blocks = blocks_of(bond_ref, slots // 2)
    own = [jnp.concatenate([atom, x[:, :feature]], axis=1) for x in blocks]
    own += [jnp.concatenate([atom, x[:, feature:]], axis=1) for x in blocks]
    own = jnp.concatenate(own, axis=0)
    own_ref[...] = own
    for copy in copies:
        copy.wait()


def gated(values):
    half = values.shape[1] // 2
    first, second = values[:, :half], values[:, half:]
    return first * jax.nn.sigmoid(first) * jax.nn.sigmoid(second)


def main_kernel(
    near_ref,
    up_ref,
    down_ref,
    two_ref,
    one_ref,
    angular_ref,
    chosen_ref,
    right_ref,
    own_ref,
    bond_weight_ref,
    mix_weight_ref,
    pair_weight_ref,
    hidden_weight_ref,
    out_weight_ref,
    atom_in_weight_ref,
    sum_weight_ref,
    atom_out_weight_ref,
    atom_result_hbm,
    bond_result_hbm,
    atom_result_ref,
    bond_result_ref,
    first_ref,
    second_ref,
    pair_ref,
    sems,
):
    slots, pairs, _ = angular_ref.shape
    bonds = 2 * pairs
    atoms = bonds // slots
    feature = own_ref.shape[1] // 2
    width = 2 * feature
    half = CAP // 2
    near_refs = (near_ref, up_ref, down_ref)
    away_refs = (one_ref, two_ref)
    sent = [ref[:half] for ref in near_refs] + [ref[: 3 * half] for ref in away_refs]
    sent = jnp.concatenate(sent, axis=0)
    sent_atom = jnp.concatenate([ref[3 * half :] for ref in near_refs + away_refs], axis=0)
    blank = jnp.zeros((sent.shape[0], feature), BF16)
    blank_atom = jnp.zeros((sent_atom.shape[0], feature), BF16)
    received = jnp.concatenate(
        [
            jnp.concatenate([sent[:, :feature], blank, sent[:, feature:], blank], axis=1),
            jnp.concatenate(
                [blank_atom, sent_atom[:, :feature], blank_atom, sent_atom[:, feature:]], axis=1
            ),
        ],
        axis=0,
    )
    far = jnp.dot(chosen_ref[...], received, preferred_element_type=F32)
    far = jnp.where(right_ref[...] > 0.0, far[:, width:], far[:, :width])
    own = own_ref[...]
    incoming = jnp.dot(
        jnp.concatenate([far.astype(BF16), own], axis=1),
        bond_weight_ref[...],
        preferred_element_type=F32,
    )
    hidden = gated(incoming).astype(BF16)
    old = jnp.where(left_lanes((bonds, width)), far, own.astype(F32))
    both = jnp.concatenate([hidden, old.astype(BF16)], axis=1)
    even, odd = both[:pairs], both[pairs:]
    projected = jnp.dot(
        jnp.concatenate([even, odd], axis=1), pair_weight_ref[...], preferred_element_type=F32
    )
    first_ref[...] = projected[:, : 2 * width]
    second_ref[0] = projected[:, 2 * width :]
    shifted = jnp.concatenate([even[atoms:], even[:atoms]], axis=0)
    second_ref[1] = jnp.dot(
        jnp.concatenate([odd, shifted], axis=1),
        pair_weight_ref[:, 2 * width :],
        preferred_element_type=F32,
    )
    mixed = jnp.dot(hidden, mix_weight_ref[...], preferred_element_type=F32)
    new = (old + mixed).astype(BF16).astype(F32)
    average = ((new + pltpu.roll(new, feature, 1)) * 0.5).astype(BF16).astype(F32)
    packed = jnp.where(left_lanes((pairs, width)), average[:pairs], average[pairs:])
    group = 2

    def first_gates(base):
        for start in range(0, pairs, atoms):
            here = first_ref[pl.ds(start, atoms)]
            for diagonal in range(base, base + group):
                there = (start + diagonal // 2 * atoms) % pairs
                mixture = angular_ref[diagonal, pl.ds(start, atoms)] + (
                    here + second_ref[diagonal % 2, pl.ds(there, atoms)]
                )
                pair_ref[pl.ds(diagonal * pairs + start, atoms)] = gated(mixture).astype(
                    BF16
                )

    def summed(rows):
        parts = [rows[k * atoms : (k + 1) * atoms] for k in range(slots // 2)]
        while len(parts) > 1:
            parts = [x + y for x, y in zip(parts[::2], parts[1::2])]
        return parts[0]

    atom = own[0:atoms]
    atom_incoming = jnp.dot(
        jnp.concatenate([atom[:, :feature], summed(packed).astype(BF16)], axis=1),
        atom_in_weight_ref[...],
        preferred_element_type=F32,
    )
    total = jnp.zeros((pairs, width), F32)
    first_gates(0)
    for base in range(0, slots, group):
        if base + group < slots:
            first_gates(base + group)
        second = jnp.dot(
            pair_ref[pl.ds(base * pairs, group * pairs)],
            hidden_weight_ref[...],
            preferred_element_type=F32,
        )
        gates = gated(second)
        for k in range(group):
            total = total + gates[k * pairs : (k + 1) * pairs]
    bond_out = packed + jnp.dot(
        total.astype(BF16), out_weight_ref[...], preferred_element_type=F32
    )
    bond_out = bond_out.astype(BF16)
    for k in range(slots // 2):
        bond_result_ref[0, 0, :, k * width : (k + 1) * width] = bond_out[
            k * atoms : (k + 1) * atoms
        ]
    copies = [pltpu.make_async_copy(bond_result_ref, bond_result_hbm, sems.at[0])]
    copies[0].start()
    sums = summed(total).astype(BF16)
    atom_incoming = atom_incoming + jnp.dot(
        jnp.concatenate([sums, sums], axis=1), sum_weight_ref[...], preferred_element_type=F32
    )
    atom_hidden = gated(atom_incoming).astype(BF16)
    atom_new = atom.astype(F32) + jnp.dot(
        atom_hidden, atom_out_weight_ref[...], preferred_element_type=F32
    )
    atom_result_ref[0, 0] = atom_new[:, :feature].astype(BF16)
    copies.append(pltpu.make_async_copy(atom_result_ref, atom_result_hbm, sems.at[1]))
    copies[-1].start()
    for copy in copies:
        copy.wait()


def per_device(
    atom_feat,
    bond_feat,
    neighbours,
    bond_dirs,
    bond_in_weight,
    bond_mix_weight,
    pair_weight,
    angle_weight,
    pair_hidden_weight,
    pair_out_weight,
    atom_in_weight,
    atom_out_weight,
):
    atoms, feature = atom_feat.shape[2], atom_feat.shape[3]
    slots = neighbours.shape[3]
    bonds = atoms * slots
    pairs = bonds // 2
    half = CAP // 2
    extents = (lax.axis_size("gx"), lax.axis_size("gy"))
    paired = (extents[0] % 2 == 0, False)
    targets = neighbours[0, 0].T
    hbm = pl.BlockSpec(memory_space=pltpu.HBM)
    vmem = pl.BlockSpec(memory_space=pltpu.VMEM)
    params = pltpu.CompilerParams(vmem_limit_bytes=32 * 2**20)

    def shaped(shape, dtype):
        return jax.ShapeDtypeStruct(shape, dtype)

    def in_hbm(arrays):
        return tuple(pltpu.with_memory_space_constraint(x, pltpu.HBM) for x in arrays)

    payload = shaped((3 * half + atoms // 2, 2 * feature), BF16)
    inputs = (targets, atom_feat, bond_feat)
    up, down, *held = pl.pallas_call(
        functools.partial(pack_kernel, extents, paired),
        out_shape=(payload, payload, shaped((1, bonds), jnp.int32))
        + tuple(shaped(x.shape, x.dtype) for x in inputs),
        in_specs=[hbm] * 3,
        out_specs=(vmem,) * 6,
        scratch_shapes=[pltpu.SemaphoreType.DMA((3,))],
        compiler_params=params,
        name="pack",
    )(*in_hbm(inputs))
    first, second = moves(extents[1], paired[1])
    up = lax.ppermute(up, "gy", first)
    down = lax.ppermute(down, "gy", second)
    weights = (bond_in_weight, bond_mix_weight, pair_weight, pair_hidden_weight)
    weights += (pair_out_weight, atom_in_weight, atom_out_weight)
    near, *prepared, bond_dirs, angle_weight = pl.pallas_call(
        functools.partial(prepare_kernel, extents, paired),
        out_shape=(
            payload,
            shaped((bonds, 9 * half + 9 * atoms // 2), BF16),
            shaped((bonds, 2 * feature), F32),
            shaped((bonds, 2 * feature), BF16),
            shaped(bond_dirs.shape, F32),
            shaped(angle_weight.shape, BF16),
        ),
        in_specs=[vmem] * 4 + [hbm] * 2,
        out_specs=(vmem,) * 6,
        scratch_shapes=[pltpu.SemaphoreType.DMA((2,))],
        compiler_params=params,
        cost_estimate=pl.CostEstimate(flops=64 * 2**20, bytes_accessed=2**21, transcendentals=0),
        name="prepare",
    )(*held, *in_hbm((bond_dirs, angle_weight)))
    near, up, down, prepared = lax.optimization_barrier((near, up, down, prepared))
    first, second = moves(extents[0], paired[0])

    def forwarded(block):
        parts = [x[block * half : (block + 1) * half] for x in (near, up, down)]
        return jnp.concatenate(parts + [x[3 * half :] for x in (near, up, down)], axis=0)

    one = lax.ppermute(forwarded(1), "gx", first)
    two = lax.ppermute(forwarded(2), "gx", second)
    angular, *made = pl.pallas_call(
        functools.partial(angular_kernel, atoms),
        out_shape=(
            shaped((slots, pairs, 4 * feature), F32),
            shaped((4 * feature, 4 * feature), BF16),
            shaped((2 * feature, 2 * feature), BF16),
            shaped((8 * feature, 8 * feature), BF16),
            shaped((2 * feature, 4 * feature), BF16),
            shaped((2 * feature, 2 * feature), BF16),
            shaped((3 * feature, 4 * feature), BF16),
            shaped((4 * feature, 4 * feature), BF16),
            shaped((2 * feature, 2 * feature), BF16),
        ),
        in_specs=[vmem] * 2 + [hbm] * 7,
        out_specs=(vmem,) * 9,
        scratch_shapes=[pltpu.VMEM(x.shape, BF16) for x in weights]
        + [pltpu.SemaphoreType.DMA((7,))],
        compiler_params=params,
        cost_estimate=pl.CostEstimate(
            flops=256 * 2**20, bytes_accessed=2**22, transcendentals=4096
        ),
        name="angular",
    )(bond_dirs, angle_weight, *in_hbm(weights))
    return pl.pallas_call(
        main_kernel,
        out_shape=(shaped(atom_feat.shape, BF16), shaped(bond_feat.shape, BF16)),
        in_specs=[vmem] * 17,
        out_specs=(hbm, hbm),
        scratch_shapes=[
            pltpu.VMEM(atom_feat.shape, BF16),
            pltpu.VMEM(bond_feat.shape, BF16),
            pltpu.VMEM((pairs, 4 * feature), F32),
            pltpu.VMEM((2, pairs, 4 * feature), F32),
            pltpu.VMEM((slots * pairs, 2 * feature), BF16),
            pltpu.SemaphoreType.DMA((2,)),
        ],
        compiler_params=params,
        name="main",
    )(near, up, down, two, one, angular, *prepared, *made)


def solution(mesh):
    placed = (
        P("gx", "gy", None, None),
        P("gx", "gy", None, None),
        P("gx", "gy", None, None),
        P(None, "gx", "gy", None),
        P(),
        P(),
        P(),
        P(),
        P(),
        P(),
        P(),
        P(),
    )
    return jax.shard_map(
        per_device,
        mesh=mesh,
        in_specs=placed,
        out_specs=(P("gx", "gy", None, None), P("gx", "gy", None, None)),
        check_vma=False,
    )
```

```python
import functools

import jax
import jax.numpy as jnp
from jax import lax
from jax.experimental import pallas as pl
from jax.experimental.pallas import tpu as pltpu
from jax.sharding import PartitionSpec as P

F32 = jnp.float32
BF16 = jnp.bfloat16
CAP = 64


def quotient(values, size):
    if size & (size - 1) == 0:
        return values >> (size.bit_length() - 1)
    return lax.div(values, jnp.int32(size))


def remainder(values, size):
    if size & (size - 1) == 0:
        return values & (size - 1)
    return lax.rem(values, jnp.int32(size))


def step_code(owner, home, extent, paired, receives):
    step = remainder(owner - home + 1 + extent, extent)
    if paired:
        ahead = jnp.where(remainder(home, 2) == 0, 0, 2)
    else:
        ahead = 0 if receives else 2
    return jnp.where(step == 1, 0, jnp.where(step == ahead, 1, 2))


def moves(extent, paired):
    if paired:
        near = [(i, i ^ 1) for i in range(extent)]
        return [(i, (((i + 1) ^ 1) - 1) % extent) for i in range(extent)], near
    up = [(i, (i + 1) % extent) for i in range(extent)]
    return up, [(j, i) for i, j in up]


def slot_at(position, slots):
    half = slots // 2
    return jnp.where(position < half, 2 * position, 2 * (position - half) + 1)


def bond_row(table):
    slots, atoms = table.shape
    per_group = 128 // atoms
    tiled = jnp.concatenate([table.astype(F32)] * per_group, axis=1)
    row = lax.broadcasted_iota(jnp.int32, tiled.shape, 0)
    position = quotient(lax.broadcasted_iota(jnp.int32, tiled.shape, 1), atoms)
    pieces = []
    for group in range(slots // per_group):
        chosen = row == slot_at(position + group * per_group, slots)
        pieces.append(jnp.sum(jnp.where(chosen, tiled, 0.0), axis=0, keepdims=True))
    return jnp.concatenate(pieces, axis=1).astype(jnp.int32)


def bond_codes(targets, atoms, extents, paired, receives):
    owner = quotient(targets, atoms)
    block = (quotient(owner, extents[1]), remainder(owner, extents[1]))
    return tuple(
        step_code(block[k], lax.axis_index(axis), extents[k], paired[k], receives)
        for k, axis in enumerate(("gx", "gy"))
    )


def left_lanes(shape):
    return lax.broadcasted_iota(jnp.int32, shape, 1) < shape[1] // 2


def swapped(rows):
    half = rows.shape[1] // 2
    return jnp.concatenate([rows[:, half:], rows[:, :half]], axis=1)


def blocks_of(bond_ref, pairs):
    width = bond_ref.shape[3] // pairs
    return [bond_ref[0, 0, :, k * width : (k + 1) * width] for k in range(pairs)]


def pack_kernel(
    extents,
    paired,
    targets_hbm,
    atom_hbm,
    bond_hbm,
    up_ref,
    down_ref,
    spot_ref,
    targets_ref,
    atom_ref,
    bond_ref,
    sems,
):
    sources = ((targets_hbm, targets_ref), (bond_hbm, bond_ref), (atom_hbm, atom_ref))
    copies = [
        pltpu.make_async_copy(source, target, sems.at[k])
        for k, (source, target) in enumerate(sources)
    ]
    for copy in copies:
        copy.start()
    atoms, feature = atom_ref.shape[2], atom_ref.shape[3]
    slots = targets_ref.shape[0]
    bonds = slots * atoms
    lanes = 128
    groups = bonds // lanes
    copies[0].wait()
    code_x, code_y = bond_codes(bond_row(targets_ref[...]), atoms, extents, paired, False)
    code = 3 * code_y + code_x
    rows = lax.broadcasted_iota(jnp.int32, (16, lanes), 0)
    marks = [rows == code[:, g * lanes : (g + 1) * lanes] for g in range(groups)]
    stacked = jnp.concatenate([m.astype(F32) for m in marks], axis=0).astype(BF16)
    before = lax.broadcasted_iota(jnp.int32, (lanes, 2 * lanes), 0)
    after = lax.broadcasted_iota(jnp.int32, (lanes, 2 * lanes), 1)
    sums = jnp.where((before < after) | (after >= lanes), 1.0, 0.0).astype(BF16)
    counted = jnp.dot(stacked, sums, preferred_element_type=F32)
    place = []
    earlier = jnp.zeros((16, lanes), F32)
    for g in range(groups):
        part = counted[g * 16 : (g + 1) * 16]
        place.append(
            jnp.sum(jnp.where(marks[g], part[:, :lanes] + earlier, 0.0), axis=0, keepdims=True)
        )
        earlier = earlier + part[:, lanes:]
    place = jnp.concatenate(place, axis=1).astype(jnp.int32)
    half = CAP // 2
    right = quotient(place, half)
    spot = place - half * right + half * code
    spot_ref[...] = jnp.where(code < 3, spot + 3 * half * right, -1)
    wanted = jnp.where(code < 3, -1, spot - 3 * half + 6 * half * right)
    copies[1].wait()
    copies[2].wait()
    packed = packed_rows(wanted, bond_ref, slots, 6 * half)
    for k, ref in enumerate((up_ref, down_ref)):
        ref[: 3 * half] = packed[3 * half * k : 3 * half * (k + 1)]
        ref[3 * half :] = atom_rows(atom_ref)


def packed_rows(wanted, bond_ref, slots, count):
    spot = lax.broadcasted_iota(jnp.int32, (2 * count, wanted.shape[1]), 0)
    chosen = jnp.where(spot == wanted, 1.0, 0.0).astype(BF16)
    blocks = blocks_of(bond_ref, slots // 2)
    feature = blocks[0].shape[1] // 2
    values = [jnp.concatenate([x[:, :feature]] * 2, axis=1) for x in blocks]
    values += [jnp.concatenate([x[:, feature:]] * 2, axis=1) for x in blocks]
    packed = jnp.dot(chosen, jnp.concatenate(values, axis=0), preferred_element_type=F32)
    left = left_lanes((count, 2 * feature))
    return jnp.where(left, packed[:count], packed[count:]).astype(BF16)


def atom_rows(atom_ref):
    atom = atom_ref[0, 0]
    half = atom.shape[0] // 2
    return jnp.concatenate([atom[:half], atom[half:]], axis=1)


def crossed(left, right):
    half = left.shape[1] // 2
    parts = [left[:, :half], right[:, :half], left[:, half:], right[:, half:]]
    return jnp.concatenate(parts, axis=1)


def two_blocks(weight):
    blank = jnp.zeros_like(weight)
    return jnp.concatenate([crossed(weight, blank), crossed(blank, weight)], axis=0)


def diagonal_blocks(weight):
    blank = jnp.zeros_like(weight)
    return jnp.concatenate(
        [jnp.concatenate([weight, blank], axis=1), jnp.concatenate([blank, weight], axis=1)],
        axis=0,
    )


def angular_kernel(atoms, dirs_ref, angle_ref, *refs):
    sources, angular_ref, results, held, sems = refs[:7], refs[7], refs[8:16], refs[16:23], refs[23]
    copies = [
        pltpu.make_async_copy(source, target, sems.at[k])
        for k, (source, target) in enumerate(zip(sources, held))
    ]
    for copy in copies:
        copy.start()
    slots, pairs, _ = angular_ref.shape
    bonds = 2 * pairs
    degrees = angle_ref.shape[0]
    weight = two_blocks(angle_ref[...].astype(F32)).astype(BF16)
    polar, azimuth = dirs_ref[0, 0], dirs_ref[1, 0]
    unit = jnp.concatenate(
        [
            jnp.sin(polar) * jnp.cos(azimuth),
            jnp.sin(polar) * jnp.sin(azimuth),
            jnp.cos(polar),
            jnp.zeros((5, bonds), F32),
        ],
        axis=0,
    )
    high = unit.astype(BF16).astype(F32)
    middle = (unit - high).astype(BF16).astype(F32)
    parts = jnp.concatenate([high, middle, unit - high - middle], axis=0).astype(BF16)
    bond = lax.broadcasted_iota(jnp.int32, (1, bonds), 1)
    source = remainder(bond, atoms) * slots + slot_at(quotient(bond, atoms), slots)
    spot = lax.broadcasted_iota(jnp.int32, (bonds, bonds), 0)
    chosen = jnp.where(spot == source, 1.0, 0.0).astype(BF16)
    unit = jnp.dot(parts, chosen, preferred_element_type=F32)
    unit = unit[0:8] + unit[8:16] + unit[16:24]
    even = [jnp.broadcast_to(unit[k : k + 1, :pairs], (8, pairs)) for k in range(3)]
    odd = [jnp.broadcast_to(unit[k : k + 1, pairs:], (8, pairs)) for k in range(3)]
    row = lax.broadcasted_iota(jnp.int32, (8, pairs), 0)

    def turned(vector, places):
        places = places % (pairs // atoms)
        if places == 0:
            return vector
        return [pltpu.roll(part, pairs - atoms * places, 1) for part in vector]

    def basis(first, second):
        cosine = first[0] * second[0] + first[1] * second[1] + first[2] * second[2]
        series = [jnp.ones_like(cosine), cosine]
        double = cosine + cosine
        for _ in range(7):
            series.append(double * series[-1] - series[-2])
        lower = series[7]
        upper = series[1]
        for index in range(1, 8):
            lower = jnp.where(row == index, series[7 - index], lower)
            upper = jnp.where(row == index, series[1 + index], upper)
        double = series[8] + series[8]
        blocks = [lower, upper]
        for _ in range(degrees // 8 - 1):
            blocks.append(double * blocks[-1] - blocks[-2])
        return blocks[1:]

    for diagonal in range(slots):
        places = diagonal // 2
        if diagonal % 2 == 0:
            blocks = basis(even, turned(even, places)) + basis(odd, turned(odd, places))
        else:
            blocks = basis(even, turned(odd, places)) + basis(odd, turned(even, places + 1))
        series = jnp.concatenate(blocks, axis=0).T.astype(BF16)
        angular_ref[diagonal] = jnp.dot(series, weight, preferred_element_type=F32)
    for copy in copies:
        copy.wait()
    prepare_weights(slots, held, results)


def prepare_weights(slots, held, results):
    bond_in_ref, bond_mix_ref, pair_ref, pair_hidden_ref, pair_out_ref, atom_in_ref = held[:6]
    atom_out_ref = held[6]
    bond_weight_ref, mix_weight_ref, pair_weight_ref, hidden_weight_ref = results[:4]
    out_weight_ref, atom_in_weight_ref, sum_weight_ref, atom_out_weight_ref = results[4:]
    feature = bond_mix_ref.shape[0]
    weight = bond_in_ref[...].astype(F32)
    source, other, bond_part = (weight[k * feature : (k + 1) * feature] for k in range(3))
    blank = jnp.zeros_like(source)
    away = [crossed(bond_part, blank), crossed(source, other)]
    near = [crossed(other, source), crossed(blank, bond_part)]
    bond_weight_ref[...] = jnp.concatenate(away + near, axis=0).astype(BF16)
    mix_weight_ref[...] = diagonal_blocks(bond_mix_ref[...].astype(F32)).astype(BF16)
    old = pair_ref[...].astype(F32) * 0.5
    hidden = jnp.dot(bond_mix_ref[...], pair_ref[...], preferred_element_type=F32) * 0.5
    weight = jnp.concatenate([hidden, hidden, old, old], axis=0).astype(BF16)
    pair_weight_ref[...] = jnp.concatenate(
        [two_blocks(weight[:, : 2 * feature]), two_blocks(weight[:, 2 * feature :])], axis=1
    )
    hidden_weight_ref[...] = two_blocks(pair_hidden_ref[...].astype(F32)).astype(BF16)
    out_weight_ref[...] = diagonal_blocks(pair_out_ref[...].astype(F32)).astype(BF16)
    weight = atom_in_ref[...].astype(F32)
    weight = crossed(weight, jnp.zeros_like(weight))
    mean = weight[feature:] * (1.0 / slots)
    atom_in_weight_ref[...] = jnp.concatenate([weight[:feature], mean, mean], axis=0).astype(BF16)
    folded = jnp.dot(
        pair_out_ref[...], mean.astype(BF16), preferred_element_type=F32
    )
    high = folded.astype(BF16)
    low = (folded - high.astype(F32)).astype(BF16)
    sum_weight_ref[...] = jnp.concatenate([high, high, low, low], axis=0)
    weight = atom_out_ref[...].astype(F32)
    blank = jnp.zeros_like(weight)
    weight = jnp.concatenate([weight, blank], axis=1)
    atom_out_weight_ref[...] = jnp.concatenate([weight, jnp.zeros_like(weight)], axis=0).astype(
        BF16
    )


def prepare_kernel(
    extents,
    paired,
    spot_ref,
    targets_ref,
    atom_ref,
    bond_ref,
    dirs_hbm,
    angle_hbm,
    near_ref,
    chosen_ref,
    right_ref,
    own_ref,
    dirs_ref,
    angle_ref,
    sems,
):
    copies = [
        pltpu.make_async_copy(source, target, sems.at[k])
        for k, (source, target) in enumerate(((dirs_hbm, dirs_ref), (angle_hbm, angle_ref)))
    ]
    for copy in copies:
        copy.start()
    atoms, feature = atom_ref.shape[2], atom_ref.shape[3]
    slots = targets_ref.shape[0]
    bonds = slots * atoms
    near_ref[: 3 * CAP // 2] = packed_rows(spot_ref[...], bond_ref, slots, 3 * CAP // 2)
    near_ref[3 * CAP // 2 :] = atom_rows(atom_ref)
    targets = bond_row(targets_ref[...])
    code_x, code_y = bond_codes(targets, atoms, extents, paired, True)
    code = 3 * code_x + code_y
    bond = lax.broadcasted_iota(jnp.int32, (1, bonds), 1)
    far_slot = slots - 1 - slot_at(quotient(bond, atoms), slots)
    far_atom = remainder(targets, atoms)
    far = (remainder(far_slot, 2) * (slots // 2) + quotient(far_slot, 2)) * atoms + far_atom
    base = (code * bonds).astype(F32)
    key = base + far.astype(F32)

    def column(values):
        return jnp.broadcast_to(values.astype(F32), (128, bonds)).T

    keys = column(key)
    place = []
    for group in range(bonds // 128):
        here = slice(group * 128, (group + 1) * 128)
        inside = (keys < key[:, here]) & (keys >= base[:, here])
        place.append(jnp.sum(jnp.where(inside, 1.0, 0.0), axis=0, keepdims=True))
    place = jnp.concatenate(place, axis=1).astype(jnp.int32)
    half, tall = CAP // 2, atoms // 2
    bond_spot = column(half * code + remainder(place, half))
    atom_spot = column(9 * half + tall * code + remainder(far_atom, tall))
    right = (column(quotient(place, half)), column(quotient(far_atom, tall)))
    right_ref[...] = jnp.where(left_lanes((bonds, 128)), right[0], right[1])
    total = 9 * half + 9 * tall
    for start in range(0, total, 128):
        width = min(128, total - start)
        spot = lax.broadcasted_iota(jnp.int32, (bonds, 128), 1).astype(F32) + float(start)
        chosen = jnp.where((spot == bond_spot) | (spot == atom_spot), 1.0, 0.0).astype(BF16)
        chosen_ref[:, start : start + width] = chosen[:, :width]

    atom = atom_ref[0, 0]
    blocks = blocks_of(bond_ref, slots // 2)
    own = [jnp.concatenate([atom, x[:, :feature]], axis=1) for x in blocks]
    own += [jnp.concatenate([atom, x[:, feature:]], axis=1) for x in blocks]
    own = jnp.concatenate(own, axis=0)
    own_ref[...] = own
    for copy in copies:
        copy.wait()


def gated(values):
    half = values.shape[1] // 2
    first, second = values[:, :half], values[:, half:]
    return first * jax.nn.sigmoid(first) * jax.nn.sigmoid(second)


def main_kernel(
    near_ref,
    up_ref,
    down_ref,
    two_ref,
    one_ref,
    angular_ref,
    chosen_ref,
    right_ref,
    own_ref,
    bond_weight_ref,
    mix_weight_ref,
    pair_weight_ref,
    hidden_weight_ref,
    out_weight_ref,
    atom_in_weight_ref,
    sum_weight_ref,
    atom_out_weight_ref,
    atom_result_hbm,
    bond_result_hbm,
    atom_result_ref,
    bond_result_ref,
    first_ref,
    second_ref,
    pair_ref,
    sems,
):
    slots, pairs, _ = angular_ref.shape
    bonds = 2 * pairs
    atoms = bonds // slots
    feature = own_ref.shape[1] // 2
    width = 2 * feature
    half = CAP // 2
    near_refs = (near_ref, up_ref, down_ref)
    away_refs = (one_ref, two_ref)
    sent = [ref[:half] for ref in near_refs] + [ref[: 3 * half] for ref in away_refs]
    sent = jnp.concatenate(sent, axis=0)
    sent_atom = jnp.concatenate([ref[3 * half :] for ref in near_refs + away_refs], axis=0)
    blank = jnp.zeros((sent.shape[0], feature), BF16)
    blank_atom = jnp.zeros((sent_atom.shape[0], feature), BF16)
    received = jnp.concatenate(
        [
            jnp.concatenate([sent[:, :feature], blank, sent[:, feature:], blank], axis=1),
            jnp.concatenate(
                [blank_atom, sent_atom[:, :feature], blank_atom, sent_atom[:, feature:]], axis=1
            ),
        ],
        axis=0,
    )
    far = jnp.dot(chosen_ref[...], received, preferred_element_type=F32)
    far = jnp.where(right_ref[...] > 0.0, far[:, width:], far[:, :width])
    own = own_ref[...]
    incoming = jnp.dot(
        jnp.concatenate([far.astype(BF16), own], axis=1),
        bond_weight_ref[...],
        preferred_element_type=F32,
    )
    hidden = gated(incoming).astype(BF16)
    old = jnp.where(left_lanes((bonds, width)), far, own.astype(F32))
    both = jnp.concatenate([hidden, old.astype(BF16)], axis=1)
    even, odd = both[:pairs], both[pairs:]
    projected = jnp.dot(
        jnp.concatenate([even, odd], axis=1), pair_weight_ref[...], preferred_element_type=F32
    )
    first_ref[...] = projected[:, : 2 * width]
    second_ref[0] = projected[:, 2 * width :]
    shifted = jnp.concatenate([even[atoms:], even[:atoms]], axis=0)
    second_ref[1] = jnp.dot(
        jnp.concatenate([odd, shifted], axis=1),
        pair_weight_ref[:, 2 * width :],
        preferred_element_type=F32,
    )
    mixed = jnp.dot(hidden, mix_weight_ref[...], preferred_element_type=F32)
    new = (old + mixed).astype(BF16).astype(F32)
    average = ((new + pltpu.roll(new, feature, 1)) * 0.5).astype(BF16).astype(F32)
    packed = jnp.where(left_lanes((pairs, width)), average[:pairs], average[pairs:])
    group = 2

    def first_gates(base):
        for start in range(0, pairs, atoms):
            here = first_ref[pl.ds(start, atoms)]
            for diagonal in range(base, base + group):
                there = (start + diagonal // 2 * atoms) % pairs
                mixture = angular_ref[diagonal, pl.ds(start, atoms)] + (
                    here + second_ref[diagonal % 2, pl.ds(there, atoms)]
                )
                pair_ref[pl.ds(diagonal * pairs + start, atoms)] = gated(mixture).astype(
                    BF16
                )

    def summed(rows):
        parts = [rows[k * atoms : (k + 1) * atoms] for k in range(slots // 2)]
        while len(parts) > 1:
            parts = [x + y for x, y in zip(parts[::2], parts[1::2])]
        return parts[0]

    atom = own[0:atoms]
    atom_incoming = jnp.dot(
        jnp.concatenate([atom[:, :feature], summed(packed).astype(BF16)], axis=1),
        atom_in_weight_ref[...],
        preferred_element_type=F32,
    )
    total = jnp.zeros((pairs, width), F32)
    first_gates(0)
    for base in range(0, slots, group):
        second = jnp.dot(
            pair_ref[pl.ds(base * pairs, group * pairs)],
            hidden_weight_ref[...],
            preferred_element_type=F32,
        )
        if base + group < slots:
            first_gates(base + group)
        gates = gated(second)
        for k in range(group):
            total = total + gates[k * pairs : (k + 1) * pairs]
    bond_out = packed + jnp.dot(
        total.astype(BF16), out_weight_ref[...], preferred_element_type=F32
    )
    bond_out = bond_out.astype(BF16)
    for k in range(slots // 2):
        bond_result_ref[0, 0, :, k * width : (k + 1) * width] = bond_out[
            k * atoms : (k + 1) * atoms
        ]
    copies = [pltpu.make_async_copy(bond_result_ref, bond_result_hbm, sems.at[0])]
    copies[0].start()
    sums = summed(total).astype(BF16)
    atom_incoming = atom_incoming + jnp.dot(
        jnp.concatenate([sums, sums], axis=1), sum_weight_ref[...], preferred_element_type=F32
    )
    atom_hidden = gated(atom_incoming).astype(BF16)
    atom_new = atom.astype(F32) + jnp.dot(
        atom_hidden, atom_out_weight_ref[...], preferred_element_type=F32
    )
    atom_result_ref[0, 0] = atom_new[:, :feature].astype(BF16)
    copies.append(pltpu.make_async_copy(atom_result_ref, atom_result_hbm, sems.at[1]))
    copies[-1].start()
    for copy in copies:
        copy.wait()


def per_device(
    atom_feat,
    bond_feat,
    neighbours,
    bond_dirs,
    bond_in_weight,
    bond_mix_weight,
    pair_weight,
    angle_weight,
    pair_hidden_weight,
    pair_out_weight,
    atom_in_weight,
    atom_out_weight,
):
    atoms, feature = atom_feat.shape[2], atom_feat.shape[3]
    slots = neighbours.shape[3]
    bonds = atoms * slots
    pairs = bonds // 2
    half = CAP // 2
    extents = (lax.axis_size("gx"), lax.axis_size("gy"))
    paired = (extents[0] % 2 == 0, False)
    targets = neighbours[0, 0].T
    hbm = pl.BlockSpec(memory_space=pltpu.HBM)
    vmem = pl.BlockSpec(memory_space=pltpu.VMEM)
    params = pltpu.CompilerParams(vmem_limit_bytes=32 * 2**20)

    def shaped(shape, dtype):
        return jax.ShapeDtypeStruct(shape, dtype)

    def in_hbm(arrays):
        return tuple(pltpu.with_memory_space_constraint(x, pltpu.HBM) for x in arrays)

    payload = shaped((3 * half + atoms // 2, 2 * feature), BF16)
    inputs = (targets, atom_feat, bond_feat)
    up, down, *held = pl.pallas_call(
        functools.partial(pack_kernel, extents, paired),
        out_shape=(payload, payload, shaped((1, bonds), jnp.int32))
        + tuple(shaped(x.shape, x.dtype) for x in inputs),
        in_specs=[hbm] * 3,
        out_specs=(vmem,) * 6,
        scratch_shapes=[pltpu.SemaphoreType.DMA((3,))],
        compiler_params=params,
        name="pack",
    )(*in_hbm(inputs))
    first, second = moves(extents[1], paired[1])
    up = lax.ppermute(up, "gy", first)
    down = lax.ppermute(down, "gy", second)
    weights = (bond_in_weight, bond_mix_weight, pair_weight, pair_hidden_weight)
    weights += (pair_out_weight, atom_in_weight, atom_out_weight)
    near, *prepared, bond_dirs, angle_weight = pl.pallas_call(
        functools.partial(prepare_kernel, extents, paired),
        out_shape=(
            payload,
            shaped((bonds, 9 * half + 9 * atoms // 2), BF16),
            shaped((bonds, 2 * feature), F32),
            shaped((bonds, 2 * feature), BF16),
            shaped(bond_dirs.shape, F32),
            shaped(angle_weight.shape, BF16),
        ),
        in_specs=[vmem] * 4 + [hbm] * 2,
        out_specs=(vmem,) * 6,
        scratch_shapes=[pltpu.SemaphoreType.DMA((2,))],
        compiler_params=params,
        cost_estimate=pl.CostEstimate(flops=64 * 2**20, bytes_accessed=2**21, transcendentals=0),
        name="prepare",
    )(*held, *in_hbm((bond_dirs, angle_weight)))
    near, up, down, prepared = lax.optimization_barrier((near, up, down, prepared))
    first, second = moves(extents[0], paired[0])

    def forwarded(block):
        parts = [x[block * half : (block + 1) * half] for x in (near, up, down)]
        return jnp.concatenate(parts + [x[3 * half :] for x in (near, up, down)], axis=0)

    one = lax.ppermute(forwarded(1), "gx", first)
    two = lax.ppermute(forwarded(2), "gx", second)
    angular, *made = pl.pallas_call(
        functools.partial(angular_kernel, atoms),
        out_shape=(
            shaped((slots, pairs, 4 * feature), F32),
            shaped((4 * feature, 4 * feature), BF16),
            shaped((2 * feature, 2 * feature), BF16),
            shaped((8 * feature, 8 * feature), BF16),
            shaped((2 * feature, 4 * feature), BF16),
            shaped((2 * feature, 2 * feature), BF16),
            shaped((3 * feature, 4 * feature), BF16),
            shaped((4 * feature, 4 * feature), BF16),
            shaped((2 * feature, 2 * feature), BF16),
        ),
        in_specs=[vmem] * 2 + [hbm] * 7,
        out_specs=(vmem,) * 9,
        scratch_shapes=[pltpu.VMEM(x.shape, BF16) for x in weights]
        + [pltpu.SemaphoreType.DMA((7,))],
        compiler_params=params,
        cost_estimate=pl.CostEstimate(
            flops=256 * 2**20, bytes_accessed=2**22, transcendentals=4096
        ),
        name="angular",
    )(bond_dirs, angle_weight, *in_hbm(weights))
    return pl.pallas_call(
        main_kernel,
        out_shape=(shaped(atom_feat.shape, BF16), shaped(bond_feat.shape, BF16)),
        in_specs=[vmem] * 17,
        out_specs=(hbm, hbm),
        scratch_shapes=[
            pltpu.VMEM(atom_feat.shape, BF16),
            pltpu.VMEM(bond_feat.shape, BF16),
            pltpu.VMEM((pairs, 4 * feature), F32),
            pltpu.VMEM((2, pairs, 4 * feature), F32),
            pltpu.VMEM((slots * pairs, 2 * feature), BF16),
            pltpu.SemaphoreType.DMA((2,)),
        ],
        compiler_params=params,
        name="main",
    )(near, up, down, two, one, angular, *prepared, *made)


def solution(mesh):
    placed = (
        P("gx", "gy", None, None),
        P("gx", "gy", None, None),
        P("gx", "gy", None, None),
        P(None, "gx", "gy", None),
        P(),
        P(),
        P(),
        P(),
        P(),
        P(),
        P(),
        P(),
    )
    return jax.shard_map(
        per_device,
        mesh=mesh,
        in_specs=placed,
        out_specs=(P("gx", "gy", None, None), P("gx", "gy", None, None)),
        check_vma=False,
    )
```

```python
import functools

import jax
import jax.numpy as jnp
from jax import lax
from jax.experimental import pallas as pl
from jax.experimental.pallas import tpu as pltpu
from jax.sharding import PartitionSpec as P

F32 = jnp.float32
BF16 = jnp.bfloat16
CAP = 64


def quotient(values, size):
    if size & (size - 1) == 0:
        return values >> (size.bit_length() - 1)
    return lax.div(values, jnp.int32(size))


def remainder(values, size):
    if size & (size - 1) == 0:
        return values & (size - 1)
    return lax.rem(values, jnp.int32(size))


def step_code(owner, home, extent, paired, receives):
    step = remainder(owner - home + 1 + extent, extent)
    if paired:
        ahead = jnp.where(remainder(home, 2) == 0, 0, 2)
    else:
        ahead = 0 if receives else 2
    return jnp.where(step == 1, 0, jnp.where(step == ahead, 1, 2))


def moves(extent, paired):
    if paired:
        near = [(i, i ^ 1) for i in range(extent)]
        return [(i, (((i + 1) ^ 1) - 1) % extent) for i in range(extent)], near
    up = [(i, (i + 1) % extent) for i in range(extent)]
    return up, [(j, i) for i, j in up]


def slot_at(position, slots):
    half = slots // 2
    return jnp.where(position < half, 2 * position, 2 * (position - half) + 1)


def bond_row(table):
    slots, atoms = table.shape
    per_group = 128 // atoms
    tiled = jnp.concatenate([table.astype(F32)] * per_group, axis=1)
    row = lax.broadcasted_iota(jnp.int32, tiled.shape, 0)
    position = quotient(lax.broadcasted_iota(jnp.int32, tiled.shape, 1), atoms)
    pieces = []
    for group in range(slots // per_group):
        chosen = row == slot_at(position + group * per_group, slots)
        pieces.append(jnp.sum(jnp.where(chosen, tiled, 0.0), axis=0, keepdims=True))
    return jnp.concatenate(pieces, axis=1).astype(jnp.int32)


def bond_codes(targets, atoms, extents, paired, receives):
    owner = quotient(targets, atoms)
    block = (quotient(owner, extents[1]), remainder(owner, extents[1]))
    return tuple(
        step_code(block[k], lax.axis_index(axis), extents[k], paired[k], receives)
        for k, axis in enumerate(("gx", "gy"))
    )


def left_lanes(shape):
    return lax.broadcasted_iota(jnp.int32, shape, 1) < shape[1] // 2


def swapped(rows):
    half = rows.shape[1] // 2
    return jnp.concatenate([rows[:, half:], rows[:, :half]], axis=1)


def blocks_of(bond_ref, pairs):
    width = bond_ref.shape[3] // pairs
    return [bond_ref[0, 0, :, k * width : (k + 1) * width] for k in range(pairs)]


def pack_kernel(
    extents,
    paired,
    targets_hbm,
    atom_hbm,
    bond_hbm,
    up_ref,
    down_ref,
    spot_ref,
    targets_ref,
    atom_ref,
    bond_ref,
    sems,
):
    sources = ((targets_hbm, targets_ref), (bond_hbm, bond_ref), (atom_hbm, atom_ref))
    copies = [
        pltpu.make_async_copy(source, target, sems.at[k])
        for k, (source, target) in enumerate(sources)
    ]
    for copy in copies:
        copy.start()
    atoms, feature = atom_ref.shape[2], atom_ref.shape[3]
    slots = targets_ref.shape[0]
    bonds = slots * atoms
    lanes = 128
    groups = bonds // lanes
    copies[0].wait()
    code_x, code_y = bond_codes(bond_row(targets_ref[...]), atoms, extents, paired, False)
    code = 3 * code_y + code_x
    rows = lax.broadcasted_iota(jnp.int32, (16, lanes), 0)
    marks = [rows == code[:, g * lanes : (g + 1) * lanes] for g in range(groups)]
    stacked = jnp.concatenate([m.astype(F32) for m in marks], axis=0).astype(BF16)
    before = lax.broadcasted_iota(jnp.int32, (lanes, 2 * lanes), 0)
    after = lax.broadcasted_iota(jnp.int32, (lanes, 2 * lanes), 1)
    sums = jnp.where((before < after) | (after >= lanes), 1.0, 0.0).astype(BF16)
    counted = jnp.dot(stacked, sums, preferred_element_type=F32)
    place = []
    earlier = jnp.zeros((16, lanes), F32)
    for g in range(groups):
        part = counted[g * 16 : (g + 1) * 16]
        place.append(
            jnp.sum(jnp.where(marks[g], part[:, :lanes] + earlier, 0.0), axis=0, keepdims=True)
        )
        earlier = earlier + part[:, lanes:]
    place = jnp.concatenate(place, axis=1).astype(jnp.int32)
    half = CAP // 2
    right = quotient(place, half)
    spot = place - half * right + half * code
    spot_ref[...] = jnp.where(code < 3, spot + 3 * half * right, -1)
    wanted = jnp.where(code < 3, -1, spot - 3 * half + 6 * half * right)
    copies[1].wait()
    copies[2].wait()
    packed = packed_rows(wanted, bond_ref, slots, 6 * half)
    for k, ref in enumerate((up_ref, down_ref)):
        ref[: 3 * half] = packed[3 * half * k : 3 * half * (k + 1)]
        ref[3 * half :] = atom_rows(atom_ref)


def packed_rows(wanted, bond_ref, slots, count):
    spot = lax.broadcasted_iota(jnp.int32, (2 * count, wanted.shape[1]), 0)
    chosen = jnp.where(spot == wanted, 1.0, 0.0).astype(BF16)
    blocks = blocks_of(bond_ref, slots // 2)
    feature = blocks[0].shape[1] // 2
    values = [jnp.concatenate([x[:, :feature]] * 2, axis=1) for x in blocks]
    values += [jnp.concatenate([x[:, feature:]] * 2, axis=1) for x in blocks]
    packed = jnp.dot(chosen, jnp.concatenate(values, axis=0), preferred_element_type=F32)
    left = left_lanes((count, 2 * feature))
    return jnp.where(left, packed[:count], packed[count:]).astype(BF16)


def atom_rows(atom_ref):
    atom = atom_ref[0, 0]
    half = atom.shape[0] // 2
    return jnp.concatenate([atom[:half], atom[half:]], axis=1)


def crossed(left, right):
    half = left.shape[1] // 2
    parts = [left[:, :half], right[:, :half], left[:, half:], right[:, half:]]
    return jnp.concatenate(parts, axis=1)


def two_blocks(weight):
    blank = jnp.zeros_like(weight)
    return jnp.concatenate([crossed(weight, blank), crossed(blank, weight)], axis=0)


def diagonal_blocks(weight):
    blank = jnp.zeros_like(weight)
    return jnp.concatenate(
        [jnp.concatenate([weight, blank], axis=1), jnp.concatenate([blank, weight], axis=1)],
        axis=0,
    )


def angular_kernel(atoms, dirs_ref, angle_ref, *refs):
    sources, angular_ref, results, held, sems = refs[:7], refs[7], refs[8:16], refs[16:23], refs[23]
    copies = [
        pltpu.make_async_copy(source, target, sems.at[k])
        for k, (source, target) in enumerate(zip(sources, held))
    ]
    for copy in copies:
        copy.start()
    slots, pairs, _ = angular_ref.shape
    bonds = 2 * pairs
    degrees = angle_ref.shape[0]
    weight = two_blocks(angle_ref[...].astype(F32)).astype(BF16)
    polar, azimuth = dirs_ref[0, 0], dirs_ref[1, 0]
    unit = jnp.concatenate(
        [
            jnp.sin(polar) * jnp.cos(azimuth),
            jnp.sin(polar) * jnp.sin(azimuth),
            jnp.cos(polar),
            jnp.zeros((5, bonds), F32),
        ],
        axis=0,
    )
    high = unit.astype(BF16).astype(F32)
    middle = (unit - high).astype(BF16).astype(F32)
    parts = jnp.concatenate([high, middle, unit - high - middle], axis=0).astype(BF16)
    bond = lax.broadcasted_iota(jnp.int32, (1, bonds), 1)
    source = remainder(bond, atoms) * slots + slot_at(quotient(bond, atoms), slots)
    spot = lax.broadcasted_iota(jnp.int32, (bonds, bonds), 0)
    chosen = jnp.where(spot == source, 1.0, 0.0).astype(BF16)
    unit = jnp.dot(parts, chosen, preferred_element_type=F32)
    unit = unit[0:8] + unit[8:16] + unit[16:24]
    even = [jnp.broadcast_to(unit[k : k + 1, :pairs], (8, pairs)) for k in range(3)]
    odd = [jnp.broadcast_to(unit[k : k + 1, pairs:], (8, pairs)) for k in range(3)]
    row = lax.broadcasted_iota(jnp.int32, (8, pairs), 0)

    def turned(vector, places):
        places = places % (pairs // atoms)
        if places == 0:
            return vector
        return [pltpu.roll(part, pairs - atoms * places, 1) for part in vector]

    def basis(first, second):
        cosine = first[0] * second[0] + first[1] * second[1] + first[2] * second[2]
        series = [jnp.ones_like(cosine), cosine]
        double = cosine + cosine
        for _ in range(7):
            series.append(double * series[-1] - series[-2])
        lower = series[7]
        upper = series[1]
        for index in range(1, 8):
            lower = jnp.where(row == index, series[7 - index], lower)
            upper = jnp.where(row == index, series[1 + index], upper)
        double = series[8] + series[8]
        blocks = [lower, upper]
        for _ in range(degrees // 8 - 1):
            blocks.append(double * blocks[-1] - blocks[-2])
        return blocks[1:]

    for diagonal in range(slots):
        places = diagonal // 2
        if diagonal % 2 == 0:
            blocks = basis(even, turned(even, places)) + basis(odd, turned(odd, places))
        else:
            blocks = basis(even, turned(odd, places)) + basis(odd, turned(even, places + 1))
        series = jnp.concatenate(blocks, axis=0).T.astype(BF16)
        angular_ref[diagonal] = jnp.dot(series, weight, preferred_element_type=F32)
    for copy in copies:
        copy.wait()
    prepare_weights(slots, held, results)


def prepare_weights(slots, held, results):
    bond_in_ref, bond_mix_ref, pair_ref, pair_hidden_ref, pair_out_ref, atom_in_ref = held[:6]
    atom_out_ref = held[6]
    bond_weight_ref, mix_weight_ref, pair_weight_ref, hidden_weight_ref = results[:4]
    out_weight_ref, atom_in_weight_ref, sum_weight_ref, atom_out_weight_ref = results[4:]
    feature = bond_mix_ref.shape[0]
    weight = bond_in_ref[...].astype(F32)
    source, other, bond_part = (weight[k * feature : (k + 1) * feature] for k in range(3))
    blank = jnp.zeros_like(source)
    away = [crossed(bond_part, blank), crossed(source, other)]
    near = [crossed(other, source), crossed(blank, bond_part)]
    bond_weight_ref[...] = jnp.concatenate(away + near, axis=0).astype(BF16)
    mix_weight_ref[...] = diagonal_blocks(bond_mix_ref[...].astype(F32)).astype(BF16)
    old = pair_ref[...].astype(F32) * 0.5
    hidden = jnp.dot(bond_mix_ref[...], pair_ref[...], preferred_element_type=F32) * 0.5
    weight = jnp.concatenate([hidden, hidden, old, old], axis=0).astype(BF16)
    pair_weight_ref[...] = jnp.concatenate(
        [two_blocks(weight[:, : 2 * feature]), two_blocks(weight[:, 2 * feature :])], axis=1
    )
    hidden_weight_ref[...] = two_blocks(pair_hidden_ref[...].astype(F32)).astype(BF16)
    out_weight_ref[...] = diagonal_blocks(pair_out_ref[...].astype(F32)).astype(BF16)
    weight = atom_in_ref[...].astype(F32)
    weight = crossed(weight, jnp.zeros_like(weight))
    mean = weight[feature:] * (1.0 / slots)
    atom_in_weight_ref[...] = jnp.concatenate([weight[:feature], mean, mean], axis=0).astype(BF16)
    folded = jnp.dot(
        pair_out_ref[...], mean.astype(BF16), preferred_element_type=F32
    )
    high = folded.astype(BF16)
    low = (folded - high.astype(F32)).astype(BF16)
    sum_weight_ref[...] = jnp.concatenate([high, high, low, low], axis=0)
    weight = atom_out_ref[...].astype(F32)
    blank = jnp.zeros_like(weight)
    weight = jnp.concatenate([weight, blank], axis=1)
    atom_out_weight_ref[...] = jnp.concatenate([weight, jnp.zeros_like(weight)], axis=0).astype(
        BF16
    )


def prepare_kernel(
    extents,
    paired,
    spot_ref,
    targets_ref,
    atom_ref,
    bond_ref,
    dirs_hbm,
    angle_hbm,
    near_ref,
    chosen_ref,
    right_ref,
    own_ref,
    dirs_ref,
    angle_ref,
    sems,
):
    copies = [
        pltpu.make_async_copy(source, target, sems.at[k])
        for k, (source, target) in enumerate(((dirs_hbm, dirs_ref), (angle_hbm, angle_ref)))
    ]
    for copy in copies:
        copy.start()
    atoms, feature = atom_ref.shape[2], atom_ref.shape[3]
    slots = targets_ref.shape[0]
    bonds = slots * atoms
    near_ref[: 3 * CAP // 2] = packed_rows(spot_ref[...], bond_ref, slots, 3 * CAP // 2)
    near_ref[3 * CAP // 2 :] = atom_rows(atom_ref)
    targets = bond_row(targets_ref[...])
    code_x, code_y = bond_codes(targets, atoms, extents, paired, True)
    code = 3 * code_x + code_y
    bond = lax.broadcasted_iota(jnp.int32, (1, bonds), 1)
    far_slot = slots - 1 - slot_at(quotient(bond, atoms), slots)
    far_atom = remainder(targets, atoms)
    far = (remainder(far_slot, 2) * (slots // 2) + quotient(far_slot, 2)) * atoms + far_atom
    base = (code * bonds).astype(F32)
    key = base + far.astype(F32)

    def column(values):
        return jnp.broadcast_to(values.astype(F32), (128, bonds)).T

    keys = column(key)
    place = []
    for group in range(bonds // 128):
        here = slice(group * 128, (group + 1) * 128)
        inside = (keys < key[:, here]) & (keys >= base[:, here])
        place.append(jnp.sum(jnp.where(inside, 1.0, 0.0), axis=0, keepdims=True))
    place = jnp.concatenate(place, axis=1).astype(jnp.int32)
    half, tall = CAP // 2, atoms // 2
    bond_spot = column(half * code + remainder(place, half))
    atom_spot = column(9 * half + tall * code + remainder(far_atom, tall))
    right = (column(quotient(place, half)), column(quotient(far_atom, tall)))
    right_ref[...] = jnp.where(left_lanes((bonds, 128)), right[0], right[1])
    total = 9 * half + 9 * tall
    for start in range(0, total, 128):
        width = min(128, total - start)
        spot = lax.broadcasted_iota(jnp.int32, (bonds, 128), 1).astype(F32) + float(start)
        chosen = jnp.where((spot == bond_spot) | (spot == atom_spot), 1.0, 0.0).astype(BF16)
        chosen_ref[:, start : start + width] = chosen[:, :width]

    atom = atom_ref[0, 0]
    blocks = blocks_of(bond_ref, slots // 2)
    own = [jnp.concatenate([atom, x[:, :feature]], axis=1) for x in blocks]
    own += [jnp.concatenate([atom, x[:, feature:]], axis=1) for x in blocks]
    own = jnp.concatenate(own, axis=0)
    own_ref[...] = own
    for copy in copies:
        copy.wait()


def gated(values):
    half = values.shape[1] // 2
    first, second = values[:, :half], values[:, half:]
    return first * jax.nn.sigmoid(first) * jax.nn.sigmoid(second)


def main_kernel(
    near_ref,
    up_ref,
    down_ref,
    two_ref,
    one_ref,
    angular_ref,
    chosen_ref,
    right_ref,
    own_ref,
    bond_weight_ref,
    mix_weight_ref,
    pair_weight_ref,
    hidden_weight_ref,
    out_weight_ref,
    atom_in_weight_ref,
    sum_weight_ref,
    atom_out_weight_ref,
    atom_result_hbm,
    bond_result_hbm,
    atom_result_ref,
    bond_result_ref,
    first_ref,
    second_ref,
    pair_ref,
    sems,
):
    slots, pairs, _ = angular_ref.shape
    bonds = 2 * pairs
    atoms = bonds // slots
    feature = own_ref.shape[1] // 2
    width = 2 * feature
    half = CAP // 2
    near_refs = (near_ref, up_ref, down_ref)
    away_refs = (one_ref, two_ref)
    sent = [ref[:half] for ref in near_refs] + [ref[: 3 * half] for ref in away_refs]
    sent = jnp.concatenate(sent, axis=0)
    sent_atom = jnp.concatenate([ref[3 * half :] for ref in near_refs + away_refs], axis=0)
    blank = jnp.zeros((sent.shape[0], feature), BF16)
    blank_atom = jnp.zeros((sent_atom.shape[0], feature), BF16)
    received = jnp.concatenate(
        [
            jnp.concatenate([sent[:, :feature], blank, sent[:, feature:], blank], axis=1),
            jnp.concatenate(
                [blank_atom, sent_atom[:, :feature], blank_atom, sent_atom[:, feature:]], axis=1
            ),
        ],
        axis=0,
    )
    far = jnp.dot(chosen_ref[...], received, preferred_element_type=F32)
    far = jnp.where(right_ref[...] > 0.0, far[:, width:], far[:, :width])
    own = own_ref[...]
    incoming = jnp.dot(
        jnp.concatenate([far.astype(BF16), own], axis=1),
        bond_weight_ref[...],
        preferred_element_type=F32,
    )
    hidden = gated(incoming).astype(BF16)
    old = jnp.where(left_lanes((bonds, width)), far, own.astype(F32))
    both = jnp.concatenate([hidden, old.astype(BF16)], axis=1)
    even, odd = both[:pairs], both[pairs:]
    projected = jnp.dot(
        jnp.concatenate([even, odd], axis=1), pair_weight_ref[...], preferred_element_type=F32
    )
    first_ref[...] = projected[:, : 2 * width]
    second_ref[0] = projected[:, 2 * width :]
    shifted = jnp.concatenate([even[atoms:], even[:atoms]], axis=0)
    second_ref[1] = jnp.dot(
        jnp.concatenate([odd, shifted], axis=1),
        pair_weight_ref[:, 2 * width :],
        preferred_element_type=F32,
    )
    mixed = jnp.dot(hidden, mix_weight_ref[...], preferred_element_type=F32)
    new = (old + mixed).astype(BF16).astype(F32)
    average = ((new + pltpu.roll(new, feature, 1)) * 0.5).astype(BF16).astype(F32)
    packed = jnp.where(left_lanes((pairs, width)), average[:pairs], average[pairs:])
    group = 2

    def first_gates(base):
        for start in range(0, pairs, atoms):
            here = first_ref[pl.ds(start, atoms)]
            for diagonal in range(base, base + group):
                there = (start + diagonal // 2 * atoms) % pairs
                mixture = angular_ref[diagonal, pl.ds(start, atoms)] + (
                    here + second_ref[diagonal % 2, pl.ds(there, atoms)]
                )
                pair_ref[pl.ds(diagonal * pairs + start, atoms)] = gated(mixture).astype(
                    BF16
                )

    def summed(rows):
        parts = [rows[k * atoms : (k + 1) * atoms] for k in range(slots // 2)]
        while len(parts) > 1:
            parts = [x + y for x, y in zip(parts[::2], parts[1::2])]
        return parts[0]

    atom = own[0:atoms]
    atom_incoming = jnp.dot(
        jnp.concatenate([atom[:, :feature], summed(packed).astype(BF16)], axis=1),
        atom_in_weight_ref[...],
        preferred_element_type=F32,
    )
    total = jnp.zeros((pairs, width), F32)
    first_gates(0)
    for base in range(0, slots, group):
        if base + group < slots:
            first_gates(base + group)
        second = jnp.dot(
            pair_ref[pl.ds(base * pairs, group * pairs)],
            hidden_weight_ref[...],
            preferred_element_type=F32,
        )
        gates = gated(second)
        for k in range(group):
            total = total + gates[k * pairs : (k + 1) * pairs]
    sums = summed(total).astype(BF16)
    atom_incoming = atom_incoming + jnp.dot(
        jnp.concatenate([sums, sums], axis=1), sum_weight_ref[...], preferred_element_type=F32
    )
    atom_hidden = gated(atom_incoming).astype(BF16)
    atom_new = atom.astype(F32) + jnp.dot(
        atom_hidden, atom_out_weight_ref[...], preferred_element_type=F32
    )
    atom_result_ref[0, 0] = atom_new[:, :feature].astype(BF16)
    copies = []
    copies.append(pltpu.make_async_copy(atom_result_ref, atom_result_hbm, sems.at[1]))
    copies[-1].start()
    bond_out = packed + jnp.dot(
        total.astype(BF16), out_weight_ref[...], preferred_element_type=F32
    )
    bond_out = bond_out.astype(BF16)
    for k in range(slots // 2):
        bond_result_ref[0, 0, :, k * width : (k + 1) * width] = bond_out[
            k * atoms : (k + 1) * atoms
        ]
    copies.append(pltpu.make_async_copy(bond_result_ref, bond_result_hbm, sems.at[0]))
    copies[-1].start()
    for copy in copies:
        copy.wait()


def per_device(
    atom_feat,
    bond_feat,
    neighbours,
    bond_dirs,
    bond_in_weight,
    bond_mix_weight,
    pair_weight,
    angle_weight,
    pair_hidden_weight,
    pair_out_weight,
    atom_in_weight,
    atom_out_weight,
):
    atoms, feature = atom_feat.shape[2], atom_feat.shape[3]
    slots = neighbours.shape[3]
    bonds = atoms * slots
    pairs = bonds // 2
    half = CAP // 2
    extents = (lax.axis_size("gx"), lax.axis_size("gy"))
    paired = (extents[0] % 2 == 0, False)
    targets = neighbours[0, 0].T
    hbm = pl.BlockSpec(memory_space=pltpu.HBM)
    vmem = pl.BlockSpec(memory_space=pltpu.VMEM)
    params = pltpu.CompilerParams(vmem_limit_bytes=32 * 2**20)

    def shaped(shape, dtype):
        return jax.ShapeDtypeStruct(shape, dtype)

    def in_hbm(arrays):
        return tuple(pltpu.with_memory_space_constraint(x, pltpu.HBM) for x in arrays)

    payload = shaped((3 * half + atoms // 2, 2 * feature), BF16)
    inputs = (targets, atom_feat, bond_feat)
    up, down, *held = pl.pallas_call(
        functools.partial(pack_kernel, extents, paired),
        out_shape=(payload, payload, shaped((1, bonds), jnp.int32))
        + tuple(shaped(x.shape, x.dtype) for x in inputs),
        in_specs=[hbm] * 3,
        out_specs=(vmem,) * 6,
        scratch_shapes=[pltpu.SemaphoreType.DMA((3,))],
        compiler_params=params,
        name="pack",
    )(*in_hbm(inputs))
    first, second = moves(extents[1], paired[1])
    up = lax.ppermute(up, "gy", first)
    down = lax.ppermute(down, "gy", second)
    weights = (bond_in_weight, bond_mix_weight, pair_weight, pair_hidden_weight)
    weights += (pair_out_weight, atom_in_weight, atom_out_weight)
    near, *prepared, bond_dirs, angle_weight = pl.pallas_call(
        functools.partial(prepare_kernel, extents, paired),
        out_shape=(
            payload,
            shaped((bonds, 9 * half + 9 * atoms // 2), BF16),
            shaped((bonds, 2 * feature), F32),
            shaped((bonds, 2 * feature), BF16),
            shaped(bond_dirs.shape, F32),
            shaped(angle_weight.shape, BF16),
        ),
        in_specs=[vmem] * 4 + [hbm] * 2,
        out_specs=(vmem,) * 6,
        scratch_shapes=[pltpu.SemaphoreType.DMA((2,))],
        compiler_params=params,
        cost_estimate=pl.CostEstimate(flops=64 * 2**20, bytes_accessed=2**21, transcendentals=0),
        name="prepare",
    )(*held, *in_hbm((bond_dirs, angle_weight)))
    near, up, down, prepared = lax.optimization_barrier((near, up, down, prepared))
    first, second = moves(extents[0], paired[0])

    def forwarded(block):
        parts = [x[block * half : (block + 1) * half] for x in (near, up, down)]
        return jnp.concatenate(parts + [x[3 * half :] for x in (near, up, down)], axis=0)

    one = lax.ppermute(forwarded(1), "gx", first)
    two = lax.ppermute(forwarded(2), "gx", second)
    angular, *made = pl.pallas_call(
        functools.partial(angular_kernel, atoms),
        out_shape=(
            shaped((slots, pairs, 4 * feature), F32),
            shaped((4 * feature, 4 * feature), BF16),
            shaped((2 * feature, 2 * feature), BF16),
            shaped((8 * feature, 8 * feature), BF16),
            shaped((2 * feature, 4 * feature), BF16),
            shaped((2 * feature, 2 * feature), BF16),
            shaped((3 * feature, 4 * feature), BF16),
            shaped((4 * feature, 4 * feature), BF16),
            shaped((2 * feature, 2 * feature), BF16),
        ),
        in_specs=[vmem] * 2 + [hbm] * 7,
        out_specs=(vmem,) * 9,
        scratch_shapes=[pltpu.VMEM(x.shape, BF16) for x in weights]
        + [pltpu.SemaphoreType.DMA((7,))],
        compiler_params=params,
        cost_estimate=pl.CostEstimate(
            flops=256 * 2**20, bytes_accessed=2**22, transcendentals=4096
        ),
        name="angular",
    )(bond_dirs, angle_weight, *in_hbm(weights))
    return pl.pallas_call(
        main_kernel,
        out_shape=(shaped(atom_feat.shape, BF16), shaped(bond_feat.shape, BF16)),
        in_specs=[vmem] * 17,
        out_specs=(hbm, hbm),
        scratch_shapes=[
            pltpu.VMEM(atom_feat.shape, BF16),
            pltpu.VMEM(bond_feat.shape, BF16),
            pltpu.VMEM((pairs, 4 * feature), F32),
            pltpu.VMEM((2, pairs, 4 * feature), F32),
            pltpu.VMEM((slots * pairs, 2 * feature), BF16),
            pltpu.SemaphoreType.DMA((2,)),
        ],
        compiler_params=params,
        name="main",
    )(near, up, down, two, one, angular, *prepared, *made)


def solution(mesh):
    placed = (
        P("gx", "gy", None, None),
        P("gx", "gy", None, None),
        P("gx", "gy", None, None),
        P(None, "gx", "gy", None),
        P(),
        P(),
        P(),
        P(),
        P(),
        P(),
        P(),
        P(),
    )
    return jax.shard_map(
        per_device,
        mesh=mesh,
        in_specs=placed,
        out_specs=(P("gx", "gy", None, None), P("gx", "gy", None, None)),
        check_vma=False,
    )
```

```python
import functools

import jax
import jax.numpy as jnp
from jax import lax
from jax.experimental import pallas as pl
from jax.experimental.pallas import tpu as pltpu
from jax.sharding import PartitionSpec as P

F32 = jnp.float32
BF16 = jnp.bfloat16
CAP = 64


def quotient(values, size):
    if size & (size - 1) == 0:
        return values >> (size.bit_length() - 1)
    return lax.div(values, jnp.int32(size))


def remainder(values, size):
    if size & (size - 1) == 0:
        return values & (size - 1)
    return lax.rem(values, jnp.int32(size))


def step_code(owner, home, extent, paired, receives):
    step = remainder(owner - home + 1 + extent, extent)
    if paired:
        ahead = jnp.where(remainder(home, 2) == 0, 0, 2)
    else:
        ahead = 0 if receives else 2
    return jnp.where(step == 1, 0, jnp.where(step == ahead, 1, 2))


def moves(extent, paired):
    if paired:
        near = [(i, i ^ 1) for i in range(extent)]
        return [(i, (((i + 1) ^ 1) - 1) % extent) for i in range(extent)], near
    up = [(i, (i + 1) % extent) for i in range(extent)]
    return up, [(j, i) for i, j in up]


def slot_at(position, slots):
    half = slots // 2
    return jnp.where(position < half, 2 * position, 2 * (position - half) + 1)


def bond_row(table):
    slots, atoms = table.shape
    per_group = 128 // atoms
    tiled = jnp.concatenate([table.astype(F32)] * per_group, axis=1)
    row = lax.broadcasted_iota(jnp.int32, tiled.shape, 0)
    position = quotient(lax.broadcasted_iota(jnp.int32, tiled.shape, 1), atoms)
    pieces = []
    for group in range(slots // per_group):
        chosen = row == slot_at(position + group * per_group, slots)
        pieces.append(jnp.sum(jnp.where(chosen, tiled, 0.0), axis=0, keepdims=True))
    return jnp.concatenate(pieces, axis=1).astype(jnp.int32)


def bond_codes(targets, atoms, extents, paired, receives):
    owner = quotient(targets, atoms)
    block = (quotient(owner, extents[1]), remainder(owner, extents[1]))
    return tuple(
        step_code(block[k], lax.axis_index(axis), extents[k], paired[k], receives)
        for k, axis in enumerate(("gx", "gy"))
    )


def left_lanes(shape):
    return lax.broadcasted_iota(jnp.int32, shape, 1) < shape[1] // 2


def swapped(rows):
    half = rows.shape[1] // 2
    return jnp.concatenate([rows[:, half:], rows[:, :half]], axis=1)


def blocks_of(bond_ref, pairs):
    width = bond_ref.shape[3] // pairs
    return [bond_ref[0, 0, :, k * width : (k + 1) * width] for k in range(pairs)]


def pack_kernel(
    extents,
    paired,
    targets_hbm,
    atom_hbm,
    bond_hbm,
    up_ref,
    down_ref,
    spot_ref,
    targets_ref,
    atom_ref,
    bond_ref,
    sems,
):
    sources = ((targets_hbm, targets_ref), (bond_hbm, bond_ref), (atom_hbm, atom_ref))
    copies = [
        pltpu.make_async_copy(source, target, sems.at[k])
        for k, (source, target) in enumerate(sources)
    ]
    for copy in copies:
        copy.start()
    atoms, feature = atom_ref.shape[2], atom_ref.shape[3]
    slots = targets_ref.shape[0]
    bonds = slots * atoms
    lanes = 128
    groups = bonds // lanes
    copies[0].wait()
    code_x, code_y = bond_codes(bond_row(targets_ref[...]), atoms, extents, paired, False)
    code = 3 * code_y + code_x
    rows = lax.broadcasted_iota(jnp.int32, (16, lanes), 0)
    marks = [rows == code[:, g * lanes : (g + 1) * lanes] for g in range(groups)]
    stacked = jnp.concatenate([m.astype(F32) for m in marks], axis=0).astype(BF16)
    before = lax.broadcasted_iota(jnp.int32, (lanes, 2 * lanes), 0)
    after = lax.broadcasted_iota(jnp.int32, (lanes, 2 * lanes), 1)
    sums = jnp.where((before < after) | (after >= lanes), 1.0, 0.0).astype(BF16)
    counted = jnp.dot(stacked, sums, preferred_element_type=F32)
    place = []
    earlier = jnp.zeros((16, lanes), F32)
    for g in range(groups):
        part = counted[g * 16 : (g + 1) * 16]
        place.append(
            jnp.sum(jnp.where(marks[g], part[:, :lanes] + earlier, 0.0), axis=0, keepdims=True)
        )
        earlier = earlier + part[:, lanes:]
    place = jnp.concatenate(place, axis=1).astype(jnp.int32)
    half = CAP // 2
    right = quotient(place, half)
    spot = place - half * right + half * code
    spot_ref[...] = jnp.where(code < 3, spot + 3 * half * right, -1)
    wanted = jnp.where(code < 3, -1, spot - 3 * half + 6 * half * right)
    copies[1].wait()
    copies[2].wait()
    packed = packed_rows(wanted, bond_ref, slots, 6 * half)
    for k, ref in enumerate((up_ref, down_ref)):
        ref[: 3 * half] = packed[3 * half * k : 3 * half * (k + 1)]
        ref[3 * half :] = atom_rows(atom_ref)


def packed_rows(wanted, bond_ref, slots, count):
    spot = lax.broadcasted_iota(jnp.int32, (2 * count, wanted.shape[1]), 0)
    chosen = jnp.where(spot == wanted, 1.0, 0.0).astype(BF16)
    blocks = blocks_of(bond_ref, slots // 2)
    feature = blocks[0].shape[1] // 2
    values = [jnp.concatenate([x[:, :feature]] * 2, axis=1) for x in blocks]
    values += [jnp.concatenate([x[:, feature:]] * 2, axis=1) for x in blocks]
    packed = jnp.dot(chosen, jnp.concatenate(values, axis=0), preferred_element_type=F32)
    left = left_lanes((count, 2 * feature))
    return jnp.where(left, packed[:count], packed[count:]).astype(BF16)


def atom_rows(atom_ref):
    atom = atom_ref[0, 0]
    half = atom.shape[0] // 2
    return jnp.concatenate([atom[:half], atom[half:]], axis=1)


def crossed(left, right):
    half = left.shape[1] // 2
    parts = [left[:, :half], right[:, :half], left[:, half:], right[:, half:]]
    return jnp.concatenate(parts, axis=1)


def two_blocks(weight):
    blank = jnp.zeros_like(weight)
    return jnp.concatenate([crossed(weight, blank), crossed(blank, weight)], axis=0)


def diagonal_blocks(weight):
    blank = jnp.zeros_like(weight)
    return jnp.concatenate(
        [jnp.concatenate([weight, blank], axis=1), jnp.concatenate([blank, weight], axis=1)],
        axis=0,
    )


def angular_kernel(atoms, dirs_ref, angle_ref, *refs):
    sources, angular_ref, results, held, sems = refs[:7], refs[7], refs[8:16], refs[16:23], refs[23]
    copies = [
        pltpu.make_async_copy(source, target, sems.at[k])
        for k, (source, target) in enumerate(zip(sources, held))
    ]
    for copy in copies:
        copy.start()
    slots, pairs, _ = angular_ref.shape
    bonds = 2 * pairs
    degrees = angle_ref.shape[0]
    weight = two_blocks(angle_ref[...].astype(F32)).astype(BF16)
    polar, azimuth = dirs_ref[0, 0], dirs_ref[1, 0]
    unit = jnp.concatenate(
        [
            jnp.sin(polar) * jnp.cos(azimuth),
            jnp.sin(polar) * jnp.sin(azimuth),
            jnp.cos(polar),
            jnp.zeros((5, bonds), F32),
        ],
        axis=0,
    )
    high = unit.astype(BF16).astype(F32)
    middle = (unit - high).astype(BF16).astype(F32)
    parts = jnp.concatenate([high, middle, unit - high - middle], axis=0).astype(BF16)
    bond = lax.broadcasted_iota(jnp.int32, (1, bonds), 1)
    source = remainder(bond, atoms) * slots + slot_at(quotient(bond, atoms), slots)
    spot = lax.broadcasted_iota(jnp.int32, (bonds, bonds), 0)
    chosen = jnp.where(spot == source, 1.0, 0.0).astype(BF16)
    unit = jnp.dot(parts, chosen, preferred_element_type=F32)
    unit = unit[0:8] + unit[8:16] + unit[16:24]
    even = [jnp.broadcast_to(unit[k : k + 1, :pairs], (8, pairs)) for k in range(3)]
    odd = [jnp.broadcast_to(unit[k : k + 1, pairs:], (8, pairs)) for k in range(3)]
    row = lax.broadcasted_iota(jnp.int32, (8, pairs), 0)

    def turned(vector, places):
        places = places % (pairs // atoms)
        if places == 0:
            return vector
        return [pltpu.roll(part, pairs - atoms * places, 1) for part in vector]

    def basis(first, second):
        cosine = first[0] * second[0] + first[1] * second[1] + first[2] * second[2]
        series = [jnp.ones_like(cosine), cosine]
        double = cosine + cosine
        for _ in range(7):
            series.append(double * series[-1] - series[-2])
        lower = series[7]
        upper = series[1]
        for index in range(1, 8):
            lower = jnp.where(row == index, series[7 - index], lower)
            upper = jnp.where(row == index, series[1 + index], upper)
        double = series[8] + series[8]
        blocks = [lower, upper]
        for _ in range(degrees // 8 - 1):
            blocks.append(double * blocks[-1] - blocks[-2])
        return blocks[1:]

    for diagonal in range(slots):
        places = diagonal // 2
        if diagonal % 2 == 0:
            blocks = basis(even, turned(even, places)) + basis(odd, turned(odd, places))
        else:
            blocks = basis(even, turned(odd, places)) + basis(odd, turned(even, places + 1))
        series = jnp.concatenate(blocks, axis=0).T.astype(BF16)
        angular_ref[diagonal] = jnp.dot(series, weight, preferred_element_type=F32)
    for copy in copies:
        copy.wait()
    prepare_weights(slots, held, results)


def prepare_weights(slots, held, results):
    bond_in_ref, bond_mix_ref, pair_ref, pair_hidden_ref, pair_out_ref, atom_in_ref = held[:6]
    atom_out_ref = held[6]
    bond_weight_ref, mix_weight_ref, pair_weight_ref, hidden_weight_ref = results[:4]
    out_weight_ref, atom_in_weight_ref, sum_weight_ref, atom_out_weight_ref = results[4:]
    feature = bond_mix_ref.shape[0]
    weight = bond_in_ref[...].astype(F32)
    source, other, bond_part = (weight[k * feature : (k + 1) * feature] for k in range(3))
    blank = jnp.zeros_like(source)
    away = [crossed(bond_part, blank), crossed(source, other)]
    near = [crossed(other, source), crossed(blank, bond_part)]
    bond_weight_ref[...] = jnp.concatenate(away + near, axis=0).astype(BF16)
    mix_weight_ref[...] = diagonal_blocks(bond_mix_ref[...].astype(F32)).astype(BF16)
    old = pair_ref[...].astype(F32) * 0.5
    hidden = jnp.dot(bond_mix_ref[...], pair_ref[...], preferred_element_type=F32) * 0.5
    weight = jnp.concatenate([hidden, hidden, old, old], axis=0).astype(BF16)
    pair_weight_ref[...] = jnp.concatenate(
        [two_blocks(weight[:, : 2 * feature]), two_blocks(weight[:, 2 * feature :])], axis=1
    )
    hidden_weight_ref[...] = two_blocks(pair_hidden_ref[...].astype(F32)).astype(BF16)
    out_weight_ref[...] = diagonal_blocks(pair_out_ref[...].astype(F32)).astype(BF16)
    weight = atom_in_ref[...].astype(F32)
    weight = crossed(weight, jnp.zeros_like(weight))
    mean = weight[feature:] * (1.0 / slots)
    atom_in_weight_ref[...] = jnp.concatenate([weight[:feature], mean, mean], axis=0).astype(BF16)
    folded = jnp.dot(
        pair_out_ref[...], mean.astype(BF16), preferred_element_type=F32
    )
    high = folded.astype(BF16)
    low = (folded - high.astype(F32)).astype(BF16)
    sum_weight_ref[...] = jnp.concatenate([high, high, low, low], axis=0)
    weight = atom_out_ref[...].astype(F32)
    blank = jnp.zeros_like(weight)
    weight = jnp.concatenate([weight, blank], axis=1)
    atom_out_weight_ref[...] = jnp.concatenate([weight, jnp.zeros_like(weight)], axis=0).astype(
        BF16
    )


def prepare_kernel(
    extents,
    paired,
    spot_ref,
    targets_ref,
    atom_ref,
    bond_ref,
    dirs_hbm,
    angle_hbm,
    near_ref,
    chosen_ref,
    right_ref,
    own_ref,
    dirs_ref,
    angle_ref,
    sems,
):
    copies = [
        pltpu.make_async_copy(source, target, sems.at[k])
        for k, (source, target) in enumerate(((dirs_hbm, dirs_ref), (angle_hbm, angle_ref)))
    ]
    for copy in copies:
        copy.start()
    atoms, feature = atom_ref.shape[2], atom_ref.shape[3]
    slots = targets_ref.shape[0]
    bonds = slots * atoms
    near_ref[: 3 * CAP // 2] = packed_rows(spot_ref[...], bond_ref, slots, 3 * CAP // 2)
    near_ref[3 * CAP // 2 :] = atom_rows(atom_ref)
    targets = bond_row(targets_ref[...])
    code_x, code_y = bond_codes(targets, atoms, extents, paired, True)
    code = 3 * code_x + code_y
    bond = lax.broadcasted_iota(jnp.int32, (1, bonds), 1)
    far_slot = slots - 1 - slot_at(quotient(bond, atoms), slots)
    far_atom = remainder(targets, atoms)
    far = (remainder(far_slot, 2) * (slots // 2) + quotient(far_slot, 2)) * atoms + far_atom
    base = (code * bonds).astype(F32)
    key = base + far.astype(F32)

    def column(values):
        return jnp.broadcast_to(values.astype(F32), (128, bonds)).T

    keys = column(key)
    place = []
    for group in range(bonds // 128):
        here = slice(group * 128, (group + 1) * 128)
        inside = (keys < key[:, here]) & (keys >= base[:, here])
        place.append(jnp.sum(jnp.where(inside, 1.0, 0.0), axis=0, keepdims=True))
    place = jnp.concatenate(place, axis=1).astype(jnp.int32)
    half, tall = CAP // 2, atoms // 2
    bond_spot = column(half * code + remainder(place, half))
    atom_spot = column(9 * half + tall * code + remainder(far_atom, tall))
    right = (column(quotient(place, half)), column(quotient(far_atom, tall)))
    right_ref[...] = jnp.where(left_lanes((bonds, 128)), right[0], right[1])
    total = 9 * half + 9 * tall
    for start in range(0, total, 128):
        width = min(128, total - start)
        spot = lax.broadcasted_iota(jnp.int32, (bonds, 128), 1).astype(F32) + float(start)
        chosen = jnp.where((spot == bond_spot) | (spot == atom_spot), 1.0, 0.0).astype(BF16)
        chosen_ref[:, start : start + width] = chosen[:, :width]

    atom = atom_ref[0, 0]
    blocks = blocks_of(bond_ref, slots // 2)
    own = [jnp.concatenate([atom, x[:, :feature]], axis=1) for x in blocks]
    own += [jnp.concatenate([atom, x[:, feature:]], axis=1) for x in blocks]
    own = jnp.concatenate(own, axis=0)
    own_ref[...] = own
    for copy in copies:
        copy.wait()


def gated(values):
    half = values.shape[1] // 2
    first, second = values[:, :half], values[:, half:]
    return first * jax.nn.sigmoid(first) * jax.nn.sigmoid(second)


def main_kernel(
    near_ref,
    up_ref,
    down_ref,
    two_ref,
    one_ref,
    angular_ref,
    chosen_ref,
    right_ref,
    own_ref,
    bond_weight_ref,
    mix_weight_ref,
    pair_weight_ref,
    hidden_weight_ref,
    out_weight_ref,
    atom_in_weight_ref,
    sum_weight_ref,
    atom_out_weight_ref,
    atom_result_hbm,
    bond_result_hbm,
    atom_result_ref,
    bond_result_ref,
    first_ref,
    second_ref,
    pair_ref,
    sems,
):
    slots, pairs, _ = angular_ref.shape
    bonds = 2 * pairs
    atoms = bonds // slots
    feature = own_ref.shape[1] // 2
    width = 2 * feature
    half = CAP // 2
    near_refs = (near_ref, up_ref, down_ref)
    away_refs = (one_ref, two_ref)
    sent = [ref[:half] for ref in near_refs] + [ref[: 3 * half] for ref in away_refs]
    sent = jnp.concatenate(sent, axis=0)
    sent_atom = jnp.concatenate([ref[3 * half :] for ref in near_refs + away_refs], axis=0)
    blank = jnp.zeros((sent.shape[0], feature), BF16)
    blank_atom = jnp.zeros((sent_atom.shape[0], feature), BF16)
    received = jnp.concatenate(
        [
            jnp.concatenate([sent[:, :feature], blank, sent[:, feature:], blank], axis=1),
            jnp.concatenate(
                [blank_atom, sent_atom[:, :feature], blank_atom, sent_atom[:, feature:]], axis=1
            ),
        ],
        axis=0,
    )
    far = jnp.dot(chosen_ref[...], received, preferred_element_type=F32)
    far = jnp.where(right_ref[...] > 0.0, far[:, width:], far[:, :width])
    own = own_ref[...]
    incoming = jnp.dot(
        jnp.concatenate([far.astype(BF16), own], axis=1),
        bond_weight_ref[...],
        preferred_element_type=F32,
    )
    hidden = gated(incoming).astype(BF16)
    old = jnp.where(left_lanes((bonds, width)), far, own.astype(F32))
    both = jnp.concatenate([hidden, old.astype(BF16)], axis=1)
    even, odd = both[:pairs], both[pairs:]
    projected = jnp.dot(
        jnp.concatenate([even, odd], axis=1), pair_weight_ref[...], preferred_element_type=F32
    )
    first_ref[...] = projected[:, : 2 * width]
    second_ref[0] = projected[:, 2 * width :]
    shifted = jnp.concatenate([even[atoms:], even[:atoms]], axis=0)
    second_ref[1] = jnp.dot(
        jnp.concatenate([odd, shifted], axis=1),
        pair_weight_ref[:, 2 * width :],
        preferred_element_type=F32,
    )
    mixed = jnp.dot(hidden, mix_weight_ref[...], preferred_element_type=F32)
    new = (old + mixed).astype(BF16).astype(F32)
    average = ((new + pltpu.roll(new, feature, 1)) * 0.5).astype(BF16).astype(F32)
    packed = jnp.where(left_lanes((pairs, width)), average[:pairs], average[pairs:])
    group = 2

    def first_gates(base):
        for start in range(0, pairs, atoms):
            here = first_ref[pl.ds(start, atoms)]
            for diagonal in range(base, base + group):
                there = (start + diagonal // 2 * atoms) % pairs
                mixture = angular_ref[diagonal, pl.ds(start, atoms)] + (
                    here + second_ref[diagonal % 2, pl.ds(there, atoms)]
                )
                pair_ref[pl.ds(diagonal * pairs + start, atoms)] = gated(mixture).astype(
                    BF16
                )

    def summed(rows):
        parts = [rows[k * atoms : (k + 1) * atoms] for k in range(slots // 2)]
        while len(parts) > 1:
            parts = [x + y for x, y in zip(parts[::2], parts[1::2])]
        return parts[0]

    atom = own[0:atoms]
    atom_incoming = jnp.dot(
        jnp.concatenate([atom[:, :feature], summed(packed).astype(BF16)], axis=1),
        atom_in_weight_ref[...],
        preferred_element_type=F32,
    )
    total = jnp.zeros((pairs, width), F32)
    first_gates(0)
    for base in range(0, slots, group):
        if base + group < slots:
            first_gates(base + group)
        second = jnp.dot(
            pair_ref[pl.ds(base * pairs, group * pairs)],
            hidden_weight_ref[...],
            preferred_element_type=F32,
        )
        gates = gated(second)
        for k in range(group):
            total = total + gates[k * pairs : (k + 1) * pairs]
    sums = summed(total).astype(BF16)
    atom_incoming = atom_incoming + jnp.dot(
        jnp.concatenate([sums, sums], axis=1), sum_weight_ref[...], preferred_element_type=F32
    )
    atom_hidden = gated(atom_incoming).astype(BF16)
    atom_new = atom.astype(F32) + jnp.dot(
        atom_hidden, atom_out_weight_ref[...], preferred_element_type=F32
    )
    atom_result_ref[0, 0] = atom_new[:, :feature].astype(BF16)
    copies = []
    copies.append(pltpu.make_async_copy(atom_result_ref, atom_result_hbm, sems.at[1]))
    copies[-1].start()
    height = pairs // 2
    for part in range(2):
        rows = slice(part * height, (part + 1) * height)
        bond_out = packed[rows] + jnp.dot(
            total[rows].astype(BF16), out_weight_ref[...], preferred_element_type=F32
        )
        bond_out = bond_out.astype(BF16)
        first = part * height // atoms
        count = height // atoms
        for k in range(count):
            place = (first + k) * width
            bond_result_ref[0, 0, :, place : place + width] = bond_out[k * atoms : (k + 1) * atoms]
        columns = pl.ds(first * width, count * width)
        source, target = (x.at[0, 0, :, columns] for x in (bond_result_ref, bond_result_hbm))
        copies.append(pltpu.make_async_copy(source, target, sems.at[2 * part]))
        copies[-1].start()
    for copy in copies:
        copy.wait()


def per_device(
    atom_feat,
    bond_feat,
    neighbours,
    bond_dirs,
    bond_in_weight,
    bond_mix_weight,
    pair_weight,
    angle_weight,
    pair_hidden_weight,
    pair_out_weight,
    atom_in_weight,
    atom_out_weight,
):
    atoms, feature = atom_feat.shape[2], atom_feat.shape[3]
    slots = neighbours.shape[3]
    bonds = atoms * slots
    pairs = bonds // 2
    half = CAP // 2
    extents = (lax.axis_size("gx"), lax.axis_size("gy"))
    paired = (extents[0] % 2 == 0, False)
    targets = neighbours[0, 0].T
    hbm = pl.BlockSpec(memory_space=pltpu.HBM)
    vmem = pl.BlockSpec(memory_space=pltpu.VMEM)
    params = pltpu.CompilerParams(vmem_limit_bytes=32 * 2**20)

    def shaped(shape, dtype):
        return jax.ShapeDtypeStruct(shape, dtype)

    def in_hbm(arrays):
        return tuple(pltpu.with_memory_space_constraint(x, pltpu.HBM) for x in arrays)

    payload = shaped((3 * half + atoms // 2, 2 * feature), BF16)
    inputs = (targets, atom_feat, bond_feat)
    up, down, *held = pl.pallas_call(
        functools.partial(pack_kernel, extents, paired),
        out_shape=(payload, payload, shaped((1, bonds), jnp.int32))
        + tuple(shaped(x.shape, x.dtype) for x in inputs),
        in_specs=[hbm] * 3,
        out_specs=(vmem,) * 6,
        scratch_shapes=[pltpu.SemaphoreType.DMA((3,))],
        compiler_params=params,
        name="pack",
    )(*in_hbm(inputs))
    first, second = moves(extents[1], paired[1])
    up = lax.ppermute(up, "gy", first)
    down = lax.ppermute(down, "gy", second)
    weights = (bond_in_weight, bond_mix_weight, pair_weight, pair_hidden_weight)
    weights += (pair_out_weight, atom_in_weight, atom_out_weight)
    near, *prepared, bond_dirs, angle_weight = pl.pallas_call(
        functools.partial(prepare_kernel, extents, paired),
        out_shape=(
            payload,
            shaped((bonds, 9 * half + 9 * atoms // 2), BF16),
            shaped((bonds, 2 * feature), F32),
            shaped((bonds, 2 * feature), BF16),
            shaped(bond_dirs.shape, F32),
            shaped(angle_weight.shape, BF16),
        ),
        in_specs=[vmem] * 4 + [hbm] * 2,
        out_specs=(vmem,) * 6,
        scratch_shapes=[pltpu.SemaphoreType.DMA((2,))],
        compiler_params=params,
        cost_estimate=pl.CostEstimate(flops=64 * 2**20, bytes_accessed=2**21, transcendentals=0),
        name="prepare",
    )(*held, *in_hbm((bond_dirs, angle_weight)))
    near, up, down, prepared = lax.optimization_barrier((near, up, down, prepared))
    first, second = moves(extents[0], paired[0])

    def forwarded(block):
        parts = [x[block * half : (block + 1) * half] for x in (near, up, down)]
        return jnp.concatenate(parts + [x[3 * half :] for x in (near, up, down)], axis=0)

    one = lax.ppermute(forwarded(1), "gx", first)
    two = lax.ppermute(forwarded(2), "gx", second)
    angular, *made = pl.pallas_call(
        functools.partial(angular_kernel, atoms),
        out_shape=(
            shaped((slots, pairs, 4 * feature), F32),
            shaped((4 * feature, 4 * feature), BF16),
            shaped((2 * feature, 2 * feature), BF16),
            shaped((8 * feature, 8 * feature), BF16),
            shaped((2 * feature, 4 * feature), BF16),
            shaped((2 * feature, 2 * feature), BF16),
            shaped((3 * feature, 4 * feature), BF16),
            shaped((4 * feature, 4 * feature), BF16),
            shaped((2 * feature, 2 * feature), BF16),
        ),
        in_specs=[vmem] * 2 + [hbm] * 7,
        out_specs=(vmem,) * 9,
        scratch_shapes=[pltpu.VMEM(x.shape, BF16) for x in weights]
        + [pltpu.SemaphoreType.DMA((7,))],
        compiler_params=params,
        cost_estimate=pl.CostEstimate(
            flops=256 * 2**20, bytes_accessed=2**22, transcendentals=4096
        ),
        name="angular",
    )(bond_dirs, angle_weight, *in_hbm(weights))
    return pl.pallas_call(
        main_kernel,
        out_shape=(shaped(atom_feat.shape, BF16), shaped(bond_feat.shape, BF16)),
        in_specs=[vmem] * 17,
        out_specs=(hbm, hbm),
        scratch_shapes=[
            pltpu.VMEM(atom_feat.shape, BF16),
            pltpu.VMEM(bond_feat.shape, BF16),
            pltpu.VMEM((pairs, 4 * feature), F32),
            pltpu.VMEM((2, pairs, 4 * feature), F32),
            pltpu.VMEM((slots * pairs, 2 * feature), BF16),
            pltpu.SemaphoreType.DMA((3,)),
        ],
        compiler_params=params,
        name="main",
    )(near, up, down, two, one, angular, *prepared, *made)


def solution(mesh):
    placed = (
        P("gx", "gy", None, None),
        P("gx", "gy", None, None),
        P("gx", "gy", None, None),
        P(None, "gx", "gy", None),
        P(),
        P(),
        P(),
        P(),
        P(),
        P(),
        P(),
        P(),
    )
    return jax.shard_map(
        per_device,
        mesh=mesh,
        in_specs=placed,
        out_specs=(P("gx", "gy", None, None), P("gx", "gy", None, None)),
        check_vma=False,
    )
```
